256 devices in a mesh: gx: 4 (over x), gy: 4 (over z_hi, core), gz: 16 (over z_lo, y).
Axes of the slice: x: 4, y: 4, z: 8 (z_hi: 2, z_lo: 4; z = z_hi * 4 + z_lo), core: 2. Of those that a mesh axis runs over, the one named last changes fastest.
Arguments:
- charges: float32 [98304, 128], P(('gx', 'gy', 'gz')), may hold values from -6 to 6
- counts: int32 [98304], P(('gx', 'gy', 'gz')), may hold values from 1 to 128
- slots: int32 [98304], P(('gx', 'gy', 'gz')), may hold values from 0 to 511, as said below
- spline: bfloat16 [98304, 3, 4, 128], P(('gx', 'gy', 'gz')), may hold values from 0.049804688 to 1
- kernel_fine: float32 [5, 5, 5], replicated, may hold values from -0.6 to 0.6
- kernel_mid: float32 [5, 5, 5], replicated, may hold values from -0.6 to 0.6
- kernel_coarse: float32 [5, 5, 5], replicated, may hold values from -0.6 to 0.6
Outputs:
- potential: float32 [128, 128, 512], P('gx', 'gy', 'gz')
The draws below stay inside these ranges and needn't reach their ends.
Inputs may be any that keep to these rules, and one draw needn't show every extreme that they name: Within the 384 cells of one grid block the slots are distinct.
All inputs are finite; a program needn't handle non-finite values.
Results may differ from the reference program's by a relative error of at most 0.0003.
Values sent between devices are 32-bit elements; how exact they have to be, the bound alone decides.
No kernel may reach another device: no remote copies, remote signals or barrier semaphores. Data moves between devices by JAX's collectives and lax.ppermute only.
A program may use at most 64 MiB of HBM per device.

```python
import jax
import jax.numpy as jnp
from jax import lax

ATOMS = 128
BX = 32
BY = 32
CELL_DEV = 384
BZ = 32
FX = 128
FY = 128
FZ = 512
CELLS = 98304
N_GY = 4
N_GZ = 16
DEVICES = 256


def draw_slots(key, part):
    key = jax.random.fold_in(key, 7)
    keys = jax.random.split(key, DEVICES)

    def one_device(device_key):
        return jax.random.permutation(device_key, BX // 4 * (BY // 4) * (BZ // 4))[:CELL_DEV]
    return jax.vmap(one_device)(keys).reshape(CELLS).astype(jnp.int32)


def with_ends(entries, rng, low, high):
    extent = entries.shape
    place = [jax.random.randint(jax.random.fold_in(rng, axis), (), 0, extent[axis]) for axis in range(len(extent))]
    entries = entries.at[tuple(place)].set(low)
    longest = extent.index(max(extent))
    place[longest] = (place[longest] + 1) % extent[longest]
    return entries.at[tuple(place)].set(high)


def levels(key, shape, pieces, low, largest):
    level = 1.0
    for position, shards_of in pieces:
        draws = jax.random.uniform(jax.random.fold_in(jax.random.fold_in(key, 6), position), (shards_of,), jnp.float32, low / len(pieces), largest / len(pieces))
        level = level * jnp.repeat(jnp.exp(draws), shape[position] // shards_of).reshape((-1,) + (1,) * (len(shape) - 1 - position))
    return level


def scatter_about(stream_key, extent, scale, reach, cuts=(), kind=jnp.bfloat16):
    loudness = levels(stream_key, extent, cuts, -0.22, 0.18) if cuts else 1.0
    drawn = jax.random.normal(stream_key, extent, jnp.float32) * scale * loudness
    return jnp.minimum(jnp.maximum(drawn, -reach), reach).astype(kind)


def setup_inputs(seed: int = 0) -> dict:
    streams_of = jax.random.split(jax.random.key(seed), 8)
    return {
        "charges": scatter_about(streams_of[0], (CELLS, ATOMS), 1.0, 6.0, ((0, 256),), jnp.float32),
        "counts": with_ends(jax.random.randint(streams_of[1], (CELLS,), 1, ATOMS + 1), jax.random.fold_in(streams_of[1], 1), 1, ATOMS).astype(jnp.int32),
        "slots": draw_slots(jax.random.fold_in(streams_of[7], 71), 0),
        "spline": jnp.clip(0.049804688 + 0.9501953 * jax.random.uniform(streams_of[3], (CELLS, 3, 4, ATOMS), jnp.float32) ** levels(streams_of[3], (CELLS, 3, 4, ATOMS), ((0, 256),), -0.2, 0.2), 0.049804688, 1.0).astype(jnp.bfloat16),
        "kernel_fine": scatter_about(streams_of[4], (5, 5, 5), 0.1, 0.6, (), jnp.float32),
        "kernel_mid": scatter_about(streams_of[5], (5, 5, 5), 0.1, 0.6, (), jnp.float32),
        "kernel_coarse": scatter_about(streams_of[6], (5, 5, 5), 0.1, 0.6, (), jnp.float32),
    }


WEIGHTS = (0.125, 0.5, 0.75, 0.5, 0.125)
PRECISION_HIGH = lax.Precision.HIGHEST

def pad_along(values, along, margin):
    spec = [(0, 0)] * values.ndim
    spec[along] = (margin, margin)
    return jnp.pad(values, spec)

def restrict_along(values, along):
    padded = pad_along(values, along, 2)
    amount = values.shape[along] // 2
    summed = WEIGHTS[0] * lax.slice_in_dim(padded, 0, 2 * amount - 1, 2, along)
    for shift_amount in range(1, 5):
        summed = summed + WEIGHTS[shift_amount] * lax.slice_in_dim(padded, shift_amount, shift_amount + 2 * amount - 1, 2, along)
    return summed

def restrict_grid(values):
    return restrict_along(restrict_along(restrict_along(values, 0), 1), 2)

def prolong_framed(framed, along):
    length = framed.shape[along]
    middle = lax.slice_in_dim(framed, 1, length - 1, 1, along)
    lowered = lax.slice_in_dim(framed, 0, length - 2, 1, along)
    raised = lax.slice_in_dim(framed, 2, length, 1, along)
    even_rows = 0.75 * middle + 0.125 * (lowered + raised)
    odd_rows = 0.5 * (middle + raised)
    joined = jnp.stack([even_rows, odd_rows], axis=along + 1)
    target = list(middle.shape)
    target[along] = 2 * target[along]
    return joined.reshape(target)

def prolong_grid(values):
    for along in range(3):
        values = prolong_framed(pad_along(values, along, 1), along)
    return values

def near_field(values, kernel):
    padded = jnp.pad(values, 2)
    size_x, size_y, size_z = values.shape
    summed = jnp.zeros(values.shape, jnp.float32)
    for shift_x in range(5):
        for shift_y in range(5):
            for shift_z in range(5):
                summed = summed + kernel[shift_x, shift_y, shift_z] * padded[shift_x:shift_x + size_x, shift_y:shift_y + size_y, shift_z:shift_z + size_z]
    return summed

def green_block(target_x, target_y, target_z, source, flat):
    delta = target_x[:, None] - source[0][None, :]
    dist = delta * delta
    delta = target_y[:, None] - source[1][None, :]
    dist = dist + delta * delta
    delta = target_z[:, None] - source[2][None, :]
    dist = dist + delta * delta
    green = 0.0625 / jnp.sqrt(1.0 + dist)
    return jnp.dot(green, flat, precision=PRECISION_HIGH)

def top_level(coarse):
    size_x, size_y, size_z = coarse.shape
    points = size_x * size_y * size_z
    flat = coarse.reshape(points)
    indices = jnp.arange(points, dtype=jnp.int32)
    source = jnp.stack([indices // (size_y * size_z), indices // size_z % size_y, indices % size_z]).astype(jnp.float32)
    block_len = min(1024, points)
    blocked = source.reshape(3, points // block_len, block_len).transpose(1, 0, 2)

    def one_block(target):
        return green_block(target[0], target[1], target[2], source, flat)
    return lax.map(one_block, blocked).reshape(size_x, size_y, size_z)

def deposit(charges, counts, slots, spline):
    live = (lax.broadcasted_iota(jnp.int32, charges.shape, 1) < counts[:, None]).astype(jnp.float32)
    weighted = charges * live
    splines = spline.astype(jnp.float32)
    local_patches = jnp.einsum('ca,cia,cja,cka->cijk', weighted, splines[:, 0], splines[:, 1], splines[:, 2], precision=PRECISION_HIGH)
    cell_ids = jnp.arange(CELLS, dtype=jnp.int32)
    device = cell_ids // CELL_DEV
    block_x = device // (N_GY * N_GZ)
    block_y = device // N_GZ % N_GY
    block_z = device % N_GZ
    per_y = BY // 4
    per_z = BZ // 4
    base_x = block_x * BX + 4 * (slots // (per_y * per_z))
    base_y = block_y * BY + 4 * (slots // per_z % per_y)
    base_z = block_z * BZ + 4 * (slots % per_z)
    steps = jnp.arange(4, dtype=jnp.int32)
    shape = (CELLS, 4, 4, 4)
    x_index_grid = jnp.broadcast_to(base_x[:, None, None, None] + steps[None, :, None, None], shape)
    index_y = jnp.broadcast_to(base_y[:, None, None, None] + steps[None, None, :, None], shape)
    index_z = jnp.broadcast_to(base_z[:, None, None, None] + steps[None, None, None, :], shape)
    return jnp.zeros((FX, FY, FZ), jnp.float32).at[x_index_grid, index_y, index_z].add(local_patches)

def reference(charges, counts, slots, spline, kernel_fine, kernel_mid, kernel_coarse):
    first = deposit(charges, counts, slots, spline)
    second = restrict_grid(first)
    third = restrict_grid(second)
    fourth = restrict_grid(third)
    top = top_level(fourth)
    third_total = near_field(third, kernel_coarse) + prolong_grid(top)
    second_total = near_field(second, kernel_mid) + prolong_grid(third_total)
    return near_field(first, kernel_fine) + prolong_grid(second_total)
```

```python
import jax
import jax.numpy as jnp
import numpy as np
from jax import lax
from jax.experimental import pallas as pl
from jax.experimental.pallas import tpu as pltpu
from jax.sharding import PartitionSpec as P

W = (0.125, 0.5, 0.75, 0.5, 0.125)
F32 = jnp.float32
BF16 = jnp.bfloat16
CELLS = 384
ATOMS = 128
SPAN_2 = 18
SPAN_3 = 11
SPAN_4 = 7
SEC = 32
THI = 64
VMEM = pl.BlockSpec(memory_space=pltpu.VMEM)
SMEM = pl.BlockSpec(memory_space=pltpu.SMEM)


def weight(t):
    return W[t] if 0 <= t <= 4 else 0.0


def table(rows, columns, offset, turned):
    out = np.zeros((128, 128), np.float32)
    for r in range(rows):
        for c in range(columns):
            out[r, c] = weight(c - 2 * r + offset if turned else r - 2 * c + offset)
    return out


REST_2 = table(32, SPAN_2, 4, False)
REST_3 = table(SPAN_2, SPAN_3, 3, False)
PROL_2 = table(SPAN_3, SPAN_2, 3, True)
PROL_1 = table(SPAN_2, 32, 4, True)


def near_codes(shape, mains, lows, highs, group, outs):
    codes = np.full(shape, 99, np.int32)
    for start, count, first in (mains, lows, highs):
        for a in range(5):
            for k in range(count):
                for b in range(5):
                    for zo in range(outs):
                        c = first + k - zo
                        if 0 <= c <= 4:
                            codes[start + a * count + k, b * group + zo] = 5 * a + c
    return codes


CODES_1 = near_codes((256, 256), (0, 32, 2), (160, 2, 0), (192, 2, 34), 32, 32)
CODES_2 = near_codes((256, 128), (0, 18, 2), (128, 4, 0), (160, 4, 18), 24, 18)
CODES_3 = near_codes((128, 128), (0, 11, 2), (64, 5, 0), (96, 5, 10), 16, 11)


def spread_table():
    out = np.zeros((512, 64), np.float32)
    for r in range(512):
        out[r, r // 32 * 4 + r % 4] = 1.0
    return out


def composite(first, last):
    p3 = np.array([[weight(i - 2 * j + 3) for j in range(7)] for i in range(11)])
    p2 = np.array([[weight(i - 2 * j + 3) for j in range(11)] for i in range(18)])
    p1 = np.array([[weight(i - 2 * j + 4) for j in range(18)] for i in range(32)])
    m4, m3, m2 = np.ones(7), np.ones(11), np.ones(18)
    if first:
        m4[0] = m3[0] = m2[0] = 0
    if last:
        m4[5:] = 0
        m3[9:] = 0
        m2[17:] = 0
    return (p1 * m2) @ (p2 * m3) @ (p3 * m4)


def composites():
    qx = np.zeros((4, 32, 8), np.float32)
    qy = np.zeros((4, 32, 128), np.float32)
    qz = np.zeros((4, 128, 128), np.float32)
    for v in range(4):
        q = composite(v % 2 == 1, v >= 2)
        qx[v, :, :7] = q
        for lane in range(64):
            if lane // 8 < 7:
                qy[v, :, lane] = q[:, lane // 8]
            if lane % 8 < 7:
                qz[v, lane, :32] = q[:, lane % 8]
    return qx, qy, qz


def split(x):
    high = x.astype(BF16)
    return high, (x - high.astype(F32)).astype(BF16)


def dot(a, b):
    return jnp.dot(a, b, preferred_element_type=F32)


def dot_exact(x, right):
    high, low = split(x)
    return dot(high, right) + dot(low, right)


def dot_split(x, right_high, right_low):
    high, low = split(x)
    return dot(high, right_high) + (dot(low, right_high) + dot(high, right_low))


def iota(shape, dim):
    return lax.broadcasted_iota(jnp.int32, shape, dim)


def roll(x, shift, axis=None):
    axis = x.ndim - 1 if axis is None else axis
    shift = shift % x.shape[axis]
    return x if shift == 0 else pltpu.roll(x, shift, axis)


def lanes_of(x, low, count):
    lane = iota(x.shape, x.ndim - 1)
    return jnp.where((lane >= low) & (lane < low + count), x, 0.0)


def as_rows(x):
    return x.reshape(x.shape[0] * x.shape[1], x.shape[2])


def taps(pieces):
    total = None
    for factor, value in pieces:
        term = value if factor == 1.0 else factor * value
        total = term if total is None else total + term
    return total


def restrict_planes(read, span, size, offset):
    planes = []
    for p in range(span):
        planes.append(
            taps([(W[t], read(2 * p + t - offset)) for t in range(5) if 0 <= 2 * p + t - offset < size])
        )
    return planes


def place():
    sizes = [lax.axis_size(a) for a in ("gx", "gy", "gz")]
    index = [lax.axis_index(a) for a in ("gx", "gy", "gz")]
    return index, sizes


def inside_mask(shape, spans, high, place_of):
    index, sizes = place_of
    keep = None
    for dim in range(3):
        at = iota(shape, dim)
        low = jnp.where(index[dim] == 0, 1, 0)
        top = jnp.where(index[dim] == sizes[dim] - 1, high, spans)
        part = (at >= low) & (at < top)
        keep = part if keep is None else keep & part
    return keep


def deposit_kernel(
    charges, counts, slots, spline, spread, rest_2, rest_3,
    packed, fourth, to_high, to_low,
    wide, patch, fine, buf_2, buf_3, buf_4,
):
    where = place()
    index, sizes = where
    wide[...] = spline[...].astype(F32)
    alive = iota((ATOMS, CELLS), 0) < counts[...]
    weighted = jnp.where(alive, charges[...].T, 0.0)
    for chunk in range(CELLS // 128):
        lanes = slice(128 * chunk, 128 * chunk + 128)

        def column(d, i):
            return wide[pl.ds(chunk * 128 * 12 + 4 * d + i, 128, stride=12), :].T

        charge = weighted[:, lanes]
        depth = [charge * column(2, k) for k in range(4)]
        ys = [column(1, j) for j in range(4)]
        for i in range(4):
            xs = column(0, i)
            for j in range(4):
                cross = xs * ys[j]
                for k in range(4):
                    patch[16 * i + 4 * j + k : 16 * i + 4 * j + k + 1, lanes] = jnp.sum(
                        cross * depth[k], axis=0, keepdims=True
                    )
    slot = slots[...]
    high, low = split(patch[...])
    fits = (iota((512, CELLS), 0) // 4 % 8) == slot % 8
    spread_high = jnp.where(fits, dot(spread[...], high), 0.0).astype(BF16)
    spread_low = jnp.where(fits, dot(spread[...], low), 0.0).astype(BF16)
    hot = (iota((64, CELLS), 0) == slot // 8).astype(BF16)
    nt = (((1,), (1,)), ((), ()))
    placed = lax.dot_general(hot, spread_high, nt, preferred_element_type=F32) + lax.dot_general(
        hot, spread_low, nt, preferred_element_type=F32
    )
    for i in range(4):
        for j in range(4):
            rows = lanes_of(roll(placed[:, 128 * i : 128 * i + 128], -32 * j), 0, 32)
            for sx in range(8):
                fine[4 * sx + i, pl.ds(j, 8, stride=4), :] = rows[8 * sx : 8 * sx + 8]

    buf_2[...] = jnp.zeros_like(buf_2)
    buf_3[...] = jnp.zeros_like(buf_3)
    buf_4[...] = jnp.zeros_like(buf_4)
    for p, plane in enumerate(restrict_planes(lambda x: fine[x], SPAN_2, 32, 4)):
        buf_2[p, 4:36, :] = plane
    second = taps([(W[t], buf_2[:, pl.ds(t, 24, stride=2), :]) for t in range(5)])
    second = dot_exact(as_rows(second), rest_2[...]).reshape(SPAN_2, 24, 128)
    second = jnp.where(inside_mask(second.shape, SPAN_2, 17, where), second, 0.0)
    for p, plane in enumerate(restrict_planes(lambda x: second[x], SPAN_3, SPAN_2, 3)):
        buf_3[p, 3:27, :] = plane
    third = taps([(W[t], buf_3[:, pl.ds(t, 16, stride=2), :]) for t in range(5)])
    third = dot_exact(as_rows(third), rest_3[...]).reshape(SPAN_3, 16, 128)
    third = jnp.where(inside_mask(third.shape, SPAN_3, 9, where), third, 0.0)
    for p, plane in enumerate(restrict_planes(lambda x: third[x], SPAN_4, SPAN_3, 3)):
        buf_4[p, 3:19, :] = plane
    last = taps([(W[t], buf_4[:, pl.ds(t, 8, stride=2), :]) for t in range(5)])
    row, column = iota((128, 128), 0), iota((128, 128), 1)
    t = 8 * index[2] + row + 1 - 2 * column
    rest_4 = jnp.zeros((128, 128), F32)
    for tap in range(5):
        rest_4 = jnp.where(t == tap, W[tap], rest_4)
    rest_4 = jnp.where((row < SPAN_3) & (column < 4 * sizes[2]), rest_4, 0.0).astype(BF16)
    last = dot_exact(as_rows(last), rest_4).reshape(SPAN_4, 8, 128)
    y_at = iota(last.shape, 1) + 4 * index[1] - 1
    x_at = iota(last.shape, 0) + 4 * index[0] - 1
    legal = (y_at >= 0) & (y_at < 4 * sizes[1]) & (x_at >= 0) & (x_at < 4 * sizes[0])
    last = jnp.where(legal & (iota(last.shape, 1) < SPAN_4), last, 0.0)
    halves = []
    for half in range(2):
        total = jnp.zeros_like(last)
        for by in range(sizes[1]):
            shift = 4 * by - 1 - 8 * half
            if -8 < shift < 8:
                moved = roll(last, shift, 1)
                at = iota(last.shape, 1)
                moved = jnp.where((at >= shift) & (at < 8 + shift), moved, 0.0)
                total = total + jnp.where(index[1] == by, moved, 0.0)
        halves.append(total)
    fourth[...] = halves[0] + roll(halves[1], 64)

    packed[...] = fine[...]
    packed[0:SPAN_2, 0:24, :] += roll(second, SEC)
    packed[0:SPAN_3, 0:16, :] += roll(third, THI)
    lane = iota((5, 32, 128), 2)
    to_low[...] = packed[0:5]
    to_high[...] = (
        jnp.where((lane >= SEC) & (lane < THI), packed[14:19], 0.0)
        + jnp.where(lane >= THI, packed[6:11], 0.0)
    )
    to_high[0:2] += lanes_of(packed[30:32], 0, 32)


def widen_x_kernel(packed, from_low, from_high, out, to_high, to_low):
    out[0:2] = jnp.zeros((2, 32, 128), F32)
    out[34:36] = jnp.zeros((2, 32, 128), F32)
    out[2:34] = packed[...]
    low, high = from_low[...], from_high[...]
    first = lanes_of(low[2:5], SEC, 96)
    out[0:2] = low[0:2]
    out[2:5] += first
    out[34:36] += lanes_of(high[0:2], 0, 32)
    out[18:22] += lanes_of(high[0:4], SEC, 32)
    out[10:15] += lanes_of(high, THI, 64)
    def pack(fine_at, second_at, third_at):
        def rows(start, count, first, planes, low, width):
            slab = out[first : first + planes, start : start + 8, :]
            row = iota(slab.shape, 1)
            return jnp.where(row < count, lanes_of(slab, low, width), 0.0)

        base = rows(fine_at, 2, 0, 18, 0, 32) + rows(second_at, 4, 0, 18, SEC, 32)
        base = base + rows(third_at, 5, 0, 18, THI, 32)
        other = roll(rows(fine_at, 2, 18, 18, 0, 32), 2, 1)
        extra = roll(rows(second_at, 4, 18, 4, SEC, 32), 64)
        return base + other, extra

    for ref, at in ((to_low, (0, 0, 0)), (to_high, (24, 14, 6))):
        if at[0] == 24:
            body, extra = pack_high(out)
        else:
            body, extra = pack(*at)
        ref[...] = body
        ref[0:4] += extra


def pack_high(out):
    def rows(start, count, skip, first, planes, low, width):
        slab = out[first : first + planes, start : start + 8, :]
        slab = roll(slab, -skip, 1)
        row = iota(slab.shape, 1)
        return jnp.where(row < count, lanes_of(slab, low, width), 0.0)

    base = rows(24, 2, 6, 0, 18, 0, 32) + rows(14, 4, 0, 0, 18, SEC, 32) + rows(6, 5, 0, 0, 18, THI, 32)
    other = roll(rows(24, 2, 6, 18, 18, 0, 32), 2, 1)
    extra = roll(rows(14, 4, 0, 18, 4, SEC, 32), 64)
    return base + other, extra


def widen_y_kernel(wide_x, from_low, from_high, out, to_high, to_low):
    out[...] = jnp.zeros_like(out)
    out[:, 2:34, :] = wide_x[...]

    def parts(ref):
        body = ref[...]
        row = iota(body.shape, 1)
        fine_low = jnp.where(row < 2, lanes_of(body, 0, 32), 0.0)
        fine_far = roll(lanes_of(body, 0, 32), -2, 1)
        fine_far = jnp.where(row < 2, fine_far, 0.0)
        second = lanes_of(body, SEC, 32)
        far = lanes_of(roll(body[0:4], -64), SEC, 32)
        third = lanes_of(body, THI, 32)
        return fine_low, fine_far, second, far, third

    for ref, at in ((from_low, (0, 0, 0)), (from_high, (34, 18, 10))):
        fine_low, fine_far, second, far, third = parts(ref)
        out[0:18, at[0] : at[0] + 2, :] += fine_low[:, 0:2]
        out[18:36, at[0] : at[0] + 2, :] += fine_far[:, 0:2]
        out[0:18, at[1] : at[1] + 4, :] += second[:, 0:4]
        out[18:22, at[1] : at[1] + 4, :] += far[:, 0:4]
        out[0:18, at[2] : at[2] + 5, :] += third[:, 0:5]

    for ref, at in ((to_low, (0, 0, 0)), (to_high, (30, 14, 6))):
        for base, rows, planes, count, start in (
            (0, 40, 36, 2, at[0]),
            (40, 24, 22, 4, SEC + at[1]),
            (64, 16, 15, 5, THI + at[2]),
        ):
            total = jnp.zeros((rows, 128), F32)
            for x in range(planes):
                total = total + lanes_of(roll(out[x, 0:rows, :], count * x - start), count * x, count)
            ref[base : base + rows, :] = total


def build_bands(kernel, codes):
    lanes = codes.shape[1]
    group = {256: 32, 128: 24}[lanes] if codes.shape[0] == 256 else 16
    block = iota((8, lanes), 1) // group
    total = jnp.zeros(codes.shape, F32)
    code = codes[...]
    for a in range(5):
        for c in range(5):
            row = jnp.zeros((8, lanes), F32)
            for b in range(5):
                row = jnp.where(block == b, kernel[a, b, c], row)
            total = jnp.where(code == 5 * a + c, row[0:1], total)
    return split(total)


def tables_kernel(
    after, kernel_1, kernel_2, kernel_3, codes_1, codes_2, codes_3,
    green_high, green_low, b1h, b1l, b2h, b2l, b3h, b3l,
):
    index, sizes = place()
    for kernel, codes, high_ref, low_ref in (
        (kernel_1, codes_1, b1h, b1l),
        (kernel_2, codes_2, b2h, b2l),
        (kernel_3, codes_3, b3h, b3l),
    ):
        high, low = build_bands(kernel, codes)
        high_ref[...] = high
        low_ref[...] = low
    row, lane = iota((128, 128), 0), iota((128, 128), 1)
    target_y = 4 * index[1] - 1 + lane // 8 % 8
    target_z = 4 * index[2] - 1 + lane % 8
    delta_z = (target_z - row % 64).astype(F32)
    plain = delta_z * delta_z + 1.0
    for s in range(8):
        delta_y = (target_y - (s + 8 * (row // 64))).astype(F32)
        base = plain + delta_y * delta_y
        for pair in range(8):
            delta_x = (2 * pair + lane // 64).astype(F32)
            green = 0.0625 * lax.rsqrt(base + delta_x * delta_x)
            high, low = split(green)
            green_high[128 * s : 128 * s + 128, 128 * pair : 128 * pair + 128] = high
            green_low[128 * s : 128 * s + 128, 128 * pair : 128 * pair + 128] = low


def prolong_rows(source, target, count, whole):
    size = target.shape[1] // 2
    q0 = source[:, 0:size, :]
    q1 = source[:, 1 : size + 1, :]
    q2 = source[:, 2 : size + 2, :]
    even = 0.75 * q1 + 0.125 * (q0 + q2)
    odd = 0.5 * (q0 + q1) if whole else 0.5 * (q1 + q2)
    target[:, pl.ds(1 if whole else 0, size, stride=2), :] = even
    target[:, pl.ds(0 if whole else 1, size, stride=2), :] = odd


def prolong_plane(read, p, whole):
    half = p // 2
    if (p % 2 == 1) == whole:
        return 0.75 * read(half + 1) + 0.125 * (read(half) + read(half + 2))
    first = half if whole else half + 1
    return 0.5 * (read(first) + read(first + 1))


def near_kernel(
    wide, from_low, from_high, b1h, b1l, b2h, b2l, b3h, b3l, prol_2, prol_1,
    out,
    near_1, near_2, near_3, tall_3, tall_3y, tall_2, tall_2y,
):
    where = place()
    low_msg, high_msg = from_low[...], from_high[...]

    def halo(x, rows, base, count, low_at, high_at):
        low = roll(low_msg[base : base + rows], low_at - count * x)
        high = roll(high_msg[base : base + rows], high_at - count * x)
        return lanes_of(low, low_at, 5 * count) + lanes_of(high, high_at, 5 * count)

    planes = [lanes_of(wide[x, 0:16, :], THI, 11) for x in range(15)]
    left = []
    for x in range(SPAN_3):
        main = taps([(1.0, roll(planes[x + a], 11 * a - THI)) for a in range(5)])
        left.append(main + halo(x, 16, 64, 5, 64, 96))
    left = jnp.concatenate(left, axis=0)
    near_3[...] = jnp.zeros_like(near_3)
    near_3[:, 0:16, :] = dot_split(left, b3h[...], b3l[...]).reshape(SPAN_3, 16, 128)
    third = taps([(1.0, roll(near_3[:, b : b + 16, :], -16 * b)) for b in range(5)])
    third = jnp.where(inside_mask(third.shape, SPAN_3, 9, where), third, 0.0)
    tall_3[...] = jnp.zeros_like(tall_3)
    tall_3[:, 0:16, :] = dot_exact(as_rows(third), prol_2[...]).reshape(SPAN_3, 16, 128)
    prolong_rows(tall_3, tall_3y, SPAN_2, True)

    planes = [lanes_of(wide[x, 0:24, :], SEC, 18) for x in range(22)]
    left_a, left_b = [], []
    for x in range(SPAN_2):
        left_a.append(taps([(1.0, roll(planes[x + a], 18 * a - SEC)) for a in range(5)]))
        left_b.append(halo(x, 24, 40, 4, 0, 32))
    left = jnp.concatenate(
        [jnp.concatenate(left_a, axis=0), jnp.concatenate(left_b, axis=0)], axis=1
    )
    near_2[...] = jnp.zeros_like(near_2)
    near_2[:, 0:24, :] = dot_split(left, b2h[...], b2l[...]).reshape(SPAN_2, 24, 128)
    second = taps([(1.0, roll(near_2[:, b : b + 24, :], -24 * b)) for b in range(5)])
    raised = jnp.stack(
        [prolong_plane(lambda x: tall_3y[x], p, True) for p in range(SPAN_2)], axis=0
    )
    second = jnp.where(inside_mask(second.shape, SPAN_2, 17, where), second + raised, 0.0)
    tall_2[...] = jnp.zeros_like(tall_2)
    tall_2[:, 0:24, :] = dot_exact(as_rows(second), prol_1[...]).reshape(SPAN_2, 24, 128)
    prolong_rows(tall_2, tall_2y, 32, False)

    planes = [lanes_of(wide[x], 0, 32) for x in range(36)]
    left_a, left_b = [], []
    for x in range(32):
        left_a.append(taps([(1.0, roll(planes[x + a], 32 * a)) for a in range(4)]))
        left_b.append(planes[x + 4] + halo(x, 40, 0, 2, 32, 64))
    left = jnp.concatenate(
        [jnp.concatenate(left_a, axis=0), jnp.concatenate(left_b, axis=0)], axis=1
    )
    near_1[...] = dot_split(left, b1h[...], b1l[...]).reshape(32, 40, 256)
    for x in range(32):
        first = taps(
            [(1.0, roll(near_1[x, b : b + 32, 0:128], -32 * b)) for b in range(4)]
            + [(1.0, near_1[x, 4:36, 128:256])]
        )
        out[x] = first + prolong_plane(lambda q: tall_2y[q], x, False)


def top_kernel(
    base, piece_0, piece_1, piece_2, piece_3, green_high, green_low, qx, qy, qz_high, qz_low,
    out,
    fourth,
):
    index, sizes = place()
    fourth[...] = jnp.zeros_like(fourth)
    for step, piece in enumerate((piece_0, piece_1, piece_2, piece_3)[: sizes[0]]):
        source = jnp.bitwise_xor(index[0], step)
        for r in range(SPAN_4):
            at = 4 * source + 3 + r
            fourth[at] = fourth[at] + piece[r]
    total = jnp.zeros((32, 1024), F32)
    extra = jnp.zeros((16, 1024), F32)
    for s in range(0, 8, 2):
        left = jnp.concatenate([fourth[4:20, s, :], fourth[4:20, s + 1, :]], axis=1)
        high, low = split(left)
        rows = slice(128 * s, 128 * s + 256)
        total = total + dot(jnp.concatenate([high, low], axis=0), green_high[rows, :])
        extra = extra + dot(high, green_low[rows, :])
    sums = total[0:16] + (total[16:32] + extra)
    row, lane = iota((16, 128), 0), iota((16, 128), 1)
    tops = []
    target_y = 4 * index[1] - 1 + lane // 8 % 8
    target_z = 4 * index[2] - 1 + lane % 8
    legal = (target_y >= 0) & (target_y < 4 * sizes[1]) & (target_z >= 0) & (target_z < 4 * sizes[2])
    legal = legal & (lane < 64)
    for tx in range(SPAN_4):
        target_x = 4 * index[0] - 1 + tx
        apart = jnp.abs(target_x - row)
        picked = jnp.zeros((16, 128), F32)
        for pair in range(8):
            picked = jnp.where(
                apart == 2 * pair + lane // 64, sums[:, 128 * pair : 128 * pair + 128], picked
            )
        picked = picked + roll(picked, 64)
        fits = legal & (target_x >= 0) & (target_x < 4 * sizes[0])
        tops.append(jnp.sum(jnp.where(fits, picked, 0.0), axis=0, keepdims=True))
    variant = [
        jnp.where(index[d] == 0, 1, 0) + jnp.where(index[d] == sizes[d] - 1, 2, 0) for d in range(3)
    ]
    spread_x = qx[variant[0]]
    raised = None
    for tx in range(SPAN_4):
        term = spread_x[:, tx : tx + 1] * tops[tx]
        raised = term if raised is None else raised + term
    spread = raised[:, None, :] * qy[variant[1]][None, :, :]
    far = dot_split(as_rows(spread), qz_high[variant[2]], qz_low[variant[2]])
    out[...] = (base[...] + far.reshape(32, 32, 128))[:, :, 0:32]


def call(kernel, outs, ins, scratch=(), megabytes=16, flops=1000000, spaces=None):
    spaces = spaces or {}
    return pl.pallas_call(
        kernel,
        out_shape=outs,
        in_specs=[spaces.get(i, VMEM) for i in range(len(ins))],
        out_specs=jax.tree.map(lambda _: VMEM, outs),
        scratch_shapes=list(scratch),
        compiler_params=pltpu.CompilerParams(vmem_limit_bytes=megabytes * 2**20),
        cost_estimate=pl.CostEstimate(flops=flops, bytes_accessed=2**21, transcendentals=0),
    )(*ins)


def shape(*dims, dtype=F32):
    return jax.ShapeDtypeStruct(dims, dtype)


def halo_pair(to_high, to_low, axis):
    size = lax.axis_size(axis)
    up = [(i, i + 1) for i in range(size - 1)]
    down = [(i + 1, i) for i in range(size - 1)]
    return lax.ppermute(to_high, axis, up), lax.ppermute(to_low, axis, down)


def partners(value, axis, stride):
    size = lax.axis_size(axis)
    got = []
    for step in range(1, min(4, size // stride)):
        got.append(lax.ppermute(value, axis, [(i, i ^ (step * stride)) for i in range(size)]))
    return got


def shards(charges, counts, slots, spline, kernel_fine, kernel_mid, kernel_coarse):
    cells = charges.shape[0]
    table_shapes = (shape(*CODES_1.shape, dtype=BF16), shape(*CODES_2.shape, dtype=BF16), shape(*CODES_3.shape, dtype=BF16))
    packed, fourth, to_high, to_low = call(
        deposit_kernel,
        (shape(32, 32, 128), shape(SPAN_4, 8, 128), shape(5, 32, 128), shape(5, 32, 128)),
        (
            charges,
            counts.reshape(1, cells),
            slots.reshape(1, cells),
            spline.reshape(cells * 12, ATOMS),
            jnp.asarray(spread_table(), BF16),
            jnp.asarray(REST_2, BF16),
            jnp.asarray(REST_3, BF16),
        ),
        (
            pltpu.VMEM((cells * 12, 128), F32),
            pltpu.VMEM((64, cells), F32),
            pltpu.VMEM((32, 32, 128), F32),
            pltpu.VMEM((SPAN_2, 56, 128), F32),
            pltpu.VMEM((SPAN_3, 40, 128), F32),
            pltpu.VMEM((SPAN_4, 24, 128), F32),
        ),
    )
    value = fourth
    size_z = lax.axis_size("gz")
    stride = 1
    while stride < size_z:
        for got in partners(value, "gz", stride):
            value = value + got
        stride *= 4
    for got in partners(value, "gy", 1):
        value = value + got
    pieces = [value] + partners(value, "gx", 1)
    while len(pieces) < 4:
        pieces.append(value)
    from_low, from_high = halo_pair(to_high, to_low, "gx")
    wide_x, to_high, to_low = call(
        widen_x_kernel,
        (shape(36, 32, 128), shape(18, 8, 128), shape(18, 8, 128)),
        (packed, from_low, from_high),
    )
    from_low, from_high = halo_pair(to_high, to_low, "gy")
    wide_y, to_high, to_low = call(
        widen_y_kernel,
        (shape(36, 40, 128), shape(80, 128), shape(80, 128)),
        (wide_x, from_low, from_high),
    )
    from_low, from_high = halo_pair(to_high, to_low, "gz")
    tables = call(
        tables_kernel,
        (shape(1024, 1024, dtype=BF16), shape(1024, 1024, dtype=BF16))
        + tuple(s for s in table_shapes for _ in range(2)),
        (
            fourth, kernel_fine, kernel_mid, kernel_coarse,
            jnp.asarray(CODES_1), jnp.asarray(CODES_2), jnp.asarray(CODES_3),
        ),
        spaces={1: SMEM, 2: SMEM, 3: SMEM, 0: pl.BlockSpec(memory_space=pl.ANY)},
    )
    base = call(
        near_kernel,
        shape(32, 32, 128),
        (
            wide_y, from_low, from_high, *tables[2:],
            jnp.asarray(PROL_2, BF16), jnp.asarray(PROL_1, BF16),
        ),
        (
            pltpu.VMEM((32, 40, 256), F32),
            pltpu.VMEM((SPAN_2, 32, 128), F32),
            pltpu.VMEM((SPAN_3, 24, 128), F32),
            pltpu.VMEM((SPAN_3, 24, 128), F32),
            pltpu.VMEM((SPAN_3, 24, 128), F32),
            pltpu.VMEM((SPAN_2, 32, 128), F32),
            pltpu.VMEM((SPAN_2, 32, 128), F32),
        ),
    )
    qx, qy, qz = composites()
    qz_high = jnp.asarray(qz).astype(BF16)
    qz_low = jnp.asarray(qz - np.asarray(qz.astype(BF16)).astype(np.float32)).astype(BF16)
    return call(
        top_kernel,
        shape(32, 32, 32),
        (base, *pieces, *tables[:2], jnp.asarray(qx), jnp.asarray(qy), qz_high, qz_low),
        (pltpu.VMEM((28, 8, 128), F32),),
    )


def solution(mesh):
    return jax.shard_map(
        shards,
        mesh=mesh,
        in_specs=(
            P(("gx", "gy", "gz"), None),
            P(("gx", "gy", "gz")),
            P(("gx", "gy", "gz")),
            P(("gx", "gy", "gz"), None, None, None),
            P(),
            P(),
            P(),
        ),
        out_specs=P("gx", "gy", "gz"),
        check_vma=False,
    )
```

```python
import jax
import jax.numpy as jnp
import numpy as np
from jax import lax
from jax.experimental import pallas as pl
from jax.experimental.pallas import tpu as pltpu
from jax.sharding import PartitionSpec as P

W = (0.125, 0.5, 0.75, 0.5, 0.125)
F32 = jnp.float32
BF16 = jnp.bfloat16
CELLS = 384
ATOMS = 128
SPAN_2 = 18
SPAN_3 = 11
SPAN_4 = 7
SEC = 32
THI = 64
VMEM = pl.BlockSpec(memory_space=pltpu.VMEM)
SMEM = pl.BlockSpec(memory_space=pltpu.SMEM)
HBM = pl.BlockSpec(memory_space=pltpu.HBM)


def weight(t):
    return W[t] if 0 <= t <= 4 else 0.0


def table(rows, columns, offset, turned):
    out = np.zeros((128, 128), np.float32)
    for r in range(rows):
        for c in range(columns):
            out[r, c] = weight(c - 2 * r + offset if turned else r - 2 * c + offset)
    return out


PROL_2 = table(SPAN_3, SPAN_2, 3, True)
PROL_1 = table(SPAN_2, 32, 4, True)


BANDS = (
    (256, 256, ((0, 32, 2), (160, 2, 0), (192, 2, 34)), 32, 32),
    (256, 128, ((0, 18, 2), (128, 4, 0), (160, 4, 18)), 24, 18),
    (128, 128, ((0, 11, 2), (64, 5, 0), (96, 5, 10)), 16, 11),
)
DIVIDE = {32: (1, 5), 2: (1, 1), 18: (57, 10), 4: (1, 2), 11: (94, 10), 5: (52, 8), 24: (43, 10), 16: (1, 4)}


def composite(first, last):
    p3 = np.array([[weight(i - 2 * j + 3) for j in range(7)] for i in range(11)])
    p2 = np.array([[weight(i - 2 * j + 3) for j in range(11)] for i in range(18)])
    p1 = np.array([[weight(i - 2 * j + 4) for j in range(18)] for i in range(32)])
    m4, m3, m2 = np.ones(7), np.ones(11), np.ones(18)
    if first:
        m4[0] = m3[0] = m2[0] = 0
    if last:
        m4[5:] = 0
        m3[9:] = 0
        m2[17:] = 0
    return (p1 * m2) @ (p2 * m3) @ (p3 * m4)


def composites():
    qx = np.zeros((4, 32, 128), np.float32)
    qy = np.zeros((4, 32, 128), np.float32)
    qz = np.zeros((4, 128, 128), np.float32)
    for v in range(4):
        q = composite(v % 2 == 1, v >= 2)
        for lane in range(64):
            if lane // 8 < 7 and lane % 8 < 7:
                qx[v, :, lane] = q[:, lane // 8]
                qy[v, :, lane] = q[:, lane % 8]
        for row in range(128):
            if row % 8 < 7:
                qz[v, row, :32] = q[:, row % 8]
    return qx, qy, qz


def split(x):
    high = x.astype(BF16)
    return high, (x - high.astype(F32)).astype(BF16)


def dot(a, b):
    return jnp.dot(a, b, preferred_element_type=F32)


def dot_exact(x, right):
    high, low = split(x)
    return dot(high, right) + dot(low, right)


def dot_split(x, right_high, right_low):
    high, low = split(x)
    return dot(high, right_high) + (dot(low, right_high) + dot(high, right_low))


def iota(shape, dim):
    return lax.broadcasted_iota(jnp.int32, shape, dim)


def roll(x, shift, axis=None):
    axis = x.ndim - 1 if axis is None else axis
    shift = shift % x.shape[axis]
    return x if shift == 0 else pltpu.roll(x, shift, axis)


def lanes_of(x, low, count):
    lane = iota(x.shape, x.ndim - 1)
    return jnp.where((lane >= low) & (lane < low + count), x, 0.0)


def as_rows(x):
    return x.reshape(x.shape[0] * x.shape[1], x.shape[2])


def taps(pieces):
    total = None
    for factor, value in pieces:
        term = value if factor == 1.0 else factor * value
        total = term if total is None else total + term
    return total


def restrict_planes(read, span, size, offset):
    planes = []
    for p in range(span):
        planes.append(
            taps([(W[t], read(2 * p + t - offset)) for t in range(5) if 0 <= 2 * p + t - offset < size])
        )
    return planes


def place():
    sizes = [lax.axis_size(a) for a in ("gx", "gy", "gz")]
    index = [lax.axis_index(a) for a in ("gx", "gy", "gz")]
    return index, sizes


def inside_mask(shape, spans, high, place_of):
    index, sizes = place_of
    keep = None
    for dim in range(3):
        at = iota(shape, dim)
        low = jnp.where(index[dim] == 0, 1, 0)
        top = jnp.where(index[dim] == sizes[dim] - 1, high, spans)
        part = (at >= low) & (at < top)
        keep = part if keep is None else keep & part
    return keep


def nearest(index):
    even = lax.rem(index, 2) == 0
    return even, index == 1, index == 2


def deposit_kernel(
    codes, charges_hbm, spline_hbm,
    packed, raw_out, face,
    charges, spline, wide, patch, fine, buf_2, buf_3, buf_4, second_ref, third_ref, sems,
):
    where = place()
    index, sizes = where
    part = CELLS * 12 // 3
    copies = [pltpu.make_async_copy(charges_hbm, charges, sems.at[3])]
    for chunk in range(3):
        rows = slice(part * chunk, part * chunk + part)
        copies.append(
            pltpu.make_async_copy(spline_hbm.at[rows, :], spline.at[rows, :], sems.at[chunk])
        )
    for copy in copies:
        copy.start()
    buf_2[...] = jnp.zeros_like(buf_2)
    buf_3[...] = jnp.zeros_like(buf_3)
    buf_4[...] = jnp.zeros_like(buf_4)
    row, column = iota((512, 64), 0), iota((512, 64), 1)
    spread = (row // 32 * 4 + row % 4 == column).astype(F32).astype(BF16)
    row, column = iota((128, 128), 0), iota((128, 128), 1)

    def restriction(rows, columns, offset):
        t = row - 2 * column + offset
        out = jnp.zeros((128, 128), F32)
        for tap in range(5):
            out = jnp.where(t == tap, W[tap], out)
        return jnp.where((row < rows) & (column < columns), out, 0.0).astype(BF16)

    rest_2 = restriction(32, SPAN_2, 4)
    rest_3 = restriction(SPAN_2, SPAN_3, 3)
    rest_4 = restriction(SPAN_3, SPAN_4, 3)
    slot = lax.shift_right_logical(codes[...].reshape(1, CELLS), 8)
    fits = (iota((512, CELLS), 0) // 4 % 8) == slot % 8
    hot = (iota((64, CELLS), 0) == slot // 8).astype(F32).astype(BF16)
    copies[0].wait()
    alive = iota((ATOMS, CELLS), 0) < (codes[...].reshape(1, CELLS) & 255)
    weighted = jnp.where(alive, charges[...].T, 0.0)
    for chunk in range(CELLS // 128):
        lanes = slice(128 * chunk, 128 * chunk + 128)
        copies[1 + chunk].wait()
        rows = slice(part * chunk, part * chunk + part)
        wide[rows, :] = spline[rows, :].astype(F32)

        def column_of(d, i):
            return wide[pl.ds(chunk * part + 4 * d + i, 128, stride=12), :].T

        charge = weighted[:, lanes]
        depth = [charge * column_of(2, k) for k in range(4)]
        ys = [column_of(1, j) for j in range(4)]
        for i in range(4):
            xs = column_of(0, i)
            for j in range(4):
                cross = xs * ys[j]
                for k in range(4):
                    patch[16 * i + 4 * j + k : 16 * i + 4 * j + k + 1, lanes] = jnp.sum(
                        cross * depth[k], axis=0, keepdims=True
                    )
    high, low = split(patch[...])
    spread_high = jnp.where(fits, dot(spread, high), 0.0).astype(BF16)
    spread_low = jnp.where(fits, dot(spread, low), 0.0).astype(BF16)
    nt = (((1,), (1,)), ((), ()))
    placed = lax.dot_general(hot, spread_high, nt, preferred_element_type=F32) + lax.dot_general(
        hot, spread_low, nt, preferred_element_type=F32
    )
    for i in range(4):
        for j in range(4):
            rows = lanes_of(roll(placed[:, 128 * i : 128 * i + 128], -32 * j), 0, 32)
            for sx in range(8):
                fine[4 * sx + i, pl.ds(j, 8, stride=4), :] = rows[8 * sx : 8 * sx + 8]

    for p, plane in enumerate(restrict_planes(lambda x: fine[x], SPAN_2, 32, 4)):
        buf_2[p, 4:36, :] = plane
    second = taps([(W[t], buf_2[:, pl.ds(t, 24, stride=2), :]) for t in range(5)])
    second = dot_exact(as_rows(second), rest_2).reshape(SPAN_2, 24, 128)
    second = jnp.where(inside_mask(second.shape, SPAN_2, 17, where), second, 0.0)
    second_ref[...] = second
    for p, plane in enumerate(restrict_planes(lambda x: second[x], SPAN_3, SPAN_2, 3)):
        buf_3[p, 3:27, :] = plane
    third = taps([(W[t], buf_3[:, pl.ds(t, 16, stride=2), :]) for t in range(5)])
    third = dot_exact(as_rows(third), rest_3).reshape(SPAN_3, 16, 128)
    third = jnp.where(inside_mask(third.shape, SPAN_3, 9, where), third, 0.0)
    third_ref[...] = third
    for p, plane in enumerate(restrict_planes(lambda x: third[x], SPAN_4, SPAN_3, 3)):
        buf_4[p, 3:19, :] = plane
    last = taps([(W[t], buf_4[:, pl.ds(t, 8, stride=2), :]) for t in range(5)])
    last = dot_exact(as_rows(last), rest_4).reshape(SPAN_4, 8, 128)
    last = jnp.where(inside_mask(last.shape, SPAN_4, 5, where), last, 0.0)
    raw = taps([(1.0, roll(last[x], 8 * x)) for x in range(SPAN_4)])
    raw_out[...] = raw

    packed[...] = fine[...]
    packed[0:SPAN_2, 0:24, :] += roll(second, SEC)
    packed[0:SPAN_3, 0:16, :] += roll(third, THI)
    even, _, _ = nearest(index[1])
    low = pack_y(packed, (0, 0, 0))
    high = pack_y(packed, (30, 14, 6))
    for v in range(5):
        face[8 * v : 8 * v + 8, :] = jnp.where(even, high[v], low[v])
        face[40 + 8 * v : 48 + 8 * v, :] = jnp.where(even, low[v], high[v])
    face[80:88, :] = raw


def spot_1(p):
    return p // 16, p % 16 // 4 * 2, p % 4 * 32


def spot_2(p):
    return 2 + p // 14, p % 14 // 7 * 4, p % 7 * 18


def spot_3(p):
    return 4, 0, p * 11


LEVELS = ((32, 2, 0, 32, spot_1), (SPAN_2, 4, SEC, 18, spot_2), (SPAN_3, 5, THI, 11, spot_3))


def pack_y(source, at):
    tiles = [jnp.zeros((8, 128), F32) for _ in range(5)]
    row, at_lane = iota((8, 128), 0), iota((8, 128), 1)
    for (planes, count, lane, width, spot), start in zip(LEVELS, at):
        for p in range(planes):
            v, r, to = spot(p)
            if start == 30:
                slab = roll(source[p, 24:32, :], r - 6, 0)
            else:
                slab = roll(source[p, start : start + 8, :], r, 0)
            slab = roll(slab, to - lane)
            keep = (row >= r) & (row < r + count) & (at_lane >= to) & (at_lane < to + width)
            tiles[v] = jnp.where(keep, slab, tiles[v])
    return tiles


def place_y(tile, index):
    tall = jnp.concatenate([tile, jnp.zeros((8, 128), F32)], axis=0)
    tall = pltpu.roll(tall, lax.rem(4 * index + 15, 16), 0)
    return tall[0:8] + roll(tall[8:16], 64)


def relay_kernel(raw, got, out):
    index, _ = place()
    out[0:40, :] = got[40:80, :]
    partner = jnp.bitwise_xor(index[1], 1)
    out[40:48, :] = place_y(raw[...], index[1]) + place_y(got[80:88, :], partner)


def widen_y_kernel(packed, own, got_1, got_2, after, out, raw_out, face_1, face_3):
    index, _ = place()
    even, one, two = nearest(index[1])
    total = own[40:48, :] + got_2[40:48, :]
    raw_out[...] = total
    out[...] = jnp.zeros_like(out)
    out[:, 2:34, :] = packed[...]
    a, b = got_1[0:40, :], got_2[0:40, :]
    low = jnp.where(even, 0.0, a) + jnp.where(two, b, 0.0)
    high = jnp.where(even, a, 0.0) + jnp.where(one, b, 0.0)
    for face, at in ((low, (0, 0, 0)), (high, (34, 18, 10))):
        for (planes, count, lane, width, spot), start in zip(LEVELS, at):
            for p in range(planes):
                v, r, to = spot(p)
                slab = roll(roll(face[8 * v : 8 * v + 8], -r, 0), lane - to)
                slab = lanes_of(slab, lane, width)
                out[p, start : start + count, :] += slab[0:count]
    even, one, _ = nearest(index[0])
    for ref, to_high in ((face_1, even), (face_3, one)):
        f = jnp.where(to_high, 30, 0)
        s = jnp.where(to_high, 14, 0)
        t = jnp.where(to_high, 6, 0)
        ref[0:40, :] = lanes_of(out[f], 0, 32) + lanes_of(roll(out[f + 1], 32), 32, 32)
        ref[0:16, :] += taps(
            [(1.0, lanes_of(roll(out[t + k, 0:16, :], 11 * k), THI + 11 * k, 11)) for k in range(5)]
        )
        ref[40:64, :] = taps(
            [(1.0, lanes_of(roll(out[s + k, 0:24, :], 18 * k - SEC), 18 * k, 18)) for k in range(4)]
        )
        ref[64:72, :] = total


def widen_x_kernel(wide_y, own, got_1, got_3, got_2, after, out, raw_out, face_1, face_2):
    index, _ = place()
    even, one, two = nearest(index[0])
    total = None
    lane = iota((16, 128), 1)
    for step, tile in ((0, own[...]), (1, got_1[64:72, :]), (2, got_2[...]), (3, got_3[64:72, :])):
        tall = jnp.concatenate([tile, roll(tile, 64)], axis=0)
        tall = jnp.where(lane < 64, tall, 0.0)
        at = lax.rem(32 * jnp.bitwise_xor(index[0], step) + 120, 128)
        moved = pltpu.roll(tall, at, 1)
        total = moved if total is None else total + moved
    raw_out[...] = total
    a, b = got_1[...], got_3[...]
    low = jnp.where(even, 0.0, a) + jnp.where(two, b, 0.0)
    high = jnp.where(even, a, 0.0) + jnp.where(one, b, 0.0)
    out[0:2] = jnp.zeros((2, 40, 128), F32)
    out[34:36] = jnp.zeros((2, 40, 128), F32)
    out[2:34] = wide_y[...]
    for face, at in ((low, (0, 0, 0)), (high, (34, 18, 10))):
        for k in range(2):
            out[at[0] + k] += lanes_of(roll(face[0:40], -32 * k), 0, 32)
        for k in range(4):
            out[at[1] + k, 0:24, :] += lanes_of(roll(face[40:64], SEC - 18 * k), SEC, 18)
        for k in range(5):
            out[at[2] + k, 0:16, :] += lanes_of(roll(face[0:16], -11 * k), THI, 11)
    even, _, _ = nearest(index[2])
    for base, rows, planes, count, lane in ((0, 40, 36, 2, 0), (40, 24, 22, 4, SEC), (64, 16, 15, 5, THI)):
        at = {2: 30, 4: 14, 5: 6}[count]
        sums = [jnp.zeros((rows, 128), F32) for _ in range(2)]
        for x in range(planes):
            slab = out[x, 0:rows, :]
            for n, start in enumerate((lane, lane + at)):
                sums[n] = sums[n] + lanes_of(roll(slab, count * x - start), count * x, count)
        face_1[base : base + rows, :] = jnp.where(even, sums[1], sums[0])
        face_2[base : base + rows, :] = jnp.where(even, sums[0], sums[1])
    face_1[80:96, :] = total


def window_kernel(own, got_1, got_2, got_3, out):
    index, _ = place()
    pieces = (own[...], got_1[80:96, :], got_2[...], got_3[...])
    for group in range(4):
        total = None
        for step, piece in enumerate(pieces):
            apart = taps(
                [(1.0, lanes_of(roll(piece, 24 * q - 32 * group), 32 * q, 8)) for q in range(4)]
            )
            at = 4 * lax.rem(jnp.bitwise_xor(index[2], step), 4)
            moved = pltpu.roll(apart, at, 1)
            total = moved if total is None else total + moved
        out[group] = total


def divided(n, d):
    factor, bits = DIVIDE[d]
    return lax.shift_right_logical(n * factor, bits)


def build_bands(kernel, band):
    rows, columns, runs, group, outs = band
    row = iota((rows, 128), 0)
    shift = jnp.full((rows, 128), 99, jnp.int32)
    point = jnp.full((rows, 128), 99, jnp.int32)
    for start, count, offset in runs:
        at = row - start
        a = divided(at, count)
        inside = (at >= 0) & (at < 5 * count)
        shift = jnp.where(inside, a, shift)
        point = jnp.where(inside, offset + at - a * count, point)
    chosen = (shift == iota((rows, 128), 1)).astype(F32).astype(BF16)
    column = iota((8, columns), 1)
    block = divided(column, group)
    out_at = (column - block * group)[0:1]
    block = jnp.where((column - block * group) < outs, block, 9)
    sub = iota((8, columns), 0)
    entry = jnp.concatenate([point] * (columns // 128), axis=1) - out_at
    total_high = jnp.zeros((rows, columns), F32)
    total_low = jnp.zeros((rows, columns), F32)
    for c in range(5):
        source = jnp.zeros((8, columns), F32)
        for b in range(5):
            column_of = jnp.zeros((8, columns), F32)
            for a in range(5):
                column_of = jnp.where(sub == a, kernel[a, b, c], column_of)
            source = jnp.where(block == b, column_of, source)
        source = jnp.concatenate([source, jnp.zeros((120, columns), F32)], axis=0)
        high, low = split(source)
        fits = entry == c
        total_high = jnp.where(fits, dot(chosen, high), total_high)
        total_low = jnp.where(fits, dot(chosen, low), total_low)
    return total_high.astype(BF16), total_low.astype(BF16)


def bands_kernel(kernel_1, kernel_2, kernel_3, b1h, b1l, b2h, b2l, b3h, b3l):
    outs = ((b1h, b1l), (b2h, b2l), (b3h, b3l))
    for kernel, band, (high_ref, low_ref) in zip((kernel_1, kernel_2, kernel_3), BANDS, outs):
        high, low = build_bands(kernel, band)
        high_ref[...] = high
        low_ref[...] = low


def green_kernel(factors, green_high, green_low, rise, block_high, block_low):
    index, sizes = place()
    row, lane = iota((64, 128), 0), iota((64, 128), 1)
    delta_x = (lane // 8).astype(F32)
    delta_z = (4 * index[2] - 1 + lane % 8 - row).astype(F32)
    plain = delta_z * delta_z + (1.0 + delta_x * delta_x)
    for apart in range(18):
        high, low = split(0.0625 * lax.rsqrt(plain + float(apart * apart)))
        block_high[apart] = high
        block_low[apart] = low
    for ty in range(SPAN_4):
        columns = slice(128 * ty, 128 * ty + 128)
        for sy in range(16):
            apart = jnp.abs(4 * index[1] - 1 + ty - sy)
            first = sy % 8 * 128 + sy // 8 * 64
            green_high[first : first + 64, columns] = block_high[apart]
            green_low[first : first + 64, columns] = block_low[apart]
    variant = [
        jnp.where(index[d] == 0, 1, 0) + jnp.where(index[d] == sizes[d] - 1, 2, 0) for d in range(3)
    ]
    factor_x, factor_y = factors[variant[0]], factors[4 + variant[1]]
    kept = as_rows(factor_x[:, None, :] * factor_y[None, :, :])
    high, low = split(kept)
    rise[:, 0:128] = (high.astype(F32) + roll(low.astype(F32), 64)).astype(BF16)
    rise[:, 128:256] = high


def prolong_rows(source, target, count, whole):
    size = target.shape[1] // 2
    q0 = source[:, 0:size, :]
    q1 = source[:, 1 : size + 1, :]
    q2 = source[:, 2 : size + 2, :]
    even = 0.75 * q1 + 0.125 * (q0 + q2)
    odd = 0.5 * (q0 + q1) if whole else 0.5 * (q1 + q2)
    target[:, pl.ds(1 if whole else 0, size, stride=2), :] = even
    target[:, pl.ds(0 if whole else 1, size, stride=2), :] = odd


def prolong_plane(read, p, whole):
    half = p // 2
    if (p % 2 == 1) == whole:
        return 0.75 * read(half + 1) + 0.125 * (read(half) + read(half + 2))
    first = half if whole else half + 1
    return 0.5 * (read(first) + read(first + 1))


def near_kernel(
    wide, got_1, got_2, b1h, b1l, b2h, b2l, b3h, b3l, prol_2, prol_1,
    out,
    near_1, near_2, near_3, tall_3, tall_3y, tall_2, tall_2y,
):
    where = place()
    index, sizes = where
    even, _, _ = nearest(index[2])
    swapped, matched = got_1[0:80, :], got_2[...]
    low_msg = jnp.where(index[2] == 0, 0.0, jnp.where(even, matched, swapped))
    high_msg = jnp.where(index[2] == sizes[2] - 1, 0.0, jnp.where(even, swapped, matched))

    def halo(x, rows, base, count, low_at, high_at):
        low = roll(low_msg[base : base + rows], low_at - count * x)
        high = roll(high_msg[base : base + rows], high_at - count * x)
        return lanes_of(low, low_at, 5 * count) + lanes_of(high, high_at, 5 * count)

    planes = [lanes_of(wide[x, 0:16, :], THI, 11) for x in range(15)]
    left = []
    for x in range(SPAN_3):
        main = taps([(1.0, roll(planes[x + a], 11 * a - THI)) for a in range(5)])
        left.append(main + halo(x, 16, 64, 5, 64, 96))
    left = jnp.concatenate(left, axis=0)
    near_3[...] = jnp.zeros_like(near_3)
    near_3[:, 0:16, :] = dot_split(left, b3h[...], b3l[...]).reshape(SPAN_3, 16, 128)
    third = taps([(1.0, roll(near_3[:, b : b + 16, :], -16 * b)) for b in range(5)])
    third = jnp.where(inside_mask(third.shape, SPAN_3, 9, where), third, 0.0)
    tall_3[...] = jnp.zeros_like(tall_3)
    tall_3[:, 0:16, :] = dot_exact(as_rows(third), prol_2[...]).reshape(SPAN_3, 16, 128)
    prolong_rows(tall_3, tall_3y, SPAN_2, True)

    planes = [lanes_of(wide[x, 0:24, :], SEC, 18) for x in range(22)]
    left_a, left_b = [], []
    for x in range(SPAN_2):
        left_a.append(taps([(1.0, roll(planes[x + a], 18 * a - SEC)) for a in range(5)]))
        left_b.append(halo(x, 24, 40, 4, 0, 32))
    left = jnp.concatenate(
        [jnp.concatenate(left_a, axis=0), jnp.concatenate(left_b, axis=0)], axis=1
    )
    near_2[...] = jnp.zeros_like(near_2)
    near_2[:, 0:24, :] = dot_split(left, b2h[...], b2l[...]).reshape(SPAN_2, 24, 128)
    second = taps([(1.0, roll(near_2[:, b : b + 24, :], -24 * b)) for b in range(5)])
    raised = jnp.stack(
        [prolong_plane(lambda x: tall_3y[x], p, True) for p in range(SPAN_2)], axis=0
    )
    second = jnp.where(inside_mask(second.shape, SPAN_2, 17, where), second + raised, 0.0)
    tall_2[...] = jnp.zeros_like(tall_2)
    tall_2[:, 0:24, :] = dot_exact(as_rows(second), prol_1[...]).reshape(SPAN_2, 24, 128)
    prolong_rows(tall_2, tall_2y, 32, False)

    planes = [lanes_of(wide[x], 0, 32) for x in range(36)]
    left_a, left_b = [], []
    for x in range(32):
        left_a.append(taps([(1.0, roll(planes[x + a], 32 * a)) for a in range(4)]))
        left_b.append(planes[x + 4] + halo(x, 40, 0, 2, 32, 64))
    left = jnp.concatenate(
        [jnp.concatenate(left_a, axis=0), jnp.concatenate(left_b, axis=0)], axis=1
    )
    near_1[...] = dot_split(left, b1h[...], b1l[...]).reshape(32, 40, 256)
    for x in range(32):
        first = taps(
            [(1.0, roll(near_1[x, b : b + 32, 0:128], -32 * b)) for b in range(4)]
            + [(1.0, near_1[x, 4:36, 128:256])]
        )
        out[x] = first + prolong_plane(lambda q: tall_2y[q], x, False)


def top_kernel(
    base, piece_0, piece_1, piece_2, piece_3, green_high, green_low, rise, qz,
    out,
    fourth,
):
    index, sizes = place()
    lane = iota((8, 128), 1)
    sources = [lax.rem(16 * (jnp.bitwise_xor(index[2], 4 * s) // 4) + 127, 128) for s in range(4)]
    for x in range(16):
        total = None
        for piece, at in zip((piece_0, piece_1, piece_2, piece_3), sources):
            kept = lanes_of(piece[x // 4], 32 * (x % 4), 32)
            moved = pltpu.roll(kept, lax.rem(at + 128 - 32 * (x % 4), 128), 1)
            total = moved if total is None else total + moved
        total = total + roll(total, 64)
        fourth[x] = jnp.where(lane < 64, total[0:8], total[8:16])
    total = jnp.zeros((32, 128 * SPAN_4), F32)
    extra = jnp.zeros((16, 128 * SPAN_4), F32)
    for s in range(0, 8, 2):
        left = jnp.concatenate([fourth[:, s, :], fourth[:, s + 1, :]], axis=1)
        high, low = split(left)
        rows = slice(128 * s, 128 * s + 256)
        total = total + dot(jnp.concatenate([high, low], axis=0), green_high[rows, :])
        extra = extra + dot(high, green_low[rows, :])
    sums = total[0:16] + (total[16:32] + extra)
    row, lane = iota((16, 128), 0), iota((16, 128), 1)
    tops = []
    for tx in range(SPAN_4):
        keep = jnp.abs(4 * index[0] - 1 + tx - row) == lane // 8
        for ty in range(SPAN_4):
            picked = jnp.where(keep, sums[:, 128 * ty : 128 * ty + 128], 0.0)
            tops.append(jnp.sum(picked, axis=0, keepdims=True))
        tops.append(jnp.zeros((1, 128), F32))
    tops = jnp.concatenate(tops + [jnp.zeros((8, 128), F32)], axis=0)
    variant = jnp.where(index[2] == 0, 1, 0) + jnp.where(index[2] == sizes[2] - 1, 2, 0)
    high, low = split(dot_split(tops, qz[variant], qz[4 + variant]))
    right = jnp.concatenate([high, high, low, jnp.zeros_like(low)], axis=0)
    far = dot(rise[...], right)
    out[...] = (base[...] + far.reshape(32, 32, 128))[:, :, 0:32]


def call(kernel, outs, ins, scratch=(), megabytes=16, flops=1000000, spaces=None):
    spaces = spaces or {}
    return pl.pallas_call(
        kernel,
        out_shape=outs,
        in_specs=[spaces.get(i, VMEM) for i in range(len(ins))],
        out_specs=jax.tree.map(lambda _: VMEM, outs),
        scratch_shapes=list(scratch),
        compiler_params=pltpu.CompilerParams(vmem_limit_bytes=megabytes * 2**20),
        cost_estimate=pl.CostEstimate(flops=flops, bytes_accessed=2**21, transcendentals=0),
    )(*ins)


def shape(*dims, dtype=F32):
    return jax.ShapeDtypeStruct(dims, dtype)


def exchange(values, axis, steps):
    size = lax.axis_size(axis)
    return [
        lax.ppermute(value, axis, [(i, i ^ step) for i in range(size)])
        for value, step in zip(values, steps)
    ]


def match(value, axis):
    size = lax.axis_size(axis)
    pairs = [(0, 0), (size - 1, size - 1)]
    for i in range(1, size - 1, 2):
        pairs += [(i, i + 1), (i + 1, i)]
    return lax.ppermute(value, axis, pairs)


ANY = pl.BlockSpec(memory_space=pl.ANY)


def shards(charges, counts, slots, spline, kernel_fine, kernel_mid, kernel_coarse):
    cells = charges.shape[0]
    packed, raw, face = call(
        deposit_kernel,
        (shape(32, 32, 128), shape(8, 128), shape(88, 128)),
        (256 * slots + counts, charges, spline.reshape(cells * 12, ATOMS)),
        (
            pltpu.VMEM((cells, ATOMS), F32),
            pltpu.VMEM((cells * 12, 128), BF16),
            pltpu.VMEM((cells * 12, 128), F32),
            pltpu.VMEM((64, cells), F32),
            pltpu.VMEM((32, 32, 128), F32),
            pltpu.VMEM((SPAN_2, 56, 128), F32),
            pltpu.VMEM((SPAN_3, 40, 128), F32),
            pltpu.VMEM((SPAN_4, 24, 128), F32),
            pltpu.VMEM((SPAN_2, 24, 128), F32),
            pltpu.VMEM((SPAN_3, 16, 128), F32),
            pltpu.SemaphoreType.DMA((4,)),
        ),
        spaces={1: HBM, 2: HBM},
        megabytes=53,
    )
    (got_1,) = exchange((face,), "gy", (1,))
    relay = call(relay_kernel, shape(48, 128), (raw, got_1))
    (got_2,) = exchange((relay,), "gy", (2,))
    qx, qy, qz = composites()
    qz_high = qz.astype(BF16)
    qz_low = (qz - qz_high.astype(np.float32)).astype(BF16)
    green_high, green_low, rise = call(
        green_kernel,
        (
            shape(1024, 128 * SPAN_4, dtype=BF16),
            shape(1024, 128 * SPAN_4, dtype=BF16),
            shape(1024, 256, dtype=BF16),
        ),
        (jnp.asarray(np.concatenate([qx, qy])),),
        (pltpu.VMEM((18, 64, 128), BF16), pltpu.VMEM((18, 64, 128), BF16)),
    )
    wide_y, raw, face_1, face_3 = call(
        widen_y_kernel,
        (shape(32, 40, 128), shape(8, 128), shape(72, 128), shape(72, 128)),
        (packed, relay, got_1, got_2, rise),
        spaces={4: ANY},
    )
    got_1, got_3, got_2 = exchange((face_1, face_3, raw), "gx", (1, 3, 2))
    bands = call(
        bands_kernel,
        tuple(shape(band[0], band[1], dtype=BF16) for band in BANDS for _ in range(2)),
        (kernel_fine, kernel_mid, kernel_coarse),
        spaces={0: SMEM, 1: SMEM, 2: SMEM},
    )
    wide_x, raw, face_1, face_2 = call(
        widen_x_kernel,
        (shape(36, 40, 128), shape(16, 128), shape(96, 128), shape(80, 128)),
        (wide_y, raw, got_1, got_3, got_2, bands[0]),
        spaces={5: ANY},
    )
    got_1, got_3, got_2 = exchange((face_1, raw, raw), "gz", (1, 3, 2))
    matched = match(face_2, "gz")
    window = call(window_kernel, shape(4, 16, 128), (raw, got_1, got_2, got_3))
    pieces = [window] + exchange((window, window, window), "gz", (4, 8, 12))
    base = call(
        near_kernel,
        shape(32, 32, 128),
        (wide_x, got_1, matched, *bands, jnp.asarray(PROL_2, BF16), jnp.asarray(PROL_1, BF16)),
        (
            pltpu.VMEM((32, 40, 256), F32),
            pltpu.VMEM((SPAN_2, 32, 128), F32),
            pltpu.VMEM((SPAN_3, 24, 128), F32),
            pltpu.VMEM((SPAN_3, 24, 128), F32),
            pltpu.VMEM((SPAN_3, 24, 128), F32),
            pltpu.VMEM((SPAN_2, 32, 128), F32),
            pltpu.VMEM((SPAN_2, 32, 128), F32),
        ),
    )
    return call(
        top_kernel,
        shape(32, 32, 32),
        (base, *pieces, green_high, green_low, rise, jnp.asarray(np.concatenate([qz_high, qz_low]))),
        (pltpu.VMEM((16, 8, 128), F32),),
    )


def solution(mesh):
    return jax.shard_map(
        shards,
        mesh=mesh,
        in_specs=(
            P(("gx", "gy", "gz"), None),
            P(("gx", "gy", "gz")),
            P(("gx", "gy", "gz")),
            P(("gx", "gy", "gz"), None, None, None),
            P(),
            P(),
            P(),
        ),
        out_specs=P("gx", "gy", "gz"),
        check_vma=False,
    )
```

```python
import jax
import jax.numpy as jnp
import numpy as np
from jax import lax
from jax.experimental import pallas as pl
from jax.experimental.pallas import tpu as pltpu
from jax.sharding import PartitionSpec as P

W = (0.125, 0.5, 0.75, 0.5, 0.125)
F32 = jnp.float32
BF16 = jnp.bfloat16
CELLS = 384
ATOMS = 128
SPAN_2 = 18
SPAN_3 = 11
SPAN_4 = 7
SEC = 32
THI = 64
VMEM = pl.BlockSpec(memory_space=pltpu.VMEM)
SMEM = pl.BlockSpec(memory_space=pltpu.SMEM)
HBM = pl.BlockSpec(memory_space=pltpu.HBM)


def weight(t):
    return W[t] if 0 <= t <= 4 else 0.0


def table(rows, columns, offset, turned):
    out = np.zeros((128, 128), np.float32)
    for r in range(rows):
        for c in range(columns):
            out[r, c] = weight(c - 2 * r + offset if turned else r - 2 * c + offset)
    return out


PROL_2 = table(SPAN_3, SPAN_2, 3, True)
PROL_1 = table(SPAN_2, 32, 4, True)


BANDS = (
    (256, 256, ((0, 32, 2), (160, 2, 0), (192, 2, 34)), 32, 32),
    (256, 128, ((0, 18, 2), (128, 4, 0), (160, 4, 18)), 24, 18),
    (128, 128, ((0, 11, 2), (64, 5, 0), (96, 5, 10)), 16, 11),
)
DIVIDE = {32: (1, 5), 2: (1, 1), 18: (57, 10), 4: (1, 2), 11: (94, 10), 5: (52, 8), 24: (43, 10), 16: (1, 4)}


def composite(first, last):
    p3 = np.array([[weight(i - 2 * j + 3) for j in range(7)] for i in range(11)])
    p2 = np.array([[weight(i - 2 * j + 3) for j in range(11)] for i in range(18)])
    p1 = np.array([[weight(i - 2 * j + 4) for j in range(18)] for i in range(32)])
    m4, m3, m2 = np.ones(7), np.ones(11), np.ones(18)
    if first:
        m4[0] = m3[0] = m2[0] = 0
    if last:
        m4[5:] = 0
        m3[9:] = 0
        m2[17:] = 0
    return (p1 * m2) @ (p2 * m3) @ (p3 * m4)


def composites():
    qx = np.zeros((4, 32, 128), np.float32)
    qy = np.zeros((4, 32, 128), np.float32)
    qz = np.zeros((4, 128, 128), np.float32)
    for v in range(4):
        q = composite(v % 2 == 1, v >= 2)
        for lane in range(64):
            if lane // 8 < 7 and lane % 8 < 7:
                qx[v, :, lane] = q[:, lane // 8]
                qy[v, :, lane] = q[:, lane % 8]
        for row in range(128):
            if row % 8 < 7:
                qz[v, row, :32] = q[:, row % 8]
    return qx, qy, qz


def split(x):
    high = x.astype(BF16)
    return high, (x - high.astype(F32)).astype(BF16)


def dot(a, b):
    return jnp.dot(a, b, preferred_element_type=F32)


def dot_exact(x, right):
    high, low = split(x)
    return dot(high, right) + dot(low, right)


def dot_split(x, right_high, right_low):
    high, low = split(x)
    return dot(high, right_high) + (dot(low, right_high) + dot(high, right_low))


def iota(shape, dim):
    return lax.broadcasted_iota(jnp.int32, shape, dim)


def roll(x, shift, axis=None):
    axis = x.ndim - 1 if axis is None else axis
    shift = shift % x.shape[axis]
    return x if shift == 0 else pltpu.roll(x, shift, axis)


def lanes_of(x, low, count):
    lane = iota(x.shape, x.ndim - 1)
    return jnp.where((lane >= low) & (lane < low + count), x, 0.0)


def as_rows(x):
    return x.reshape(x.shape[0] * x.shape[1], x.shape[2])


def taps(pieces):
    total = None
    for factor, value in pieces:
        term = value if factor == 1.0 else factor * value
        total = term if total is None else total + term
    return total


def restrict_planes(read, span, size, offset):
    planes = []
    for p in range(span):
        planes.append(
            taps([(W[t], read(2 * p + t - offset)) for t in range(5) if 0 <= 2 * p + t - offset < size])
        )
    return planes


def place():
    sizes = [lax.axis_size(a) for a in ("gx", "gy", "gz")]
    index = [lax.axis_index(a) for a in ("gx", "gy", "gz")]
    return index, sizes


def inside_mask(shape, spans, high, place_of):
    index, sizes = place_of
    keep = None
    for dim in range(3):
        at = iota(shape, dim)
        low = jnp.where(index[dim] == 0, 1, 0)
        top = jnp.where(index[dim] == sizes[dim] - 1, high, spans)
        part = (at >= low) & (at < top)
        keep = part if keep is None else keep & part
    return keep


def nearest(index):
    even = lax.rem(index, 2) == 0
    return even, index == 1, index == 2


def deposit_kernel(
    codes, charges_hbm, spline_hbm,
    packed, raw_out, face,
    charges, spline, wide, patch, fine, buf_2, buf_3, buf_4, second_ref, third_ref, sems,
):
    where = place()
    index, sizes = where
    part = CELLS * 12 // 3
    copies = [pltpu.make_async_copy(charges_hbm, charges, sems.at[3])]
    for chunk in range(3):
        rows = slice(part * chunk, part * chunk + part)
        copies.append(
            pltpu.make_async_copy(spline_hbm.at[rows, :], spline.at[rows, :], sems.at[chunk])
        )
    for copy in copies:
        copy.start()
    buf_2[...] = jnp.zeros_like(buf_2)
    buf_3[...] = jnp.zeros_like(buf_3)
    buf_4[...] = jnp.zeros_like(buf_4)
    row, column = iota((512, 64), 0), iota((512, 64), 1)
    spread = (row // 32 * 4 + row % 4 == column).astype(F32).astype(BF16)
    row, column = iota((128, 128), 0), iota((128, 128), 1)

    def restriction(rows, columns, offset):
        t = row - 2 * column + offset
        out = jnp.zeros((128, 128), F32)
        for tap in range(5):
            out = jnp.where(t == tap, W[tap], out)
        return jnp.where((row < rows) & (column < columns), out, 0.0).astype(BF16)

    rest_2 = restriction(32, SPAN_2, 4)
    rest_3 = restriction(SPAN_2, SPAN_3, 3)
    rest_4 = restriction(SPAN_3, SPAN_4, 3)
    slot = lax.shift_right_logical(codes[...].reshape(1, CELLS), 8)
    fits = (iota((512, CELLS), 0) // 4 % 8) == slot % 8
    hot = (iota((64, CELLS), 0) == slot // 8).astype(F32).astype(BF16)
    copies[0].wait()
    alive = iota((ATOMS, CELLS), 0) < (codes[...].reshape(1, CELLS) & 255)
    weighted = jnp.where(alive, charges[...].T, 0.0)
    for chunk in range(CELLS // 128):
        lanes = slice(128 * chunk, 128 * chunk + 128)
        copies[1 + chunk].wait()
        rows = slice(part * chunk, part * chunk + part)
        wide[rows, :] = spline[rows, :].astype(F32)

        def column_of(d, i):
            return wide[pl.ds(chunk * part + 4 * d + i, 128, stride=12), :].T

        charge = weighted[:, lanes]
        depth = [charge * column_of(2, k) for k in range(4)]
        ys = [column_of(1, j) for j in range(4)]
        for i in range(4):
            xs = column_of(0, i)
            for j in range(4):
                cross = xs * ys[j]
                for k in range(4):
                    patch[16 * i + 4 * j + k : 16 * i + 4 * j + k + 1, lanes] = jnp.sum(
                        cross * depth[k], axis=0, keepdims=True
                    )
    high, low = split(patch[...])
    spread_high = jnp.where(fits, dot(spread, high), 0.0).astype(BF16)
    spread_low = jnp.where(fits, dot(spread, low), 0.0).astype(BF16)
    nt = (((1,), (1,)), ((), ()))
    placed = lax.dot_general(hot, spread_high, nt, preferred_element_type=F32) + lax.dot_general(
        hot, spread_low, nt, preferred_element_type=F32
    )
    for i in range(4):
        for j in range(4):
            rows = lanes_of(roll(placed[:, 128 * i : 128 * i + 128], -32 * j), 0, 32)
            for sx in range(8):
                fine[4 * sx + i, pl.ds(j, 8, stride=4), :] = rows[8 * sx : 8 * sx + 8]

    for p, plane in enumerate(restrict_planes(lambda x: fine[x], SPAN_2, 32, 4)):
        buf_2[p, 4:36, :] = plane
    second = taps([(W[t], buf_2[:, pl.ds(t, 24, stride=2), :]) for t in range(5)])
    second = dot_exact(as_rows(second), rest_2).reshape(SPAN_2, 24, 128)
    second = jnp.where(inside_mask(second.shape, SPAN_2, 17, where), second, 0.0)
    second_ref[...] = second
    for p, plane in enumerate(restrict_planes(lambda x: second[x], SPAN_3, SPAN_2, 3)):
        buf_3[p, 3:27, :] = plane
    third = taps([(W[t], buf_3[:, pl.ds(t, 16, stride=2), :]) for t in range(5)])
    third = dot_exact(as_rows(third), rest_3).reshape(SPAN_3, 16, 128)
    third = jnp.where(inside_mask(third.shape, SPAN_3, 9, where), third, 0.0)
    third_ref[...] = third
    for p, plane in enumerate(restrict_planes(lambda x: third[x], SPAN_4, SPAN_3, 3)):
        buf_4[p, 3:19, :] = plane
    last = taps([(W[t], buf_4[:, pl.ds(t, 8, stride=2), :]) for t in range(5)])
    last = dot_exact(as_rows(last), rest_4).reshape(SPAN_4, 8, 128)
    last = jnp.where(inside_mask(last.shape, SPAN_4, 5, where), last, 0.0)
    raw = taps([(1.0, roll(last[x], 8 * x)) for x in range(SPAN_4)])
    raw_out[...] = raw

    packed[...] = fine[...]
    packed[0:SPAN_2, 0:24, :] += roll(second, SEC)
    packed[0:SPAN_3, 0:16, :] += roll(third, THI)
    even, _, _ = nearest(index[1])
    low = pack_y(packed, (0, 0, 0))
    high = pack_y(packed, (30, 14, 6))
    for v in range(5):
        face[8 * v : 8 * v + 8, :] = jnp.where(even, high[v], low[v])
        face[40 + 8 * v : 48 + 8 * v, :] = jnp.where(even, low[v], high[v])
    face[80:88, :] = raw


def spot_1(p):
    return p // 16, p % 16 // 4 * 2, p % 4 * 32


def spot_2(p):
    return 2 + p // 14, p % 14 // 7 * 4, p % 7 * 18


def spot_3(p):
    return 4, 0, p * 11


LEVELS = ((32, 2, 0, 32, spot_1), (SPAN_2, 4, SEC, 18, spot_2), (SPAN_3, 5, THI, 11, spot_3))


def pack_y(source, at):
    tiles = [jnp.zeros((8, 128), F32) for _ in range(5)]
    row, at_lane = iota((8, 128), 0), iota((8, 128), 1)
    for (planes, count, lane, width, spot), start in zip(LEVELS, at):
        for p in range(planes):
            v, r, to = spot(p)
            if start == 30:
                slab = roll(source[p, 24:32, :], r - 6, 0)
            else:
                slab = roll(source[p, start : start + 8, :], r, 0)
            slab = roll(slab, to - lane)
            keep = (row >= r) & (row < r + count) & (at_lane >= to) & (at_lane < to + width)
            tiles[v] = jnp.where(keep, slab, tiles[v])
    return tiles


def place_y(tile, index):
    tall = jnp.concatenate([tile, jnp.zeros((8, 128), F32)], axis=0)
    tall = pltpu.roll(tall, lax.rem(4 * index + 15, 16), 0)
    return tall[0:8] + roll(tall[8:16], 64)


def relay_kernel(raw, got, out):
    index, _ = place()
    out[0:40, :] = got[40:80, :]
    partner = jnp.bitwise_xor(index[1], 1)
    out[40:48, :] = place_y(raw[...], index[1]) + place_y(got[80:88, :], partner)


def widen_y_kernel(packed, own, got_1, got_2, after, out, raw_out, face_1, face_3):
    index, _ = place()
    even, one, two = nearest(index[1])
    total = own[40:48, :] + got_2[40:48, :]
    raw_out[...] = total
    out[...] = jnp.zeros_like(out)
    out[:, 2:34, :] = packed[...]
    a, b = got_1[0:40, :], got_2[0:40, :]
    low = jnp.where(even, 0.0, a) + jnp.where(two, b, 0.0)
    high = jnp.where(even, a, 0.0) + jnp.where(one, b, 0.0)
    for face, at in ((low, (0, 0, 0)), (high, (34, 18, 10))):
        for (planes, count, lane, width, spot), start in zip(LEVELS, at):
            for p in range(planes):
                v, r, to = spot(p)
                slab = roll(roll(face[8 * v : 8 * v + 8], -r, 0), lane - to)
                slab = lanes_of(slab, lane, width)
                out[p, start : start + count, :] += slab[0:count]
    even, one, _ = nearest(index[0])
    for ref, to_high in ((face_1, even), (face_3, one)):
        f = jnp.where(to_high, 30, 0)
        s = jnp.where(to_high, 14, 0)
        t = jnp.where(to_high, 6, 0)
        ref[0:40, :] = lanes_of(out[f], 0, 32) + lanes_of(roll(out[f + 1], 32), 32, 32)
        ref[0:16, :] += taps(
            [(1.0, lanes_of(roll(out[t + k, 0:16, :], 11 * k), THI + 11 * k, 11)) for k in range(5)]
        )
        ref[40:64, :] = taps(
            [(1.0, lanes_of(roll(out[s + k, 0:24, :], 18 * k - SEC), 18 * k, 18)) for k in range(4)]
        )
        ref[64:72, :] = total


def widen_x_kernel(wide_y, own, got_1, got_3, got_2, after, out, raw_out, to_high, to_low):
    index, _ = place()
    even, one, two = nearest(index[0])
    total = None
    lane = iota((16, 128), 1)
    for step, tile in ((0, own[...]), (1, got_1[64:72, :]), (2, got_2[...]), (3, got_3[64:72, :])):
        tall = jnp.concatenate([tile, roll(tile, 64)], axis=0)
        tall = jnp.where(lane < 64, tall, 0.0)
        at = lax.rem(32 * jnp.bitwise_xor(index[0], step) + 120, 128)
        moved = pltpu.roll(tall, at, 1)
        total = moved if total is None else total + moved
    raw_out[...] = total
    a, b = got_1[...], got_3[...]
    low = jnp.where(even, 0.0, a) + jnp.where(two, b, 0.0)
    high = jnp.where(even, a, 0.0) + jnp.where(one, b, 0.0)
    out[0:2] = jnp.zeros((2, 40, 128), F32)
    out[34:36] = jnp.zeros((2, 40, 128), F32)
    out[2:34] = wide_y[...]
    for face, at in ((low, (0, 0, 0)), (high, (34, 18, 10))):
        for k in range(2):
            out[at[0] + k] += lanes_of(roll(face[0:40], -32 * k), 0, 32)
        for k in range(4):
            out[at[1] + k, 0:24, :] += lanes_of(roll(face[40:64], SEC - 18 * k), SEC, 18)
        for k in range(5):
            out[at[2] + k, 0:16, :] += lanes_of(roll(face[0:16], -11 * k), THI, 11)
    for ref, high in ((to_high, True), (to_low, False)):
        pack_z(out, ref, high)
        ref[80:96, :] = total


def pack_z(source, face, to_high):
    for base, rows, planes, count, lane, high in (
        (0, 40, 36, 2, 0, 30),
        (40, 24, 22, 4, SEC, 14),
        (64, 16, 15, 5, THI, 6),
    ):
        first = lane + high if to_high else lane
        total = jnp.zeros((rows, 128), F32)
        for x in range(planes):
            kept = roll(source[x, 0:rows, :], count * x - first)
            total = total + lanes_of(kept, count * x, count)
        face[base : base + rows, :] = total


def window_kernel(own, from_low, from_high, got_2, got_3, out):
    index, _ = place()
    even, _, _ = nearest(index[2])
    next_one = jnp.where(even, from_high[80:96, :], from_low[80:96, :])
    pieces = (own[...], next_one, got_2[...], got_3[...])
    for group in range(4):
        total = None
        for step, piece in enumerate(pieces):
            apart = taps(
                [(1.0, lanes_of(roll(piece, 24 * q - 32 * group), 32 * q, 8)) for q in range(4)]
            )
            at = 4 * lax.rem(jnp.bitwise_xor(index[2], step), 4)
            moved = pltpu.roll(apart, at, 1)
            total = moved if total is None else total + moved
        out[group] = total


def divided(n, d):
    factor, bits = DIVIDE[d]
    return lax.shift_right_logical(n * factor, bits)


def build_bands(kernel, band):
    rows, columns, runs, group, outs = band
    row = iota((rows, 128), 0)
    shift = jnp.full((rows, 128), 99, jnp.int32)
    point = jnp.full((rows, 128), 99, jnp.int32)
    for start, count, offset in runs:
        at = row - start
        a = divided(at, count)
        inside = (at >= 0) & (at < 5 * count)
        shift = jnp.where(inside, a, shift)
        point = jnp.where(inside, offset + at - a * count, point)
    chosen = (shift == iota((rows, 128), 1)).astype(F32).astype(BF16)
    column = iota((8, columns), 1)
    block = divided(column, group)
    out_at = (column - block * group)[0:1]
    block = jnp.where((column - block * group) < outs, block, 9)
    sub = iota((8, columns), 0)
    entry = jnp.concatenate([point] * (columns // 128), axis=1) - out_at
    total_high = jnp.zeros((rows, columns), F32)
    total_low = jnp.zeros((rows, columns), F32)
    for c in range(5):
        source = jnp.zeros((8, columns), F32)
        for b in range(5):
            column_of = jnp.zeros((8, columns), F32)
            for a in range(5):
                column_of = jnp.where(sub == a, kernel[a, b, c], column_of)
            source = jnp.where(block == b, column_of, source)
        source = jnp.concatenate([source, jnp.zeros((120, columns), F32)], axis=0)
        high, low = split(source)
        fits = entry == c
        total_high = jnp.where(fits, dot(chosen, high), total_high)
        total_low = jnp.where(fits, dot(chosen, low), total_low)
    return total_high.astype(BF16), total_low.astype(BF16)


def bands_kernel(kernel_1, kernel_2, kernel_3, b1h, b1l, b2h, b2l, b3h, b3l):
    outs = ((b1h, b1l), (b2h, b2l), (b3h, b3l))
    for kernel, band, (high_ref, low_ref) in zip((kernel_1, kernel_2, kernel_3), BANDS, outs):
        high, low = build_bands(kernel, band)
        high_ref[...] = high
        low_ref[...] = low


def green_kernel(factors, green_high, green_low, rise, block_high, block_low):
    index, sizes = place()
    row, lane = iota((64, 128), 0), iota((64, 128), 1)
    delta_x = (lane // 8).astype(F32)
    delta_z = (4 * index[2] - 1 + lane % 8 - row).astype(F32)
    plain = delta_z * delta_z + (1.0 + delta_x * delta_x)
    for apart in range(18):
        high, low = split(0.0625 * lax.rsqrt(plain + float(apart * apart)))
        block_high[apart] = high
        block_low[apart] = low
    for ty in range(SPAN_4):
        columns = slice(128 * ty, 128 * ty + 128)
        for sy in range(16):
            apart = jnp.abs(4 * index[1] - 1 + ty - sy)
            first = sy % 8 * 128 + sy // 8 * 64
            green_high[first : first + 64, columns] = block_high[apart]
            green_low[first : first + 64, columns] = block_low[apart]
    variant = [
        jnp.where(index[d] == 0, 1, 0) + jnp.where(index[d] == sizes[d] - 1, 2, 0) for d in range(3)
    ]
    factor_x, factor_y = factors[variant[0]], factors[4 + variant[1]]
    kept = as_rows(factor_x[:, None, :] * factor_y[None, :, :])
    high, low = split(kept)
    rise[:, 0:128] = (high.astype(F32) + roll(low.astype(F32), 64)).astype(BF16)
    rise[:, 128:256] = high


def prolong_rows(source, target, count, whole):
    size = target.shape[1] // 2
    q0 = source[:, 0:size, :]
    q1 = source[:, 1 : size + 1, :]
    q2 = source[:, 2 : size + 2, :]
    even = 0.75 * q1 + 0.125 * (q0 + q2)
    odd = 0.5 * (q0 + q1) if whole else 0.5 * (q1 + q2)
    target[:, pl.ds(1 if whole else 0, size, stride=2), :] = even
    target[:, pl.ds(0 if whole else 1, size, stride=2), :] = odd


def prolong_plane(read, p, whole):
    half = p // 2
    if (p % 2 == 1) == whole:
        return 0.75 * read(half + 1) + 0.125 * (read(half) + read(half + 2))
    first = half if whole else half + 1
    return 0.5 * (read(first) + read(first + 1))


def near_kernel(
    wide, from_low, from_high, b1h, b1l, b2h, b2l, b3h, b3l, prol_2, prol_1,
    out,
    near_1, near_2, near_3, tall_3, tall_3y, tall_2, tall_2y,
):
    where = place()
    index, sizes = where
    low_msg = jnp.where(index[2] == 0, 0.0, from_low[...])
    high_msg = jnp.where(index[2] == sizes[2] - 1, 0.0, from_high[...])

    def halo(x, rows, base, count, low_at, high_at):
        low = roll(low_msg[base : base + rows], low_at - count * x)
        high = roll(high_msg[base : base + rows], high_at - count * x)
        return lanes_of(low, low_at, 5 * count) + lanes_of(high, high_at, 5 * count)

    planes = [lanes_of(wide[x, 0:16, :], THI, 11) for x in range(15)]
    left = []
    for x in range(SPAN_3):
        main = taps([(1.0, roll(planes[x + a], 11 * a - THI)) for a in range(5)])
        left.append(main + halo(x, 16, 64, 5, 64, 96))
    left = jnp.concatenate(left, axis=0)
    near_3[...] = jnp.zeros_like(near_3)
    near_3[:, 0:16, :] = dot_split(left, b3h[...], b3l[...]).reshape(SPAN_3, 16, 128)
    third = taps([(1.0, roll(near_3[:, b : b + 16, :], -16 * b)) for b in range(5)])
    third = jnp.where(inside_mask(third.shape, SPAN_3, 9, where), third, 0.0)
    tall_3[...] = jnp.zeros_like(tall_3)
    tall_3[:, 0:16, :] = dot_exact(as_rows(third), prol_2[...]).reshape(SPAN_3, 16, 128)
    prolong_rows(tall_3, tall_3y, SPAN_2, True)

    planes = [lanes_of(wide[x, 0:24, :], SEC, 18) for x in range(22)]
    left_a, left_b = [], []
    for x in range(SPAN_2):
        left_a.append(taps([(1.0, roll(planes[x + a], 18 * a - SEC)) for a in range(5)]))
        left_b.append(halo(x, 24, 40, 4, 0, 32))
    left = jnp.concatenate(
        [jnp.concatenate(left_a, axis=0), jnp.concatenate(left_b, axis=0)], axis=1
    )
    near_2[...] = jnp.zeros_like(near_2)
    near_2[:, 0:24, :] = dot_split(left, b2h[...], b2l[...]).reshape(SPAN_2, 24, 128)
    second = taps([(1.0, roll(near_2[:, b : b + 24, :], -24 * b)) for b in range(5)])
    raised = jnp.stack(
        [prolong_plane(lambda x: tall_3y[x], p, True) for p in range(SPAN_2)], axis=0
    )
    second = jnp.where(inside_mask(second.shape, SPAN_2, 17, where), second + raised, 0.0)
    tall_2[...] = jnp.zeros_like(tall_2)
    tall_2[:, 0:24, :] = dot_exact(as_rows(second), prol_1[...]).reshape(SPAN_2, 24, 128)
    prolong_rows(tall_2, tall_2y, 32, False)

    planes = [lanes_of(wide[x], 0, 32) for x in range(36)]
    left_a, left_b = [], []
    for x in range(32):
        left_a.append(taps([(1.0, roll(planes[x + a], 32 * a)) for a in range(4)]))
        left_b.append(planes[x + 4] + halo(x, 40, 0, 2, 32, 64))
    left = jnp.concatenate(
        [jnp.concatenate(left_a, axis=0), jnp.concatenate(left_b, axis=0)], axis=1
    )
    near_1[...] = dot_split(left, b1h[...], b1l[...]).reshape(32, 40, 256)
    for x in range(32):
        first = taps(
            [(1.0, roll(near_1[x, b : b + 32, 0:128], -32 * b)) for b in range(4)]
            + [(1.0, near_1[x, 4:36, 128:256])]
        )
        out[x] = first + prolong_plane(lambda q: tall_2y[q], x, False)


def top_kernel(
    base, piece_0, piece_1, piece_2, piece_3, green_high, green_low, rise, qz,
    out,
    fourth,
):
    index, sizes = place()
    lane = iota((8, 128), 1)
    sources = [lax.rem(16 * (jnp.bitwise_xor(index[2], 4 * s) // 4) + 127, 128) for s in range(4)]
    for x in range(16):
        total = None
        for piece, at in zip((piece_0, piece_1, piece_2, piece_3), sources):
            kept = lanes_of(piece[x // 4], 32 * (x % 4), 32)
            moved = pltpu.roll(kept, lax.rem(at + 128 - 32 * (x % 4), 128), 1)
            total = moved if total is None else total + moved
        total = total + roll(total, 64)
        fourth[x] = jnp.where(lane < 64, total[0:8], total[8:16])
    total = jnp.zeros((32, 128 * SPAN_4), F32)
    extra = jnp.zeros((16, 128 * SPAN_4), F32)
    for s in range(0, 8, 2):
        left = jnp.concatenate([fourth[:, s, :], fourth[:, s + 1, :]], axis=1)
        high, low = split(left)
        rows = slice(128 * s, 128 * s + 256)
        total = total + dot(jnp.concatenate([high, low], axis=0), green_high[rows, :])
        extra = extra + dot(high, green_low[rows, :])
    sums = total[0:16] + (total[16:32] + extra)
    row, lane = iota((16, 128), 0), iota((16, 128), 1)
    tops = []
    for tx in range(SPAN_4):
        keep = jnp.abs(4 * index[0] - 1 + tx - row) == lane // 8
        for ty in range(SPAN_4):
            picked = jnp.where(keep, sums[:, 128 * ty : 128 * ty + 128], 0.0)
            tops.append(jnp.sum(picked, axis=0, keepdims=True))
        tops.append(jnp.zeros((1, 128), F32))
    tops = jnp.concatenate(tops + [jnp.zeros((8, 128), F32)], axis=0)
    variant = jnp.where(index[2] == 0, 1, 0) + jnp.where(index[2] == sizes[2] - 1, 2, 0)
    high, low = split(dot_split(tops, qz[variant], qz[4 + variant]))
    right = jnp.concatenate([high, high, low, jnp.zeros_like(low)], axis=0)
    far = dot(rise[...], right)
    out[...] = (base[...] + far.reshape(32, 32, 128))[:, :, 0:32]


def call(kernel, outs, ins, scratch=(), megabytes=16, flops=1000000, spaces=None):
    spaces = spaces or {}
    return pl.pallas_call(
        kernel,
        out_shape=outs,
        in_specs=[spaces.get(i, VMEM) for i in range(len(ins))],
        out_specs=jax.tree.map(lambda _: VMEM, outs),
        scratch_shapes=list(scratch),
        compiler_params=pltpu.CompilerParams(vmem_limit_bytes=megabytes * 2**20),
        cost_estimate=pl.CostEstimate(flops=flops, bytes_accessed=2**21, transcendentals=0),
    )(*ins)


def shape(*dims, dtype=F32):
    return jax.ShapeDtypeStruct(dims, dtype)


def exchange(values, axis, steps):
    size = lax.axis_size(axis)
    return [
        lax.ppermute(value, axis, [(i, i ^ step) for i in range(size)])
        for value, step in zip(values, steps)
    ]


def shift(value, axis, by):
    size = lax.axis_size(axis)
    return lax.ppermute(value, axis, [(i, (i + by) % size) for i in range(size)])


ANY = pl.BlockSpec(memory_space=pl.ANY)


def shards(charges, counts, slots, spline, kernel_fine, kernel_mid, kernel_coarse):
    cells = charges.shape[0]
    packed, raw, face = call(
        deposit_kernel,
        (shape(32, 32, 128), shape(8, 128), shape(88, 128)),
        (256 * slots + counts, charges, spline.reshape(cells * 12, ATOMS)),
        (
            pltpu.VMEM((cells, ATOMS), F32),
            pltpu.VMEM((cells * 12, 128), BF16),
            pltpu.VMEM((cells * 12, 128), F32),
            pltpu.VMEM((64, cells), F32),
            pltpu.VMEM((32, 32, 128), F32),
            pltpu.VMEM((SPAN_2, 56, 128), F32),
            pltpu.VMEM((SPAN_3, 40, 128), F32),
            pltpu.VMEM((SPAN_4, 24, 128), F32),
            pltpu.VMEM((SPAN_2, 24, 128), F32),
            pltpu.VMEM((SPAN_3, 16, 128), F32),
            pltpu.SemaphoreType.DMA((4,)),
        ),
        spaces={1: HBM, 2: HBM},
        megabytes=53,
    )
    (got_1,) = exchange((face,), "gy", (1,))
    relay = call(relay_kernel, shape(48, 128), (raw, got_1))
    (got_2,) = exchange((relay,), "gy", (2,))
    qx, qy, qz = composites()
    qz_high = qz.astype(BF16)
    qz_low = (qz - qz_high.astype(np.float32)).astype(BF16)
    green_high, green_low, rise = call(
        green_kernel,
        (
            shape(1024, 128 * SPAN_4, dtype=BF16),
            shape(1024, 128 * SPAN_4, dtype=BF16),
            shape(1024, 256, dtype=BF16),
        ),
        (jnp.asarray(np.concatenate([qx, qy])),),
        (pltpu.VMEM((18, 64, 128), BF16), pltpu.VMEM((18, 64, 128), BF16)),
    )
    wide_y, raw, face_1, face_3 = call(
        widen_y_kernel,
        (shape(32, 40, 128), shape(8, 128), shape(72, 128), shape(72, 128)),
        (packed, relay, got_1, got_2, rise),
        spaces={4: ANY},
    )
    got_2, got_3, got_1 = exchange((raw, face_3, face_1), "gx", (2, 3, 1))
    bands = call(
        bands_kernel,
        tuple(shape(band[0], band[1], dtype=BF16) for band in BANDS for _ in range(2)),
        (kernel_fine, kernel_mid, kernel_coarse),
        spaces={0: SMEM, 1: SMEM, 2: SMEM},
    )
    wide_x, raw, to_high, to_low = call(
        widen_x_kernel,
        (shape(36, 40, 128), shape(16, 128), shape(96, 128), shape(96, 128)),
        (wide_y, raw, got_1, got_3, got_2, bands[0]),
        spaces={5: ANY},
    )
    from_low, from_high = shift(to_high, "gz", 1), shift(to_low, "gz", -1)
    got_2, got_3 = exchange((raw, raw), "gz", (2, 3))
    window = call(window_kernel, shape(4, 16, 128), (raw, from_low, from_high, got_2, got_3))
    pieces = [window] + exchange((window, window, window), "gz", (4, 8, 12))
    base = call(
        near_kernel,
        shape(32, 32, 128),
        (wide_x, from_low, from_high, *bands, jnp.asarray(PROL_2, BF16), jnp.asarray(PROL_1, BF16)),
        (
            pltpu.VMEM((32, 40, 256), F32),
            pltpu.VMEM((SPAN_2, 32, 128), F32),
            pltpu.VMEM((SPAN_3, 24, 128), F32),
            pltpu.VMEM((SPAN_3, 24, 128), F32),
            pltpu.VMEM((SPAN_3, 24, 128), F32),
            pltpu.VMEM((SPAN_2, 32, 128), F32),
            pltpu.VMEM((SPAN_2, 32, 128), F32),
        ),
    )
    return call(
        top_kernel,
        shape(32, 32, 32),
        (base, *pieces, green_high, green_low, rise, jnp.asarray(np.concatenate([qz_high, qz_low]))),
        (pltpu.VMEM((16, 8, 128), F32),),
    )


def solution(mesh):
    return jax.shard_map(
        shards,
        mesh=mesh,
        in_specs=(
            P(("gx", "gy", "gz"), None),
            P(("gx", "gy", "gz")),
            P(("gx", "gy", "gz")),
            P(("gx", "gy", "gz"), None, None, None),
            P(),
            P(),
            P(),
        ),
        out_specs=P("gx", "gy", "gz"),
        check_vma=False,
    )
```

```python
import jax
import jax.numpy as jnp
import numpy as np
from jax import lax
from jax.experimental import pallas as pl
from jax.experimental.pallas import tpu as pltpu
from jax.sharding import PartitionSpec as P

W = (0.125, 0.5, 0.75, 0.5, 0.125)
F32 = jnp.float32
BF16 = jnp.bfloat16
CELLS = 384
ATOMS = 128
SPAN_2 = 18
SPAN_3 = 11
SPAN_4 = 7
SEC = 32
THI = 64
VMEM = pl.BlockSpec(memory_space=pltpu.VMEM)
SMEM = pl.BlockSpec(memory_space=pltpu.SMEM)
HBM = pl.BlockSpec(memory_space=pltpu.HBM)


def weight(t):
    return W[t] if 0 <= t <= 4 else 0.0


def table(rows, columns, offset, turned):
    out = np.zeros((128, 128), np.float32)
    for r in range(rows):
        for c in range(columns):
            out[r, c] = weight(c - 2 * r + offset if turned else r - 2 * c + offset)
    return out


PROL_2 = table(SPAN_3, SPAN_2, 3, True)
PROL_1 = table(SPAN_2, 32, 4, True)


BANDS = (
    (256, 256, ((0, 32, 2), (160, 2, 0), (192, 2, 34)), 32, 32),
    (256, 128, ((0, 18, 2), (128, 4, 0), (160, 4, 18)), 24, 18),
    (128, 128, ((0, 11, 2), (64, 5, 0), (96, 5, 10)), 16, 11),
)
DIVIDE = {32: (1, 5), 2: (1, 1), 18: (57, 10), 4: (1, 2), 11: (94, 10), 5: (52, 8), 24: (43, 10), 16: (1, 4)}


def composite(first, last):
    p3 = np.array([[weight(i - 2 * j + 3) for j in range(7)] for i in range(11)])
    p2 = np.array([[weight(i - 2 * j + 3) for j in range(11)] for i in range(18)])
    p1 = np.array([[weight(i - 2 * j + 4) for j in range(18)] for i in range(32)])
    m4, m3, m2 = np.ones(7), np.ones(11), np.ones(18)
    if first:
        m4[0] = m3[0] = m2[0] = 0
    if last:
        m4[5:] = 0
        m3[9:] = 0
        m2[17:] = 0
    return (p1 * m2) @ (p2 * m3) @ (p3 * m4)


def composites():
    qx = np.zeros((4, 32, 128), np.float32)
    qy = np.zeros((4, 32, 128), np.float32)
    qz = np.zeros((4, 128, 128), np.float32)
    for v in range(4):
        q = composite(v % 2 == 1, v >= 2)
        for lane in range(64):
            if lane // 8 < 7 and lane % 8 < 7:
                qx[v, :, lane] = q[:, lane // 8]
                qy[v, :, lane] = q[:, lane % 8]
        for row in range(128):
            if row % 8 < 7:
                qz[v, row, :32] = q[:, row % 8]
    return qx, qy, qz


def split(x):
    high = x.astype(BF16)
    return high, (x - high.astype(F32)).astype(BF16)


def dot(a, b):
    return jnp.dot(a, b, preferred_element_type=F32)


def dot_exact(x, right):
    high, low = split(x)
    return dot(high, right) + dot(low, right)


def dot_split(x, right_high, right_low):
    high, low = split(x)
    return dot(high, right_high) + (dot(low, right_high) + dot(high, right_low))


def iota(shape, dim):
    return lax.broadcasted_iota(jnp.int32, shape, dim)


def roll(x, shift, axis=None):
    axis = x.ndim - 1 if axis is None else axis
    shift = shift % x.shape[axis]
    return x if shift == 0 else pltpu.roll(x, shift, axis)


def lanes_of(x, low, count):
    lane = iota(x.shape, x.ndim - 1)
    return jnp.where((lane >= low) & (lane < low + count), x, 0.0)


def as_rows(x):
    return x.reshape(x.shape[0] * x.shape[1], x.shape[2])


def taps(pieces):
    total = None
    for factor, value in pieces:
        term = value if factor == 1.0 else factor * value
        total = term if total is None else total + term
    return total


def restrict_planes(read, span, size, offset):
    planes = []
    for p in range(span):
        planes.append(
            taps([(W[t], read(2 * p + t - offset)) for t in range(5) if 0 <= 2 * p + t - offset < size])
        )
    return planes


def place():
    sizes = [lax.axis_size(a) for a in ("gx", "gy", "gz")]
    index = [lax.axis_index(a) for a in ("gx", "gy", "gz")]
    return index, sizes


def inside_mask(shape, spans, high, place_of):
    index, sizes = place_of
    keep = None
    for dim in range(3):
        at = iota(shape, dim)
        low = jnp.where(index[dim] == 0, 1, 0)
        top = jnp.where(index[dim] == sizes[dim] - 1, high, spans)
        part = (at >= low) & (at < top)
        keep = part if keep is None else keep & part
    return keep


def nearest(index):
    even = lax.rem(index, 2) == 0
    return even, index == 1, index == 2


def deposit_kernel(
    codes, charges_hbm, spline_hbm,
    packed, raw_out, face,
    charges, spline, wide, patch, fine, buf_2, buf_3, buf_4, second_ref, third_ref, sems,
):
    where = place()
    index, sizes = where
    part = CELLS * 12 // 3
    copies = [pltpu.make_async_copy(charges_hbm, charges, sems.at[3])]
    for chunk in range(3):
        rows = slice(part * chunk, part * chunk + part)
        copies.append(
            pltpu.make_async_copy(spline_hbm.at[rows, :], spline.at[rows, :], sems.at[chunk])
        )
    for copy in copies:
        copy.start()
    buf_2[...] = jnp.zeros_like(buf_2)
    buf_3[...] = jnp.zeros_like(buf_3)
    buf_4[...] = jnp.zeros_like(buf_4)
    row, column = iota((512, 64), 0), iota((512, 64), 1)
    spread = (row // 32 * 4 + row % 4 == column).astype(F32).astype(BF16)
    row, column = iota((128, 128), 0), iota((128, 128), 1)

    def restriction(rows, columns, offset):
        t = row - 2 * column + offset
        out = jnp.zeros((128, 128), F32)
        for tap in range(5):
            out = jnp.where(t == tap, W[tap], out)
        return jnp.where((row < rows) & (column < columns), out, 0.0).astype(BF16)

    rest_2 = restriction(32, SPAN_2, 4)
    rest_3 = restriction(SPAN_2, SPAN_3, 3)
    rest_4 = restriction(SPAN_3, SPAN_4, 3)
    slot = lax.shift_right_logical(codes[...].reshape(1, CELLS), 8)
    fits = (iota((512, CELLS), 0) // 4 % 8) == slot % 8
    hot = (iota((64, CELLS), 0) == slot // 8).astype(F32).astype(BF16)
    copies[0].wait()
    alive = iota((ATOMS, CELLS), 0) < (codes[...].reshape(1, CELLS) & 255)
    weighted = jnp.where(alive, charges[...].T, 0.0)
    for chunk in range(CELLS // 128):
        lanes = slice(128 * chunk, 128 * chunk + 128)
        copies[1 + chunk].wait()
        rows = slice(part * chunk, part * chunk + part)
        wide[rows, :] = spline[rows, :].astype(F32)

        def column_of(d, i):
            return wide[pl.ds(chunk * part + 4 * d + i, 128, stride=12), :].T

        charge = weighted[:, lanes]
        depth = [charge * column_of(2, k) for k in range(4)]
        ys = [column_of(1, j) for j in range(4)]
        for i in range(4):
            xs = column_of(0, i)
            for j in range(4):
                cross = xs * ys[j]
                for k in range(4):
                    patch[16 * i + 4 * j + k : 16 * i + 4 * j + k + 1, lanes] = jnp.sum(
                        cross * depth[k], axis=0, keepdims=True
                    )
    high, low = split(patch[...])
    spread_high = jnp.where(fits, dot(spread, high), 0.0).astype(BF16)
    spread_low = jnp.where(fits, dot(spread, low), 0.0).astype(BF16)
    nt = (((1,), (1,)), ((), ()))
    placed = lax.dot_general(hot, spread_high, nt, preferred_element_type=F32) + lax.dot_general(
        hot, spread_low, nt, preferred_element_type=F32
    )
    for i in range(4):
        for j in range(4):
            rows = lanes_of(roll(placed[:, 128 * i : 128 * i + 128], -32 * j), 0, 32)
            for sx in range(8):
                fine[4 * sx + i, pl.ds(j, 8, stride=4), :] = rows[8 * sx : 8 * sx + 8]

    for p, plane in enumerate(restrict_planes(lambda x: fine[x], SPAN_2, 32, 4)):
        buf_2[p, 4:36, :] = plane
    second = taps([(W[t], buf_2[:, pl.ds(t, 24, stride=2), :]) for t in range(5)])
    second = dot_exact(as_rows(second), rest_2).reshape(SPAN_2, 24, 128)
    second = jnp.where(inside_mask(second.shape, SPAN_2, 17, where), second, 0.0)
    second_ref[...] = second
    for p, plane in enumerate(restrict_planes(lambda x: second[x], SPAN_3, SPAN_2, 3)):
        buf_3[p, 3:27, :] = plane
    third = taps([(W[t], buf_3[:, pl.ds(t, 16, stride=2), :]) for t in range(5)])
    third = dot_exact(as_rows(third), rest_3).reshape(SPAN_3, 16, 128)
    third = jnp.where(inside_mask(third.shape, SPAN_3, 9, where), third, 0.0)
    third_ref[...] = third
    for p, plane in enumerate(restrict_planes(lambda x: third[x], SPAN_4, SPAN_3, 3)):
        buf_4[p, 3:19, :] = plane
    last = taps([(W[t], buf_4[:, pl.ds(t, 8, stride=2), :]) for t in range(5)])
    last = dot_exact(as_rows(last), rest_4).reshape(SPAN_4, 8, 128)
    last = jnp.where(inside_mask(last.shape, SPAN_4, 5, where), last, 0.0)
    raw = taps([(1.0, roll(last[x], 8 * x)) for x in range(SPAN_4)])
    raw_out[...] = raw

    packed[...] = fine[...]
    packed[0:SPAN_2, 0:24, :] += roll(second, SEC)
    packed[0:SPAN_3, 0:16, :] += roll(third, THI)
    even, _, _ = nearest(index[1])
    low = pack_y(packed, (0, 0, 0))
    high = pack_y(packed, (30, 14, 6))
    for v in range(5):
        face[8 * v : 8 * v + 8, :] = jnp.where(even, high[v], low[v])
        face[40 + 8 * v : 48 + 8 * v, :] = jnp.where(even, low[v], high[v])
    face[80:88, :] = raw


def spot_1(p):
    return p // 16, p % 16 // 4 * 2, p % 4 * 32


def spot_2(p):
    return 2 + p // 14, p % 14 // 7 * 4, p % 7 * 18


def spot_3(p):
    return 4, 0, p * 11


LEVELS = ((32, 2, 0, 32, spot_1), (SPAN_2, 4, SEC, 18, spot_2), (SPAN_3, 5, THI, 11, spot_3))


def pack_y(source, at):
    tiles = [jnp.zeros((8, 128), F32) for _ in range(5)]
    row, at_lane = iota((8, 128), 0), iota((8, 128), 1)
    for (planes, count, lane, width, spot), start in zip(LEVELS, at):
        for p in range(planes):
            v, r, to = spot(p)
            if start == 30:
                slab = roll(source[p, 24:32, :], r - 6, 0)
            else:
                slab = roll(source[p, start : start + 8, :], r, 0)
            slab = roll(slab, to - lane)
            keep = (row >= r) & (row < r + count) & (at_lane >= to) & (at_lane < to + width)
            tiles[v] = jnp.where(keep, slab, tiles[v])
    return tiles


def place_y(tile, index):
    tall = jnp.concatenate([tile, jnp.zeros((8, 128), F32)], axis=0)
    tall = pltpu.roll(tall, lax.rem(4 * index + 15, 16), 0)
    return tall[0:8] + roll(tall[8:16], 64)


def relay_kernel(raw, got, out):
    index, _ = place()
    out[0:40, :] = got[40:80, :]
    partner = jnp.bitwise_xor(index[1], 1)
    out[40:48, :] = place_y(raw[...], index[1]) + place_y(got[80:88, :], partner)


def widen_y_kernel(framed, own, got_1, got_2, after, out, raw_out, face_1, face_3):
    index, _ = place()
    even, one, two = nearest(index[1])
    total = own[40:48, :] + got_2[40:48, :]
    raw_out[...] = total
    a, b = got_1[0:40, :], got_2[0:40, :]
    low = jnp.where(even, 0.0, a) + jnp.where(two, b, 0.0)
    high = jnp.where(even, a, 0.0) + jnp.where(one, b, 0.0)
    for face, at in ((low, (0, 0, 0)), (high, (34, 18, 10))):
        for (planes, count, lane, width, spot), start in zip(LEVELS, at):
            for p in range(planes):
                v, r, to = spot(p)
                slab = roll(roll(face[8 * v : 8 * v + 8], -r, 0), lane - to)
                slab = lanes_of(slab, lane, width)
                out[p, start : start + count, :] += slab[0:count]
    even, one, _ = nearest(index[0])
    for ref, to_high in ((face_1, even), (face_3, one)):
        f = jnp.where(to_high, 30, 0)
        s = jnp.where(to_high, 14, 0)
        t = jnp.where(to_high, 6, 0)
        ref[0:40, :] = lanes_of(out[f], 0, 32) + lanes_of(roll(out[f + 1], 32), 32, 32)
        ref[0:16, :] += taps(
            [(1.0, lanes_of(roll(out[t + k, 0:16, :], 11 * k), THI + 11 * k, 11)) for k in range(5)]
        )
        ref[40:64, :] = taps(
            [(1.0, lanes_of(roll(out[s + k, 0:24, :], 18 * k - SEC), 18 * k, 18)) for k in range(4)]
        )
        ref[64:72, :] = total


def widen_x_kernel(wide_y, own, got_1, got_3, got_2, after, out, raw_out, to_high, to_low):
    index, _ = place()
    even, one, two = nearest(index[0])
    total = None
    lane = iota((16, 128), 1)
    for step, tile in ((0, own[...]), (1, got_1[64:72, :]), (2, got_2[...]), (3, got_3[64:72, :])):
        tall = jnp.concatenate([tile, roll(tile, 64)], axis=0)
        tall = jnp.where(lane < 64, tall, 0.0)
        at = lax.rem(32 * jnp.bitwise_xor(index[0], step) + 120, 128)
        moved = pltpu.roll(tall, at, 1)
        total = moved if total is None else total + moved
    raw_out[...] = total
    a, b = got_1[...], got_3[...]
    low = jnp.where(even, 0.0, a) + jnp.where(two, b, 0.0)
    high = jnp.where(even, a, 0.0) + jnp.where(one, b, 0.0)
    out[0:2] = jnp.zeros((2, 40, 128), F32)
    out[34:36] = jnp.zeros((2, 40, 128), F32)
    out[2:34] = wide_y[...]
    for face, at in ((low, (0, 0, 0)), (high, (34, 18, 10))):
        for k in range(2):
            out[at[0] + k] += lanes_of(roll(face[0:40], -32 * k), 0, 32)
        for k in range(4):
            out[at[1] + k, 0:24, :] += lanes_of(roll(face[40:64], SEC - 18 * k), SEC, 18)
        for k in range(5):
            out[at[2] + k, 0:16, :] += lanes_of(roll(face[0:16], -11 * k), THI, 11)
    for ref, high in ((to_high, True), (to_low, False)):
        pack_z(out, ref, high)
        ref[80:96, :] = total


def pack_z(source, face, to_high):
    for base, rows, planes, count, lane, high in (
        (0, 40, 36, 2, 0, 30),
        (40, 24, 22, 4, SEC, 14),
        (64, 16, 15, 5, THI, 6),
    ):
        first = lane + high if to_high else lane
        at = iota((rows, 128), 1)
        wanted = (at >= first) & (at < first + count)
        total = jnp.zeros((rows, 128), F32)
        for x in range(planes):
            kept = jnp.where(wanted, source[x, 0:rows, :], 0.0)
            total = total + roll(kept, count * x - first)
        face[base : base + rows, :] = total


def window_kernel(own, from_low, from_high, got_2, got_3, out):
    index, _ = place()
    even, _, _ = nearest(index[2])
    next_one = jnp.where(even, from_high[80:96, :], from_low[80:96, :])
    pieces = (own[...], next_one, got_2[...], got_3[...])
    for group in range(4):
        total = None
        for step, piece in enumerate(pieces):
            apart = taps(
                [(1.0, lanes_of(roll(piece, 24 * q - 32 * group), 32 * q, 8)) for q in range(4)]
            )
            at = 4 * lax.rem(jnp.bitwise_xor(index[2], step), 4)
            moved = pltpu.roll(apart, at, 1)
            total = moved if total is None else total + moved
        out[group] = total


def divided(n, d):
    factor, bits = DIVIDE[d]
    return lax.shift_right_logical(n * factor, bits)


def build_bands(kernel, band):
    rows, columns, runs, group, outs = band
    row = iota((rows, 128), 0)
    shift = jnp.full((rows, 128), 99, jnp.int32)
    point = jnp.full((rows, 128), 99, jnp.int32)
    for start, count, offset in runs:
        at = row - start
        a = divided(at, count)
        inside = (at >= 0) & (at < 5 * count)
        shift = jnp.where(inside, a, shift)
        point = jnp.where(inside, offset + at - a * count, point)
    chosen = (shift == iota((rows, 128), 1)).astype(F32).astype(BF16)
    column = iota((8, columns), 1)
    block = divided(column, group)
    out_at = (column - block * group)[0:1]
    block = jnp.where((column - block * group) < outs, block, 9)
    sub = iota((8, columns), 0)
    entry = jnp.concatenate([point] * (columns // 128), axis=1) - out_at
    total_high = jnp.zeros((rows, columns), F32)
    total_low = jnp.zeros((rows, columns), F32)
    for c in range(5):
        source = jnp.zeros((8, columns), F32)
        for b in range(5):
            column_of = jnp.zeros((8, columns), F32)
            for a in range(5):
                column_of = jnp.where(sub == a, kernel[a, b, c], column_of)
            source = jnp.where(block == b, column_of, source)
        source = jnp.concatenate([source, jnp.zeros((120, columns), F32)], axis=0)
        high, low = split(source)
        fits = entry == c
        total_high = jnp.where(fits, dot(chosen, high), total_high)
        total_low = jnp.where(fits, dot(chosen, low), total_low)
    return total_high.astype(BF16), total_low.astype(BF16)


def bands_kernel(kernel_1, kernel_2, kernel_3, b1h, b1l, b2h, b2l, b3h, b3l):
    outs = ((b1h, b1l), (b2h, b2l), (b3h, b3l))
    for kernel, band, (high_ref, low_ref) in zip((kernel_1, kernel_2, kernel_3), BANDS, outs):
        high, low = build_bands(kernel, band)
        high_ref[...] = high
        low_ref[...] = low


def green_kernel(factors, packed, green_high, green_low, rise, framed, block_high, block_low):
    index, sizes = place()
    row, lane = iota((64, 128), 0), iota((64, 128), 1)
    delta_x = (lane // 8).astype(F32)
    delta_z = (4 * index[2] - 1 + lane % 8 - row).astype(F32)
    plain = delta_z * delta_z + (1.0 + delta_x * delta_x)
    for apart in range(18):
        high, low = split(0.0625 * lax.rsqrt(plain + float(apart * apart)))
        block_high[apart] = high
        block_low[apart] = low
    for ty in range(SPAN_4):
        columns = slice(128 * ty, 128 * ty + 128)
        for sy in range(16):
            apart = jnp.abs(4 * index[1] - 1 + ty - sy)
            first = sy % 8 * 128 + sy // 8 * 64
            green_high[first : first + 64, columns] = block_high[apart]
            green_low[first : first + 64, columns] = block_low[apart]
    variant = [
        jnp.where(index[d] == 0, 1, 0) + jnp.where(index[d] == sizes[d] - 1, 2, 0) for d in range(3)
    ]
    factor_x, factor_y = factors[variant[0]], factors[4 + variant[1]]
    kept = as_rows(factor_x[:, None, :] * factor_y[None, :, :])
    high, low = split(kept)
    rise[:, 0:128] = (high.astype(F32) + roll(low.astype(F32), 64)).astype(BF16)
    rise[:, 128:256] = high
    framed[:, 0:2, :] = jnp.zeros((32, 2, 128), F32)
    framed[:, 34:40, :] = jnp.zeros((32, 6, 128), F32)
    framed[:, 2:34, :] = packed[...]


def prolong_rows(source, target, count, whole):
    size = target.shape[1] // 2
    q0 = source[:, 0:size, :]
    q1 = source[:, 1 : size + 1, :]
    q2 = source[:, 2 : size + 2, :]
    even = 0.75 * q1 + 0.125 * (q0 + q2)
    odd = 0.5 * (q0 + q1) if whole else 0.5 * (q1 + q2)
    target[:, pl.ds(1 if whole else 0, size, stride=2), :] = even
    target[:, pl.ds(0 if whole else 1, size, stride=2), :] = odd


def prolong_plane(read, p, whole):
    half = p // 2
    if (p % 2 == 1) == whole:
        return 0.75 * read(half + 1) + 0.125 * (read(half) + read(half + 2))
    first = half if whole else half + 1
    return 0.5 * (read(first) + read(first + 1))


def near_kernel(
    wide, from_low, from_high, b1h, b1l, b2h, b2l, b3h, b3l, prol_2, prol_1,
    out,
    near_1, near_2, near_3, tall_3, tall_3y, tall_2, tall_2y,
):
    where = place()
    index, sizes = where
    low_msg = jnp.where(index[2] == 0, 0.0, from_low[...])
    high_msg = jnp.where(index[2] == sizes[2] - 1, 0.0, from_high[...])

    def halo(x, rows, base, count, low_at, high_at):
        low = roll(low_msg[base : base + rows], low_at - count * x)
        high = roll(high_msg[base : base + rows], high_at - count * x)
        return lanes_of(low, low_at, 5 * count) + lanes_of(high, high_at, 5 * count)

    planes = [lanes_of(wide[x, 0:16, :], THI, 11) for x in range(15)]
    left = []
    for x in range(SPAN_3):
        main = taps([(1.0, roll(planes[x + a], 11 * a - THI)) for a in range(5)])
        left.append(main + halo(x, 16, 64, 5, 64, 96))
    left = jnp.concatenate(left, axis=0)
    near_3[...] = jnp.zeros_like(near_3)
    near_3[:, 0:16, :] = dot_split(left, b3h[...], b3l[...]).reshape(SPAN_3, 16, 128)
    third = taps([(1.0, roll(near_3[:, b : b + 16, :], -16 * b)) for b in range(5)])
    third = jnp.where(inside_mask(third.shape, SPAN_3, 9, where), third, 0.0)
    tall_3[...] = jnp.zeros_like(tall_3)
    tall_3[:, 0:16, :] = dot_exact(as_rows(third), prol_2[...]).reshape(SPAN_3, 16, 128)
    prolong_rows(tall_3, tall_3y, SPAN_2, True)

    planes = [lanes_of(wide[x, 0:24, :], SEC, 18) for x in range(22)]
    left_a, left_b = [], []
    for x in range(SPAN_2):
        left_a.append(taps([(1.0, roll(planes[x + a], 18 * a - SEC)) for a in range(5)]))
        left_b.append(halo(x, 24, 40, 4, 0, 32))
    left = jnp.concatenate(
        [jnp.concatenate(left_a, axis=0), jnp.concatenate(left_b, axis=0)], axis=1
    )
    near_2[...] = jnp.zeros_like(near_2)
    near_2[:, 0:24, :] = dot_split(left, b2h[...], b2l[...]).reshape(SPAN_2, 24, 128)
    second = taps([(1.0, roll(near_2[:, b : b + 24, :], -24 * b)) for b in range(5)])
    raised = jnp.stack(
        [prolong_plane(lambda x: tall_3y[x], p, True) for p in range(SPAN_2)], axis=0
    )
    second = jnp.where(inside_mask(second.shape, SPAN_2, 17, where), second + raised, 0.0)
    tall_2[...] = jnp.zeros_like(tall_2)
    tall_2[:, 0:24, :] = dot_exact(as_rows(second), prol_1[...]).reshape(SPAN_2, 24, 128)
    prolong_rows(tall_2, tall_2y, 32, False)

    planes = [lanes_of(wide[x], 0, 32) for x in range(36)]
    left_a, left_b = [], []
    for x in range(32):
        left_a.append(taps([(1.0, roll(planes[x + a], 32 * a)) for a in range(4)]))
        left_b.append(planes[x + 4] + halo(x, 40, 0, 2, 32, 64))
    left = jnp.concatenate(
        [jnp.concatenate(left_a, axis=0), jnp.concatenate(left_b, axis=0)], axis=1
    )
    near_1[...] = dot_split(left, b1h[...], b1l[...]).reshape(32, 40, 256)
    for x in range(32):
        first = taps(
            [(1.0, roll(near_1[x, b : b + 32, 0:128], -32 * b)) for b in range(4)]
            + [(1.0, near_1[x, 4:36, 128:256])]
        )
        out[x] = first + prolong_plane(lambda q: tall_2y[q], x, False)


def top_kernel(
    base, piece_0, piece_1, piece_2, piece_3, green_high, green_low, rise, qz,
    out,
    fourth,
):
    index, sizes = place()
    lane = iota((8, 128), 1)
    sources = [lax.rem(16 * (jnp.bitwise_xor(index[2], 4 * s) // 4) + 127, 128) for s in range(4)]
    for x in range(16):
        total = None
        for piece, at in zip((piece_0, piece_1, piece_2, piece_3), sources):
            kept = lanes_of(piece[x // 4], 32 * (x % 4), 32)
            moved = pltpu.roll(kept, lax.rem(at + 128 - 32 * (x % 4), 128), 1)
            total = moved if total is None else total + moved
        total = total + roll(total, 64)
        fourth[x] = jnp.where(lane < 64, total[0:8], total[8:16])
    total = jnp.zeros((32, 128 * SPAN_4), F32)
    extra = jnp.zeros((16, 128 * SPAN_4), F32)
    for s in range(0, 8, 2):
        left = jnp.concatenate([fourth[:, s, :], fourth[:, s + 1, :]], axis=1)
        high, low = split(left)
        rows = slice(128 * s, 128 * s + 256)
        total = total + dot(jnp.concatenate([high, low], axis=0), green_high[rows, :])
        extra = extra + dot(high, green_low[rows, :])
    sums = total[0:16] + (total[16:32] + extra)
    row, lane = iota((16, 128), 0), iota((16, 128), 1)
    tops = []
    for tx in range(SPAN_4):
        keep = jnp.abs(4 * index[0] - 1 + tx - row) == lane // 8
        for ty in range(SPAN_4):
            picked = jnp.where(keep, sums[:, 128 * ty : 128 * ty + 128], 0.0)
            tops.append(jnp.sum(picked, axis=0, keepdims=True))
        tops.append(jnp.zeros((1, 128), F32))
    tops = jnp.concatenate(tops + [jnp.zeros((8, 128), F32)], axis=0)
    variant = jnp.where(index[2] == 0, 1, 0) + jnp.where(index[2] == sizes[2] - 1, 2, 0)
    high, low = split(dot_split(tops, qz[variant], qz[4 + variant]))
    right = jnp.concatenate([high, high, low, jnp.zeros_like(low)], axis=0)
    far = dot(rise[...], right)
    out[...] = (base[...] + far.reshape(32, 32, 128))[:, :, 0:32]


def call(kernel, outs, ins, scratch=(), megabytes=16, spaces=None, aliases=None):
    spaces = spaces or {}
    return pl.pallas_call(
        kernel,
        out_shape=outs,
        in_specs=[spaces.get(i, VMEM) for i in range(len(ins))],
        out_specs=jax.tree.map(lambda _: VMEM, outs),
        scratch_shapes=list(scratch),
        input_output_aliases=aliases or {},
        compiler_params=pltpu.CompilerParams(vmem_limit_bytes=int(megabytes * 2**20)),
        cost_estimate=pl.CostEstimate(flops=1000000, bytes_accessed=2**21, transcendentals=0),
    )(*ins)


def shape(*dims, dtype=F32):
    return jax.ShapeDtypeStruct(dims, dtype)


def exchange(values, axis, steps):
    size = lax.axis_size(axis)
    return [
        lax.ppermute(value, axis, [(i, i ^ step) for i in range(size)])
        for value, step in zip(values, steps)
    ]


def shift(value, by):
    size_y, size_z = lax.axis_size("gy"), lax.axis_size("gz")
    half = size_y // 2
    pairs = []
    for core in range(half):
        ring = [(high * half + core) * size_z + z for high in range(2) for z in range(size_z)]
        pairs += [(ring[n], ring[(n + by) % len(ring)]) for n in range(len(ring))]
    return lax.ppermute(value, ("gy", "gz"), pairs)


ANY = pl.BlockSpec(memory_space=pl.ANY)


def shards(charges, counts, slots, spline, kernel_fine, kernel_mid, kernel_coarse):
    cells = charges.shape[0]
    packed, raw, face = call(
        deposit_kernel,
        (shape(32, 32, 128), shape(8, 128), shape(88, 128)),
        (256 * slots + counts, charges, spline.reshape(cells * 12, ATOMS)),
        (
            pltpu.VMEM((cells, ATOMS), F32),
            pltpu.VMEM((cells * 12, 128), BF16),
            pltpu.VMEM((cells * 12, 128), F32),
            pltpu.VMEM((64, cells), F32),
            pltpu.VMEM((32, 32, 128), F32),
            pltpu.VMEM((SPAN_2, 56, 128), F32),
            pltpu.VMEM((SPAN_3, 40, 128), F32),
            pltpu.VMEM((SPAN_4, 24, 128), F32),
            pltpu.VMEM((SPAN_2, 24, 128), F32),
            pltpu.VMEM((SPAN_3, 16, 128), F32),
            pltpu.SemaphoreType.DMA((4,)),
        ),
        spaces={1: HBM, 2: HBM},
        megabytes=53.75,
    )
    (got_1,) = exchange((face,), "gy", (1,))
    relay = call(relay_kernel, shape(48, 128), (raw, got_1))
    (got_2,) = exchange((relay,), "gy", (2,))
    qx, qy, qz = composites()
    qz_high = qz.astype(BF16)
    qz_low = (qz - qz_high.astype(np.float32)).astype(BF16)
    green_high, green_low, rise, framed = call(
        green_kernel,
        (
            shape(1024, 128 * SPAN_4, dtype=BF16),
            shape(1024, 128 * SPAN_4, dtype=BF16),
            shape(1024, 256, dtype=BF16),
            shape(32, 40, 128),
        ),
        (jnp.asarray(np.concatenate([qx, qy])), packed),
        (pltpu.VMEM((18, 64, 128), BF16), pltpu.VMEM((18, 64, 128), BF16)),
    )
    wide_y, raw, face_1, face_3 = call(
        widen_y_kernel,
        (shape(32, 40, 128), shape(8, 128), shape(72, 128), shape(72, 128)),
        (framed, relay, got_1, got_2, rise),
        spaces={4: ANY},
        aliases={0: 0},
    )
    got_2, got_3, got_1 = exchange((raw, face_3, face_1), "gx", (2, 3, 1))
    bands = call(
        bands_kernel,
        tuple(shape(band[0], band[1], dtype=BF16) for band in BANDS for _ in range(2)),
        (kernel_fine, kernel_mid, kernel_coarse),
        spaces={0: SMEM, 1: SMEM, 2: SMEM},
    )
    wide_x, raw, to_high, to_low = call(
        widen_x_kernel,
        (shape(36, 40, 128), shape(16, 128), shape(96, 128), shape(96, 128)),
        (wide_y, raw, got_1, got_3, got_2, bands[0]),
        spaces={5: ANY},
    )
    from_low, from_high = shift(to_high, 1), shift(to_low, -1)
    got_2, got_3 = exchange((raw, raw), "gz", (2, 3))
    window = call(window_kernel, shape(4, 16, 128), (raw, from_low, from_high, got_2, got_3))
    pieces = [window] + exchange((window, window, window), "gz", (4, 8, 12))
    base = call(
        near_kernel,
        shape(32, 32, 128),
        (wide_x, from_low, from_high, *bands, jnp.asarray(PROL_2, BF16), jnp.asarray(PROL_1, BF16)),
        (
            pltpu.VMEM((32, 40, 256), F32),
            pltpu.VMEM((SPAN_2, 32, 128), F32),
            pltpu.VMEM((SPAN_3, 24, 128), F32),
            pltpu.VMEM((SPAN_3, 24, 128), F32),
            pltpu.VMEM((SPAN_3, 24, 128), F32),
            pltpu.VMEM((SPAN_2, 32, 128), F32),
            pltpu.VMEM((SPAN_2, 32, 128), F32),
        ),
    )
    return call(
        top_kernel,
        shape(32, 32, 32),
        (base, *pieces, green_high, green_low, rise, jnp.asarray(np.concatenate([qz_high, qz_low]))),
        (pltpu.VMEM((16, 8, 128), F32),),
    )


def solution(mesh):
    return jax.shard_map(
        shards,
        mesh=mesh,
        in_specs=(
            P(("gx", "gy", "gz"), None),
            P(("gx", "gy", "gz")),
            P(("gx", "gy", "gz")),
            P(("gx", "gy", "gz"), None, None, None),
            P(),
            P(),
            P(),
        ),
        out_specs=P("gx", "gy", "gz"),
        check_vma=False,
    )
```

```python
import jax
import jax.numpy as jnp
import numpy as np
from jax import lax
from jax.experimental import pallas as pl
from jax.experimental.pallas import tpu as pltpu
from jax.sharding import PartitionSpec as P

W = (0.125, 0.5, 0.75, 0.5, 0.125)
F32 = jnp.float32
BF16 = jnp.bfloat16
CELLS = 384
ATOMS = 128
SPAN_2 = 18
SPAN_3 = 11
SPAN_4 = 7
SEC = 32
THI = 64
VMEM = pl.BlockSpec(memory_space=pltpu.VMEM)
SMEM = pl.BlockSpec(memory_space=pltpu.SMEM)
HBM = pl.BlockSpec(memory_space=pltpu.HBM)


def weight(t):
    return W[t] if 0 <= t <= 4 else 0.0


def table(rows, columns, offset, turned):
    out = np.zeros((128, 128), np.float32)
    for r in range(rows):
        for c in range(columns):
            out[r, c] = weight(c - 2 * r + offset if turned else r - 2 * c + offset)
    return out


PROL_2 = table(SPAN_3, SPAN_2, 3, True)
PROL_1 = table(SPAN_2, 32, 4, True)


BANDS = (
    (256, 256, ((0, 32, 2), (160, 2, 0), (192, 2, 34)), 32, 32),
    (256, 128, ((0, 18, 2), (128, 4, 0), (160, 4, 18)), 24, 18),
    (128, 128, ((0, 11, 2), (64, 5, 0), (96, 5, 10)), 16, 11),
)
DIVIDE = {32: (1, 5), 2: (1, 1), 18: (57, 10), 4: (1, 2), 11: (94, 10), 5: (52, 8), 24: (43, 10), 16: (1, 4)}


def composite(first, last):
    p3 = np.array([[weight(i - 2 * j + 3) for j in range(7)] for i in range(11)])
    p2 = np.array([[weight(i - 2 * j + 3) for j in range(11)] for i in range(18)])
    p1 = np.array([[weight(i - 2 * j + 4) for j in range(18)] for i in range(32)])
    m4, m3, m2 = np.ones(7), np.ones(11), np.ones(18)
    if first:
        m4[0] = m3[0] = m2[0] = 0
    if last:
        m4[5:] = 0
        m3[9:] = 0
        m2[17:] = 0
    return (p1 * m2) @ (p2 * m3) @ (p3 * m4)


def composites():
    qx = np.zeros((4, 32, 128), np.float32)
    qy = np.zeros((4, 32, 128), np.float32)
    qz = np.zeros((4, 128, 128), np.float32)
    for v in range(4):
        q = composite(v % 2 == 1, v >= 2)
        for lane in range(64):
            if lane // 8 < 7 and lane % 8 < 7:
                qx[v, :, lane] = q[:, lane // 8]
                qy[v, :, lane] = q[:, lane % 8]
        for row in range(128):
            if row % 8 < 7:
                qz[v, row, :32] = q[:, row % 8]
    return qx, qy, qz


def split(x):
    high = x.astype(BF16)
    return high, (x - high.astype(F32)).astype(BF16)


def dot(a, b):
    return jnp.dot(a, b, preferred_element_type=F32)


def dot_exact(x, right):
    high, low = split(x)
    return dot(high, right) + dot(low, right)


def dot_split(x, right_high, right_low):
    high, low = split(x)
    return dot(high, right_high) + (dot(low, right_high) + dot(high, right_low))


def iota(shape, dim):
    return lax.broadcasted_iota(jnp.int32, shape, dim)


def roll(x, shift, axis=None):
    axis = x.ndim - 1 if axis is None else axis
    shift = shift % x.shape[axis]
    return x if shift == 0 else pltpu.roll(x, shift, axis)


def lanes_of(x, low, count):
    lane = iota(x.shape, x.ndim - 1)
    return jnp.where((lane >= low) & (lane < low + count), x, 0.0)


def as_rows(x):
    return x.reshape(x.shape[0] * x.shape[1], x.shape[2])


def taps(pieces):
    total = None
    for factor, value in pieces:
        term = value if factor == 1.0 else factor * value
        total = term if total is None else total + term
    return total


def restrict_planes(read, span, size, offset):
    planes = []
    for p in range(span):
        planes.append(
            taps([(W[t], read(2 * p + t - offset)) for t in range(5) if 0 <= 2 * p + t - offset < size])
        )
    return planes


def place():
    sizes = [lax.axis_size(a) for a in ("gx", "gy", "gz")]
    index = [lax.axis_index(a) for a in ("gx", "gy", "gz")]
    return index, sizes


def inside_mask(shape, spans, high, place_of):
    index, sizes = place_of
    keep = None
    for dim in range(3):
        at = iota(shape, dim)
        low = jnp.where(index[dim] == 0, 1, 0)
        top = jnp.where(index[dim] == sizes[dim] - 1, high, spans)
        part = (at >= low) & (at < top)
        keep = part if keep is None else keep & part
    return keep


def nearest(index):
    even = lax.rem(index, 2) == 0
    return even, index == 1, index == 2


def deposit_kernel(
    codes, charges_hbm, spline_hbm,
    packed, raw_out, face,
    charges, spline, wide, patch, fine, buf_2, buf_3, buf_4, second_ref, third_ref, sems,
):
    where = place()
    index, sizes = where
    part = CELLS * 12 // 3
    copies = [pltpu.make_async_copy(charges_hbm, charges, sems.at[3])]
    for chunk in range(3):
        rows = slice(part * chunk, part * chunk + part)
        copies.append(
            pltpu.make_async_copy(spline_hbm.at[rows, :], spline.at[rows, :], sems.at[chunk])
        )
    for copy in copies:
        copy.start()
    buf_2[...] = jnp.zeros_like(buf_2)
    buf_3[...] = jnp.zeros_like(buf_3)
    buf_4[...] = jnp.zeros_like(buf_4)
    row, column = iota((512, 64), 0), iota((512, 64), 1)
    spread = (row // 32 * 4 + row % 4 == column).astype(F32).astype(BF16)
    row, column = iota((128, 128), 0), iota((128, 128), 1)

    def restriction(rows, columns, offset):
        t = row - 2 * column + offset
        out = jnp.zeros((128, 128), F32)
        for tap in range(5):
            out = jnp.where(t == tap, W[tap], out)
        return jnp.where((row < rows) & (column < columns), out, 0.0).astype(BF16)

    rest_2 = restriction(32, SPAN_2, 4)
    rest_3 = restriction(SPAN_2, SPAN_3, 3)
    rest_4 = restriction(SPAN_3, SPAN_4, 3)
    slot = lax.shift_right_logical(codes[...].reshape(1, CELLS), 8)
    fits = (iota((512, CELLS), 0) // 4 % 8) == slot % 8
    hot = (iota((64, CELLS), 0) == slot // 8).astype(F32).astype(BF16)
    copies[0].wait()
    alive = iota((ATOMS, CELLS), 0) < (codes[...].reshape(1, CELLS) & 255)
    weighted = jnp.where(alive, charges[...].T, 0.0)
    for chunk in range(CELLS // 128):
        lanes = slice(128 * chunk, 128 * chunk + 128)
        copies[1 + chunk].wait()
        rows = slice(part * chunk, part * chunk + part)
        wide[rows, :] = spline[rows, :].astype(F32)

        def column_of(d, i):
            return wide[pl.ds(chunk * part + 4 * d + i, 128, stride=12), :].T

        charge = weighted[:, lanes]
        depth = [charge * column_of(2, k) for k in range(4)]
        ys = [column_of(1, j) for j in range(4)]
        for i in range(4):
            xs = column_of(0, i)
            for j in range(4):
                cross = xs * ys[j]
                for k in range(4):
                    patch[16 * i + 4 * j + k : 16 * i + 4 * j + k + 1, lanes] = jnp.sum(
                        cross * depth[k], axis=0, keepdims=True
                    )
    high, low = split(patch[...])
    spread_high = jnp.where(fits, dot(spread, high), 0.0).astype(BF16)
    spread_low = jnp.where(fits, dot(spread, low), 0.0).astype(BF16)
    nt = (((1,), (1,)), ((), ()))
    placed = lax.dot_general(hot, spread_high, nt, preferred_element_type=F32) + lax.dot_general(
        hot, spread_low, nt, preferred_element_type=F32
    )
    for i in range(4):
        for j in range(4):
            rows = lanes_of(roll(placed[:, 128 * i : 128 * i + 128], -32 * j), 0, 32)
            for sx in range(8):
                fine[4 * sx + i, pl.ds(j, 8, stride=4), :] = rows[8 * sx : 8 * sx + 8]

    for p, plane in enumerate(restrict_planes(lambda x: fine[x], SPAN_2, 32, 4)):
        buf_2[p, 4:36, :] = plane
    second = taps([(W[t], buf_2[:, pl.ds(t, 24, stride=2), :]) for t in range(5)])
    second = dot_exact(as_rows(second), rest_2).reshape(SPAN_2, 24, 128)
    second = jnp.where(inside_mask(second.shape, SPAN_2, 17, where), second, 0.0)
    second_ref[...] = second
    for p, plane in enumerate(restrict_planes(lambda x: second[x], SPAN_3, SPAN_2, 3)):
        buf_3[p, 3:27, :] = plane
    third = taps([(W[t], buf_3[:, pl.ds(t, 16, stride=2), :]) for t in range(5)])
    third = dot_exact(as_rows(third), rest_3).reshape(SPAN_3, 16, 128)
    third = jnp.where(inside_mask(third.shape, SPAN_3, 9, where), third, 0.0)
    third_ref[...] = third
    for p, plane in enumerate(restrict_planes(lambda x: third[x], SPAN_4, SPAN_3, 3)):
        buf_4[p, 3:19, :] = plane
    last = taps([(W[t], buf_4[:, pl.ds(t, 8, stride=2), :]) for t in range(5)])
    last = dot_exact(as_rows(last), rest_4).reshape(SPAN_4, 8, 128)
    last = jnp.where(inside_mask(last.shape, SPAN_4, 5, where), last, 0.0)
    raw = taps([(1.0, roll(last[x], 8 * x)) for x in range(SPAN_4)])
    raw_out[...] = raw

    packed[...] = fine[...]
    packed[0:SPAN_2, 0:24, :] += roll(second, SEC)
    packed[0:SPAN_3, 0:16, :] += roll(third, THI)
    even, _, _ = nearest(index[1])
    low = pack_y(packed, (0, 0, 0))
    high = pack_y(packed, (30, 14, 6))
    for v in range(5):
        face[8 * v : 8 * v + 8, :] = jnp.where(even, high[v], low[v])
        face[40 + 8 * v : 48 + 8 * v, :] = jnp.where(even, low[v], high[v])
    face[80:88, :] = raw


def spot_1(p):
    return p // 16, p % 16 // 4 * 2, p % 4 * 32


def spot_2(p):
    return 2 + p // 14, p % 14 // 7 * 4, p % 7 * 18


def spot_3(p):
    return 4, 0, p * 11


LEVELS = ((32, 2, 0, 32, spot_1), (SPAN_2, 4, SEC, 18, spot_2), (SPAN_3, 5, THI, 11, spot_3))


def pack_y(source, at):
    tiles = [jnp.zeros((8, 128), F32) for _ in range(5)]
    row, at_lane = iota((8, 128), 0), iota((8, 128), 1)
    for (planes, count, lane, width, spot), start in zip(LEVELS, at):
        for p in range(planes):
            v, r, to = spot(p)
            if start == 30:
                slab = roll(source[p, 24:32, :], r - 6, 0)
            else:
                slab = roll(source[p, start : start + 8, :], r, 0)
            slab = roll(slab, to - lane)
            keep = (row >= r) & (row < r + count) & (at_lane >= to) & (at_lane < to + width)
            tiles[v] = jnp.where(keep, slab, tiles[v])
    return tiles


def place_y(tile, index):
    tall = jnp.concatenate([tile, jnp.zeros((8, 128), F32)], axis=0)
    tall = pltpu.roll(tall, lax.rem(4 * index + 15, 16), 0)
    return tall[0:8] + roll(tall[8:16], 64)


def relay_kernel(raw, got, out):
    index, _ = place()
    out[0:40, :] = got[40:80, :]
    partner = jnp.bitwise_xor(index[1], 1)
    out[40:48, :] = place_y(raw[...], index[1]) + place_y(got[80:88, :], partner)


def widen_y_kernel(framed, own, got_1, got_2, after, out, raw_out, face_1, face_3):
    index, _ = place()
    even, one, two = nearest(index[1])
    total = own[40:48, :] + got_2[40:48, :]
    raw_out[...] = total
    a, b = got_1[0:40, :], got_2[0:40, :]
    low = jnp.where(even, 0.0, a) + jnp.where(two, b, 0.0)
    high = jnp.where(even, a, 0.0) + jnp.where(one, b, 0.0)
    for face, at in ((low, (0, 0, 0)), (high, (34, 18, 10))):
        for (planes, count, lane, width, spot), start in zip(LEVELS, at):
            for p in range(planes):
                v, r, to = spot(p)
                slab = roll(roll(face[8 * v : 8 * v + 8], -r, 0), lane - to)
                slab = lanes_of(slab, lane, width)
                out[p, start : start + count, :] += slab[0:count]
    even, one, _ = nearest(index[0])
    for ref, to_high in ((face_1, even), (face_3, one)):
        f = jnp.where(to_high, 30, 0)
        s = jnp.where(to_high, 14, 0)
        t = jnp.where(to_high, 6, 0)
        ref[0:40, :] = lanes_of(out[f], 0, 32) + lanes_of(roll(out[f + 1], 32), 32, 32)
        ref[0:16, :] += taps(
            [(1.0, lanes_of(roll(out[t + k, 0:16, :], 11 * k), THI + 11 * k, 11)) for k in range(5)]
        )
        ref[40:64, :] = taps(
            [(1.0, lanes_of(roll(out[s + k, 0:24, :], 18 * k - SEC), 18 * k, 18)) for k in range(4)]
        )
        ref[64:72, :] = total


def widen_x_kernel(wide_y, own, got_1, got_3, got_2, after, out, raw_out, to_high, to_low):
    index, _ = place()
    even, one, two = nearest(index[0])
    total = None
    lane = iota((16, 128), 1)
    for step, tile in ((0, own[...]), (1, got_1[64:72, :]), (2, got_2[...]), (3, got_3[64:72, :])):
        tall = jnp.concatenate([tile, roll(tile, 64)], axis=0)
        tall = jnp.where(lane < 64, tall, 0.0)
        at = lax.rem(32 * jnp.bitwise_xor(index[0], step) + 120, 128)
        moved = pltpu.roll(tall, at, 1)
        total = moved if total is None else total + moved
    raw_out[...] = total
    a, b = got_1[...], got_3[...]
    low = jnp.where(even, 0.0, a) + jnp.where(two, b, 0.0)
    high = jnp.where(even, a, 0.0) + jnp.where(one, b, 0.0)
    out[0:2] = jnp.zeros((2, 40, 128), F32)
    out[34:36] = jnp.zeros((2, 40, 128), F32)
    out[2:34] = wide_y[...]
    for face, at in ((low, (0, 0, 0)), (high, (34, 18, 10))):
        for k in range(2):
            out[at[0] + k] += lanes_of(roll(face[0:40], -32 * k), 0, 32)
        for k in range(4):
            out[at[1] + k, 0:24, :] += lanes_of(roll(face[40:64], SEC - 18 * k), SEC, 18)
        for k in range(5):
            out[at[2] + k, 0:16, :] += lanes_of(roll(face[0:16], -11 * k), THI, 11)
    for ref, high in ((to_high, True), (to_low, False)):
        pack_z(out, ref, high)
        ref[80:96, :] = total


def pack_z(source, face, to_high):
    for base, rows, planes, count, lane, high in (
        (0, 40, 36, 2, 0, 30),
        (40, 24, 22, 4, SEC, 14),
        (64, 16, 15, 5, THI, 6),
    ):
        first = lane + high if to_high else lane
        at = iota((rows, 128), 1)
        wanted = (at >= first) & (at < first + count)
        total = jnp.zeros((rows, 128), F32)
        for x in range(planes):
            kept = jnp.where(wanted, source[x, 0:rows, :], 0.0)
            total = total + roll(kept, count * x - first)
        face[base : base + rows, :] = total


def window_kernel(own, from_low, from_high, got_2, out):
    index, _ = place()
    early = lax.rem(index[2], 4) < 2
    ends = got_2[...]
    first, second, third = from_low[80:96, :], own[...], from_high[80:96, :]
    pieces = (
        jnp.where(early, first, ends),
        jnp.where(early, second, first),
        jnp.where(early, third, second),
        jnp.where(early, ends, third),
    )
    for group in range(4):
        total = None
        for q in range(4):
            for d, piece in enumerate(pieces):
                to = 32 * q + 4 * d
                moved = lanes_of(roll(piece, to - 32 * group - 8 * q), to, 8)
                total = moved if total is None else total + moved
        out[group] = total


def divided(n, d):
    factor, bits = DIVIDE[d]
    return lax.shift_right_logical(n * factor, bits)


def build_bands(kernel, band):
    rows, columns, runs, group, outs = band
    row = iota((rows, 128), 0)
    shift = jnp.full((rows, 128), 99, jnp.int32)
    point = jnp.full((rows, 128), 99, jnp.int32)
    for start, count, offset in runs:
        at = row - start
        a = divided(at, count)
        inside = (at >= 0) & (at < 5 * count)
        shift = jnp.where(inside, a, shift)
        point = jnp.where(inside, offset + at - a * count, point)
    chosen = (shift == iota((rows, 128), 1)).astype(F32).astype(BF16)
    column = iota((8, columns), 1)
    block = divided(column, group)
    out_at = (column - block * group)[0:1]
    block = jnp.where((column - block * group) < outs, block, 9)
    sub = iota((8, columns), 0)
    entry = jnp.concatenate([point] * (columns // 128), axis=1) - out_at
    total_high = jnp.zeros((rows, columns), F32)
    total_low = jnp.zeros((rows, columns), F32)
    for c in range(5):
        source = jnp.zeros((8, columns), F32)
        for b in range(5):
            column_of = jnp.zeros((8, columns), F32)
            for a in range(5):
                column_of = jnp.where(sub == a, kernel[a, b, c], column_of)
            source = jnp.where(block == b, column_of, source)
        source = jnp.concatenate([source, jnp.zeros((120, columns), F32)], axis=0)
        high, low = split(source)
        fits = entry == c
        total_high = jnp.where(fits, dot(chosen, high), total_high)
        total_low = jnp.where(fits, dot(chosen, low), total_low)
    return total_high.astype(BF16), total_low.astype(BF16)


def bands_kernel(kernel_1, kernel_2, kernel_3, b1h, b1l, b2h, b2l, b3h, b3l):
    outs = ((b1h, b1l), (b2h, b2l), (b3h, b3l))
    for kernel, band, (high_ref, low_ref) in zip((kernel_1, kernel_2, kernel_3), BANDS, outs):
        high, low = build_bands(kernel, band)
        high_ref[...] = high
        low_ref[...] = low


def green_kernel(factors, packed, green_high, green_low, rise, framed, block_high, block_low):
    index, sizes = place()
    row, lane = iota((64, 128), 0), iota((64, 128), 1)
    delta_x = (lane // 8).astype(F32)
    delta_z = (4 * index[2] - 1 + lane % 8 - row).astype(F32)
    plain = delta_z * delta_z + (1.0 + delta_x * delta_x)
    for apart in range(18):
        high, low = split(0.0625 * lax.rsqrt(plain + float(apart * apart)))
        block_high[apart] = high
        block_low[apart] = low
    for ty in range(SPAN_4):
        columns = slice(128 * ty, 128 * ty + 128)
        for sy in range(16):
            apart = jnp.abs(4 * index[1] - 1 + ty - sy)
            first = sy % 8 * 128 + sy // 8 * 64
            green_high[first : first + 64, columns] = block_high[apart]
            green_low[first : first + 64, columns] = block_low[apart]
    variant = [
        jnp.where(index[d] == 0, 1, 0) + jnp.where(index[d] == sizes[d] - 1, 2, 0) for d in range(3)
    ]
    factor_x, factor_y = factors[variant[0]], factors[4 + variant[1]]
    kept = as_rows(factor_x[:, None, :] * factor_y[None, :, :])
    high, low = split(kept)
    rise[:, 0:128] = (high.astype(F32) + roll(low.astype(F32), 64)).astype(BF16)
    rise[:, 128:256] = high
    framed[:, 0:2, :] = jnp.zeros((32, 2, 128), F32)
    framed[:, 34:40, :] = jnp.zeros((32, 6, 128), F32)
    framed[:, 2:34, :] = packed[...]


def prolong_rows(source, target, count, whole):
    size = target.shape[1] // 2
    q0 = source[:, 0:size, :]
    q1 = source[:, 1 : size + 1, :]
    q2 = source[:, 2 : size + 2, :]
    even = 0.75 * q1 + 0.125 * (q0 + q2)
    odd = 0.5 * (q0 + q1) if whole else 0.5 * (q1 + q2)
    target[:, pl.ds(1 if whole else 0, size, stride=2), :] = even
    target[:, pl.ds(0 if whole else 1, size, stride=2), :] = odd


def prolong_plane(read, p, whole):
    half = p // 2
    if (p % 2 == 1) == whole:
        return 0.75 * read(half + 1) + 0.125 * (read(half) + read(half + 2))
    first = half if whole else half + 1
    return 0.5 * (read(first) + read(first + 1))


def near_kernel(
    wide, from_low, from_high, b1h, b1l, b2h, b2l, b3h, b3l, prol_2, prol_1,
    out,
    near_1, near_2, near_3, tall_3, tall_3y, tall_2, tall_2y,
):
    where = place()
    index, sizes = where
    low_msg = jnp.where(index[2] == 0, 0.0, from_low[...])
    high_msg = jnp.where(index[2] == sizes[2] - 1, 0.0, from_high[...])

    def halo(x, rows, base, count, low_at, high_at):
        low = roll(low_msg[base : base + rows], low_at - count * x)
        high = roll(high_msg[base : base + rows], high_at - count * x)
        return lanes_of(low, low_at, 5 * count) + lanes_of(high, high_at, 5 * count)

    planes = [lanes_of(wide[x, 0:16, :], THI, 11) for x in range(15)]
    left = []
    for x in range(SPAN_3):
        main = taps([(1.0, roll(planes[x + a], 11 * a - THI)) for a in range(5)])
        left.append(main + halo(x, 16, 64, 5, 64, 96))
    left = jnp.concatenate(left, axis=0)
    near_3[...] = jnp.zeros_like(near_3)
    near_3[:, 0:16, :] = dot_split(left, b3h[...], b3l[...]).reshape(SPAN_3, 16, 128)
    third = taps([(1.0, roll(near_3[:, b : b + 16, :], -16 * b)) for b in range(5)])
    third = jnp.where(inside_mask(third.shape, SPAN_3, 9, where), third, 0.0)
    tall_3[...] = jnp.zeros_like(tall_3)
    tall_3[:, 0:16, :] = dot_exact(as_rows(third), prol_2[...]).reshape(SPAN_3, 16, 128)
    prolong_rows(tall_3, tall_3y, SPAN_2, True)

    planes = [lanes_of(wide[x, 0:24, :], SEC, 18) for x in range(22)]
    left_a, left_b = [], []
    for x in range(SPAN_2):
        left_a.append(taps([(1.0, roll(planes[x + a], 18 * a - SEC)) for a in range(5)]))
        left_b.append(halo(x, 24, 40, 4, 0, 32))
    left = jnp.concatenate(
        [jnp.concatenate(left_a, axis=0), jnp.concatenate(left_b, axis=0)], axis=1
    )
    near_2[...] = jnp.zeros_like(near_2)
    near_2[:, 0:24, :] = dot_split(left, b2h[...], b2l[...]).reshape(SPAN_2, 24, 128)
    second = taps([(1.0, roll(near_2[:, b : b + 24, :], -24 * b)) for b in range(5)])
    raised = jnp.stack(
        [prolong_plane(lambda x: tall_3y[x], p, True) for p in range(SPAN_2)], axis=0
    )
    second = jnp.where(inside_mask(second.shape, SPAN_2, 17, where), second + raised, 0.0)
    tall_2[...] = jnp.zeros_like(tall_2)
    tall_2[:, 0:24, :] = dot_exact(as_rows(second), prol_1[...]).reshape(SPAN_2, 24, 128)
    prolong_rows(tall_2, tall_2y, 32, False)

    planes = [lanes_of(wide[x], 0, 32) for x in range(36)]
    left_a, left_b = [], []
    for x in range(32):
        left_a.append(taps([(1.0, roll(planes[x + a], 32 * a)) for a in range(4)]))
        left_b.append(planes[x + 4] + halo(x, 40, 0, 2, 32, 64))
    left = jnp.concatenate(
        [jnp.concatenate(left_a, axis=0), jnp.concatenate(left_b, axis=0)], axis=1
    )
    near_1[...] = dot_split(left, b1h[...], b1l[...]).reshape(32, 40, 256)
    for x in range(32):
        first = taps(
            [(1.0, roll(near_1[x, b : b + 32, 0:128], -32 * b)) for b in range(4)]
            + [(1.0, near_1[x, 4:36, 128:256])]
        )
        out[x] = first + prolong_plane(lambda q: tall_2y[q], x, False)


def top_kernel(
    base, piece_0, piece_1, piece_2, piece_3, green_high, green_low, rise, qz,
    out,
    fourth,
):
    index, sizes = place()
    lane = iota((8, 128), 1)
    ring = lax.rem(index[2], 4)
    first = 4 * (ring == 3).astype(jnp.int32) - 4 * (ring == 0).astype(jnp.int32) + 127
    sources = [lax.rem(16 * lax.rem(index[2] // 4 + step, 4) + first, 128) for step in (0, 3, 1, 2)]
    for x in range(16):
        total = None
        for piece, at in zip((piece_0, piece_1, piece_2, piece_3), sources):
            kept = lanes_of(piece[x // 4], 32 * (x % 4), 32)
            moved = pltpu.roll(kept, lax.rem(at + 128 - 32 * (x % 4), 128), 1)
            total = moved if total is None else total + moved
        total = total + roll(total, 64)
        fourth[x] = jnp.where(lane < 64, total[0:8], total[8:16])
    total = jnp.zeros((32, 128 * SPAN_4), F32)
    extra = jnp.zeros((16, 128 * SPAN_4), F32)
    for s in range(0, 8, 2):
        left = jnp.concatenate([fourth[:, s, :], fourth[:, s + 1, :]], axis=1)
        high, low = split(left)
        rows = slice(128 * s, 128 * s + 256)
        total = total + dot(jnp.concatenate([high, low], axis=0), green_high[rows, :])
        extra = extra + dot(high, green_low[rows, :])
    sums = total[0:16] + (total[16:32] + extra)
    row, lane = iota((16, 128), 0), iota((16, 128), 1)
    tops = []
    for tx in range(SPAN_4):
        keep = jnp.abs(4 * index[0] - 1 + tx - row) == lane // 8
        for ty in range(SPAN_4):
            picked = jnp.where(keep, sums[:, 128 * ty : 128 * ty + 128], 0.0)
            tops.append(jnp.sum(picked, axis=0, keepdims=True))
        tops.append(jnp.zeros((1, 128), F32))
    tops = jnp.concatenate(tops + [jnp.zeros((8, 128), F32)], axis=0)
    variant = jnp.where(index[2] == 0, 1, 0) + jnp.where(index[2] == sizes[2] - 1, 2, 0)
    high, low = split(dot_split(tops, qz[variant], qz[4 + variant]))
    right = jnp.concatenate([high, high, low, jnp.zeros_like(low)], axis=0)
    far = dot(rise[...], right)
    out[...] = (base[...] + far.reshape(32, 32, 128))[:, :, 0:32]


def call(kernel, outs, ins, scratch=(), megabytes=16, spaces=None, aliases=None):
    spaces = spaces or {}
    return pl.pallas_call(
        kernel,
        out_shape=outs,
        in_specs=[spaces.get(i, VMEM) for i in range(len(ins))],
        out_specs=jax.tree.map(lambda _: VMEM, outs),
        scratch_shapes=list(scratch),
        input_output_aliases=aliases or {},
        compiler_params=pltpu.CompilerParams(vmem_limit_bytes=int(megabytes * 2**20)),
        cost_estimate=pl.CostEstimate(flops=1000000, bytes_accessed=2**21, transcendentals=0),
    )(*ins)


def shape(*dims, dtype=F32):
    return jax.ShapeDtypeStruct(dims, dtype)


def exchange(values, axis, steps):
    size = lax.axis_size(axis)
    return [
        lax.ppermute(value, axis, [(i, i ^ step) for i in range(size)])
        for value, step in zip(values, steps)
    ]


def turn(value, by):
    size_y, size_z = lax.axis_size("gy"), lax.axis_size("gz")
    half = size_y // 2
    pairs = []
    for core in range(half):
        ring = [(high * half + core) * size_z + z for high in range(2) for z in range(size_z)]
        pairs += [(ring[n], ring[(n + by) % len(ring)]) for n in range(len(ring))]
    return lax.ppermute(value, ("gy", "gz"), pairs)


ANY = pl.BlockSpec(memory_space=pl.ANY)


def shards(charges, counts, slots, spline, kernel_fine, kernel_mid, kernel_coarse):
    cells = charges.shape[0]
    packed, raw, face = call(
        deposit_kernel,
        (shape(32, 32, 128), shape(8, 128), shape(88, 128)),
        (256 * slots + counts, charges, spline.reshape(cells * 12, ATOMS)),
        (
            pltpu.VMEM((cells, ATOMS), F32),
            pltpu.VMEM((cells * 12, 128), BF16),
            pltpu.VMEM((cells * 12, 128), F32),
            pltpu.VMEM((64, cells), F32),
            pltpu.VMEM((32, 32, 128), F32),
            pltpu.VMEM((SPAN_2, 56, 128), F32),
            pltpu.VMEM((SPAN_3, 40, 128), F32),
            pltpu.VMEM((SPAN_4, 24, 128), F32),
            pltpu.VMEM((SPAN_2, 24, 128), F32),
            pltpu.VMEM((SPAN_3, 16, 128), F32),
            pltpu.SemaphoreType.DMA((4,)),
        ),
        spaces={1: HBM, 2: HBM},
        megabytes=53.75,
    )
    (got_1,) = exchange((face,), "gy", (1,))
    relay = call(relay_kernel, shape(48, 128), (raw, got_1))
    (got_2,) = exchange((relay,), "gy", (2,))
    qx, qy, qz = composites()
    qz_high = qz.astype(BF16)
    qz_low = (qz - qz_high.astype(np.float32)).astype(BF16)
    green_high, green_low, rise, framed = call(
        green_kernel,
        (
            shape(1024, 128 * SPAN_4, dtype=BF16),
            shape(1024, 128 * SPAN_4, dtype=BF16),
            shape(1024, 256, dtype=BF16),
            shape(32, 40, 128),
        ),
        (jnp.asarray(np.concatenate([qx, qy])), packed),
        (pltpu.VMEM((18, 64, 128), BF16), pltpu.VMEM((18, 64, 128), BF16)),
    )
    wide_y, raw, face_1, face_3 = call(
        widen_y_kernel,
        (shape(32, 40, 128), shape(8, 128), shape(72, 128), shape(72, 128)),
        (framed, relay, got_1, got_2, rise),
        spaces={4: ANY},
        aliases={0: 0},
    )
    got_2, got_3, got_1 = exchange((raw, face_3, face_1), "gx", (2, 3, 1))
    bands = call(
        bands_kernel,
        tuple(shape(band[0], band[1], dtype=BF16) for band in BANDS for _ in range(2)),
        (kernel_fine, kernel_mid, kernel_coarse),
        spaces={0: SMEM, 1: SMEM, 2: SMEM},
    )
    wide_x, raw, to_high, to_low = call(
        widen_x_kernel,
        (shape(36, 40, 128), shape(16, 128), shape(96, 128), shape(96, 128)),
        (wide_y, raw, got_1, got_3, got_2, bands[0]),
        spaces={5: ANY},
    )
    from_low, from_high = turn(to_high, 1), turn(to_low, -1)
    (got_2,) = exchange((raw,), "gz", (2,))
    window = call(window_kernel, shape(4, 16, 128), (raw, from_low, from_high, got_2))
    pieces = [window] + [turn(window, by) for by in (4, -4, 8)]
    base = call(
        near_kernel,
        shape(32, 32, 128),
        (wide_x, from_low, from_high, *bands, jnp.asarray(PROL_2, BF16), jnp.asarray(PROL_1, BF16)),
        (
            pltpu.VMEM((32, 40, 256), F32),
            pltpu.VMEM((SPAN_2, 32, 128), F32),
            pltpu.VMEM((SPAN_3, 24, 128), F32),
            pltpu.VMEM((SPAN_3, 24, 128), F32),
            pltpu.VMEM((SPAN_3, 24, 128), F32),
            pltpu.VMEM((SPAN_2, 32, 128), F32),
            pltpu.VMEM((SPAN_2, 32, 128), F32),
        ),
    )
    return call(
        top_kernel,
        shape(32, 32, 32),
        (base, *pieces, green_high, green_low, rise, jnp.asarray(np.concatenate([qz_high, qz_low]))),
        (pltpu.VMEM((16, 8, 128), F32),),
    )


def solution(mesh):
    return jax.shard_map(
        shards,
        mesh=mesh,
        in_specs=(
            P(("gx", "gy", "gz"), None),
            P(("gx", "gy", "gz")),
            P(("gx", "gy", "gz")),
            P(("gx", "gy", "gz"), None, None, None),
            P(),
            P(),
            P(),
        ),
        out_specs=P("gx", "gy", "gz"),
        check_vma=False,
    )
```

```python
import jax
import jax.numpy as jnp
import numpy as np
from jax import lax
from jax.experimental import pallas as pl
from jax.experimental.pallas import tpu as pltpu
from jax.sharding import PartitionSpec as P

W = (0.125, 0.5, 0.75, 0.5, 0.125)
F32 = jnp.float32
BF16 = jnp.bfloat16
CELLS = 384
ATOMS = 128
SPAN_2 = 18
SPAN_3 = 11
SPAN_4 = 7
SEC = 32
THI = 64
VMEM = pl.BlockSpec(memory_space=pltpu.VMEM)
SMEM = pl.BlockSpec(memory_space=pltpu.SMEM)
HBM = pl.BlockSpec(memory_space=pltpu.HBM)
ANY = pl.BlockSpec(memory_space=pl.ANY)


def weight(t):
    return W[t] if 0 <= t <= 4 else 0.0


def table(rows, columns, offset, turned):
    out = np.zeros((128, 128), np.float32)
    for r in range(rows):
        for c in range(columns):
            out[r, c] = weight(c - 2 * r + offset if turned else r - 2 * c + offset)
    return out


PROL_2 = table(SPAN_3, SPAN_2, 3, True)
PROL_1 = table(SPAN_2, 32, 4, True)


BANDS = (
    (256, 256, ((0, 32, 2), (160, 2, 0), (192, 2, 34)), 32, 32),
    (256, 128, ((0, 18, 2), (128, 4, 0), (160, 4, 18)), 24, 18),
    (128, 128, ((0, 11, 2), (64, 5, 0), (96, 5, 10)), 16, 11),
)
DIVIDE = {32: (1, 5), 2: (1, 1), 18: (57, 10), 4: (1, 2), 11: (94, 10), 5: (52, 8), 24: (43, 10), 16: (1, 4)}


def composite(first, last):
    p3 = np.array([[weight(i - 2 * j + 3) for j in range(7)] for i in range(11)])
    p2 = np.array([[weight(i - 2 * j + 3) for j in range(11)] for i in range(18)])
    p1 = np.array([[weight(i - 2 * j + 4) for j in range(18)] for i in range(32)])
    m4, m3, m2 = np.ones(7), np.ones(11), np.ones(18)
    if first:
        m4[0] = m3[0] = m2[0] = 0
    if last:
        m4[5:] = 0
        m3[9:] = 0
        m2[17:] = 0
    return (p1 * m2) @ (p2 * m3) @ (p3 * m4)


def composites():
    qx = np.zeros((4, 32, 128), np.float32)
    qy = np.zeros((4, 32, 128), np.float32)
    qz = np.zeros((4, 128, 128), np.float32)
    for v in range(4):
        q = composite(v % 2 == 1, v >= 2)
        for lane in range(64):
            if lane // 8 < 7 and lane % 8 < 7:
                qx[v, :, lane] = q[:, lane // 8]
                qy[v, :, lane] = q[:, lane % 8]
        for row in range(128):
            if row % 8 < 7:
                qz[v, row, :32] = q[:, row % 8]
    return qx, qy, qz


def split(x):
    high = x.astype(BF16)
    return high, (x - high.astype(F32)).astype(BF16)


def dot(a, b):
    return jnp.dot(a, b, preferred_element_type=F32)


def dot_exact(x, right):
    high, low = split(x)
    return dot(high, right) + dot(low, right)


def dot_split(x, right_high, right_low):
    high, low = split(x)
    return dot(high, right_high) + (dot(low, right_high) + dot(high, right_low))


def iota(shape, dim):
    return lax.broadcasted_iota(jnp.int32, shape, dim)


def roll(x, shift, axis=None):
    axis = x.ndim - 1 if axis is None else axis
    shift = shift % x.shape[axis]
    return x if shift == 0 else pltpu.roll(x, shift, axis)


def lanes_of(x, low, count):
    lane = iota(x.shape, x.ndim - 1)
    return jnp.where((lane >= low) & (lane < low + count), x, 0.0)


def as_rows(x):
    return x.reshape(x.shape[0] * x.shape[1], x.shape[2])


def taps(pieces):
    total = None
    for factor, value in pieces:
        term = value if factor == 1.0 else factor * value
        total = term if total is None else total + term
    return total


def restrict_planes(read, span, size, offset):
    planes = []
    for p in range(span):
        planes.append(
            taps([(W[t], read(2 * p + t - offset)) for t in range(5) if 0 <= 2 * p + t - offset < size])
        )
    return planes


def place():
    sizes = [lax.axis_size(a) for a in ("gx", "gy", "gz")]
    index = [lax.axis_index(a) for a in ("gx", "gy", "gz")]
    return index, sizes


def inside_mask(shape, spans, high, place_of):
    index, sizes = place_of
    keep = None
    for dim in range(3):
        at = iota(shape, dim)
        low = jnp.where(index[dim] == 0, 1, 0)
        top = jnp.where(index[dim] == sizes[dim] - 1, high, spans)
        part = (at >= low) & (at < top)
        keep = part if keep is None else keep & part
    return keep


def nearest(index):
    even = lax.rem(index, 2) == 0
    return even, index == 1, index == 2


def deposit_kernel(
    codes, charges_hbm, spline_hbm,
    packed_hbm, raw_out, face,
    packed, charges, spline, wide, patch, fine, buf_2, buf_3, buf_4, sems,
):
    where = place()
    index, sizes = where
    part = CELLS * 12 // 3
    copies = [pltpu.make_async_copy(charges_hbm, charges, sems.at[3])]
    for chunk in range(3):
        rows = slice(part * chunk, part * chunk + part)
        copies.append(
            pltpu.make_async_copy(spline_hbm.at[rows, :], spline.at[rows, :], sems.at[chunk])
        )
    for copy in copies:
        copy.start()
    buf_2[...] = jnp.zeros_like(buf_2)
    buf_3[...] = jnp.zeros_like(buf_3)
    buf_4[...] = jnp.zeros_like(buf_4)
    row, column = iota((512, 64), 0), iota((512, 64), 1)
    spread = (row // 32 * 4 + row % 4 == column).astype(F32).astype(BF16)
    row, column = iota((128, 128), 0), iota((128, 128), 1)

    def restriction(rows, columns, offset):
        t = row - 2 * column + offset
        out = jnp.zeros((128, 128), F32)
        for tap in range(5):
            out = jnp.where(t == tap, W[tap], out)
        return jnp.where((row < rows) & (column < columns), out, 0.0).astype(BF16)

    rest_2 = restriction(32, SPAN_2, 4)
    rest_3 = restriction(SPAN_2, SPAN_3, 3)
    rest_4 = restriction(SPAN_3, SPAN_4, 3)
    slot = lax.shift_right_logical(codes[...].reshape(1, CELLS), 8)
    fits = (iota((512, CELLS), 0) // 4 % 8) == slot % 8
    hot = (iota((64, CELLS), 0) == slot // 8).astype(F32).astype(BF16)
    copies[0].wait()
    alive = iota((ATOMS, CELLS), 0) < (codes[...].reshape(1, CELLS) & 255)
    weighted = jnp.where(alive, charges[...].T, 0.0)
    for chunk in range(CELLS // 128):
        lanes = slice(128 * chunk, 128 * chunk + 128)
        copies[1 + chunk].wait()
        rows = slice(part * chunk, part * chunk + part)
        wide[rows, :] = spline[rows, :].astype(F32)

        def column_of(d, i):
            return wide[pl.ds(chunk * part + 4 * d + i, 128, stride=12), :].T

        charge = weighted[:, lanes]
        depth = [charge * column_of(2, k) for k in range(4)]
        ys = [column_of(1, j) for j in range(4)]
        for i in range(4):
            xs = column_of(0, i)
            for j in range(4):
                cross = xs * ys[j]
                for k in range(4):
                    patch[16 * i + 4 * j + k : 16 * i + 4 * j + k + 1, lanes] = jnp.sum(
                        cross * depth[k], axis=0, keepdims=True
                    )
    high, low = split(patch[...])
    spread_high = jnp.where(fits, dot(spread, high), 0.0).astype(BF16)
    spread_low = jnp.where(fits, dot(spread, low), 0.0).astype(BF16)
    nt = (((1,), (1,)), ((), ()))
    placed = lax.dot_general(hot, spread_high, nt, preferred_element_type=F32) + lax.dot_general(
        hot, spread_low, nt, preferred_element_type=F32
    )
    for i in range(4):
        for j in range(4):
            rows = lanes_of(roll(placed[:, 128 * i : 128 * i + 128], -32 * j), 0, 32)
            for sx in range(8):
                fine[4 * sx + i, pl.ds(j, 8, stride=4), :] = rows[8 * sx : 8 * sx + 8]

    for p, plane in enumerate(restrict_planes(lambda x: fine[x], SPAN_2, 32, 4)):
        buf_2[p, 4:36, :] = plane
    second = taps([(W[t], buf_2[:, pl.ds(t, 24, stride=2), :]) for t in range(5)])
    second = dot_exact(as_rows(second), rest_2).reshape(SPAN_2, 24, 128)
    second = jnp.where(inside_mask(second.shape, SPAN_2, 17, where), second, 0.0)
    for p, plane in enumerate(restrict_planes(lambda x: second[x], SPAN_3, SPAN_2, 3)):
        buf_3[p, 3:27, :] = plane
    third = taps([(W[t], buf_3[:, pl.ds(t, 16, stride=2), :]) for t in range(5)])
    third = dot_exact(as_rows(third), rest_3).reshape(SPAN_3, 16, 128)
    third = jnp.where(inside_mask(third.shape, SPAN_3, 9, where), third, 0.0)
    packed[...] = fine[...]
    packed[0:SPAN_2, 0:24, :] += roll(second, SEC)
    packed[0:SPAN_3, 0:16, :] += roll(third, THI)
    leave = pltpu.make_async_copy(packed, packed_hbm, sems.at[4])
    leave.start()
    for p, plane in enumerate(restrict_planes(lambda x: third[x], SPAN_4, SPAN_3, 3)):
        buf_4[p, 3:19, :] = plane
    last = taps([(W[t], buf_4[:, pl.ds(t, 8, stride=2), :]) for t in range(5)])
    last = dot_exact(as_rows(last), rest_4).reshape(SPAN_4, 8, 128)
    last = jnp.where(inside_mask(last.shape, SPAN_4, 5, where), last, 0.0)
    raw = taps([(1.0, roll(last[x], 8 * x)) for x in range(SPAN_4)])
    raw_out[...] = raw

    even, _, _ = nearest(index[1])
    low = pack_y(packed, FIRST_ROWS)
    high = pack_y(packed, LAST_ROWS)
    for v in range(4):
        face[8 * v : 8 * v + 8, :] = jnp.where(even, high[v], low[v])
        face[FACE + 8 * v : FACE + 8 * v + 8, :] = jnp.where(even, low[v], high[v])
    face[2 * FACE : 2 * FACE + 8, :] = raw
    leave.wait()


def spot_1(p):
    return p // 16, p % 16 // 4 * 2, p % 4 * 32


def spot_2(p):
    return 2 + p // 14, p % 14 // 7 * 4, p % 7 * 18


def spot_3(p):
    return 3, 4, p * 11


def spot_4(p):
    return 3, p // 5, 72 + p % 5 * 11


FACE = 32
LEVELS = (
    (32, 2, 0, 32, spot_1),
    (SPAN_2, 4, SEC, 18, spot_2),
    (SPAN_3, 4, THI, 11, spot_3),
    (SPAN_3, 1, THI, 11, spot_4),
)
FIRST_ROWS = (0, 0, 0, 4)
LAST_ROWS = (30, 14, 6, 10)
ROWS_ABOVE = (34, 18, 10, 14)


def pack_y(source, at):
    tiles = [jnp.zeros((8, 128), F32) for _ in range(4)]
    row, at_lane = iota((8, 128), 0), iota((8, 128), 1)
    for (planes, count, lane, width, spot), start in zip(LEVELS, at):
        for p in range(planes):
            v, r, to = spot(p)
            if start == 30:
                slab = roll(source[p, 24:32, :], r - 6, 0)
            else:
                slab = roll(source[p, start : start + 8, :], r, 0)
            slab = roll(slab, to - lane)
            keep = (row >= r) & (row < r + count) & (at_lane >= to) & (at_lane < to + width)
            tiles[v] = jnp.where(keep, slab, tiles[v])
    return tiles


def place_y(tile, index):
    tall = jnp.concatenate([tile, jnp.zeros((8, 128), F32)], axis=0)
    tall = pltpu.roll(tall, lax.rem(4 * index + 15, 16), 0)
    return tall[0:8] + roll(tall[8:16], 64)


def relay_kernel(raw, got, out):
    index, _ = place()
    out[0:FACE, :] = got[FACE : 2 * FACE, :]
    partner = jnp.bitwise_xor(index[1], 1)
    other = got[2 * FACE : 2 * FACE + 8, :]
    out[FACE : FACE + 8, :] = place_y(raw[...], index[1]) + place_y(other, partner)


def widen_y_kernel(framed, own, got_1, got_2, after, out, raw_out, face_1, face_3):
    index, _ = place()
    even, one, two = nearest(index[1])
    total = own[FACE : FACE + 8, :] + got_2[FACE : FACE + 8, :]
    raw_out[...] = total
    a, b = got_1[0:FACE, :], got_2[0:FACE, :]
    low = jnp.where(even, 0.0, a) + jnp.where(two, b, 0.0)
    high = jnp.where(even, a, 0.0) + jnp.where(one, b, 0.0)
    for face, at in ((low, FIRST_ROWS), (high, ROWS_ABOVE)):
        for (planes, count, lane, width, spot), start in zip(LEVELS, at):
            for p in range(planes):
                v, r, to = spot(p)
                slab = roll(roll(face[8 * v : 8 * v + 8], -r, 0), lane - to)
                slab = lanes_of(slab, lane, width)
                out[p, start : start + count, :] += slab[0:count]
    even, one, _ = nearest(index[0])
    for ref, to_high in ((face_1, even), (face_3, one)):
        f = jnp.where(to_high, 30, 0)
        s = jnp.where(to_high, 14, 0)
        t = jnp.where(to_high, 6, 0)
        ref[0:40, :] = lanes_of(out[f], 0, 32) + lanes_of(roll(out[f + 1], 32), 32, 32)
        ref[0:16, :] += taps(
            [(1.0, lanes_of(roll(out[t + k, 0:16, :], 11 * k), THI + 11 * k, 11)) for k in range(5)]
        )
        ref[40:64, :] = taps(
            [(1.0, lanes_of(roll(out[s + k, 0:24, :], 18 * k - SEC), 18 * k, 18)) for k in range(4)]
        )
        ref[64:72, :] = total


def widen_x_kernel(wide_y, own, got_1, got_3, got_2, after, out, raw_out, to_high, to_low):
    index, _ = place()
    even, one, two = nearest(index[0])
    total = None
    lane = iota((16, 128), 1)
    for step, tile in ((0, own[...]), (1, got_1[64:72, :]), (2, got_2[...]), (3, got_3[64:72, :])):
        tall = jnp.concatenate([tile, roll(tile, 64)], axis=0)
        tall = jnp.where(lane < 64, tall, 0.0)
        at = lax.rem(32 * jnp.bitwise_xor(index[0], step) + 120, 128)
        moved = pltpu.roll(tall, at, 1)
        total = moved if total is None else total + moved
    raw_out[...] = total
    a, b = got_1[...], got_3[...]
    low = jnp.where(even, 0.0, a) + jnp.where(two, b, 0.0)
    high = jnp.where(even, a, 0.0) + jnp.where(one, b, 0.0)
    out[0:2] = jnp.zeros((2, 40, 128), F32)
    out[34:36] = jnp.zeros((2, 40, 128), F32)
    out[2:34] = wide_y[...]
    for face, at in ((low, (0, 0, 0)), (high, (34, 18, 10))):
        for k in range(2):
            out[at[0] + k] += lanes_of(roll(face[0:40], -32 * k), 0, 32)
        for k in range(4):
            out[at[1] + k, 0:24, :] += lanes_of(roll(face[40:64], SEC - 18 * k), SEC, 18)
        for k in range(5):
            out[at[2] + k, 0:16, :] += lanes_of(roll(face[0:16], -11 * k), THI, 11)
    for ref, high in ((to_high, True), (to_low, False)):
        pack_z(out, ref, high)
        ref[64:80, :] = total


def pack_z(source, face, to_high):
    sums = []
    for rows, planes, count, lane, high in ((40, 36, 2, 0, 30), (24, 22, 4, SEC, 14), (16, 15, 5, THI, 6)):
        first = lane + high if to_high else lane
        at = iota((rows, 128), 1)
        wanted = (at >= first) & (at < first + count)
        total = jnp.zeros((rows, 128), F32)
        for x in range(planes):
            kept = jnp.where(wanted, source[x, 0:rows, :], 0.0)
            total = total + roll(kept, count * x - first)
        sums.append(total)
    face[0:40, :] = sums[0]
    face[40:64, :] = sums[1]
    face[0:16, :] += lanes_of(roll(sums[2], 72), 72, 55)
    face[40:56, :] += lanes_of(roll(sums[2], 88 - 55), 88, 20)


def unpack_z(message):
    third = lanes_of(roll(message[0:16], -72), 0, 55) + lanes_of(roll(message[40:56], 55 - 88), 55, 20)
    return message[0:40], message[40:64], third


def window_kernel(own, from_low, from_high, got_2, out):
    index, _ = place()
    early = lax.rem(index[2], 4) < 2
    ends = got_2[...]
    first, second, third = from_low[64:80, :], own[...], from_high[64:80, :]
    pieces = (
        jnp.where(early, first, ends),
        jnp.where(early, second, first),
        jnp.where(early, third, second),
        jnp.where(early, ends, third),
    )
    for group in range(3):
        total = None
        for q in range(min(6, 16 - 6 * group)):
            for d, piece in enumerate(pieces):
                to = 20 * q + 4 * d
                moved = lanes_of(roll(piece, to - 48 * group - 8 * q), to, 8)
                total = moved if total is None else total + moved
        out[group] = total


def divided(n, d):
    factor, bits = DIVIDE[d]
    return lax.shift_right_logical(n * factor, bits)


def build_bands(kernel, band):
    rows, columns, runs, group, outs = band
    row = iota((rows, 128), 0)
    shift = jnp.full((rows, 128), 99, jnp.int32)
    point = jnp.full((rows, 128), 99, jnp.int32)
    for start, count, offset in runs:
        at = row - start
        a = divided(at, count)
        inside = (at >= 0) & (at < 5 * count)
        shift = jnp.where(inside, a, shift)
        point = jnp.where(inside, offset + at - a * count, point)
    chosen = (shift == iota((rows, 128), 1)).astype(F32).astype(BF16)
    column = iota((8, columns), 1)
    block = divided(column, group)
    out_at = (column - block * group)[0:1]
    block = jnp.where((column - block * group) < outs, block, 9)
    sub = iota((8, columns), 0)
    entry = jnp.concatenate([point] * (columns // 128), axis=1) - out_at
    total_high = jnp.zeros((rows, columns), F32)
    total_low = jnp.zeros((rows, columns), F32)
    for c in range(5):
        source = jnp.zeros((8, columns), F32)
        for b in range(5):
            column_of = jnp.zeros((8, columns), F32)
            for a in range(5):
                column_of = jnp.where(sub == a, kernel[a, b, c], column_of)
            source = jnp.where(block == b, column_of, source)
        source = jnp.concatenate([source, jnp.zeros((120, columns), F32)], axis=0)
        high, low = split(source)
        fits = entry == c
        total_high = jnp.where(fits, dot(chosen, high), total_high)
        total_low = jnp.where(fits, dot(chosen, low), total_low)
    return total_high.astype(BF16), total_low.astype(BF16)


def bands_kernel(kernel_1, kernel_2, kernel_3, b1h, b1l, b2h, b2l, b3h, b3l):
    outs = ((b1h, b1l), (b2h, b2l), (b3h, b3l))
    for kernel, band, (high_ref, low_ref) in zip((kernel_1, kernel_2, kernel_3), BANDS, outs):
        high, low = build_bands(kernel, band)
        high_ref[...] = high
        low_ref[...] = low


def green_kernel(factors, packed, green_high, green_low, rise, framed, block_high, block_low):
    index, sizes = place()
    row, lane = iota((64, 128), 0), iota((64, 128), 1)
    delta_x = (lane // 8).astype(F32)
    delta_z = (4 * index[2] - 1 + lane % 8 - row).astype(F32)
    plain = delta_z * delta_z + (1.0 + delta_x * delta_x)
    for apart in range(18):
        high, low = split(0.0625 * lax.rsqrt(plain + float(apart * apart)))
        block_high[apart] = high
        block_low[apart] = low
    for ty in range(SPAN_4):
        columns = slice(128 * ty, 128 * ty + 128)
        for sy in range(16):
            apart = jnp.abs(4 * index[1] - 1 + ty - sy)
            first = sy % 8 * 128 + sy // 8 * 64
            green_high[first : first + 64, columns] = block_high[apart]
            green_low[first : first + 64, columns] = block_low[apart]
    variant = [
        jnp.where(index[d] == 0, 1, 0) + jnp.where(index[d] == sizes[d] - 1, 2, 0) for d in range(3)
    ]
    factor_x, factor_y = factors[variant[0]], factors[4 + variant[1]]
    kept = as_rows(factor_x[:, None, :] * factor_y[None, :, :])
    high, low = split(kept)
    rise[:, 0:128] = (high.astype(F32) + roll(low.astype(F32), 64)).astype(BF16)
    rise[:, 128:256] = high
    framed[:, 0:2, :] = jnp.zeros((32, 2, 128), F32)
    framed[:, 34:40, :] = jnp.zeros((32, 6, 128), F32)
    framed[:, 2:34, :] = packed[...]


def prolong_rows(source, target, count, whole):
    size = target.shape[1] // 2
    q0 = source[:, 0:size, :]
    q1 = source[:, 1 : size + 1, :]
    q2 = source[:, 2 : size + 2, :]
    even = 0.75 * q1 + 0.125 * (q0 + q2)
    odd = 0.5 * (q0 + q1) if whole else 0.5 * (q1 + q2)
    target[:, pl.ds(1 if whole else 0, size, stride=2), :] = even
    target[:, pl.ds(0 if whole else 1, size, stride=2), :] = odd


def prolong_plane(read, p, whole):
    half = p // 2
    if (p % 2 == 1) == whole:
        return 0.75 * read(half + 1) + 0.125 * (read(half) + read(half + 2))
    first = half if whole else half + 1
    return 0.5 * (read(first) + read(first + 1))


def near_kernel(
    wide, from_low, from_high, b1h, b1l, b2h, b2l, b3h, b3l, prol_2, prol_1,
    out,
    near_1, near_2, near_3, tall_3, tall_3y, tall_2, tall_2y,
):
    where = place()
    index, sizes = where
    low_faces = unpack_z(jnp.where(index[2] == 0, 0.0, from_low[0:64, :]))
    high_faces = unpack_z(jnp.where(index[2] == sizes[2] - 1, 0.0, from_high[0:64, :]))

    def halo(x, level, count, low_at, high_at):
        low = roll(low_faces[level], low_at - count * x)
        high = roll(high_faces[level], high_at - count * x)
        return lanes_of(low, low_at, 5 * count) + lanes_of(high, high_at, 5 * count)

    planes = [lanes_of(wide[x, 0:16, :], THI, 11) for x in range(15)]
    left = []
    for x in range(SPAN_3):
        main = taps([(1.0, roll(planes[x + a], 11 * a - THI)) for a in range(5)])
        left.append(main + halo(x, 2, 5, 64, 96))
    left = jnp.concatenate(left, axis=0)
    near_3[...] = jnp.zeros_like(near_3)
    near_3[:, 0:16, :] = dot_split(left, b3h[...], b3l[...]).reshape(SPAN_3, 16, 128)
    third = taps([(1.0, roll(near_3[:, b : b + 16, :], -16 * b)) for b in range(5)])
    third = jnp.where(inside_mask(third.shape, SPAN_3, 9, where), third, 0.0)
    tall_3[...] = jnp.zeros_like(tall_3)
    tall_3[:, 0:16, :] = dot_exact(as_rows(third), prol_2[...]).reshape(SPAN_3, 16, 128)
    prolong_rows(tall_3, tall_3y, SPAN_2, True)

    planes = [lanes_of(wide[x, 0:24, :], SEC, 18) for x in range(22)]
    left_a, left_b = [], []
    for x in range(SPAN_2):
        left_a.append(taps([(1.0, roll(planes[x + a], 18 * a - SEC)) for a in range(5)]))
        left_b.append(halo(x, 1, 4, 0, 32))
    left = jnp.concatenate(
        [jnp.concatenate(left_a, axis=0), jnp.concatenate(left_b, axis=0)], axis=1
    )
    near_2[...] = jnp.zeros_like(near_2)
    near_2[:, 0:24, :] = dot_split(left, b2h[...], b2l[...]).reshape(SPAN_2, 24, 128)
    second = taps([(1.0, roll(near_2[:, b : b + 24, :], -24 * b)) for b in range(5)])
    raised = jnp.stack(
        [prolong_plane(lambda x: tall_3y[x], p, True) for p in range(SPAN_2)], axis=0
    )
    second = jnp.where(inside_mask(second.shape, SPAN_2, 17, where), second + raised, 0.0)
    tall_2[...] = jnp.zeros_like(tall_2)
    tall_2[:, 0:24, :] = dot_exact(as_rows(second), prol_1[...]).reshape(SPAN_2, 24, 128)
    prolong_rows(tall_2, tall_2y, 32, False)

    planes = [lanes_of(wide[x], 0, 32) for x in range(36)]
    left_a, left_b = [], []
    for x in range(32):
        left_a.append(taps([(1.0, roll(planes[x + a], 32 * a)) for a in range(4)]))
        left_b.append(planes[x + 4] + halo(x, 0, 2, 32, 64))
    left = jnp.concatenate(
        [jnp.concatenate(left_a, axis=0), jnp.concatenate(left_b, axis=0)], axis=1
    )
    near_1[...] = dot_split(left, b1h[...], b1l[...]).reshape(32, 40, 256)
    for x in range(32):
        first = taps(
            [(1.0, roll(near_1[x, b : b + 32, 0:128], -32 * b)) for b in range(4)]
            + [(1.0, near_1[x, 4:36, 128:256])]
        )
        out[x] = first + prolong_plane(lambda q: tall_2y[q], x, False)


def top_kernel(
    base, piece_0, piece_1, piece_2, piece_3, green_high, green_low, rise, qz,
    out_hbm,
    fourth, out, sems,
):
    index, sizes = place()
    lane = iota((8, 128), 1)
    ring = lax.rem(index[2], 4)
    first = 4 * (ring == 3).astype(jnp.int32) - 4 * (ring == 0).astype(jnp.int32) + 127
    sources = [lax.rem(16 * lax.rem(index[2] // 4 + step, 4) + first, 128) for step in (0, 3, 1, 2)]
    for x in range(16):
        total = None
        for piece, at in zip((piece_0, piece_1, piece_2, piece_3), sources):
            kept = lanes_of(piece[x // 6], 20 * (x % 6), 20)
            moved = pltpu.roll(kept, lax.rem(at + 128 - 20 * (x % 6), 128), 1)
            total = moved if total is None else total + moved
        total = total + roll(total, 64)
        fourth[x] = jnp.where(lane < 64, total[0:8], total[8:16])
    total = jnp.zeros((32, 128 * SPAN_4), F32)
    extra = jnp.zeros((16, 128 * SPAN_4), F32)
    for s in range(0, 8, 2):
        left = jnp.concatenate([fourth[:, s, :], fourth[:, s + 1, :]], axis=1)
        high, low = split(left)
        rows = slice(128 * s, 128 * s + 256)
        total = total + dot(jnp.concatenate([high, low], axis=0), green_high[rows, :])
        extra = extra + dot(high, green_low[rows, :])
    sums = total[0:16] + (total[16:32] + extra)
    row, lane = iota((16, 128), 0), iota((16, 128), 1)
    tops = []
    for tx in range(SPAN_4):
        keep = jnp.abs(4 * index[0] - 1 + tx - row) == lane // 8
        for ty in range(SPAN_4):
            picked = jnp.where(keep, sums[:, 128 * ty : 128 * ty + 128], 0.0)
            tops.append(jnp.sum(picked, axis=0, keepdims=True))
        tops.append(jnp.zeros((1, 128), F32))
    tops = jnp.concatenate(tops + [jnp.zeros((8, 128), F32)], axis=0)
    variant = jnp.where(index[2] == 0, 1, 0) + jnp.where(index[2] == sizes[2] - 1, 2, 0)
    high, low = split(dot_split(tops, qz[variant], qz[4 + variant]))
    right = jnp.concatenate([high, high, low, jnp.zeros_like(low)], axis=0)
    copies = []
    for part in range(4):
        planes = slice(8 * part, 8 * part + 8)
        far = dot(rise[256 * part : 256 * part + 256, :], right)
        out[planes] = (base[planes] + far.reshape(8, 32, 128))[:, :, 0:32]
        copies.append(pltpu.make_async_copy(out.at[planes], out_hbm.at[planes], sems.at[part]))
        copies[-1].start()
    for copy in copies:
        copy.wait()


def call(kernel, outs, ins, scratch=(), megabytes=16, spaces=None, out_spaces=None, aliases=None):
    spaces, out_spaces = spaces or {}, out_spaces or {}
    single = not isinstance(outs, tuple)
    out_specs = [out_spaces.get(i, VMEM) for i in range(1 if single else len(outs))]
    return pl.pallas_call(
        kernel,
        out_shape=outs,
        in_specs=[spaces.get(i, VMEM) for i in range(len(ins))],
        out_specs=out_specs[0] if single else out_specs,
        scratch_shapes=list(scratch),
        input_output_aliases=aliases or {},
        compiler_params=pltpu.CompilerParams(vmem_limit_bytes=int(megabytes * 2**20)),
        cost_estimate=pl.CostEstimate(flops=1000000, bytes_accessed=2**21, transcendentals=0),
    )(*ins)


def shape(*dims, dtype=F32):
    return jax.ShapeDtypeStruct(dims, dtype)


def exchange(values, axis, steps):
    size = lax.axis_size(axis)
    return [
        lax.ppermute(value, axis, [(i, i ^ step) for i in range(size)])
        for value, step in zip(values, steps)
    ]


def turn(value, by):
    size_y, size_z = lax.axis_size("gy"), lax.axis_size("gz")
    half = size_y // 2
    pairs = []
    for core in range(half):
        ring = [(high * half + core) * size_z + z for high in range(2) for z in range(size_z)]
        pairs += [(ring[n], ring[(n + by) % len(ring)]) for n in range(len(ring))]
    return lax.ppermute(value, ("gy", "gz"), pairs)


def shards(charges, counts, slots, spline, kernel_fine, kernel_mid, kernel_coarse):
    cells = charges.shape[0]
    packed, raw, face = call(
        deposit_kernel,
        (shape(32, 32, 128), shape(8, 128), shape(2 * FACE + 8, 128)),
        (256 * slots + counts, charges, spline.reshape(cells * 12, ATOMS)),
        (
            pltpu.VMEM((32, 32, 128), F32),
            pltpu.VMEM((cells, ATOMS), F32),
            pltpu.VMEM((cells * 12, 128), BF16),
            pltpu.VMEM((cells * 12, 128), F32),
            pltpu.VMEM((64, cells), F32),
            pltpu.VMEM((32, 32, 128), F32),
            pltpu.VMEM((SPAN_2, 56, 128), F32),
            pltpu.VMEM((SPAN_3, 40, 128), F32),
            pltpu.VMEM((SPAN_4, 24, 128), F32),
            pltpu.SemaphoreType.DMA((5,)),
        ),
        spaces={1: HBM, 2: HBM},
        out_spaces={0: ANY},
        megabytes=53.75,
    )
    (got_1,) = exchange((face,), "gy", (1,))
    relay = call(relay_kernel, shape(FACE + 8, 128), (raw, got_1))
    (got_2,) = exchange((relay,), "gy", (2,))
    qx, qy, qz = composites()
    qz_high = qz.astype(BF16)
    qz_low = (qz - qz_high.astype(np.float32)).astype(BF16)
    green_high, green_low, rise, framed = call(
        green_kernel,
        (
            shape(1024, 128 * SPAN_4, dtype=BF16),
            shape(1024, 128 * SPAN_4, dtype=BF16),
            shape(1024, 256, dtype=BF16),
            shape(32, 40, 128),
        ),
        (jnp.asarray(np.concatenate([qx, qy])), packed),
        (pltpu.VMEM((18, 64, 128), BF16), pltpu.VMEM((18, 64, 128), BF16)),
    )
    wide_y, raw, face_1, face_3 = call(
        widen_y_kernel,
        (shape(32, 40, 128), shape(8, 128), shape(72, 128), shape(72, 128)),
        (framed, relay, got_1, got_2, rise),
        spaces={4: ANY},
        aliases={0: 0},
    )
    got_2, got_3, got_1 = exchange((raw, face_3, face_1), "gx", (2, 3, 1))
    bands = call(
        bands_kernel,
        tuple(shape(band[0], band[1], dtype=BF16) for band in BANDS for _ in range(2)),
        (kernel_fine, kernel_mid, kernel_coarse),
        spaces={0: SMEM, 1: SMEM, 2: SMEM},
    )
    wide_x, raw, to_high, to_low = call(
        widen_x_kernel,
        (shape(36, 40, 128), shape(16, 128), shape(80, 128), shape(80, 128)),
        (wide_y, raw, got_1, got_3, got_2, bands[0]),
        spaces={5: ANY},
    )
    from_low, from_high = turn(to_high, 1), turn(to_low, -1)
    (got_2,) = exchange((raw,), "gz", (2,))
    window = call(window_kernel, shape(3, 16, 128), (raw, from_low, from_high, got_2))
    pieces = [window] + [turn(window, by) for by in (4, -4, 8)]
    base = call(
        near_kernel,
        shape(32, 32, 128),
        (wide_x, from_low, from_high, *bands, jnp.asarray(PROL_2, BF16), jnp.asarray(PROL_1, BF16)),
        (
            pltpu.VMEM((32, 40, 256), F32),
            pltpu.VMEM((SPAN_2, 32, 128), F32),
            pltpu.VMEM((SPAN_3, 24, 128), F32),
            pltpu.VMEM((SPAN_3, 24, 128), F32),
            pltpu.VMEM((SPAN_3, 24, 128), F32),
            pltpu.VMEM((SPAN_2, 32, 128), F32),
            pltpu.VMEM((SPAN_2, 32, 128), F32),
        ),
    )
    return call(
        top_kernel,
        shape(32, 32, 32),
        (base, *pieces, green_high, green_low, rise, jnp.asarray(np.concatenate([qz_high, qz_low]))),
        (
            pltpu.VMEM((16, 8, 128), F32),
            pltpu.VMEM((32, 32, 32), F32),
            pltpu.SemaphoreType.DMA((4,)),
        ),
        out_spaces={0: ANY},
    )


def solution(mesh):
    return jax.shard_map(
        shards,
        mesh=mesh,
        in_specs=(
            P(("gx", "gy", "gz"), None),
            P(("gx", "gy", "gz")),
            P(("gx", "gy", "gz")),
            P(("gx", "gy", "gz"), None, None, None),
            P(),
            P(),
            P(),
        ),
        out_specs=P("gx", "gy", "gz"),
        check_vma=False,
    )
```

```python
import functools

import jax
import jax.numpy as jnp
import numpy as np
from jax import lax
from jax.experimental import pallas as pl
from jax.experimental.pallas import tpu as pltpu
from jax.sharding import PartitionSpec as P

W = (0.125, 0.5, 0.75, 0.5, 0.125)
F32 = jnp.float32
BF16 = jnp.bfloat16
CELLS = 384
ATOMS = 128
SPAN_2 = 18
SPAN_3 = 11
SPAN_4 = 7
SEC = 32
THI = 64
VMEM = pl.BlockSpec(memory_space=pltpu.VMEM)
SMEM = pl.BlockSpec(memory_space=pltpu.SMEM)
HBM = pl.BlockSpec(memory_space=pltpu.HBM)
ANY = pl.BlockSpec(memory_space=pl.ANY)


def weight(t):
    return W[t] if 0 <= t <= 4 else 0.0


def table(rows, columns, offset, turned):
    out = np.zeros((128, 128), np.float32)
    for r in range(rows):
        for c in range(columns):
            out[r, c] = weight(c - 2 * r + offset if turned else r - 2 * c + offset)
    return out


PROL_2 = table(SPAN_3, SPAN_2, 3, True)
PROL_1 = table(SPAN_2, 32, 4, True)


BANDS = (
    (256, 256, ((0, 32, 2), (160, 2, 0), (192, 2, 34)), 32, 32),
    (256, 128, ((0, 18, 2), (128, 4, 0), (160, 4, 18)), 24, 18),
    (128, 128, ((0, 11, 2), (64, 5, 0), (96, 5, 10)), 16, 11),
)
DIVIDE = {32: (1, 5), 2: (1, 1), 18: (57, 10), 4: (1, 2), 11: (94, 10), 5: (52, 8), 24: (43, 10), 16: (1, 4)}


def composite(first, last):
    p3 = np.array([[weight(i - 2 * j + 3) for j in range(7)] for i in range(11)])
    p2 = np.array([[weight(i - 2 * j + 3) for j in range(11)] for i in range(18)])
    p1 = np.array([[weight(i - 2 * j + 4) for j in range(18)] for i in range(32)])
    m4, m3, m2 = np.ones(7), np.ones(11), np.ones(18)
    if first:
        m4[0] = m3[0] = m2[0] = 0
    if last:
        m4[5:] = 0
        m3[9:] = 0
        m2[17:] = 0
    return (p1 * m2) @ (p2 * m3) @ (p3 * m4)


def composites():
    qx = np.zeros((4, 32, 128), np.float32)
    qy = np.zeros((4, 32, 128), np.float32)
    qz = np.zeros((4, 128, 128), np.float32)
    for v in range(4):
        q = composite(v % 2 == 1, v >= 2)
        for lane in range(64):
            if lane // 8 < 7 and lane % 8 < 7:
                qx[v, :, lane] = q[:, lane // 8]
                qy[v, :, lane] = q[:, lane % 8]
        for row in range(128):
            if row % 8 < 7:
                qz[v, row, :32] = q[:, row % 8]
    return qx, qy, qz


def split(x):
    high = x.astype(BF16)
    return high, (x - high.astype(F32)).astype(BF16)


def dot(a, b):
    return jnp.dot(a, b, preferred_element_type=F32)


def dot_exact(x, right):
    high, low = split(x)
    return dot(high, right) + dot(low, right)


def dot_split(x, right_high, right_low):
    high, low = split(x)
    return dot(high, right_high) + (dot(low, right_high) + dot(high, right_low))


def iota(shape, dim):
    return lax.broadcasted_iota(jnp.int32, shape, dim)


def roll(x, shift, axis=None):
    axis = x.ndim - 1 if axis is None else axis
    shift = shift % x.shape[axis]
    return x if shift == 0 else pltpu.roll(x, shift, axis)


def lanes_of(x, low, count):
    lane = iota(x.shape, x.ndim - 1)
    return jnp.where((lane >= low) & (lane < low + count), x, 0.0)


def as_rows(x):
    return x.reshape(x.shape[0] * x.shape[1], x.shape[2])


def taps(pieces):
    total = None
    for factor, value in pieces:
        term = value if factor == 1.0 else factor * value
        total = term if total is None else total + term
    return total


def restrict_planes(read, span, size, offset):
    planes = []
    for p in range(span):
        planes.append(
            taps([(W[t], read(2 * p + t - offset)) for t in range(5) if 0 <= 2 * p + t - offset < size])
        )
    return planes


def place():
    sizes = [lax.axis_size(a) for a in ("gx", "gy", "gz")]
    index = [lax.axis_index(a) for a in ("gx", "gy", "gz")]
    return index, sizes


def inside_mask(shape, spans, high, place_of):
    index, sizes = place_of
    keep = None
    for dim in range(3):
        at = iota(shape, dim)
        low = jnp.where(index[dim] == 0, 1, 0)
        top = jnp.where(index[dim] == sizes[dim] - 1, high, spans)
        part = (at >= low) & (at < top)
        keep = part if keep is None else keep & part
    return keep


def nearest(index):
    even = lax.rem(index, 2) == 0
    return even, index == 1, index == 2


def deposit_kernel(
    codes, charges_hbm, spline_hbm,
    packed_hbm, raw_out, face,
    packed, charges, spline, wide, patch, fine, buf_2, buf_3, buf_4, sems,
):
    where = place()
    index, sizes = where
    part = CELLS * 12 // 3
    copies = [pltpu.make_async_copy(charges_hbm, charges, sems.at[3])]
    for chunk in range(3):
        rows = slice(part * chunk, part * chunk + part)
        copies.append(
            pltpu.make_async_copy(spline_hbm.at[rows, :], spline.at[rows, :], sems.at[chunk])
        )
    for copy in copies:
        copy.start()
    buf_2[...] = jnp.zeros_like(buf_2)
    buf_3[...] = jnp.zeros_like(buf_3)
    buf_4[...] = jnp.zeros_like(buf_4)
    row, column = iota((512, 64), 0), iota((512, 64), 1)
    spread = (row // 32 * 4 + row % 4 == column).astype(F32).astype(BF16)
    row, column = iota((128, 128), 0), iota((128, 128), 1)

    def restriction(rows, columns, offset):
        t = row - 2 * column + offset
        out = jnp.zeros((128, 128), F32)
        for tap in range(5):
            out = jnp.where(t == tap, W[tap], out)
        return jnp.where((row < rows) & (column < columns), out, 0.0).astype(BF16)

    rest_2 = restriction(32, SPAN_2, 4)
    rest_3 = restriction(SPAN_2, SPAN_3, 3)
    rest_4 = restriction(SPAN_3, SPAN_4, 3)
    slot = lax.shift_right_logical(codes[...].reshape(1, CELLS), 8)
    fits = (iota((512, CELLS), 0) // 4 % 8) == slot % 8
    hot = (iota((64, CELLS), 0) == slot // 8).astype(F32).astype(BF16)
    copies[0].wait()
    alive = iota((ATOMS, CELLS), 0) < (codes[...].reshape(1, CELLS) & 255)
    weighted = jnp.where(alive, charges[...].T, 0.0)
    for chunk in range(CELLS // 128):
        lanes = slice(128 * chunk, 128 * chunk + 128)
        copies[1 + chunk].wait()
        rows = slice(part * chunk, part * chunk + part)
        wide[rows, :] = spline[rows, :].astype(F32)

        def column_of(d, i):
            return wide[pl.ds(chunk * part + 4 * d + i, 128, stride=12), :].T

        charge = weighted[:, lanes]
        depth = [charge * column_of(2, k) for k in range(4)]
        ys = [column_of(1, j) for j in range(4)]
        for i in range(4):
            xs = column_of(0, i)
            for j in range(4):
                cross = xs * ys[j]
                for k in range(4):
                    patch[16 * i + 4 * j + k : 16 * i + 4 * j + k + 1, lanes] = jnp.sum(
                        cross * depth[k], axis=0, keepdims=True
                    )
    high, low = split(patch[...])
    spread_high = jnp.where(fits, dot(spread, high), 0.0).astype(BF16)
    spread_low = jnp.where(fits, dot(spread, low), 0.0).astype(BF16)
    nt = (((1,), (1,)), ((), ()))
    placed = lax.dot_general(hot, spread_high, nt, preferred_element_type=F32) + lax.dot_general(
        hot, spread_low, nt, preferred_element_type=F32
    )
    for i in range(4):
        for j in range(4):
            rows = lanes_of(roll(placed[:, 128 * i : 128 * i + 128], -32 * j), 0, 32)
            for sx in range(8):
                fine[4 * sx + i, pl.ds(j, 8, stride=4), :] = rows[8 * sx : 8 * sx + 8]

    for p, plane in enumerate(restrict_planes(lambda x: fine[x], SPAN_2, 32, 4)):
        buf_2[p, 4:36, :] = plane
    second = taps([(W[t], buf_2[:, pl.ds(t, 24, stride=2), :]) for t in range(5)])
    second = dot_exact(as_rows(second), rest_2).reshape(SPAN_2, 24, 128)
    second = jnp.where(inside_mask(second.shape, SPAN_2, 17, where), second, 0.0)
    for p, plane in enumerate(restrict_planes(lambda x: second[x], SPAN_3, SPAN_2, 3)):
        buf_3[p, 3:27, :] = plane
    third = taps([(W[t], buf_3[:, pl.ds(t, 16, stride=2), :]) for t in range(5)])
    third = dot_exact(as_rows(third), rest_3).reshape(SPAN_3, 16, 128)
    third = jnp.where(inside_mask(third.shape, SPAN_3, 9, where), third, 0.0)
    packed[...] = fine[...]
    packed[0:SPAN_2, 0:24, :] += roll(second, SEC)
    packed[0:SPAN_3, 0:16, :] += roll(third, THI)
    leave = pltpu.make_async_copy(packed, packed_hbm, sems.at[4])
    leave.start()
    for p, plane in enumerate(restrict_planes(lambda x: third[x], SPAN_4, SPAN_3, 3)):
        buf_4[p, 3:19, :] = plane
    last = taps([(W[t], buf_4[:, pl.ds(t, 8, stride=2), :]) for t in range(5)])
    last = dot_exact(as_rows(last), rest_4).reshape(SPAN_4, 8, 128)
    last = jnp.where(inside_mask(last.shape, SPAN_4, 5, where), last, 0.0)
    raw = taps([(1.0, roll(last[x], 8 * x)) for x in range(SPAN_4)])
    raw_out[...] = raw

    even, _, _ = nearest(index[1])
    low = pack_y(packed, FIRST_ROWS)
    high = pack_y(packed, LAST_ROWS)
    for v in range(4):
        face[8 * v : 8 * v + 8, :] = jnp.where(even, high[v], low[v])
        face[FACE + 8 * v : FACE + 8 * v + 8, :] = jnp.where(even, low[v], high[v])
    face[2 * FACE : 2 * FACE + 8, :] = raw
    leave.wait()


def spot_1(p):
    return p // 16, p % 16 // 4 * 2, p % 4 * 32


def spot_2(p):
    return 2 + p // 14, p % 14 // 7 * 4, p % 7 * 18


def spot_3(p):
    return 3, 4, p * 11


def spot_4(p):
    return 3, p // 5, 72 + p % 5 * 11


FACE = 32
LEVELS = (
    (32, 2, 0, 32, spot_1),
    (SPAN_2, 4, SEC, 18, spot_2),
    (SPAN_3, 4, THI, 11, spot_3),
    (SPAN_3, 1, THI, 11, spot_4),
)
FIRST_ROWS = (0, 0, 0, 4)
LAST_ROWS = (30, 14, 6, 10)
ROWS_ABOVE = (34, 18, 10, 14)


def pack_y(source, at):
    tiles = [jnp.zeros((8, 128), F32) for _ in range(4)]
    row, at_lane = iota((8, 128), 0), iota((8, 128), 1)
    for (planes, count, lane, width, spot), start in zip(LEVELS, at):
        for p in range(planes):
            v, r, to = spot(p)
            if start == 30:
                slab = roll(source[p, 24:32, :], r - 6, 0)
            else:
                slab = roll(source[p, start : start + 8, :], r, 0)
            slab = roll(slab, to - lane)
            keep = (row >= r) & (row < r + count) & (at_lane >= to) & (at_lane < to + width)
            tiles[v] = jnp.where(keep, slab, tiles[v])
    return tiles


def place_y(tile, index):
    tall = jnp.concatenate([tile, jnp.zeros((8, 128), F32)], axis=0)
    tall = pltpu.roll(tall, lax.rem(4 * index + 15, 16), 0)
    return tall[0:8] + roll(tall[8:16], 64)


def relay_kernel(raw, got, out):
    index, _ = place()
    out[0:FACE, :] = got[FACE : 2 * FACE, :]
    partner = jnp.bitwise_xor(index[1], 1)
    other = got[2 * FACE : 2 * FACE + 8, :]
    out[FACE : FACE + 8, :] = place_y(raw[...], index[1]) + place_y(other, partner)


def widen_y_kernel(framed, own, got_1, got_2, after, out, raw_out, face_1, face_3):
    index, _ = place()
    even, one, two = nearest(index[1])
    total = own[FACE : FACE + 8, :] + got_2[FACE : FACE + 8, :]
    raw_out[...] = total
    a, b = got_1[0:FACE, :], got_2[0:FACE, :]
    low = jnp.where(even, 0.0, a) + jnp.where(two, b, 0.0)
    high = jnp.where(even, a, 0.0) + jnp.where(one, b, 0.0)
    for face, at in ((low, FIRST_ROWS), (high, ROWS_ABOVE)):
        for (planes, count, lane, width, spot), start in zip(LEVELS, at):
            for p in range(planes):
                v, r, to = spot(p)
                slab = roll(roll(face[8 * v : 8 * v + 8], -r, 0), lane - to)
                slab = lanes_of(slab, lane, width)
                out[p, start : start + count, :] += slab[0:count]
    even, one, _ = nearest(index[0])
    for ref, to_high in ((face_1, even), (face_3, one)):
        f = jnp.where(to_high, 30, 0)
        s = jnp.where(to_high, 14, 0)
        t = jnp.where(to_high, 6, 0)
        ref[0:40, :] = lanes_of(out[f], 0, 32) + lanes_of(roll(out[f + 1], 32), 32, 32)
        ref[0:16, :] += taps(
            [(1.0, lanes_of(roll(out[t + k, 0:16, :], 11 * k), THI + 11 * k, 11)) for k in range(5)]
        )
        ref[40:64, :] = taps(
            [(1.0, lanes_of(roll(out[s + k, 0:24, :], 18 * k - SEC), 18 * k, 18)) for k in range(4)]
        )
        ref[64:72, :] = total


def widen_x_kernel(wide_y, own, got_2, got_1, got_3, after, out, raw_out, to_high, to_low):
    index, _ = place()
    even, one, two = nearest(index[0])
    total = None
    lane = iota((16, 128), 1)
    for step, tile in ((0, own[...]), (1, got_1[64:72, :]), (2, got_2[...]), (3, got_3[64:72, :])):
        tall = jnp.concatenate([tile, roll(tile, 64)], axis=0)
        tall = jnp.where(lane < 64, tall, 0.0)
        at = lax.rem(32 * jnp.bitwise_xor(index[0], step) + 120, 128)
        moved = pltpu.roll(tall, at, 1)
        total = moved if total is None else total + moved
    raw_out[...] = total
    a, b = got_1[...], got_3[...]
    low = jnp.where(even, 0.0, a) + jnp.where(two, b, 0.0)
    high = jnp.where(even, a, 0.0) + jnp.where(one, b, 0.0)
    out[0:2] = jnp.zeros((2, 40, 128), F32)
    out[34:36] = jnp.zeros((2, 40, 128), F32)
    out[2:34] = wide_y[...]
    for face, at in ((low, (0, 0, 0)), (high, (34, 18, 10))):
        for k in range(2):
            out[at[0] + k] += lanes_of(roll(face[0:40], -32 * k), 0, 32)
        for k in range(4):
            out[at[1] + k, 0:24, :] += lanes_of(roll(face[40:64], SEC - 18 * k), SEC, 18)
        for k in range(5):
            out[at[2] + k, 0:16, :] += lanes_of(roll(face[0:16], -11 * k), THI, 11)
    for ref, high in ((to_high, True), (to_low, False)):
        pack_z(out, ref, high)
        ref[64:80, :] = total


def pack_z(source, face, to_high):
    sums = []
    for rows, planes, count, lane, high in ((40, 36, 2, 0, 30), (24, 22, 4, SEC, 14), (16, 15, 5, THI, 6)):
        first = lane + high if to_high else lane
        at = iota((rows, 128), 1)
        wanted = (at >= first) & (at < first + count)
        total = jnp.zeros((rows, 128), F32)
        for x in range(planes):
            kept = jnp.where(wanted, source[x, 0:rows, :], 0.0)
            total = total + roll(kept, count * x - first)
        sums.append(total)
    face[0:40, :] = sums[0]
    face[40:64, :] = sums[1]
    face[0:16, :] += lanes_of(roll(sums[2], 72), 72, 55)
    face[40:56, :] += lanes_of(roll(sums[2], 88 - 55), 88, 20)


def unpack_z(message):
    third = lanes_of(roll(message[0:16], -72), 0, 55) + lanes_of(roll(message[40:56], 55 - 88), 55, 20)
    return message[0:40], message[40:64], third


def window_kernel(own, got_2, from_low, from_high, after, out):
    index, _ = place()
    early = lax.rem(index[2], 4) < 2
    ends = got_2[...]
    first, second, third = from_low[64:80, :], own[...], from_high[64:80, :]
    pieces = (
        jnp.where(early, first, ends),
        jnp.where(early, second, first),
        jnp.where(early, third, second),
        jnp.where(early, ends, third),
    )
    for group in range(3):
        total = None
        for q in range(min(6, 16 - 6 * group)):
            for d, piece in enumerate(pieces):
                to = 20 * q + 4 * d
                moved = lanes_of(roll(piece, to - 48 * group - 8 * q), to, 8)
                total = moved if total is None else total + moved
        out[group] = total


def divided(n, d):
    factor, bits = DIVIDE[d]
    return lax.shift_right_logical(n * factor, bits)


def build_bands(kernel, band):
    rows, columns, runs, group, outs = band
    row = iota((rows, 128), 0)
    shift = jnp.full((rows, 128), 99, jnp.int32)
    point = jnp.full((rows, 128), 99, jnp.int32)
    for start, count, offset in runs:
        at = row - start
        a = divided(at, count)
        inside = (at >= 0) & (at < 5 * count)
        shift = jnp.where(inside, a, shift)
        point = jnp.where(inside, offset + at - a * count, point)
    chosen = (shift == iota((rows, 128), 1)).astype(F32).astype(BF16)
    column = iota((8, columns), 1)
    block = divided(column, group)
    out_at = (column - block * group)[0:1]
    block = jnp.where((column - block * group) < outs, block, 9)
    sub = iota((8, columns), 0)
    entry = jnp.concatenate([point] * (columns // 128), axis=1) - out_at
    total_high = jnp.zeros((rows, columns), F32)
    total_low = jnp.zeros((rows, columns), F32)
    for c in range(5):
        source = jnp.zeros((8, columns), F32)
        for b in range(5):
            column_of = jnp.zeros((8, columns), F32)
            for a in range(5):
                column_of = jnp.where(sub == a, kernel[a, b, c], column_of)
            source = jnp.where(block == b, column_of, source)
        source = jnp.concatenate([source, jnp.zeros((120, columns), F32)], axis=0)
        high, low = split(source)
        fits = entry == c
        total_high = jnp.where(fits, dot(chosen, high), total_high)
        total_low = jnp.where(fits, dot(chosen, low), total_low)
    return total_high.astype(BF16), total_low.astype(BF16)


def bands_kernel(bands, *refs):
    kernels, outs = refs[: len(bands)], refs[len(bands) :]
    for n, (kernel, band) in enumerate(zip(kernels, bands)):
        high, low = build_bands(kernel, band)
        outs[2 * n][...] = high
        outs[2 * n + 1][...] = low


def green_kernel(factors, packed, green_high, green_low, rise, framed, block_high, block_low):
    index, sizes = place()
    row, lane = iota((64, 128), 0), iota((64, 128), 1)
    delta_x = (lane // 8).astype(F32)
    delta_z = (4 * index[2] - 1 + lane % 8 - row).astype(F32)
    plain = delta_z * delta_z + (1.0 + delta_x * delta_x)
    for apart in range(18):
        high, low = split(0.0625 * lax.rsqrt(plain + float(apart * apart)))
        block_high[apart] = high
        block_low[apart] = low
    for ty in range(SPAN_4):
        columns = slice(128 * ty, 128 * ty + 128)
        for sy in range(16):
            apart = jnp.abs(4 * index[1] - 1 + ty - sy)
            first = sy % 8 * 128 + sy // 8 * 64
            green_high[first : first + 64, columns] = block_high[apart]
            green_low[first : first + 64, columns] = block_low[apart]
    variant = [
        jnp.where(index[d] == 0, 1, 0) + jnp.where(index[d] == sizes[d] - 1, 2, 0) for d in range(3)
    ]
    factor_x, factor_y = factors[variant[0]], factors[4 + variant[1]]
    kept = as_rows(factor_x[:, None, :] * factor_y[None, :, :])
    high, low = split(kept)
    rise[:, 0:128] = (high.astype(F32) + roll(low.astype(F32), 64)).astype(BF16)
    rise[:, 128:256] = high
    framed[:, 0:2, :] = jnp.zeros((32, 2, 128), F32)
    framed[:, 34:40, :] = jnp.zeros((32, 6, 128), F32)
    framed[:, 2:34, :] = packed[...]


def prolong_rows(source, target, count, whole):
    size = target.shape[1] // 2
    q0 = source[:, 0:size, :]
    q1 = source[:, 1 : size + 1, :]
    q2 = source[:, 2 : size + 2, :]
    even = 0.75 * q1 + 0.125 * (q0 + q2)
    odd = 0.5 * (q0 + q1) if whole else 0.5 * (q1 + q2)
    target[:, pl.ds(1 if whole else 0, size, stride=2), :] = even
    target[:, pl.ds(0 if whole else 1, size, stride=2), :] = odd


def prolong_plane(read, p, whole):
    half = p // 2
    if (p % 2 == 1) == whole:
        return 0.75 * read(half + 1) + 0.125 * (read(half) + read(half + 2))
    first = half if whole else half + 1
    return 0.5 * (read(first) + read(first + 1))


def near_kernel(
    wide, from_low, from_high, b1h, b1l, b2h, b2l, b3h, b3l, prol_2, prol_1,
    out,
    near_1, near_2, near_3, tall_3, tall_3y, tall_2, tall_2y,
):
    where = place()
    index, sizes = where
    low_faces = unpack_z(jnp.where(index[2] == 0, 0.0, from_low[0:64, :]))
    high_faces = unpack_z(jnp.where(index[2] == sizes[2] - 1, 0.0, from_high[0:64, :]))

    def halo(x, level, count, low_at, high_at):
        low = roll(low_faces[level], low_at - count * x)
        high = roll(high_faces[level], high_at - count * x)
        return lanes_of(low, low_at, 5 * count) + lanes_of(high, high_at, 5 * count)

    planes = [lanes_of(wide[x, 0:16, :], THI, 11) for x in range(15)]
    left = []
    for x in range(SPAN_3):
        main = taps([(1.0, roll(planes[x + a], 11 * a - THI)) for a in range(5)])
        left.append(main + halo(x, 2, 5, 64, 96))
    left = jnp.concatenate(left, axis=0)
    near_3[...] = jnp.zeros_like(near_3)
    near_3[:, 0:16, :] = dot_split(left, b3h[...], b3l[...]).reshape(SPAN_3, 16, 128)
    third = taps([(1.0, roll(near_3[:, b : b + 16, :], -16 * b)) for b in range(5)])
    third = jnp.where(inside_mask(third.shape, SPAN_3, 9, where), third, 0.0)
    tall_3[...] = jnp.zeros_like(tall_3)
    tall_3[:, 0:16, :] = dot_exact(as_rows(third), prol_2[...]).reshape(SPAN_3, 16, 128)
    prolong_rows(tall_3, tall_3y, SPAN_2, True)

    planes = [lanes_of(wide[x, 0:24, :], SEC, 18) for x in range(22)]
    left_a, left_b = [], []
    for x in range(SPAN_2):
        left_a.append(taps([(1.0, roll(planes[x + a], 18 * a - SEC)) for a in range(5)]))
        left_b.append(halo(x, 1, 4, 0, 32))
    left = jnp.concatenate(
        [jnp.concatenate(left_a, axis=0), jnp.concatenate(left_b, axis=0)], axis=1
    )
    near_2[...] = jnp.zeros_like(near_2)
    near_2[:, 0:24, :] = dot_split(left, b2h[...], b2l[...]).reshape(SPAN_2, 24, 128)
    second = taps([(1.0, roll(near_2[:, b : b + 24, :], -24 * b)) for b in range(5)])
    raised = jnp.stack(
        [prolong_plane(lambda x: tall_3y[x], p, True) for p in range(SPAN_2)], axis=0
    )
    second = jnp.where(inside_mask(second.shape, SPAN_2, 17, where), second + raised, 0.0)
    tall_2[...] = jnp.zeros_like(tall_2)
    tall_2[:, 0:24, :] = dot_exact(as_rows(second), prol_1[...]).reshape(SPAN_2, 24, 128)
    prolong_rows(tall_2, tall_2y, 32, False)

    planes = [lanes_of(wide[x], 0, 32) for x in range(36)]
    left_a, left_b = [], []
    for x in range(32):
        left_a.append(taps([(1.0, roll(planes[x + a], 32 * a)) for a in range(4)]))
        left_b.append(planes[x + 4] + halo(x, 0, 2, 32, 64))
    left = jnp.concatenate(
        [jnp.concatenate(left_a, axis=0), jnp.concatenate(left_b, axis=0)], axis=1
    )
    near_1[...] = dot_split(left, b1h[...], b1l[...]).reshape(32, 40, 256)
    for x in range(32):
        first = taps(
            [(1.0, roll(near_1[x, b : b + 32, 0:128], -32 * b)) for b in range(4)]
            + [(1.0, near_1[x, 4:36, 128:256])]
        )
        out[x] = first + prolong_plane(lambda q: tall_2y[q], x, False)


def top_kernel(
    base, piece_0, piece_1, piece_2, piece_3, green_high, green_low, rise, qz,
    out_hbm,
    fourth, out, sems,
):
    index, sizes = place()
    lane = iota((8, 128), 1)
    ring = lax.rem(index[2], 4)
    first = 4 * (ring == 3).astype(jnp.int32) - 4 * (ring == 0).astype(jnp.int32) + 127
    sources = [lax.rem(16 * lax.rem(index[2] // 4 + step, 4) + first, 128) for step in (0, 2, 3, 1)]
    for x in range(16):
        total = None
        for piece, at in zip((piece_0, piece_1, piece_2, piece_3), sources):
            kept = lanes_of(piece[x // 6], 20 * (x % 6), 20)
            moved = pltpu.roll(kept, lax.rem(at + 128 - 20 * (x % 6), 128), 1)
            total = moved if total is None else total + moved
        total = total + roll(total, 64)
        fourth[x] = jnp.where(lane < 64, total[0:8], total[8:16])
    total = jnp.zeros((32, 128 * SPAN_4), F32)
    extra = jnp.zeros((16, 128 * SPAN_4), F32)
    for s in range(0, 8, 2):
        left = jnp.concatenate([fourth[:, s, :], fourth[:, s + 1, :]], axis=1)
        high, low = split(left)
        rows = slice(128 * s, 128 * s + 256)
        total = total + dot(jnp.concatenate([high, low], axis=0), green_high[rows, :])
        extra = extra + dot(high, green_low[rows, :])
    sums = total[0:16] + (total[16:32] + extra)
    row, lane = iota((16, 128), 0), iota((16, 128), 1)
    tops = []
    for tx in range(SPAN_4):
        keep = jnp.abs(4 * index[0] - 1 + tx - row) == lane // 8
        for ty in range(SPAN_4):
            picked = jnp.where(keep, sums[:, 128 * ty : 128 * ty + 128], 0.0)
            tops.append(jnp.sum(picked, axis=0, keepdims=True))
        tops.append(jnp.zeros((1, 128), F32))
    tops = jnp.concatenate(tops + [jnp.zeros((8, 128), F32)], axis=0)
    variant = jnp.where(index[2] == 0, 1, 0) + jnp.where(index[2] == sizes[2] - 1, 2, 0)
    high, low = split(dot_split(tops, qz[variant], qz[4 + variant]))
    right = jnp.concatenate([high, high, low, jnp.zeros_like(low)], axis=0)
    copies = []
    for part in range(4):
        planes = slice(8 * part, 8 * part + 8)
        far = dot(rise[256 * part : 256 * part + 256, :], right)
        out[planes] = (base[planes] + far.reshape(8, 32, 128))[:, :, 0:32]
        copies.append(pltpu.make_async_copy(out.at[planes], out_hbm.at[planes], sems.at[part]))
        copies[-1].start()
    for copy in copies:
        copy.wait()


def call(kernel, outs, ins, scratch=(), megabytes=16, spaces=None, out_spaces=None, aliases=None, flops=1000000):
    spaces, out_spaces = spaces or {}, out_spaces or {}
    single = not isinstance(outs, tuple)
    out_specs = [out_spaces.get(i, VMEM) for i in range(1 if single else len(outs))]
    return pl.pallas_call(
        kernel,
        out_shape=outs,
        in_specs=[spaces.get(i, VMEM) for i in range(len(ins))],
        out_specs=out_specs[0] if single else out_specs,
        scratch_shapes=list(scratch),
        input_output_aliases=aliases or {},
        compiler_params=pltpu.CompilerParams(vmem_limit_bytes=int(megabytes * 2**20)),
        cost_estimate=pl.CostEstimate(flops=flops, bytes_accessed=2**21, transcendentals=0),
    )(*ins)


def shape(*dims, dtype=F32):
    return jax.ShapeDtypeStruct(dims, dtype)


def exchange(values, axis, steps):
    size = lax.axis_size(axis)
    return [
        lax.ppermute(value, axis, [(i, i ^ step) for i in range(size)])
        for value, step in zip(values, steps)
    ]


def turn(value, by):
    size_y, size_z = lax.axis_size("gy"), lax.axis_size("gz")
    half = size_y // 2
    pairs = []
    for core in range(half):
        ring = [(high * half + core) * size_z + z for high in range(2) for z in range(size_z)]
        pairs += [(ring[n], ring[(n + by) % len(ring)]) for n in range(len(ring))]
    return lax.ppermute(value, ("gy", "gz"), pairs)


def banded(bands, *kernels, flops=10**9):
    return call(
        functools.partial(bands_kernel, bands),
        tuple(shape(band[0], band[1], dtype=BF16) for band in bands for _ in range(2)),
        kernels,
        spaces={n: SMEM for n in range(len(kernels))},
        flops=flops,
    )


def shards(charges, counts, slots, spline, kernel_fine, kernel_mid, kernel_coarse):
    cells = charges.shape[0]
    packed, raw, face = call(
        deposit_kernel,
        (shape(32, 32, 128), shape(8, 128), shape(2 * FACE + 8, 128)),
        (256 * slots + counts, charges, spline.reshape(cells * 12, ATOMS)),
        (
            pltpu.VMEM((32, 32, 128), F32),
            pltpu.VMEM((cells, ATOMS), F32),
            pltpu.VMEM((cells * 12, 128), BF16),
            pltpu.VMEM((cells * 12, 128), F32),
            pltpu.VMEM((64, cells), F32),
            pltpu.VMEM((32, 32, 128), F32),
            pltpu.VMEM((SPAN_2, 56, 128), F32),
            pltpu.VMEM((SPAN_3, 40, 128), F32),
            pltpu.VMEM((SPAN_4, 24, 128), F32),
            pltpu.SemaphoreType.DMA((5,)),
        ),
        spaces={1: HBM, 2: HBM},
        out_spaces={0: ANY},
        megabytes=53.75,
    )
    (got_1,) = exchange((face,), "gy", (1,))
    relay = call(relay_kernel, shape(FACE + 8, 128), (raw, got_1))
    (got_2,) = exchange((relay,), "gy", (2,))
    qx, qy, qz = composites()
    qz_high = qz.astype(BF16)
    qz_low = (qz - qz_high.astype(np.float32)).astype(BF16)
    green_high, green_low, rise, framed = call(
        green_kernel,
        (
            shape(1024, 128 * SPAN_4, dtype=BF16),
            shape(1024, 128 * SPAN_4, dtype=BF16),
            shape(1024, 256, dtype=BF16),
            shape(32, 40, 128),
        ),
        (jnp.asarray(np.concatenate([qx, qy])), packed),
        (pltpu.VMEM((18, 64, 128), BF16), pltpu.VMEM((18, 64, 128), BF16)),
    )
    wide_y, raw, face_1, face_3 = call(
        widen_y_kernel,
        (shape(32, 40, 128), shape(8, 128), shape(72, 128), shape(72, 128)),
        (framed, relay, got_1, got_2, rise),
        spaces={4: ANY},
        aliases={0: 0},
    )
    got_3, got_1, got_2 = exchange((face_3, face_1, raw), "gx", (3, 1, 2))
    bands_1 = banded(BANDS[:1], kernel_fine)
    wide_x, raw, to_high, to_low = call(
        widen_x_kernel,
        (shape(36, 40, 128), shape(16, 128), shape(80, 128), shape(80, 128)),
        (wide_y, raw, got_2, got_1, got_3, bands_1[0]),
        spaces={5: ANY},
    )
    from_low, from_high = turn(to_high, 1), turn(to_low, -1)
    (got_2,) = exchange((raw,), "gz", (2,))
    bands_2 = banded(BANDS[1:], kernel_mid, kernel_coarse)
    window = call(
        window_kernel,
        shape(3, 16, 128),
        (raw, got_2, from_low, from_high, bands_2[0]),
        spaces={4: ANY},
    )
    pieces = [window] + [turn(window, by) for by in (8, 4, -4)]
    base = call(
        near_kernel,
        shape(32, 32, 128),
        (wide_x, from_low, from_high, *bands_1, *bands_2, jnp.asarray(PROL_2, BF16), jnp.asarray(PROL_1, BF16)),
        (
            pltpu.VMEM((32, 40, 256), F32),
            pltpu.VMEM((SPAN_2, 32, 128), F32),
            pltpu.VMEM((SPAN_3, 24, 128), F32),
            pltpu.VMEM((SPAN_3, 24, 128), F32),
            pltpu.VMEM((SPAN_3, 24, 128), F32),
            pltpu.VMEM((SPAN_2, 32, 128), F32),
            pltpu.VMEM((SPAN_2, 32, 128), F32),
        ),
    )
    return call(
        top_kernel,
        shape(32, 32, 32),
        (base, *pieces, green_high, green_low, rise, jnp.asarray(np.concatenate([qz_high, qz_low]))),
        (
            pltpu.VMEM((16, 8, 128), F32),
            pltpu.VMEM((32, 32, 32), F32),
            pltpu.SemaphoreType.DMA((4,)),
        ),
        out_spaces={0: ANY},
    )


def solution(mesh):
    return jax.shard_map(
        shards,
        mesh=mesh,
        in_specs=(
            P(("gx", "gy", "gz"), None),
            P(("gx", "gy", "gz")),
            P(("gx", "gy", "gz")),
            P(("gx", "gy", "gz"), None, None, None),
            P(),
            P(),
            P(),
        ),
        out_specs=P("gx", "gy", "gz"),
        check_vma=False,
    )
```

```python
import functools

import jax
import jax.numpy as jnp
import numpy as np
from jax import lax
from jax.experimental import pallas as pl
from jax.experimental.pallas import tpu as pltpu
from jax.sharding import PartitionSpec as P

W = (0.125, 0.5, 0.75, 0.5, 0.125)
F32 = jnp.float32
BF16 = jnp.bfloat16
CELLS = 384
ATOMS = 128
SPAN_2 = 18
SPAN_3 = 11
SPAN_4 = 7
SEC = 32
THI = 64
VMEM = pl.BlockSpec(memory_space=pltpu.VMEM)
SMEM = pl.BlockSpec(memory_space=pltpu.SMEM)
HBM = pl.BlockSpec(memory_space=pltpu.HBM)
ANY = pl.BlockSpec(memory_space=pl.ANY)


def weight(t):
    return W[t] if 0 <= t <= 4 else 0.0


def table(rows, columns, offset, turned):
    out = np.zeros((128, 128), np.float32)
    for r in range(rows):
        for c in range(columns):
            out[r, c] = weight(c - 2 * r + offset if turned else r - 2 * c + offset)
    return out


PROL_2 = table(SPAN_3, SPAN_2, 3, True)
PROL_1 = table(SPAN_2, 32, 4, True)


BANDS = (
    (256, 256, ((0, 32, 2), (160, 2, 0), (192, 2, 34)), 32, 32),
    (256, 128, ((0, 18, 2), (128, 4, 0), (160, 4, 18)), 24, 18),
    (128, 128, ((0, 11, 2), (64, 5, 0), (96, 5, 10)), 16, 11),
)
DIVIDE = {32: (1, 5), 2: (1, 1), 18: (57, 10), 4: (1, 2), 11: (94, 10), 5: (52, 8), 24: (43, 10), 16: (1, 4)}


def composite(first, last):
    p3 = np.array([[weight(i - 2 * j + 3) for j in range(7)] for i in range(11)])
    p2 = np.array([[weight(i - 2 * j + 3) for j in range(11)] for i in range(18)])
    p1 = np.array([[weight(i - 2 * j + 4) for j in range(18)] for i in range(32)])
    m4, m3, m2 = np.ones(7), np.ones(11), np.ones(18)
    if first:
        m4[0] = m3[0] = m2[0] = 0
    if last:
        m4[5:] = 0
        m3[9:] = 0
        m2[17:] = 0
    return (p1 * m2) @ (p2 * m3) @ (p3 * m4)


def composites():
    qx = np.zeros((4, 32, 128), np.float32)
    qy = np.zeros((4, 32, 128), np.float32)
    qz = np.zeros((4, 128, 128), np.float32)
    for v in range(4):
        q = composite(v % 2 == 1, v >= 2)
        for lane in range(64):
            if lane // 8 < 7 and lane % 8 < 7:
                qx[v, :, lane] = q[:, lane // 8]
                qy[v, :, lane] = q[:, lane % 8]
        for row in range(128):
            if row % 8 < 7:
                qz[v, row, :32] = q[:, row % 8]
    return qx, qy, qz


def split(x):
    high = x.astype(BF16)
    return high, (x - high.astype(F32)).astype(BF16)


def dot(a, b):
    return jnp.dot(a, b, preferred_element_type=F32)


def dot_exact(x, right):
    high, low = split(x)
    return dot(high, right) + dot(low, right)


def dot_split(x, right_high, right_low):
    high, low = split(x)
    return dot(high, right_high) + (dot(low, right_high) + dot(high, right_low))


def iota(shape, dim):
    return lax.broadcasted_iota(jnp.int32, shape, dim)


def roll(x, shift, axis=None):
    axis = x.ndim - 1 if axis is None else axis
    shift = shift % x.shape[axis]
    return x if shift == 0 else pltpu.roll(x, shift, axis)


def lanes_of(x, low, count):
    lane = iota(x.shape, x.ndim - 1)
    return jnp.where((lane >= low) & (lane < low + count), x, 0.0)


def as_rows(x):
    return x.reshape(x.shape[0] * x.shape[1], x.shape[2])


def taps(pieces):
    total = None
    for factor, value in pieces:
        term = value if factor == 1.0 else factor * value
        total = term if total is None else total + term
    return total


def restrict_planes(read, span, size, offset):
    planes = []
    for p in range(span):
        planes.append(
            taps([(W[t], read(2 * p + t - offset)) for t in range(5) if 0 <= 2 * p + t - offset < size])
        )
    return planes


def place():
    sizes = [lax.axis_size(a) for a in ("gx", "gy", "gz")]
    index = [lax.axis_index(a) for a in ("gx", "gy", "gz")]
    return index, sizes


def inside_mask(shape, spans, high, place_of):
    index, sizes = place_of
    keep = None
    for dim in range(3):
        at = iota(shape, dim)
        low = jnp.where(index[dim] == 0, 1, 0)
        top = jnp.where(index[dim] == sizes[dim] - 1, high, spans)
        part = (at >= low) & (at < top)
        keep = part if keep is None else keep & part
    return keep


def nearest(index):
    even = lax.rem(index, 2) == 0
    return even, index == 1, index == 2


def deposit_kernel(
    codes, charges_hbm, spline_hbm,
    packed_hbm, raw_out, face,
    packed, charges, spline, wide, patch, fine, buf_2, buf_3, buf_4, sems,
):
    where = place()
    index, sizes = where
    part = CELLS * 12 // 3
    copies = [pltpu.make_async_copy(charges_hbm, charges, sems.at[3])]
    for chunk in range(3):
        rows = slice(part * chunk, part * chunk + part)
        copies.append(
            pltpu.make_async_copy(spline_hbm.at[rows, :], spline.at[rows, :], sems.at[chunk])
        )
    for copy in copies:
        copy.start()
    buf_2[...] = jnp.zeros_like(buf_2)
    buf_3[...] = jnp.zeros_like(buf_3)
    buf_4[...] = jnp.zeros_like(buf_4)
    row, column = iota((512, 64), 0), iota((512, 64), 1)
    spread = (row // 32 * 4 + row % 4 == column).astype(F32).astype(BF16)
    row, column = iota((128, 128), 0), iota((128, 128), 1)

    def restriction(rows, columns, offset):
        t = row - 2 * column + offset
        out = jnp.zeros((128, 128), F32)
        for tap in range(5):
            out = jnp.where(t == tap, W[tap], out)
        return jnp.where((row < rows) & (column < columns), out, 0.0).astype(BF16)

    rest_2 = restriction(32, SPAN_2, 4)
    rest_3 = restriction(SPAN_2, SPAN_3, 3)
    rest_4 = restriction(SPAN_3, SPAN_4, 3)
    slot = lax.shift_right_logical(codes[...].reshape(1, CELLS), 8)
    fits = (iota((512, CELLS), 0) // 4 % 8) == slot % 8
    hot = (iota((64, CELLS), 0) == slot // 8).astype(F32).astype(BF16)
    copies[0].wait()
    alive = iota((ATOMS, CELLS), 0) < (codes[...].reshape(1, CELLS) & 255)
    weighted = jnp.where(alive, charges[...].T, 0.0)
    for chunk in range(CELLS // 128):
        lanes = slice(128 * chunk, 128 * chunk + 128)
        copies[1 + chunk].wait()
        rows = slice(part * chunk, part * chunk + part)
        wide[rows, :] = spline[rows, :].astype(F32)

        def column_of(d, i):
            return wide[pl.ds(chunk * part + 4 * d + i, 128, stride=12), :].T

        charge = weighted[:, lanes]
        depth = [charge * column_of(2, k) for k in range(4)]
        ys = [column_of(1, j) for j in range(4)]
        for i in range(4):
            xs = column_of(0, i)
            for j in range(4):
                cross = xs * ys[j]
                for k in range(4):
                    patch[16 * i + 4 * j + k : 16 * i + 4 * j + k + 1, lanes] = jnp.sum(
                        cross * depth[k], axis=0, keepdims=True
                    )
    high, low = split(patch[...])
    spread_high = jnp.where(fits, dot(spread, high), 0.0).astype(BF16)
    spread_low = jnp.where(fits, dot(spread, low), 0.0).astype(BF16)
    nt = (((1,), (1,)), ((), ()))
    placed = lax.dot_general(hot, spread_high, nt, preferred_element_type=F32) + lax.dot_general(
        hot, spread_low, nt, preferred_element_type=F32
    )
    for i in range(4):
        for j in range(4):
            rows = lanes_of(roll(placed[:, 128 * i : 128 * i + 128], -32 * j), 0, 32)
            for sx in range(8):
                fine[4 * sx + i, pl.ds(j, 8, stride=4), :] = rows[8 * sx : 8 * sx + 8]

    for p, plane in enumerate(restrict_planes(lambda x: fine[x], SPAN_2, 32, 4)):
        buf_2[p, 4:36, :] = plane
    second = taps([(W[t], buf_2[:, pl.ds(t, 24, stride=2), :]) for t in range(5)])
    second = dot_exact(as_rows(second), rest_2).reshape(SPAN_2, 24, 128)
    second = jnp.where(inside_mask(second.shape, SPAN_2, 17, where), second, 0.0)
    for p, plane in enumerate(restrict_planes(lambda x: second[x], SPAN_3, SPAN_2, 3)):
        buf_3[p, 3:27, :] = plane
    third = taps([(W[t], buf_3[:, pl.ds(t, 16, stride=2), :]) for t in range(5)])
    third = dot_exact(as_rows(third), rest_3).reshape(SPAN_3, 16, 128)
    third = jnp.where(inside_mask(third.shape, SPAN_3, 9, where), third, 0.0)
    packed[...] = fine[...]
    packed[0:SPAN_2, 0:24, :] += roll(second, SEC)
    packed[0:SPAN_3, 0:16, :] += roll(third, THI)
    leave = pltpu.make_async_copy(packed, packed_hbm, sems.at[4])
    leave.start()
    for p, plane in enumerate(restrict_planes(lambda x: third[x], SPAN_4, SPAN_3, 3)):
        buf_4[p, 3:19, :] = plane
    last = taps([(W[t], buf_4[:, pl.ds(t, 8, stride=2), :]) for t in range(5)])
    last = dot_exact(as_rows(last), rest_4).reshape(SPAN_4, 8, 128)
    last = jnp.where(inside_mask(last.shape, SPAN_4, 5, where), last, 0.0)
    raw = taps([(1.0, roll(last[x], 8 * x)) for x in range(SPAN_4)])
    raw_out[...] = raw

    even, _, _ = nearest(index[1])
    low = pack_y(packed, FIRST_ROWS)
    high = pack_y(packed, LAST_ROWS)
    for v in range(4):
        face[8 * v : 8 * v + 8, :] = jnp.where(even, high[v], low[v])
        face[FACE + 8 * v : FACE + 8 * v + 8, :] = jnp.where(even, low[v], high[v])
    face[2 * FACE : 2 * FACE + 8, :] = raw
    leave.wait()


def spot_1(p):
    return p // 16, p % 16 // 4 * 2, p % 4 * 32


def spot_2(p):
    return 2 + p // 14, p % 14 // 7 * 4, p % 7 * 18


def spot_3(p):
    return 3, 4, p * 11


def spot_4(p):
    return 3, p // 5, 72 + p % 5 * 11


FACE = 32
LEVELS = (
    (32, 2, 0, 32, spot_1),
    (SPAN_2, 4, SEC, 18, spot_2),
    (SPAN_3, 4, THI, 11, spot_3),
    (SPAN_3, 1, THI, 11, spot_4),
)
FIRST_ROWS = (0, 0, 0, 4)
LAST_ROWS = (30, 14, 6, 10)
ROWS_ABOVE = (34, 18, 10, 14)


def pack_y(source, at):
    tiles = [jnp.zeros((8, 128), F32) for _ in range(4)]
    row, at_lane = iota((8, 128), 0), iota((8, 128), 1)
    for (planes, count, lane, width, spot), start in zip(LEVELS, at):
        for p in range(planes):
            v, r, to = spot(p)
            if start == 30:
                slab = roll(source[p, 24:32, :], r - 6, 0)
            else:
                slab = roll(source[p, start : start + 8, :], r, 0)
            slab = roll(slab, to - lane)
            keep = (row >= r) & (row < r + count) & (at_lane >= to) & (at_lane < to + width)
            tiles[v] = jnp.where(keep, slab, tiles[v])
    return tiles


def place_y(tile, index):
    tall = jnp.concatenate([tile, jnp.zeros((8, 128), F32)], axis=0)
    tall = pltpu.roll(tall, lax.rem(4 * index + 15, 16), 0)
    return tall[0:8] + roll(tall[8:16], 64)


def relay_kernel(raw, got, out):
    index, _ = place()
    out[0:FACE, :] = got[FACE : 2 * FACE, :]
    partner = jnp.bitwise_xor(index[1], 1)
    other = got[2 * FACE : 2 * FACE + 8, :]
    out[FACE : FACE + 8, :] = place_y(raw[...], index[1]) + place_y(other, partner)


def widen_y_kernel(framed, own, got_1, got_2, after, out, raw_out, slots):
    index, _ = place()
    even, one, two = nearest(index[1])
    total = own[FACE : FACE + 8, :] + got_2[FACE : FACE + 8, :]
    raw_out[...] = total
    a, b = got_1[0:FACE, :], got_2[0:FACE, :]
    low = jnp.where(even, 0.0, a) + jnp.where(two, b, 0.0)
    high = jnp.where(even, a, 0.0) + jnp.where(one, b, 0.0)
    for face, at in ((low, FIRST_ROWS), (high, ROWS_ABOVE)):
        for (planes, count, lane, width, spot), start in zip(LEVELS, at):
            for p in range(planes):
                v, r, to = spot(p)
                slab = roll(roll(face[8 * v : 8 * v + 8], -r, 0), lane - to)
                slab = lanes_of(slab, lane, width)
                out[p, start : start + count, :] += slab[0:count]
    for n in range(4):
        to_high = index[0] < n
        f = jnp.where(to_high, 30, 0)
        s = jnp.where(to_high, 14, 0)
        t = jnp.where(to_high, 6, 0)
        ref = slots.at[n]
        ref[0:40, :] = lanes_of(out[f], 0, 32) + lanes_of(roll(out[f + 1], 32), 32, 32)
        ref[0:16, :] += taps(
            [(1.0, lanes_of(roll(out[t + k, 0:16, :], 11 * k), THI + 11 * k, 11)) for k in range(5)]
        )
        ref[40:64, :] = taps(
            [(1.0, lanes_of(roll(out[s + k, 0:24, :], 18 * k - SEC), 18 * k, 18)) for k in range(4)]
        )
        ref[64:72, :] = total


def widen_x_kernel(wide_y, own, got, after, out, raw_out, to_high, to_low):
    index, _ = place()
    total = None
    lane = iota((16, 128), 1)
    for n in range(4):
        tile = jnp.where(index[0] == n, own[...], got[n, 64:72, :])
        tall = jnp.concatenate([tile, roll(tile, 64)], axis=0)
        tall = jnp.where(lane < 64, tall, 0.0)
        moved = roll(tall, 32 * n - 8)
        total = moved if total is None else total + moved
    raw_out[...] = total
    low = jnp.where(index[0] == 0, 0.0, got[jnp.maximum(index[0] - 1, 0)])
    high = jnp.where(index[0] == 3, 0.0, got[jnp.minimum(index[0] + 1, 3)])
    out[0:2] = jnp.zeros((2, 40, 128), F32)
    out[34:36] = jnp.zeros((2, 40, 128), F32)
    out[2:34] = wide_y[...]
    for face, at in ((low, (0, 0, 0)), (high, (34, 18, 10))):
        for k in range(2):
            out[at[0] + k] += lanes_of(roll(face[0:40], -32 * k), 0, 32)
        for k in range(4):
            out[at[1] + k, 0:24, :] += lanes_of(roll(face[40:64], SEC - 18 * k), SEC, 18)
        for k in range(5):
            out[at[2] + k, 0:16, :] += lanes_of(roll(face[0:16], -11 * k), THI, 11)
    for ref, high in ((to_high, True), (to_low, False)):
        pack_z(out, ref, high)
        ref[64:80, :] = total


def pack_z(source, face, to_high):
    sums = []
    for rows, planes, count, lane, high in ((40, 36, 2, 0, 30), (24, 22, 4, SEC, 14), (16, 15, 5, THI, 6)):
        first = lane + high if to_high else lane
        at = iota((rows, 128), 1)
        wanted = (at >= first) & (at < first + count)
        total = jnp.zeros((rows, 128), F32)
        for x in range(planes):
            kept = jnp.where(wanted, source[x, 0:rows, :], 0.0)
            total = total + roll(kept, count * x - first)
        sums.append(total)
    face[0:40, :] = sums[0]
    face[40:64, :] = sums[1]
    face[0:16, :] += lanes_of(roll(sums[2], 72), 72, 55)
    face[40:56, :] += lanes_of(roll(sums[2], 88 - 55), 88, 20)


def unpack_z(message):
    third = lanes_of(roll(message[0:16], -72), 0, 55) + lanes_of(roll(message[40:56], 55 - 88), 55, 20)
    return message[0:40], message[40:64], third


def window_kernel(own, got_2, from_low, from_high, after, out):
    index, _ = place()
    early = lax.rem(index[2], 4) < 2
    ends = got_2[...]
    first, second, third = from_low[64:80, :], own[...], from_high[64:80, :]
    pieces = (
        jnp.where(early, first, ends),
        jnp.where(early, second, first),
        jnp.where(early, third, second),
        jnp.where(early, ends, third),
    )
    for group in range(3):
        total = None
        for q in range(min(6, 16 - 6 * group)):
            for d, piece in enumerate(pieces):
                to = 20 * q + 4 * d
                moved = lanes_of(roll(piece, to - 48 * group - 8 * q), to, 8)
                total = moved if total is None else total + moved
        out[group] = total


def divided(n, d):
    factor, bits = DIVIDE[d]
    return lax.shift_right_logical(n * factor, bits)


def build_bands(kernel, band):
    rows, columns, runs, group, outs = band
    row = iota((rows, 128), 0)
    shift = jnp.full((rows, 128), 99, jnp.int32)
    point = jnp.full((rows, 128), 99, jnp.int32)
    for start, count, offset in runs:
        at = row - start
        a = divided(at, count)
        inside = (at >= 0) & (at < 5 * count)
        shift = jnp.where(inside, a, shift)
        point = jnp.where(inside, offset + at - a * count, point)
    chosen = (shift == iota((rows, 128), 1)).astype(F32).astype(BF16)
    column = iota((8, columns), 1)
    block = divided(column, group)
    out_at = (column - block * group)[0:1]
    block = jnp.where((column - block * group) < outs, block, 9)
    sub = iota((8, columns), 0)
    entry = jnp.concatenate([point] * (columns // 128), axis=1) - out_at
    total_high = jnp.zeros((rows, columns), F32)
    total_low = jnp.zeros((rows, columns), F32)
    for c in range(5):
        source = jnp.zeros((8, columns), F32)
        for b in range(5):
            column_of = jnp.zeros((8, columns), F32)
            for a in range(5):
                column_of = jnp.where(sub == a, kernel[a, b, c], column_of)
            source = jnp.where(block == b, column_of, source)
        source = jnp.concatenate([source, jnp.zeros((120, columns), F32)], axis=0)
        high, low = split(source)
        fits = entry == c
        total_high = jnp.where(fits, dot(chosen, high), total_high)
        total_low = jnp.where(fits, dot(chosen, low), total_low)
    return total_high.astype(BF16), total_low.astype(BF16)


def bands_kernel(bands, *refs):
    kernels, outs = refs[: len(bands)], refs[len(bands) :]
    for n, (kernel, band) in enumerate(zip(kernels, bands)):
        high, low = build_bands(kernel, band)
        outs[2 * n][...] = high
        outs[2 * n + 1][...] = low


def green_kernel(factors, packed, green_high, green_low, rise, framed, block_high, block_low):
    index, sizes = place()
    row, lane = iota((64, 128), 0), iota((64, 128), 1)
    delta_x = (lane // 8).astype(F32)
    delta_z = (4 * index[2] - 1 + lane % 8 - row).astype(F32)
    plain = delta_z * delta_z + (1.0 + delta_x * delta_x)
    for apart in range(18):
        high, low = split(0.0625 * lax.rsqrt(plain + float(apart * apart)))
        block_high[apart] = high
        block_low[apart] = low
    for ty in range(SPAN_4):
        columns = slice(128 * ty, 128 * ty + 128)
        for sy in range(16):
            apart = jnp.abs(4 * index[1] - 1 + ty - sy)
            first = sy % 8 * 128 + sy // 8 * 64
            green_high[first : first + 64, columns] = block_high[apart]
            green_low[first : first + 64, columns] = block_low[apart]
    variant = [
        jnp.where(index[d] == 0, 1, 0) + jnp.where(index[d] == sizes[d] - 1, 2, 0) for d in range(3)
    ]
    factor_x, factor_y = factors[variant[0]], factors[4 + variant[1]]
    kept = as_rows(factor_x[:, None, :] * factor_y[None, :, :])
    high, low = split(kept)
    rise[:, 0:128] = (high.astype(F32) + roll(low.astype(F32), 64)).astype(BF16)
    rise[:, 128:256] = high
    framed[:, 0:2, :] = jnp.zeros((32, 2, 128), F32)
    framed[:, 34:40, :] = jnp.zeros((32, 6, 128), F32)
    framed[:, 2:34, :] = packed[...]


def prolong_rows(source, target, count, whole):
    size = target.shape[1] // 2
    q0 = source[:, 0:size, :]
    q1 = source[:, 1 : size + 1, :]
    q2 = source[:, 2 : size + 2, :]
    even = 0.75 * q1 + 0.125 * (q0 + q2)
    odd = 0.5 * (q0 + q1) if whole else 0.5 * (q1 + q2)
    target[:, pl.ds(1 if whole else 0, size, stride=2), :] = even
    target[:, pl.ds(0 if whole else 1, size, stride=2), :] = odd


def prolong_plane(read, p, whole):
    half = p // 2
    if (p % 2 == 1) == whole:
        return 0.75 * read(half + 1) + 0.125 * (read(half) + read(half + 2))
    first = half if whole else half + 1
    return 0.5 * (read(first) + read(first + 1))


def near_kernel(
    wide, from_low, from_high, b1h, b1l, b2h, b2l, b3h, b3l, prol_2, prol_1,
    out,
    near_1, near_2, near_3, tall_3, tall_3y, tall_2, tall_2y,
):
    where = place()
    index, sizes = where
    low_faces = unpack_z(jnp.where(index[2] == 0, 0.0, from_low[0:64, :]))
    high_faces = unpack_z(jnp.where(index[2] == sizes[2] - 1, 0.0, from_high[0:64, :]))

    def halo(x, level, count, low_at, high_at):
        low = roll(low_faces[level], low_at - count * x)
        high = roll(high_faces[level], high_at - count * x)
        return lanes_of(low, low_at, 5 * count) + lanes_of(high, high_at, 5 * count)

    planes = [lanes_of(wide[x, 0:16, :], THI, 11) for x in range(15)]
    left = []
    for x in range(SPAN_3):
        main = taps([(1.0, roll(planes[x + a], 11 * a - THI)) for a in range(5)])
        left.append(main + halo(x, 2, 5, 64, 96))
    left = jnp.concatenate(left, axis=0)
    near_3[...] = jnp.zeros_like(near_3)
    near_3[:, 0:16, :] = dot_split(left, b3h[...], b3l[...]).reshape(SPAN_3, 16, 128)
    third = taps([(1.0, roll(near_3[:, b : b + 16, :], -16 * b)) for b in range(5)])
    third = jnp.where(inside_mask(third.shape, SPAN_3, 9, where), third, 0.0)
    tall_3[...] = jnp.zeros_like(tall_3)
    tall_3[:, 0:16, :] = dot_exact(as_rows(third), prol_2[...]).reshape(SPAN_3, 16, 128)
    prolong_rows(tall_3, tall_3y, SPAN_2, True)

    planes = [lanes_of(wide[x, 0:24, :], SEC, 18) for x in range(22)]
    left_a, left_b = [], []
    for x in range(SPAN_2):
        left_a.append(taps([(1.0, roll(planes[x + a], 18 * a - SEC)) for a in range(5)]))
        left_b.append(halo(x, 1, 4, 0, 32))
    left = jnp.concatenate(
        [jnp.concatenate(left_a, axis=0), jnp.concatenate(left_b, axis=0)], axis=1
    )
    near_2[...] = jnp.zeros_like(near_2)
    near_2[:, 0:24, :] = dot_split(left, b2h[...], b2l[...]).reshape(SPAN_2, 24, 128)
    second = taps([(1.0, roll(near_2[:, b : b + 24, :], -24 * b)) for b in range(5)])
    raised = jnp.stack(
        [prolong_plane(lambda x: tall_3y[x], p, True) for p in range(SPAN_2)], axis=0
    )
    second = jnp.where(inside_mask(second.shape, SPAN_2, 17, where), second + raised, 0.0)
    tall_2[...] = jnp.zeros_like(tall_2)
    tall_2[:, 0:24, :] = dot_exact(as_rows(second), prol_1[...]).reshape(SPAN_2, 24, 128)
    prolong_rows(tall_2, tall_2y, 32, False)

    planes = [lanes_of(wide[x], 0, 32) for x in range(36)]
    left_a, left_b = [], []
    for x in range(32):
        left_a.append(taps([(1.0, roll(planes[x + a], 32 * a)) for a in range(4)]))
        left_b.append(planes[x + 4] + halo(x, 0, 2, 32, 64))
    left = jnp.concatenate(
        [jnp.concatenate(left_a, axis=0), jnp.concatenate(left_b, axis=0)], axis=1
    )
    near_1[...] = dot_split(left, b1h[...], b1l[...]).reshape(32, 40, 256)
    for x in range(32):
        first = taps(
            [(1.0, roll(near_1[x, b : b + 32, 0:128], -32 * b)) for b in range(4)]
            + [(1.0, near_1[x, 4:36, 128:256])]
        )
        out[x] = first + prolong_plane(lambda q: tall_2y[q], x, False)


def top_kernel(
    base, piece_0, piece_1, piece_2, piece_3, green_high, green_low, rise, qz,
    out_hbm,
    fourth, out, sems,
):
    index, sizes = place()
    lane = iota((8, 128), 1)
    ring = lax.rem(index[2], 4)
    first = 4 * (ring == 3).astype(jnp.int32) - 4 * (ring == 0).astype(jnp.int32) + 127
    sources = [lax.rem(16 * lax.rem(index[2] // 4 + step, 4) + first, 128) for step in (0, 2, 3, 1)]
    for x in range(16):
        total = None
        for piece, at in zip((piece_0, piece_1, piece_2, piece_3), sources):
            kept = lanes_of(piece[x // 6], 20 * (x % 6), 20)
            moved = pltpu.roll(kept, lax.rem(at + 128 - 20 * (x % 6), 128), 1)
            total = moved if total is None else total + moved
        total = total + roll(total, 64)
        fourth[x] = jnp.where(lane < 64, total[0:8], total[8:16])
    total = jnp.zeros((32, 128 * SPAN_4), F32)
    extra = jnp.zeros((16, 128 * SPAN_4), F32)
    for s in range(0, 8, 2):
        left = jnp.concatenate([fourth[:, s, :], fourth[:, s + 1, :]], axis=1)
        high, low = split(left)
        rows = slice(128 * s, 128 * s + 256)
        total = total + dot(jnp.concatenate([high, low], axis=0), green_high[rows, :])
        extra = extra + dot(high, green_low[rows, :])
    sums = total[0:16] + (total[16:32] + extra)
    row, lane = iota((16, 128), 0), iota((16, 128), 1)
    tops = []
    for tx in range(SPAN_4):
        keep = jnp.abs(4 * index[0] - 1 + tx - row) == lane // 8
        for ty in range(SPAN_4):
            picked = jnp.where(keep, sums[:, 128 * ty : 128 * ty + 128], 0.0)
            tops.append(jnp.sum(picked, axis=0, keepdims=True))
        tops.append(jnp.zeros((1, 128), F32))
    tops = jnp.concatenate(tops + [jnp.zeros((8, 128), F32)], axis=0)
    variant = jnp.where(index[2] == 0, 1, 0) + jnp.where(index[2] == sizes[2] - 1, 2, 0)
    high, low = split(dot_split(tops, qz[variant], qz[4 + variant]))
    right = jnp.concatenate([high, high, low, jnp.zeros_like(low)], axis=0)
    copies = []
    for part in range(4):
        planes = slice(8 * part, 8 * part + 8)
        far = dot(rise[256 * part : 256 * part + 256, :], right)
        out[planes] = (base[planes] + far.reshape(8, 32, 128))[:, :, 0:32]
        copies.append(pltpu.make_async_copy(out.at[planes], out_hbm.at[planes], sems.at[part]))
        copies[-1].start()
    for copy in copies:
        copy.wait()


def call(kernel, outs, ins, scratch=(), megabytes=16, spaces=None, out_spaces=None, aliases=None, flops=1000000):
    spaces, out_spaces = spaces or {}, out_spaces or {}
    single = not isinstance(outs, tuple)
    out_specs = [out_spaces.get(i, VMEM) for i in range(1 if single else len(outs))]
    return pl.pallas_call(
        kernel,
        out_shape=outs,
        in_specs=[spaces.get(i, VMEM) for i in range(len(ins))],
        out_specs=out_specs[0] if single else out_specs,
        scratch_shapes=list(scratch),
        input_output_aliases=aliases or {},
        compiler_params=pltpu.CompilerParams(vmem_limit_bytes=int(megabytes * 2**20)),
        cost_estimate=pl.CostEstimate(flops=flops, bytes_accessed=2**21, transcendentals=0),
    )(*ins)


def shape(*dims, dtype=F32):
    return jax.ShapeDtypeStruct(dims, dtype)


def exchange(values, axis, steps):
    size = lax.axis_size(axis)
    return [
        lax.ppermute(value, axis, [(i, i ^ step) for i in range(size)])
        for value, step in zip(values, steps)
    ]


def turn(value, by):
    size_y, size_z = lax.axis_size("gy"), lax.axis_size("gz")
    half = size_y // 2
    pairs = []
    for core in range(half):
        ring = [(high * half + core) * size_z + z for high in range(2) for z in range(size_z)]
        pairs += [(ring[n], ring[(n + by) % len(ring)]) for n in range(len(ring))]
    return lax.ppermute(value, ("gy", "gz"), pairs)


def banded(bands, *kernels, flops=10**9):
    return call(
        functools.partial(bands_kernel, bands),
        tuple(shape(band[0], band[1], dtype=BF16) for band in bands for _ in range(2)),
        kernels,
        spaces={n: SMEM for n in range(len(kernels))},
        flops=flops,
    )


def shards(charges, counts, slots, spline, kernel_fine, kernel_mid, kernel_coarse):
    cells = charges.shape[0]
    packed, raw, face = call(
        deposit_kernel,
        (shape(32, 32, 128), shape(8, 128), shape(2 * FACE + 8, 128)),
        (256 * slots + counts, charges, spline.reshape(cells * 12, ATOMS)),
        (
            pltpu.VMEM((32, 32, 128), F32),
            pltpu.VMEM((cells, ATOMS), F32),
            pltpu.VMEM((cells * 12, 128), BF16),
            pltpu.VMEM((cells * 12, 128), F32),
            pltpu.VMEM((64, cells), F32),
            pltpu.VMEM((32, 32, 128), F32),
            pltpu.VMEM((SPAN_2, 56, 128), F32),
            pltpu.VMEM((SPAN_3, 40, 128), F32),
            pltpu.VMEM((SPAN_4, 24, 128), F32),
            pltpu.SemaphoreType.DMA((5,)),
        ),
        spaces={1: HBM, 2: HBM},
        out_spaces={0: ANY},
        megabytes=53.75,
    )
    (got_1,) = exchange((face,), "gy", (1,))
    relay = call(relay_kernel, shape(FACE + 8, 128), (raw, got_1))
    (got_2,) = exchange((relay,), "gy", (2,))
    qx, qy, qz = composites()
    qz_high = qz.astype(BF16)
    qz_low = (qz - qz_high.astype(np.float32)).astype(BF16)
    green_high, green_low, rise, framed = call(
        green_kernel,
        (
            shape(1024, 128 * SPAN_4, dtype=BF16),
            shape(1024, 128 * SPAN_4, dtype=BF16),
            shape(1024, 256, dtype=BF16),
            shape(32, 40, 128),
        ),
        (jnp.asarray(np.concatenate([qx, qy])), packed),
        (pltpu.VMEM((18, 64, 128), BF16), pltpu.VMEM((18, 64, 128), BF16)),
    )
    wide_y, raw, slots = call(
        widen_y_kernel,
        (shape(32, 40, 128), shape(8, 128), shape(4, 72, 128)),
        (framed, relay, got_1, got_2, rise),
        spaces={4: ANY},
        aliases={0: 0},
    )
    got = lax.all_to_all(slots, "gx", split_axis=0, concat_axis=0, tiled=True)
    bands_1 = banded(BANDS[:1], kernel_fine)
    wide_x, raw, to_high, to_low = call(
        widen_x_kernel,
        (shape(36, 40, 128), shape(16, 128), shape(80, 128), shape(80, 128)),
        (wide_y, raw, got, bands_1[0]),
        spaces={3: ANY},
    )
    from_low, from_high = turn(to_high, 1), turn(to_low, -1)
    (got_2,) = exchange((raw,), "gz", (2,))
    bands_2 = banded(BANDS[1:], kernel_mid, kernel_coarse)
    window = call(
        window_kernel,
        shape(3, 16, 128),
        (raw, got_2, from_low, from_high, bands_2[0]),
        spaces={4: ANY},
    )
    pieces = [window] + [turn(window, by) for by in (8, 4, -4)]
    base = call(
        near_kernel,
        shape(32, 32, 128),
        (wide_x, from_low, from_high, *bands_1, *bands_2, jnp.asarray(PROL_2, BF16), jnp.asarray(PROL_1, BF16)),
        (
            pltpu.VMEM((32, 40, 256), F32),
            pltpu.VMEM((SPAN_2, 32, 128), F32),
            pltpu.VMEM((SPAN_3, 24, 128), F32),
            pltpu.VMEM((SPAN_3, 24, 128), F32),
            pltpu.VMEM((SPAN_3, 24, 128), F32),
            pltpu.VMEM((SPAN_2, 32, 128), F32),
            pltpu.VMEM((SPAN_2, 32, 128), F32),
        ),
    )
    return call(
        top_kernel,
        shape(32, 32, 32),
        (base, *pieces, green_high, green_low, rise, jnp.asarray(np.concatenate([qz_high, qz_low]))),
        (
            pltpu.VMEM((16, 8, 128), F32),
            pltpu.VMEM((32, 32, 32), F32),
            pltpu.SemaphoreType.DMA((4,)),
        ),
        out_spaces={0: ANY},
    )


def solution(mesh):
    return jax.shard_map(
        shards,
        mesh=mesh,
        in_specs=(
            P(("gx", "gy", "gz"), None),
            P(("gx", "gy", "gz")),
            P(("gx", "gy", "gz")),
            P(("gx", "gy", "gz"), None, None, None),
            P(),
            P(),
            P(),
        ),
        out_specs=P("gx", "gy", "gz"),
        check_vma=False,
    )
```

```python
import functools

import jax
import jax.numpy as jnp
import numpy as np
from jax import lax
from jax.experimental import pallas as pl
from jax.experimental.pallas import tpu as pltpu
from jax.sharding import PartitionSpec as P

W = (0.125, 0.5, 0.75, 0.5, 0.125)
F32 = jnp.float32
BF16 = jnp.bfloat16
CELLS = 384
ATOMS = 128
SPAN_2 = 18
SPAN_3 = 11
SPAN_4 = 7
SEC = 32
THI = 64
VMEM = pl.BlockSpec(memory_space=pltpu.VMEM)
SMEM = pl.BlockSpec(memory_space=pltpu.SMEM)
HBM = pl.BlockSpec(memory_space=pltpu.HBM)
ANY = pl.BlockSpec(memory_space=pl.ANY)


def weight(t):
    return W[t] if 0 <= t <= 4 else 0.0


def table(rows, columns, offset, turned):
    out = np.zeros((128, 128), np.float32)
    for r in range(rows):
        for c in range(columns):
            out[r, c] = weight(c - 2 * r + offset if turned else r - 2 * c + offset)
    return out


PROL_2 = table(SPAN_3, SPAN_2, 3, True)
PROL_1 = table(SPAN_2, 32, 4, True)


BANDS = (
    (256, 256, ((0, 32, 2), (160, 2, 0), (192, 2, 34)), 32, 32),
    (256, 128, ((0, 18, 2), (128, 4, 0), (160, 4, 18)), 24, 18),
    (128, 128, ((0, 11, 2), (64, 5, 0), (96, 5, 10)), 16, 11),
)
DIVIDE = {32: (1, 5), 2: (1, 1), 18: (57, 10), 4: (1, 2), 11: (94, 10), 5: (52, 8), 24: (43, 10), 16: (1, 4)}


def composite(first, last):
    p3 = np.array([[weight(i - 2 * j + 3) for j in range(7)] for i in range(11)])
    p2 = np.array([[weight(i - 2 * j + 3) for j in range(11)] for i in range(18)])
    p1 = np.array([[weight(i - 2 * j + 4) for j in range(18)] for i in range(32)])
    m4, m3, m2 = np.ones(7), np.ones(11), np.ones(18)
    if first:
        m4[0] = m3[0] = m2[0] = 0
    if last:
        m4[5:] = 0
        m3[9:] = 0
        m2[17:] = 0
    return (p1 * m2) @ (p2 * m3) @ (p3 * m4)


def composites():
    qx = np.zeros((4, 32, 128), np.float32)
    qy = np.zeros((4, 32, 128), np.float32)
    qz = np.zeros((4, 128, 128), np.float32)
    for v in range(4):
        q = composite(v % 2 == 1, v >= 2)
        for lane in range(64):
            if lane // 8 < 7 and lane % 8 < 7:
                qx[v, :, lane] = q[:, lane // 8]
                qy[v, :, lane] = q[:, lane % 8]
        for row in range(128):
            if row % 8 < 7:
                qz[v, row, :32] = q[:, row % 8]
    return qx, qy, qz


def split(x):
    high = x.astype(BF16)
    return high, (x - high.astype(F32)).astype(BF16)


def dot(a, b):
    return jnp.dot(a, b, preferred_element_type=F32)


def dot_exact(x, right):
    high, low = split(x)
    return dot(high, right) + dot(low, right)


def dot_split(x, right_high, right_low):
    high, low = split(x)
    return dot(high, right_high) + (dot(low, right_high) + dot(high, right_low))


def iota(shape, dim):
    return lax.broadcasted_iota(jnp.int32, shape, dim)


def roll(x, shift, axis=None):
    axis = x.ndim - 1 if axis is None else axis
    shift = shift % x.shape[axis]
    return x if shift == 0 else pltpu.roll(x, shift, axis)


def lanes_of(x, low, count):
    lane = iota(x.shape, x.ndim - 1)
    return jnp.where((lane >= low) & (lane < low + count), x, 0.0)


def as_rows(x):
    return x.reshape(x.shape[0] * x.shape[1], x.shape[2])


def taps(pieces):
    total = None
    for factor, value in pieces:
        term = value if factor == 1.0 else factor * value
        total = term if total is None else total + term
    return total


def restrict_planes(read, span, size, offset):
    planes = []
    for p in range(span):
        planes.append(
            taps([(W[t], read(2 * p + t - offset)) for t in range(5) if 0 <= 2 * p + t - offset < size])
        )
    return planes


def place():
    sizes = [lax.axis_size(a) for a in ("gx", "gy", "gz")]
    index = [lax.axis_index(a) for a in ("gx", "gy", "gz")]
    return index, sizes


def inside_mask(shape, spans, high, place_of):
    index, sizes = place_of
    keep = None
    for dim in range(3):
        at = iota(shape, dim)
        low = jnp.where(index[dim] == 0, 1, 0)
        top = jnp.where(index[dim] == sizes[dim] - 1, high, spans)
        part = (at >= low) & (at < top)
        keep = part if keep is None else keep & part
    return keep


def nearest(index):
    even = lax.rem(index, 2) == 0
    return even, index == 1, index == 2


def deposit_kernel(
    codes, charges_hbm, spline_hbm,
    packed_hbm, raw_out, face,
    packed, charges, spline, wide, patch, fine, buf_2, buf_3, buf_4, sems,
):
    where = place()
    index, sizes = where
    part = CELLS * 12 // 3
    copies = [pltpu.make_async_copy(charges_hbm, charges, sems.at[3])]
    for chunk in range(3):
        rows = slice(part * chunk, part * chunk + part)
        copies.append(
            pltpu.make_async_copy(spline_hbm.at[rows, :], spline.at[rows, :], sems.at[chunk])
        )
    for copy in copies:
        copy.start()
    buf_2[...] = jnp.zeros_like(buf_2)
    buf_3[...] = jnp.zeros_like(buf_3)
    buf_4[...] = jnp.zeros_like(buf_4)
    row, column = iota((512, 64), 0), iota((512, 64), 1)
    spread = (row // 32 * 4 + row % 4 == column).astype(F32).astype(BF16)
    row, column = iota((128, 128), 0), iota((128, 128), 1)

    def restriction(rows, columns, offset):
        t = row - 2 * column + offset
        out = jnp.zeros((128, 128), F32)
        for tap in range(5):
            out = jnp.where(t == tap, W[tap], out)
        return jnp.where((row < rows) & (column < columns), out, 0.0).astype(BF16)

    rest_2 = restriction(32, SPAN_2, 4)
    rest_3 = restriction(SPAN_2, SPAN_3, 3)
    rest_4 = restriction(SPAN_3, SPAN_4, 3)
    slot = lax.shift_right_logical(codes[...].reshape(1, CELLS), 8)
    fits = (iota((512, CELLS), 0) // 4 % 8) == slot % 8
    hot = (iota((64, CELLS), 0) == slot // 8).astype(F32).astype(BF16)
    copies[0].wait()
    alive = iota((ATOMS, CELLS), 0) < (codes[...].reshape(1, CELLS) & 255)
    weighted = jnp.where(alive, charges[...].T, 0.0)
    for chunk in range(CELLS // 128):
        lanes = slice(128 * chunk, 128 * chunk + 128)
        copies[1 + chunk].wait()
        rows = slice(part * chunk, part * chunk + part)
        wide[rows, :] = spline[rows, :].astype(F32)

        def column_of(d, i):
            return wide[pl.ds(chunk * part + 4 * d + i, 128, stride=12), :].T

        charge = weighted[:, lanes]
        depth = [charge * column_of(2, k) for k in range(4)]
        ys = [column_of(1, j) for j in range(4)]
        for i in range(4):
            xs = column_of(0, i)
            for j in range(4):
                cross = xs * ys[j]
                for k in range(4):
                    patch[16 * i + 4 * j + k : 16 * i + 4 * j + k + 1, lanes] = jnp.sum(
                        cross * depth[k], axis=0, keepdims=True
                    )
    high, low = split(patch[...])
    spread_high = jnp.where(fits, dot(spread, high), 0.0).astype(BF16)
    spread_low = jnp.where(fits, dot(spread, low), 0.0).astype(BF16)
    nt = (((1,), (1,)), ((), ()))
    placed = lax.dot_general(hot, spread_high, nt, preferred_element_type=F32) + lax.dot_general(
        hot, spread_low, nt, preferred_element_type=F32
    )
    for i in range(4):
        for j in range(4):
            rows = lanes_of(roll(placed[:, 128 * i : 128 * i + 128], -32 * j), 0, 32)
            for sx in range(8):
                fine[4 * sx + i, pl.ds(j, 8, stride=4), :] = rows[8 * sx : 8 * sx + 8]

    for p, plane in enumerate(restrict_planes(lambda x: fine[x], SPAN_2, 32, 4)):
        buf_2[p, 4:36, :] = plane
    second = taps([(W[t], buf_2[:, pl.ds(t, 24, stride=2), :]) for t in range(5)])
    second = dot_exact(as_rows(second), rest_2).reshape(SPAN_2, 24, 128)
    second = jnp.where(inside_mask(second.shape, SPAN_2, 17, where), second, 0.0)
    for p, plane in enumerate(restrict_planes(lambda x: second[x], SPAN_3, SPAN_2, 3)):
        buf_3[p, 3:27, :] = plane
    third = taps([(W[t], buf_3[:, pl.ds(t, 16, stride=2), :]) for t in range(5)])
    third = dot_exact(as_rows(third), rest_3).reshape(SPAN_3, 16, 128)
    third = jnp.where(inside_mask(third.shape, SPAN_3, 9, where), third, 0.0)
    packed[...] = fine[...]
    packed[0:SPAN_2, 0:24, :] += roll(second, SEC)
    packed[0:SPAN_3, 0:16, :] += roll(third, THI)
    leave = pltpu.make_async_copy(packed, packed_hbm, sems.at[4])
    leave.start()
    for p, plane in enumerate(restrict_planes(lambda x: third[x], SPAN_4, SPAN_3, 3)):
        buf_4[p, 3:19, :] = plane
    last = taps([(W[t], buf_4[:, pl.ds(t, 8, stride=2), :]) for t in range(5)])
    last = dot_exact(as_rows(last), rest_4).reshape(SPAN_4, 8, 128)
    last = jnp.where(inside_mask(last.shape, SPAN_4, 5, where), last, 0.0)
    raw = taps([(1.0, roll(last[x], 8 * x)) for x in range(SPAN_4)])
    raw_out[...] = raw

    even, _, _ = nearest(index[1])
    low = pack_y(packed, FIRST_ROWS)
    high = pack_y(packed, LAST_ROWS)
    for v in range(4):
        face[8 * v : 8 * v + 8, :] = jnp.where(even, high[v], low[v])
        face[FACE + 8 * v : FACE + 8 * v + 8, :] = jnp.where(even, low[v], high[v])
    face[2 * FACE : 2 * FACE + 8, :] = raw
    leave.wait()


def spot_1(p):
    return p // 16, p % 16 // 4 * 2, p % 4 * 32


def spot_2(p):
    return 2 + p // 14, p % 14 // 7 * 4, p % 7 * 18


def spot_3(p):
    return 3, 4, p * 11


def spot_4(p):
    return 3, p // 5, 72 + p % 5 * 11


FACE = 32
LEVELS = (
    (32, 2, 0, 32, spot_1),
    (SPAN_2, 4, SEC, 18, spot_2),
    (SPAN_3, 4, THI, 11, spot_3),
    (SPAN_3, 1, THI, 11, spot_4),
)
FIRST_ROWS = (0, 0, 0, 4)
LAST_ROWS = (30, 14, 6, 10)
ROWS_ABOVE = (34, 18, 10, 14)


def pack_y(source, at):
    tiles = [jnp.zeros((8, 128), F32) for _ in range(4)]
    row, at_lane = iota((8, 128), 0), iota((8, 128), 1)
    for (planes, count, lane, width, spot), start in zip(LEVELS, at):
        for p in range(planes):
            v, r, to = spot(p)
            if start == 30:
                slab = roll(source[p, 24:32, :], r - 6, 0)
            else:
                slab = roll(source[p, start : start + 8, :], r, 0)
            slab = roll(slab, to - lane)
            keep = (row >= r) & (row < r + count) & (at_lane >= to) & (at_lane < to + width)
            tiles[v] = jnp.where(keep, slab, tiles[v])
    return tiles


def place_y(tile, index):
    tall = jnp.concatenate([tile, jnp.zeros((8, 128), F32)], axis=0)
    tall = pltpu.roll(tall, lax.rem(4 * index + 15, 16), 0)
    return tall[0:8] + roll(tall[8:16], 64)


def relay_kernel(raw, got, out):
    index, _ = place()
    out[0:FACE, :] = got[FACE : 2 * FACE, :]
    partner = jnp.bitwise_xor(index[1], 1)
    other = got[2 * FACE : 2 * FACE + 8, :]
    out[FACE : FACE + 8, :] = place_y(raw[...], index[1]) + place_y(other, partner)


def widen_y_kernel(framed, own, got_1, got_2, after, out, raw_out, face_1, face_3):
    index, _ = place()
    even, one, two = nearest(index[1])
    total = own[FACE : FACE + 8, :] + got_2[FACE : FACE + 8, :]
    raw_out[...] = total
    a, b = got_1[0:FACE, :], got_2[0:FACE, :]
    low = jnp.where(even, 0.0, a) + jnp.where(two, b, 0.0)
    high = jnp.where(even, a, 0.0) + jnp.where(one, b, 0.0)
    for face, at in ((low, FIRST_ROWS), (high, ROWS_ABOVE)):
        for (planes, count, lane, width, spot), start in zip(LEVELS, at):
            for p in range(planes):
                v, r, to = spot(p)
                slab = roll(roll(face[8 * v : 8 * v + 8], -r, 0), lane - to)
                slab = lanes_of(slab, lane, width)
                out[p, start : start + count, :] += slab[0:count]
    even, one, _ = nearest(index[0])
    for ref, to_high in ((face_1, even), (face_3, one)):
        f = jnp.where(to_high, 30, 0)
        s = jnp.where(to_high, 14, 0)
        t = jnp.where(to_high, 6, 0)
        ref[0:40, :] = lanes_of(out[f], 0, 32) + lanes_of(roll(out[f + 1], 32), 32, 32)
        ref[0:16, :] += taps(
            [(1.0, lanes_of(roll(out[t + k, 0:16, :], 11 * k), THI + 11 * k, 11)) for k in range(5)]
        )
        ref[40:64, :] = taps(
            [(1.0, lanes_of(roll(out[s + k, 0:24, :], 18 * k - SEC), 18 * k, 18)) for k in range(4)]
        )
        ref[64:72, :] = total


def x_faces(index, got_1, got_3):
    even, one, two = nearest(index)
    a, b = got_1[0:64, :], got_3[0:64, :]
    low = jnp.where(even, 0.0, a) + jnp.where(two, b, 0.0)
    high = jnp.where(even, a, 0.0) + jnp.where(one, b, 0.0)
    planes = []
    for face, at in ((low, (0, 0, 0)), (high, (34, 18, 10))):
        for k in range(2):
            planes.append((0, at[0] + k, lanes_of(roll(face[0:40], -32 * k), 0, 32)))
        for k in range(4):
            planes.append((1, at[1] + k, lanes_of(roll(face[40:64], -18 * k), 0, 18)))
        for k in range(5):
            planes.append((2, at[2] + k, lanes_of(roll(face[0:16], -THI - 11 * k), 0, 11)))
    return planes


def widen_x_kernel(wide_y, after, got_1, got_3, out):
    index, _ = place()
    out[0:2] = jnp.zeros((2, 40, 128), F32)
    out[34:36] = jnp.zeros((2, 40, 128), F32)
    out[2:34] = wide_y[...]
    for level, at, values in x_faces(index[0], got_1, got_3):
        rows = values.shape[0]
        out[at, 0:rows, :] += roll(values, (0, SEC, THI)[level])


Z_LEVELS = ((40, 2, 0, 30), (24, 4, SEC, 14), (16, 5, THI, 6))


def chosen_lanes(values, first, count):
    at = iota(values.shape, 1)
    return jnp.where((at >= first) & (at < first + count), values, 0.0)


def own_z_kernel(wide_y, after, high, low):
    for ref, to_high in ((high, True), (low, False)):
        start = 0
        for (rows, count, lane, top), planes in zip(Z_LEVELS, (32, SPAN_2, SPAN_3)):
            first = lane + top if to_high else lane
            total = jnp.zeros((rows, 128), F32)
            for x in range(planes):
                kept = chosen_lanes(wide_y[x, 0:rows, :], first, count)
                total = total + roll(kept, count * (x + 2) - first)
            ref[start : start + rows, :] = total
            start += rows


def edge_x_kernel(own, got_2, got_1, got_3, high, low, raw_out, to_high, to_low):
    index, _ = place()
    total = None
    lane = iota((16, 128), 1)
    for step, tile in ((0, own[...]), (1, got_1[64:72, :]), (2, got_2[...]), (3, got_3[64:72, :])):
        tall = jnp.concatenate([tile, roll(tile, 64)], axis=0)
        tall = jnp.where(lane < 64, tall, 0.0)
        at = lax.rem(32 * jnp.bitwise_xor(index[0], step) + 120, 128)
        moved = pltpu.roll(tall, at, 1)
        total = moved if total is None else total + moved
    raw_out[...] = total
    planes = x_faces(index[0], got_1, got_3)
    for face, own_face, is_high in ((to_high, high, True), (to_low, low, False)):
        sums = [own_face[0:40, :], own_face[40:64, :], own_face[64:80, :]]
        for level, at, values in planes:
            _, count, _, top = Z_LEVELS[level]
            first = top if is_high else 0
            kept = chosen_lanes(values, first, count)
            sums[level] = sums[level] + roll(kept, count * at - first)
        face[0:40, :] = sums[0]
        face[40:64, :] = sums[1]
        face[0:16, :] += lanes_of(roll(sums[2], 72), 72, 55)
        face[40:56, :] += lanes_of(roll(sums[2], 88 - 55), 88, 20)
        face[64:80, :] = total


def unpack_z(message):
    third = lanes_of(roll(message[0:16], -72), 0, 55) + lanes_of(roll(message[40:56], 55 - 88), 55, 20)
    return message[0:40], message[40:64], third


def window_kernel(own, got_2, from_low, from_high, after_1, after_2, out):
    index, _ = place()
    early = lax.rem(index[2], 4) < 2
    ends = got_2[...]
    first, second, third = from_low[64:80, :], own[...], from_high[64:80, :]
    pieces = (
        jnp.where(early, first, ends),
        jnp.where(early, second, first),
        jnp.where(early, third, second),
        jnp.where(early, ends, third),
    )
    for group in range(3):
        total = None
        for q in range(min(6, 16 - 6 * group)):
            for d, piece in enumerate(pieces):
                to = 20 * q + 4 * d
                moved = lanes_of(roll(piece, to - 48 * group - 8 * q), to, 8)
                total = moved if total is None else total + moved
        out[group] = total


def divided(n, d):
    factor, bits = DIVIDE[d]
    return lax.shift_right_logical(n * factor, bits)


def build_bands(kernel, band):
    rows, columns, runs, group, outs = band
    row = iota((rows, 128), 0)
    shift = jnp.full((rows, 128), 99, jnp.int32)
    point = jnp.full((rows, 128), 99, jnp.int32)
    for start, count, offset in runs:
        at = row - start
        a = divided(at, count)
        inside = (at >= 0) & (at < 5 * count)
        shift = jnp.where(inside, a, shift)
        point = jnp.where(inside, offset + at - a * count, point)
    chosen = (shift == iota((rows, 128), 1)).astype(F32).astype(BF16)
    column = iota((8, columns), 1)
    block = divided(column, group)
    out_at = (column - block * group)[0:1]
    block = jnp.where((column - block * group) < outs, block, 9)
    sub = iota((8, columns), 0)
    entry = jnp.concatenate([point] * (columns // 128), axis=1) - out_at
    total_high = jnp.zeros((rows, columns), F32)
    total_low = jnp.zeros((rows, columns), F32)
    for c in range(5):
        source = jnp.zeros((8, columns), F32)
        for b in range(5):
            column_of = jnp.zeros((8, columns), F32)
            for a in range(5):
                column_of = jnp.where(sub == a, kernel[a, b, c], column_of)
            source = jnp.where(block == b, column_of, source)
        source = jnp.concatenate([source, jnp.zeros((120, columns), F32)], axis=0)
        high, low = split(source)
        fits = entry == c
        total_high = jnp.where(fits, dot(chosen, high), total_high)
        total_low = jnp.where(fits, dot(chosen, low), total_low)
    return total_high.astype(BF16), total_low.astype(BF16)


def bands_kernel(bands, *refs):
    kernels, outs = refs[: len(bands)], refs[len(bands) :]
    for n, (kernel, band) in enumerate(zip(kernels, bands)):
        high, low = build_bands(kernel, band)
        outs[2 * n][...] = high
        outs[2 * n + 1][...] = low


def green_kernel(factors, packed, green, rise, framed, block_high, block_low):
    index, sizes = place()
    row, lane = iota((64, 128), 0), iota((64, 128), 1)
    delta_x = (lane // 8).astype(F32)
    delta_z = (4 * index[2] - 1 + lane % 8 - row).astype(F32)
    plain = delta_z * delta_z + (1.0 + delta_x * delta_x)
    for apart in range(18):
        high, low = split(0.0625 * lax.rsqrt(plain + float(apart * apart)))
        block_high[apart] = high
        block_low[apart] = low
    for ty in range(SPAN_4):
        columns = slice(128 * ty, 128 * ty + 128)
        lows = slice(128 * (SPAN_4 + ty), 128 * (SPAN_4 + ty) + 128)
        for sy in range(16):
            apart = jnp.abs(4 * index[1] - 1 + ty - sy)
            first = sy % 8 * 128 + sy // 8 * 64
            green[first : first + 64, columns] = block_high[apart]
            green[first : first + 64, lows] = block_low[apart]
    variant = [
        jnp.where(index[d] == 0, 1, 0) + jnp.where(index[d] == sizes[d] - 1, 2, 0) for d in range(3)
    ]
    factor_x, factor_y = factors[variant[0]], factors[4 + variant[1]]
    kept = as_rows(factor_x[:, None, :] * factor_y[None, :, :])
    high, low = split(kept)
    rise[:, 0:128] = (high.astype(F32) + roll(low.astype(F32), 64)).astype(BF16)
    rise[:, 128:256] = high
    framed[:, 0:2, :] = jnp.zeros((32, 2, 128), F32)
    framed[:, 34:40, :] = jnp.zeros((32, 6, 128), F32)
    framed[:, 2:34, :] = packed[...]


def prolong_rows(source, target, count, whole):
    size = target.shape[1] // 2
    q0 = source[:, 0:size, :]
    q1 = source[:, 1 : size + 1, :]
    q2 = source[:, 2 : size + 2, :]
    even = 0.75 * q1 + 0.125 * (q0 + q2)
    odd = 0.5 * (q0 + q1) if whole else 0.5 * (q1 + q2)
    target[:, pl.ds(1 if whole else 0, size, stride=2), :] = even
    target[:, pl.ds(0 if whole else 1, size, stride=2), :] = odd


def prolong_plane(read, p, whole):
    half = p // 2
    if (p % 2 == 1) == whole:
        return 0.75 * read(half + 1) + 0.125 * (read(half) + read(half + 2))
    first = half if whole else half + 1
    return 0.5 * (read(first) + read(first + 1))


def near_kernel(
    wide, from_low, from_high, b1h, b1l, b2h, b2l, b3h, b3l, prol_2, prol_1,
    out,
    near_1, near_2, near_3, tall_3, tall_3y, tall_2, tall_2y,
):
    where = place()
    index, sizes = where
    low_faces = unpack_z(jnp.where(index[2] == 0, 0.0, from_low[0:64, :]))
    high_faces = unpack_z(jnp.where(index[2] == sizes[2] - 1, 0.0, from_high[0:64, :]))

    def halo(x, level, count, low_at, high_at):
        low = roll(low_faces[level], low_at - count * x)
        high = roll(high_faces[level], high_at - count * x)
        return lanes_of(low, low_at, 5 * count) + lanes_of(high, high_at, 5 * count)

    planes = [lanes_of(wide[x, 0:16, :], THI, 11) for x in range(15)]
    left = []
    for x in range(SPAN_3):
        main = taps([(1.0, roll(planes[x + a], 11 * a - THI)) for a in range(5)])
        left.append(main + halo(x, 2, 5, 64, 96))
    left = jnp.concatenate(left, axis=0)
    near_3[...] = jnp.zeros_like(near_3)
    near_3[:, 0:16, :] = dot_split(left, b3h[...], b3l[...]).reshape(SPAN_3, 16, 128)
    third = taps([(1.0, roll(near_3[:, b : b + 16, :], -16 * b)) for b in range(5)])
    third = jnp.where(inside_mask(third.shape, SPAN_3, 9, where), third, 0.0)
    tall_3[...] = jnp.zeros_like(tall_3)
    tall_3[:, 0:16, :] = dot_exact(as_rows(third), prol_2[...]).reshape(SPAN_3, 16, 128)
    prolong_rows(tall_3, tall_3y, SPAN_2, True)

    planes = [lanes_of(wide[x, 0:24, :], SEC, 18) for x in range(22)]
    left_a, left_b = [], []
    for x in range(SPAN_2):
        left_a.append(taps([(1.0, roll(planes[x + a], 18 * a - SEC)) for a in range(5)]))
        left_b.append(halo(x, 1, 4, 0, 32))
    left = jnp.concatenate(
        [jnp.concatenate(left_a, axis=0), jnp.concatenate(left_b, axis=0)], axis=1
    )
    near_2[...] = jnp.zeros_like(near_2)
    near_2[:, 0:24, :] = dot_split(left, b2h[...], b2l[...]).reshape(SPAN_2, 24, 128)
    second = taps([(1.0, roll(near_2[:, b : b + 24, :], -24 * b)) for b in range(5)])
    raised = jnp.stack(
        [prolong_plane(lambda x: tall_3y[x], p, True) for p in range(SPAN_2)], axis=0
    )
    second = jnp.where(inside_mask(second.shape, SPAN_2, 17, where), second + raised, 0.0)
    tall_2[...] = jnp.zeros_like(tall_2)
    tall_2[:, 0:24, :] = dot_exact(as_rows(second), prol_1[...]).reshape(SPAN_2, 24, 128)
    prolong_rows(tall_2, tall_2y, 32, False)

    planes = [lanes_of(wide[x], 0, 32) for x in range(36)]
    left_a, left_b = [], []
    for x in range(32):
        left_a.append(taps([(1.0, roll(planes[x + a], 32 * a)) for a in range(4)]))
        left_b.append(planes[x + 4] + halo(x, 0, 2, 32, 64))
    left = jnp.concatenate(
        [jnp.concatenate(left_a, axis=0), jnp.concatenate(left_b, axis=0)], axis=1
    )
    near_1[...] = dot_split(left, b1h[...], b1l[...]).reshape(32, 40, 256)
    for x in range(32):
        first = taps(
            [(1.0, roll(near_1[x, b : b + 32, 0:128], -32 * b)) for b in range(4)]
            + [(1.0, near_1[x, 4:36, 128:256])]
        )
        out[x] = first + prolong_plane(lambda q: tall_2y[q], x, False)


def top_kernel(
    base, piece_0, piece_1, piece_2, piece_3, green, rise, qz,
    out_hbm,
    fourth, out, sems,
):
    index, sizes = place()
    lane = iota((8, 128), 1)
    ring = lax.rem(index[2], 4)
    first = 4 * (ring == 3).astype(jnp.int32) - 4 * (ring == 0).astype(jnp.int32) + 127
    sources = [lax.rem(16 * lax.rem(index[2] // 4 + step, 4) + first, 128) for step in (0, 2, 3, 1)]
    for x in range(16):
        total = None
        for piece, at in zip((piece_0, piece_1, piece_2, piece_3), sources):
            kept = lanes_of(piece[x // 6], 20 * (x % 6), 20)
            moved = pltpu.roll(kept, lax.rem(at + 128 - 20 * (x % 6), 128), 1)
            total = moved if total is None else total + moved
        total = total + roll(total, 64)
        fourth[x] = jnp.where(lane < 64, total[0:8], total[8:16])
    width = 128 * SPAN_4
    total = jnp.zeros((32, 2 * width), F32)
    for s in range(0, 8, 2):
        left = jnp.concatenate([fourth[:, s, :], fourth[:, s + 1, :]], axis=1)
        high, low = split(left)
        rows = slice(128 * s, 128 * s + 256)
        total = total + dot(jnp.concatenate([high, low], axis=0), green[rows, :])
    sums = total[0:16, :width] + (total[16:32, :width] + total[0:16, width:])
    row, lane = iota((16, 128), 0), iota((16, 128), 1)
    tops = []
    for tx in range(SPAN_4):
        keep = jnp.abs(4 * index[0] - 1 + tx - row) == lane // 8
        for ty in range(SPAN_4):
            picked = jnp.where(keep, sums[:, 128 * ty : 128 * ty + 128], 0.0)
            tops.append(jnp.sum(picked, axis=0, keepdims=True))
        tops.append(jnp.zeros((1, 128), F32))
    tops = jnp.concatenate(tops + [jnp.zeros((8, 128), F32)], axis=0)
    variant = jnp.where(index[2] == 0, 1, 0) + jnp.where(index[2] == sizes[2] - 1, 2, 0)
    high, low = split(dot_split(tops, qz[variant], qz[4 + variant]))
    right = jnp.concatenate([high, high, low, jnp.zeros_like(low)], axis=0)
    copies = []
    for part in range(4):
        planes = slice(8 * part, 8 * part + 8)
        far = dot(rise[256 * part : 256 * part + 256, :], right)
        out[planes] = (base[planes] + far.reshape(8, 32, 128))[:, :, 0:32]
        copies.append(pltpu.make_async_copy(out.at[planes], out_hbm.at[planes], sems.at[part]))
        copies[-1].start()
    for copy in copies:
        copy.wait()


def call(kernel, outs, ins, scratch=(), megabytes=16, spaces=None, out_spaces=None, aliases=None, flops=1000000):
    spaces, out_spaces = spaces or {}, out_spaces or {}
    single = not isinstance(outs, tuple)
    out_specs = [out_spaces.get(i, VMEM) for i in range(1 if single else len(outs))]
    return pl.pallas_call(
        kernel,
        out_shape=outs,
        in_specs=[spaces.get(i, VMEM) for i in range(len(ins))],
        out_specs=out_specs[0] if single else out_specs,
        scratch_shapes=list(scratch),
        input_output_aliases=aliases or {},
        compiler_params=pltpu.CompilerParams(vmem_limit_bytes=int(megabytes * 2**20)),
        cost_estimate=pl.CostEstimate(flops=flops, bytes_accessed=2**21, transcendentals=0),
    )(*ins)


def shape(*dims, dtype=F32):
    return jax.ShapeDtypeStruct(dims, dtype)


def exchange(values, axis, steps):
    size = lax.axis_size(axis)
    return [
        lax.ppermute(value, axis, [(i, i ^ step) for i in range(size)])
        for value, step in zip(values, steps)
    ]


def turn(value, by):
    size_y, size_z = lax.axis_size("gy"), lax.axis_size("gz")
    half = size_y // 2
    pairs = []
    for core in range(half):
        ring = [(high * half + core) * size_z + z for high in range(2) for z in range(size_z)]
        pairs += [(ring[n], ring[(n + by) % len(ring)]) for n in range(len(ring))]
    return lax.ppermute(value, ("gy", "gz"), pairs)


def banded(bands, *kernels, flops=10**9):
    return call(
        functools.partial(bands_kernel, bands),
        tuple(shape(band[0], band[1], dtype=BF16) for band in bands for _ in range(2)),
        kernels,
        spaces={n: SMEM for n in range(len(kernels))},
        flops=flops,
    )


def shards(charges, counts, slots, spline, kernel_fine, kernel_mid, kernel_coarse):
    cells = charges.shape[0]
    packed, raw, face = call(
        deposit_kernel,
        (shape(32, 32, 128), shape(8, 128), shape(2 * FACE + 8, 128)),
        (256 * slots + counts, charges, spline.reshape(cells * 12, ATOMS)),
        (
            pltpu.VMEM((32, 32, 128), F32),
            pltpu.VMEM((cells, ATOMS), F32),
            pltpu.VMEM((cells * 12, 128), BF16),
            pltpu.VMEM((cells * 12, 128), F32),
            pltpu.VMEM((64, cells), F32),
            pltpu.VMEM((32, 32, 128), F32),
            pltpu.VMEM((SPAN_2, 56, 128), F32),
            pltpu.VMEM((SPAN_3, 40, 128), F32),
            pltpu.VMEM((SPAN_4, 24, 128), F32),
            pltpu.SemaphoreType.DMA((5,)),
        ),
        spaces={1: HBM, 2: HBM},
        out_spaces={0: ANY},
        megabytes=53.75,
    )
    (got_1,) = exchange((face,), "gy", (1,))
    relay = call(relay_kernel, shape(FACE + 8, 128), (raw, got_1))
    (got_2,) = exchange((relay,), "gy", (2,))
    qx, qy, qz = composites()
    qz_high = qz.astype(BF16)
    qz_low = (qz - qz_high.astype(np.float32)).astype(BF16)
    green, rise, framed = call(
        green_kernel,
        (
            shape(1024, 256 * SPAN_4, dtype=BF16),
            shape(1024, 256, dtype=BF16),
            shape(32, 40, 128),
        ),
        (jnp.asarray(np.concatenate([qx, qy])), packed),
        (pltpu.VMEM((18, 64, 128), BF16), pltpu.VMEM((18, 64, 128), BF16)),
    )
    wide_y, raw, face_1, face_3 = call(
        widen_y_kernel,
        (shape(32, 40, 128), shape(8, 128), shape(72, 128), shape(72, 128)),
        (framed, relay, got_1, got_2, rise),
        spaces={4: ANY},
        aliases={0: 0},
    )
    got_3, got_1, got_2 = exchange((face_3, face_1, raw), "gx", (3, 1, 2))
    bands_1 = banded(BANDS[:1], kernel_fine)
    own_high, own_low = call(
        own_z_kernel, (shape(80, 128), shape(80, 128)), (wide_y, bands_1[0]), spaces={1: ANY}
    )
    wide_x = call(
        widen_x_kernel, shape(36, 40, 128), (wide_y, got_2, got_1, got_3), spaces={1: ANY}
    )
    raw, to_high, to_low = call(
        edge_x_kernel,
        (shape(16, 128), shape(80, 128), shape(80, 128)),
        (raw, got_2, got_1, got_3, own_high, own_low),
    )
    from_low, from_high = turn(to_high, 1), turn(to_low, -1)
    (got_2,) = exchange((raw,), "gz", (2,))
    bands_2 = banded(BANDS[1:], kernel_mid, kernel_coarse)
    window = call(
        window_kernel,
        shape(3, 16, 128),
        (raw, got_2, from_low, from_high, bands_2[0], wide_x),
        spaces={4: ANY, 5: ANY},
    )
    pieces = [window] + [turn(window, by) for by in (8, 4, -4)]
    base = call(
        near_kernel,
        shape(32, 32, 128),
        (wide_x, from_low, from_high, *bands_1, *bands_2, jnp.asarray(PROL_2, BF16), jnp.asarray(PROL_1, BF16)),
        (
            pltpu.VMEM((32, 40, 256), F32),
            pltpu.VMEM((SPAN_2, 32, 128), F32),
            pltpu.VMEM((SPAN_3, 24, 128), F32),
            pltpu.VMEM((SPAN_3, 24, 128), F32),
            pltpu.VMEM((SPAN_3, 24, 128), F32),
            pltpu.VMEM((SPAN_2, 32, 128), F32),
            pltpu.VMEM((SPAN_2, 32, 128), F32),
        ),
    )
    return call(
        top_kernel,
        shape(32, 32, 32),
        (base, *pieces, green, rise, jnp.asarray(np.concatenate([qz_high, qz_low]))),
        (
            pltpu.VMEM((16, 8, 128), F32),
            pltpu.VMEM((32, 32, 32), F32),
            pltpu.SemaphoreType.DMA((4,)),
        ),
        out_spaces={0: ANY},
    )


def solution(mesh):
    return jax.shard_map(
        shards,
        mesh=mesh,
        in_specs=(
            P(("gx", "gy", "gz"), None),
            P(("gx", "gy", "gz")),
            P(("gx", "gy", "gz")),
            P(("gx", "gy", "gz"), None, None, None),
            P(),
            P(),
            P(),
        ),
        out_specs=P("gx", "gy", "gz"),
        check_vma=False,
    )
```

```python
import functools

import jax
import jax.numpy as jnp
import numpy as np
from jax import lax
from jax.experimental import pallas as pl
from jax.experimental.pallas import tpu as pltpu
from jax.sharding import PartitionSpec as P

W = (0.125, 0.5, 0.75, 0.5, 0.125)
F32 = jnp.float32
BF16 = jnp.bfloat16
CELLS = 384
ATOMS = 128
SPAN_2 = 18
SPAN_3 = 11
SPAN_4 = 7
SEC = 32
THI = 64
VMEM = pl.BlockSpec(memory_space=pltpu.VMEM)
SMEM = pl.BlockSpec(memory_space=pltpu.SMEM)
HBM = pl.BlockSpec(memory_space=pltpu.HBM)
ANY = pl.BlockSpec(memory_space=pl.ANY)


def weight(t):
    return W[t] if 0 <= t <= 4 else 0.0


def table(rows, columns, offset, turned):
    out = np.zeros((128, 128), np.float32)
    for r in range(rows):
        for c in range(columns):
            out[r, c] = weight(c - 2 * r + offset if turned else r - 2 * c + offset)
    return out


PROL_2 = table(SPAN_3, SPAN_2, 3, True)
PROL_1 = table(SPAN_2, 32, 4, True)


BANDS = (
    (256, 256, ((0, 32, 2), (160, 2, 0), (192, 2, 34)), 32, 32),
    (256, 128, ((0, 18, 2), (128, 4, 0), (160, 4, 18)), 24, 18),
    (128, 128, ((0, 11, 2), (64, 5, 0), (96, 5, 10)), 16, 11),
)
DIVIDE = {32: (1, 5), 2: (1, 1), 18: (57, 10), 4: (1, 2), 11: (94, 10), 5: (52, 8), 24: (43, 10), 16: (1, 4)}


def composite(first, last):
    p3 = np.array([[weight(i - 2 * j + 3) for j in range(7)] for i in range(11)])
    p2 = np.array([[weight(i - 2 * j + 3) for j in range(11)] for i in range(18)])
    p1 = np.array([[weight(i - 2 * j + 4) for j in range(18)] for i in range(32)])
    m4, m3, m2 = np.ones(7), np.ones(11), np.ones(18)
    if first:
        m4[0] = m3[0] = m2[0] = 0
    if last:
        m4[5:] = 0
        m3[9:] = 0
        m2[17:] = 0
    return (p1 * m2) @ (p2 * m3) @ (p3 * m4)


def composites():
    qx = np.zeros((4, 32, 128), np.float32)
    qy = np.zeros((4, 32, 128), np.float32)
    qz = np.zeros((4, 128, 128), np.float32)
    for v in range(4):
        q = composite(v % 2 == 1, v >= 2)
        for lane in range(64):
            if lane // 8 < 7 and lane % 8 < 7:
                qx[v, :, lane] = q[:, lane // 8]
                qy[v, :, lane] = q[:, lane % 8]
        for row in range(128):
            if row % 8 < 7:
                qz[v, row, :32] = q[:, row % 8]
    return qx, qy, qz


def split(x):
    high = x.astype(BF16)
    return high, (x - high.astype(F32)).astype(BF16)


def dot(a, b):
    return jnp.dot(a, b, preferred_element_type=F32)


def dot_exact(x, right):
    high, low = split(x)
    return dot(high, right) + dot(low, right)


def dot_split(x, right_high, right_low):
    high, low = split(x)
    return dot(high, right_high) + (dot(low, right_high) + dot(high, right_low))


def iota(shape, dim):
    return lax.broadcasted_iota(jnp.int32, shape, dim)


def roll(x, shift, axis=None):
    axis = x.ndim - 1 if axis is None else axis
    shift = shift % x.shape[axis]
    return x if shift == 0 else pltpu.roll(x, shift, axis)


def lanes_of(x, low, count):
    lane = iota(x.shape, x.ndim - 1)
    return jnp.where((lane >= low) & (lane < low + count), x, 0.0)


def as_rows(x):
    return x.reshape(x.shape[0] * x.shape[1], x.shape[2])


def taps(pieces):
    total = None
    for factor, value in pieces:
        term = value if factor == 1.0 else factor * value
        total = term if total is None else total + term
    return total


def restrict_planes(read, span, size, offset):
    planes = []
    for p in range(span):
        planes.append(
            taps([(W[t], read(2 * p + t - offset)) for t in range(5) if 0 <= 2 * p + t - offset < size])
        )
    return planes


def place():
    sizes = [lax.axis_size(a) for a in ("gx", "gy", "gz")]
    index = [lax.axis_index(a) for a in ("gx", "gy", "gz")]
    return index, sizes


def inside_mask(shape, spans, high, place_of):
    index, sizes = place_of
    keep = None
    for dim in range(3):
        at = iota(shape, dim)
        low = jnp.where(index[dim] == 0, 1, 0)
        top = jnp.where(index[dim] == sizes[dim] - 1, high, spans)
        part = (at >= low) & (at < top)
        keep = part if keep is None else keep & part
    return keep


def nearest(index):
    even = lax.rem(index, 2) == 0
    return even, index == 1, index == 2


def deposit_kernel(
    codes, charges_hbm, spline_hbm,
    packed_hbm, raw_out, face,
    packed, charges, spline, wide, patch, fine, buf_2, buf_3, buf_4, sems,
):
    where = place()
    index, sizes = where
    part = CELLS * 12 // 3
    copies = [pltpu.make_async_copy(charges_hbm, charges, sems.at[3])]
    for chunk in range(3):
        rows = slice(part * chunk, part * chunk + part)
        copies.append(
            pltpu.make_async_copy(spline_hbm.at[rows, :], spline.at[rows, :], sems.at[chunk])
        )
    for copy in copies:
        copy.start()
    buf_2[...] = jnp.zeros_like(buf_2)
    buf_3[...] = jnp.zeros_like(buf_3)
    buf_4[...] = jnp.zeros_like(buf_4)
    row, column = iota((512, 64), 0), iota((512, 64), 1)
    spread = (row // 32 * 4 + row % 4 == column).astype(F32).astype(BF16)
    row, column = iota((128, 128), 0), iota((128, 128), 1)

    def restriction(rows, columns, offset):
        t = row - 2 * column + offset
        out = jnp.zeros((128, 128), F32)
        for tap in range(5):
            out = jnp.where(t == tap, W[tap], out)
        return jnp.where((row < rows) & (column < columns), out, 0.0).astype(BF16)

    rest_2 = restriction(32, SPAN_2, 4)
    rest_3 = restriction(SPAN_2, SPAN_3, 3)
    rest_4 = restriction(SPAN_3, SPAN_4, 3)
    slot = lax.shift_right_logical(codes[...].reshape(1, CELLS), 8)
    fits = (iota((512, CELLS), 0) // 4 % 8) == slot % 8
    hot = (iota((64, CELLS), 0) == slot // 8).astype(F32).astype(BF16)
    copies[0].wait()
    alive = iota((ATOMS, CELLS), 0) < (codes[...].reshape(1, CELLS) & 255)
    weighted = jnp.where(alive, charges[...].T, 0.0)
    for chunk in range(CELLS // 128):
        lanes = slice(128 * chunk, 128 * chunk + 128)
        copies[1 + chunk].wait()
        rows = slice(part * chunk, part * chunk + part)
        wide[rows, :] = spline[rows, :].astype(F32)

        def column_of(d, i):
            return wide[pl.ds(chunk * part + 4 * d + i, 128, stride=12), :].T

        charge = weighted[:, lanes]
        depth = [charge * column_of(2, k) for k in range(4)]
        ys = [column_of(1, j) for j in range(4)]
        for i in range(4):
            xs = column_of(0, i)
            for j in range(4):
                cross = xs * ys[j]
                for k in range(4):
                    patch[16 * i + 4 * j + k : 16 * i + 4 * j + k + 1, lanes] = jnp.sum(
                        cross * depth[k], axis=0, keepdims=True
                    )
    high, low = split(patch[...])
    spread_high = jnp.where(fits, dot(spread, high), 0.0).astype(BF16)
    spread_low = jnp.where(fits, dot(spread, low), 0.0).astype(BF16)
    nt = (((1,), (1,)), ((), ()))
    placed = lax.dot_general(hot, spread_high, nt, preferred_element_type=F32) + lax.dot_general(
        hot, spread_low, nt, preferred_element_type=F32
    )
    for i in range(4):
        for j in range(4):
            rows = lanes_of(roll(placed[:, 128 * i : 128 * i + 128], -32 * j), 0, 32)
            for sx in range(8):
                fine[4 * sx + i, pl.ds(j, 8, stride=4), :] = rows[8 * sx : 8 * sx + 8]

    for p, plane in enumerate(restrict_planes(lambda x: fine[x], SPAN_2, 32, 4)):
        buf_2[p, 4:36, :] = plane
    second = taps([(W[t], buf_2[:, pl.ds(t, 24, stride=2), :]) for t in range(5)])
    second = dot_exact(as_rows(second), rest_2).reshape(SPAN_2, 24, 128)
    second = jnp.where(inside_mask(second.shape, SPAN_2, 17, where), second, 0.0)
    for p, plane in enumerate(restrict_planes(lambda x: second[x], SPAN_3, SPAN_2, 3)):
        buf_3[p, 3:27, :] = plane
    third = taps([(W[t], buf_3[:, pl.ds(t, 16, stride=2), :]) for t in range(5)])
    third = dot_exact(as_rows(third), rest_3).reshape(SPAN_3, 16, 128)
    third = jnp.where(inside_mask(third.shape, SPAN_3, 9, where), third, 0.0)
    packed[...] = fine[...]
    packed[0:SPAN_2, 0:24, :] += roll(second, SEC)
    packed[0:SPAN_3, 0:16, :] += roll(third, THI)
    leave = pltpu.make_async_copy(packed, packed_hbm, sems.at[4])
    leave.start()
    for p, plane in enumerate(restrict_planes(lambda x: third[x], SPAN_4, SPAN_3, 3)):
        buf_4[p, 3:19, :] = plane
    last = taps([(W[t], buf_4[:, pl.ds(t, 8, stride=2), :]) for t in range(5)])
    last = dot_exact(as_rows(last), rest_4).reshape(SPAN_4, 8, 128)
    last = jnp.where(inside_mask(last.shape, SPAN_4, 5, where), last, 0.0)
    raw = taps([(1.0, roll(last[x], 8 * x)) for x in range(SPAN_4)])
    raw_out[...] = raw

    even, _, _ = nearest(index[1])
    low = pack_y(packed, FIRST_ROWS)
    high = pack_y(packed, LAST_ROWS)
    for v in range(4):
        face[8 * v : 8 * v + 8, :] = jnp.where(even, high[v], low[v])
        face[FACE + 8 * v : FACE + 8 * v + 8, :] = jnp.where(even, low[v], high[v])
    face[2 * FACE : 2 * FACE + 8, :] = raw
    leave.wait()


def spot_1(p):
    return p // 16, p % 16 // 4 * 2, p % 4 * 32


def spot_2(p):
    return 2 + p // 14, p % 14 // 7 * 4, p % 7 * 18


def spot_3(p):
    return 3, 4, p * 11


def spot_4(p):
    return 3, p // 5, 72 + p % 5 * 11


FACE = 32
LEVELS = (
    (32, 2, 0, 32, spot_1),
    (SPAN_2, 4, SEC, 18, spot_2),
    (SPAN_3, 4, THI, 11, spot_3),
    (SPAN_3, 1, THI, 11, spot_4),
)
FIRST_ROWS = (0, 0, 0, 4)
LAST_ROWS = (30, 14, 6, 10)
ROWS_ABOVE = (34, 18, 10, 14)


def pack_y(source, at):
    tiles = [jnp.zeros((8, 128), F32) for _ in range(4)]
    row, at_lane = iota((8, 128), 0), iota((8, 128), 1)
    for (planes, count, lane, width, spot), start in zip(LEVELS, at):
        for p in range(planes):
            v, r, to = spot(p)
            if start == 30:
                slab = roll(source[p, 24:32, :], r - 6, 0)
            else:
                slab = roll(source[p, start : start + 8, :], r, 0)
            slab = roll(slab, to - lane)
            keep = (row >= r) & (row < r + count) & (at_lane >= to) & (at_lane < to + width)
            tiles[v] = jnp.where(keep, slab, tiles[v])
    return tiles


def place_y(tile, index):
    tall = jnp.concatenate([tile, jnp.zeros((8, 128), F32)], axis=0)
    tall = pltpu.roll(tall, lax.rem(4 * index + 15, 16), 0)
    return tall[0:8] + roll(tall[8:16], 64)


def relay_kernel(raw, got, out):
    index, _ = place()
    out[0:FACE, :] = got[FACE : 2 * FACE, :]
    partner = jnp.bitwise_xor(index[1], 1)
    other = got[2 * FACE : 2 * FACE + 8, :]
    out[FACE : FACE + 8, :] = place_y(raw[...], index[1]) + place_y(other, partner)


def widen_y_kernel(framed, own, got_1, got_2, after, out, raw_out, face_1, face_3):
    index, _ = place()
    even, one, two = nearest(index[1])
    total = own[FACE : FACE + 8, :] + got_2[FACE : FACE + 8, :]
    raw_out[...] = total
    a, b = got_1[0:FACE, :], got_2[0:FACE, :]
    low = jnp.where(even, 0.0, a) + jnp.where(two, b, 0.0)
    high = jnp.where(even, a, 0.0) + jnp.where(one, b, 0.0)
    for face, at in ((low, FIRST_ROWS), (high, ROWS_ABOVE)):
        for (planes, count, lane, width, spot), start in zip(LEVELS, at):
            for p in range(planes):
                v, r, to = spot(p)
                slab = roll(roll(face[8 * v : 8 * v + 8], -r, 0), lane - to)
                slab = lanes_of(slab, lane, width)
                out[p, start : start + count, :] += slab[0:count]
    even, one, _ = nearest(index[0])
    for ref, to_high in ((face_1, even), (face_3, one)):
        f = jnp.where(to_high, 30, 0)
        s = jnp.where(to_high, 14, 0)
        t = jnp.where(to_high, 6, 0)
        ref[0:40, :] = lanes_of(out[f], 0, 32) + lanes_of(roll(out[f + 1], 32), 32, 32)
        ref[0:16, :] += taps(
            [(1.0, lanes_of(roll(out[t + k, 0:16, :], 11 * k), THI + 11 * k, 11)) for k in range(5)]
        )
        ref[40:64, :] = taps(
            [(1.0, lanes_of(roll(out[s + k, 0:24, :], 18 * k - SEC), 18 * k, 18)) for k in range(4)]
        )
        ref[64:72, :] = total


def x_faces(index, got_1, got_3):
    even, one, two = nearest(index)
    a, b = got_1[0:64, :], got_3[0:64, :]
    low = jnp.where(even, 0.0, a) + jnp.where(two, b, 0.0)
    high = jnp.where(even, a, 0.0) + jnp.where(one, b, 0.0)
    planes = []
    for face, at in ((low, (0, 0, 0)), (high, (34, 18, 10))):
        for k in range(2):
            planes.append((0, at[0] + k, lanes_of(roll(face[0:40], -32 * k), 0, 32)))
        for k in range(4):
            planes.append((1, at[1] + k, lanes_of(roll(face[40:64], -18 * k), 0, 18)))
        for k in range(5):
            planes.append((2, at[2] + k, lanes_of(roll(face[0:16], -THI - 11 * k), 0, 11)))
    return planes


def widen_x_kernel(wide_y, after, got_1, got_3, out):
    index, _ = place()
    out[0:2] = jnp.zeros((2, 40, 128), F32)
    out[34:36] = jnp.zeros((2, 40, 128), F32)
    out[2:34] = wide_y[...]
    for level, at, values in x_faces(index[0], got_1, got_3):
        rows = values.shape[0]
        out[at, 0:rows, :] += roll(values, (0, SEC, THI)[level])


Z_LEVELS = ((40, 2, 0, 30), (24, 4, SEC, 14), (16, 5, THI, 6))


def chosen_lanes(values, first, count):
    at = iota(values.shape, 1)
    return jnp.where((at >= first) & (at < first + count), values, 0.0)


def own_z_kernel(wide_y, after, high, low):
    for ref, to_high in ((high, True), (low, False)):
        start = 0
        for (rows, count, lane, top), planes in zip(Z_LEVELS, (32, SPAN_2, SPAN_3)):
            first = lane + top if to_high else lane
            total = jnp.zeros((rows, 128), F32)
            for x in range(planes):
                kept = chosen_lanes(wide_y[x, 0:rows, :], first, count)
                total = total + roll(kept, count * (x + 2) - first)
            ref[start : start + rows, :] = total
            start += rows


def edge_x_kernel(own, got_2, got_1, got_3, high, low, raw_out, to_high, to_low):
    index, _ = place()
    total = None
    lane = iota((16, 128), 1)
    for step, tile in ((0, own[...]), (1, got_1[64:72, :]), (2, got_2[...]), (3, got_3[64:72, :])):
        tall = jnp.concatenate([tile, roll(tile, 64)], axis=0)
        tall = jnp.where(lane < 64, tall, 0.0)
        at = lax.rem(32 * jnp.bitwise_xor(index[0], step) + 120, 128)
        moved = pltpu.roll(tall, at, 1)
        total = moved if total is None else total + moved
    raw_out[...] = total
    planes = x_faces(index[0], got_1, got_3)
    for face, own_face, is_high in ((to_high, high, True), (to_low, low, False)):
        sums = [own_face[0:40, :], own_face[40:64, :], own_face[64:80, :]]
        for level, at, values in planes:
            _, count, _, top = Z_LEVELS[level]
            first = top if is_high else 0
            kept = chosen_lanes(values, first, count)
            sums[level] = sums[level] + roll(kept, count * at - first)
        face[0:40, :] = sums[0]
        face[40:64, :] = sums[1]
        face[0:16, :] += lanes_of(roll(sums[2], 72), 72, 55)
        face[40:56, :] += lanes_of(roll(sums[2], 88 - 55), 88, 20)
        face[64:80, :] = total


def unpack_z(message):
    third = lanes_of(roll(message[0:16], -72), 0, 55) + lanes_of(roll(message[40:56], 55 - 88), 55, 20)
    return message[0:40], message[40:64], third


def window_kernel(own, got_2, from_low, from_high, after_1, after_2, out):
    index, _ = place()
    early = lax.rem(index[2], 4) < 2
    ends = got_2[...]
    first, second, third = from_low[64:80, :], own[...], from_high[64:80, :]
    pieces = (
        jnp.where(early, first, ends),
        jnp.where(early, second, first),
        jnp.where(early, third, second),
        jnp.where(early, ends, third),
    )
    for group in range(3):
        total = None
        for q in range(min(6, 16 - 6 * group)):
            for d, piece in enumerate(pieces):
                to = 20 * q + 4 * d
                moved = lanes_of(roll(piece, to - 48 * group - 8 * q), to, 8)
                total = moved if total is None else total + moved
        out[group] = total


def divided(n, d):
    factor, bits = DIVIDE[d]
    return lax.shift_right_logical(n * factor, bits)


def build_bands(kernel, band):
    rows, columns, runs, group, outs = band
    row = iota((rows, 128), 0)
    shift = jnp.full((rows, 128), 99, jnp.int32)
    point = jnp.full((rows, 128), 99, jnp.int32)
    for start, count, offset in runs:
        at = row - start
        a = divided(at, count)
        inside = (at >= 0) & (at < 5 * count)
        shift = jnp.where(inside, a, shift)
        point = jnp.where(inside, offset + at - a * count, point)
    chosen = (shift == iota((rows, 128), 1)).astype(F32).astype(BF16)
    column = iota((8, columns), 1)
    block = divided(column, group)
    out_at = (column - block * group)[0:1]
    block = jnp.where((column - block * group) < outs, block, 9)
    sub = iota((8, columns), 0)
    entry = jnp.concatenate([point] * (columns // 128), axis=1) - out_at
    total_high = jnp.zeros((rows, columns), F32)
    total_low = jnp.zeros((rows, columns), F32)
    for c in range(5):
        source = jnp.zeros((8, columns), F32)
        for b in range(5):
            column_of = jnp.zeros((8, columns), F32)
            for a in range(5):
                column_of = jnp.where(sub == a, kernel[a, b, c], column_of)
            source = jnp.where(block == b, column_of, source)
        source = jnp.concatenate([source, jnp.zeros((120, columns), F32)], axis=0)
        high, low = split(source)
        fits = entry == c
        total_high = jnp.where(fits, dot(chosen, high), total_high)
        total_low = jnp.where(fits, dot(chosen, low), total_low)
    return total_high.astype(BF16), total_low.astype(BF16)


def bands_kernel(bands, *refs):
    kernels, outs = refs[: len(bands)], refs[len(bands) :]
    for n, (kernel, band) in enumerate(zip(kernels, bands)):
        high, low = build_bands(kernel, band)
        outs[2 * n][...] = high
        outs[2 * n + 1][...] = low


def green_kernel(factors, packed, green_high, green_low, rise, framed, block_high, block_low):
    index, sizes = place()
    row, lane = iota((64, 128), 0), iota((64, 128), 1)
    delta_x = (lane // 8).astype(F32)
    delta_z = (4 * index[2] - 1 + lane % 8 - row).astype(F32)
    plain = delta_z * delta_z + (1.0 + delta_x * delta_x)
    for apart in range(18):
        high, low = split(0.0625 * lax.rsqrt(plain + float(apart * apart)))
        block_high[apart] = high
        block_low[apart] = low
    for ty in range(SPAN_4):
        columns = slice(128 * ty, 128 * ty + 128)
        for sy in range(16):
            apart = jnp.abs(4 * index[1] - 1 + ty - sy)
            first = sy % 8 * 128 + sy // 8 * 64
            green_high[first : first + 64, columns] = block_high[apart]
            green_low[first : first + 64, columns] = block_low[apart]
    variant = [
        jnp.where(index[d] == 0, 1, 0) + jnp.where(index[d] == sizes[d] - 1, 2, 0) for d in range(3)
    ]
    factor_x, factor_y = factors[variant[0]], factors[4 + variant[1]]
    kept = as_rows(factor_x[:, None, :] * factor_y[None, :, :])
    high, low = split(kept)
    rise[:, 0:128] = (high.astype(F32) + roll(low.astype(F32), 64)).astype(BF16)
    rise[:, 128:256] = high
    framed[:, 0:2, :] = jnp.zeros((32, 2, 128), F32)
    framed[:, 34:40, :] = jnp.zeros((32, 6, 128), F32)
    framed[:, 2:34, :] = packed[...]


def prolong_rows(source, target, count, whole):
    size = target.shape[1] // 2
    q0 = source[:, 0:size, :]
    q1 = source[:, 1 : size + 1, :]
    q2 = source[:, 2 : size + 2, :]
    even = 0.75 * q1 + 0.125 * (q0 + q2)
    odd = 0.5 * (q0 + q1) if whole else 0.5 * (q1 + q2)
    target[:, pl.ds(1 if whole else 0, size, stride=2), :] = even
    target[:, pl.ds(0 if whole else 1, size, stride=2), :] = odd


def prolong_plane(read, p, whole):
    half = p // 2
    if (p % 2 == 1) == whole:
        return 0.75 * read(half + 1) + 0.125 * (read(half) + read(half + 2))
    first = half if whole else half + 1
    return 0.5 * (read(first) + read(first + 1))


def near_kernel(
    wide, from_low, from_high, b1h, b1l, b2h, b2l, b3h, b3l, prol_2, prol_1,
    out,
    near_1, near_2, near_3, tall_3, tall_3y, tall_2, tall_2y,
):
    where = place()
    index, sizes = where
    low_faces = unpack_z(jnp.where(index[2] == 0, 0.0, from_low[0:64, :]))
    high_faces = unpack_z(jnp.where(index[2] == sizes[2] - 1, 0.0, from_high[0:64, :]))

    def halo(x, level, count, low_at, high_at):
        low = roll(low_faces[level], low_at - count * x)
        high = roll(high_faces[level], high_at - count * x)
        return lanes_of(low, low_at, 5 * count) + lanes_of(high, high_at, 5 * count)

    planes = [lanes_of(wide[x, 0:16, :], THI, 11) for x in range(15)]
    left = []
    for x in range(SPAN_3):
        main = taps([(1.0, roll(planes[x + a], 11 * a - THI)) for a in range(5)])
        left.append(main + halo(x, 2, 5, 64, 96))
    left = jnp.concatenate(left, axis=0)
    near_3[...] = jnp.zeros_like(near_3)
    near_3[:, 0:16, :] = dot_split(left, b3h[...], b3l[...]).reshape(SPAN_3, 16, 128)
    third = taps([(1.0, roll(near_3[:, b : b + 16, :], -16 * b)) for b in range(5)])
    third = jnp.where(inside_mask(third.shape, SPAN_3, 9, where), third, 0.0)
    tall_3[...] = jnp.zeros_like(tall_3)
    tall_3[:, 0:16, :] = dot_exact(as_rows(third), prol_2[...]).reshape(SPAN_3, 16, 128)
    prolong_rows(tall_3, tall_3y, SPAN_2, True)

    planes = [lanes_of(wide[x, 0:24, :], SEC, 18) for x in range(22)]
    left_a, left_b = [], []
    for x in range(SPAN_2):
        left_a.append(taps([(1.0, roll(planes[x + a], 18 * a - SEC)) for a in range(5)]))
        left_b.append(halo(x, 1, 4, 0, 32))
    left = jnp.concatenate(
        [jnp.concatenate(left_a, axis=0), jnp.concatenate(left_b, axis=0)], axis=1
    )
    near_2[...] = jnp.zeros_like(near_2)
    near_2[:, 0:24, :] = dot_split(left, b2h[...], b2l[...]).reshape(SPAN_2, 24, 128)
    second = taps([(1.0, roll(near_2[:, b : b + 24, :], -24 * b)) for b in range(5)])
    raised = jnp.stack(
        [prolong_plane(lambda x: tall_3y[x], p, True) for p in range(SPAN_2)], axis=0
    )
    second = jnp.where(inside_mask(second.shape, SPAN_2, 17, where), second + raised, 0.0)
    tall_2[...] = jnp.zeros_like(tall_2)
    tall_2[:, 0:24, :] = dot_exact(as_rows(second), prol_1[...]).reshape(SPAN_2, 24, 128)
    prolong_rows(tall_2, tall_2y, 32, False)

    planes = [lanes_of(wide[x], 0, 32) for x in range(36)]
    left_a, left_b = [], []
    for x in range(32):
        left_a.append(taps([(1.0, roll(planes[x + a], 32 * a)) for a in range(4)]))
        left_b.append(planes[x + 4] + halo(x, 0, 2, 32, 64))
    left = jnp.concatenate(
        [jnp.concatenate(left_a, axis=0), jnp.concatenate(left_b, axis=0)], axis=1
    )
    near_1[...] = dot_split(left, b1h[...], b1l[...]).reshape(32, 40, 256)
    for x in range(32):
        first = taps(
            [(1.0, roll(near_1[x, b : b + 32, 0:128], -32 * b)) for b in range(4)]
            + [(1.0, near_1[x, 4:36, 128:256])]
        )
        out[x] = first + prolong_plane(lambda q: tall_2y[q], x, False)


def top_kernel(
    base, piece_0, piece_1, piece_2, piece_3, green_high, green_low, rise, qz,
    out_hbm,
    fourth, out, sems,
):
    index, sizes = place()
    lane = iota((8, 128), 1)
    ring = lax.rem(index[2], 4)
    first = 4 * (ring == 3).astype(jnp.int32) - 4 * (ring == 0).astype(jnp.int32) + 127
    sources = [lax.rem(16 * lax.rem(index[2] // 4 + step, 4) + first, 128) for step in (0, 2, 1, 3)]
    for x in range(16):
        total = None
        for piece, at in zip((piece_0, piece_1, piece_2, piece_3), sources):
            kept = lanes_of(piece[x // 6], 20 * (x % 6), 20)
            moved = pltpu.roll(kept, lax.rem(at + 128 - 20 * (x % 6), 128), 1)
            total = moved if total is None else total + moved
        total = total + roll(total, 64)
        fourth[x] = jnp.where(lane < 64, total[0:8], total[8:16])
    total = jnp.zeros((32, 128 * SPAN_4), F32)
    extra = jnp.zeros((16, 128 * SPAN_4), F32)
    for s in range(0, 8, 2):
        left = jnp.concatenate([fourth[:, s, :], fourth[:, s + 1, :]], axis=1)
        high, low = split(left)
        rows = slice(128 * s, 128 * s + 256)
        total = total + dot(jnp.concatenate([high, low], axis=0), green_high[rows, :])
        extra = extra + dot(high, green_low[rows, :])
    sums = total[0:16] + (total[16:32] + extra)
    row, lane = iota((16, 128), 0), iota((16, 128), 1)
    tops = []
    for tx in range(SPAN_4):
        keep = jnp.abs(4 * index[0] - 1 + tx - row) == lane // 8
        for ty in range(SPAN_4):
            picked = jnp.where(keep, sums[:, 128 * ty : 128 * ty + 128], 0.0)
            tops.append(jnp.sum(picked, axis=0, keepdims=True))
        tops.append(jnp.zeros((1, 128), F32))
    tops = jnp.concatenate(tops + [jnp.zeros((8, 128), F32)], axis=0)
    variant = jnp.where(index[2] == 0, 1, 0) + jnp.where(index[2] == sizes[2] - 1, 2, 0)
    high, low = split(dot_split(tops, qz[variant], qz[4 + variant]))
    right = jnp.concatenate([high, high, low, jnp.zeros_like(low)], axis=0)
    copies = []
    for part in range(4):
        planes = slice(8 * part, 8 * part + 8)
        far = dot(rise[256 * part : 256 * part + 256, :], right)
        out[planes] = (base[planes] + far.reshape(8, 32, 128))[:, :, 0:32]
        copies.append(pltpu.make_async_copy(out.at[planes], out_hbm.at[planes], sems.at[part]))
        copies[-1].start()
    for copy in copies:
        copy.wait()


def call(kernel, outs, ins, scratch=(), megabytes=16, spaces=None, out_spaces=None, aliases=None, flops=1000000):
    spaces, out_spaces = spaces or {}, out_spaces or {}
    single = not isinstance(outs, tuple)
    out_specs = [out_spaces.get(i, VMEM) for i in range(1 if single else len(outs))]
    return pl.pallas_call(
        kernel,
        out_shape=outs,
        in_specs=[spaces.get(i, VMEM) for i in range(len(ins))],
        out_specs=out_specs[0] if single else out_specs,
        scratch_shapes=list(scratch),
        input_output_aliases=aliases or {},
        compiler_params=pltpu.CompilerParams(vmem_limit_bytes=int(megabytes * 2**20)),
        cost_estimate=pl.CostEstimate(flops=flops, bytes_accessed=2**21, transcendentals=0),
    )(*ins)


def shape(*dims, dtype=F32):
    return jax.ShapeDtypeStruct(dims, dtype)


def exchange(values, axis, steps):
    size = lax.axis_size(axis)
    return [
        lax.ppermute(value, axis, [(i, i ^ step) for i in range(size)])
        for value, step in zip(values, steps)
    ]


def turn(value, by):
    size_y, size_z = lax.axis_size("gy"), lax.axis_size("gz")
    half = size_y // 2
    pairs = []
    for core in range(half):
        ring = [(high * half + core) * size_z + z for high in range(2) for z in range(size_z)]
        pairs += [(ring[n], ring[(n + by) % len(ring)]) for n in range(len(ring))]
    return lax.ppermute(value, ("gy", "gz"), pairs)


def banded(bands, *kernels, flops=10**9):
    return call(
        functools.partial(bands_kernel, bands),
        tuple(shape(band[0], band[1], dtype=BF16) for band in bands for _ in range(2)),
        kernels,
        spaces={n: SMEM for n in range(len(kernels))},
        flops=flops,
    )


def shards(charges, counts, slots, spline, kernel_fine, kernel_mid, kernel_coarse):
    cells = charges.shape[0]
    packed, raw, face = call(
        deposit_kernel,
        (shape(32, 32, 128), shape(8, 128), shape(2 * FACE + 8, 128)),
        (256 * slots + counts, charges, spline.reshape(cells * 12, ATOMS)),
        (
            pltpu.VMEM((32, 32, 128), F32),
            pltpu.VMEM((cells, ATOMS), F32),
            pltpu.VMEM((cells * 12, 128), BF16),
            pltpu.VMEM((cells * 12, 128), F32),
            pltpu.VMEM((64, cells), F32),
            pltpu.VMEM((32, 32, 128), F32),
            pltpu.VMEM((SPAN_2, 56, 128), F32),
            pltpu.VMEM((SPAN_3, 40, 128), F32),
            pltpu.VMEM((SPAN_4, 24, 128), F32),
            pltpu.SemaphoreType.DMA((5,)),
        ),
        spaces={1: HBM, 2: HBM},
        out_spaces={0: ANY},
        megabytes=53.75,
    )
    (got_1,) = exchange((face,), "gy", (1,))
    relay = call(relay_kernel, shape(FACE + 8, 128), (raw, got_1))
    (got_2,) = exchange((relay,), "gy", (2,))
    qx, qy, qz = composites()
    qz_high = qz.astype(BF16)
    qz_low = (qz - qz_high.astype(np.float32)).astype(BF16)
    green_high, green_low, rise, framed = call(
        green_kernel,
        (
            shape(1024, 128 * SPAN_4, dtype=BF16),
            shape(1024, 128 * SPAN_4, dtype=BF16),
            shape(1024, 256, dtype=BF16),
            shape(32, 40, 128),
        ),
        (jnp.asarray(np.concatenate([qx, qy])), packed),
        (pltpu.VMEM((18, 64, 128), BF16), pltpu.VMEM((18, 64, 128), BF16)),
    )
    wide_y, raw, face_1, face_3 = call(
        widen_y_kernel,
        (shape(32, 40, 128), shape(8, 128), shape(72, 128), shape(72, 128)),
        (framed, relay, got_1, got_2, rise),
        spaces={4: ANY},
        aliases={0: 0},
    )
    got_3, got_1, got_2 = exchange((face_3, face_1, raw), "gx", (3, 1, 2))
    bands_1 = banded(BANDS[:1], kernel_fine)
    own_high, own_low = call(
        own_z_kernel, (shape(80, 128), shape(80, 128)), (wide_y, bands_1[0]), spaces={1: ANY}
    )
    wide_x = call(
        widen_x_kernel, shape(36, 40, 128), (wide_y, got_2, got_1, got_3), spaces={1: ANY}
    )
    raw, to_high, to_low = call(
        edge_x_kernel,
        (shape(16, 128), shape(80, 128), shape(80, 128)),
        (raw, got_2, got_1, got_3, own_high, own_low),
    )
    from_low, from_high = turn(to_high, 1), turn(to_low, -1)
    (got_2,) = exchange((raw,), "gz", (2,))
    bands_2 = banded(BANDS[1:], kernel_mid, kernel_coarse)
    window = call(
        window_kernel,
        shape(3, 16, 128),
        (raw, got_2, from_low, from_high, bands_2[0], wide_x),
        spaces={4: ANY, 5: ANY},
    )
    pieces = [window] + [turn(window, by) for by in (8, -4, 4)]
    base = call(
        near_kernel,
        shape(32, 32, 128),
        (wide_x, from_low, from_high, *bands_1, *bands_2, jnp.asarray(PROL_2, BF16), jnp.asarray(PROL_1, BF16)),
        (
            pltpu.VMEM((32, 40, 256), F32),
            pltpu.VMEM((SPAN_2, 32, 128), F32),
            pltpu.VMEM((SPAN_3, 24, 128), F32),
            pltpu.VMEM((SPAN_3, 24, 128), F32),
            pltpu.VMEM((SPAN_3, 24, 128), F32),
            pltpu.VMEM((SPAN_2, 32, 128), F32),
            pltpu.VMEM((SPAN_2, 32, 128), F32),
        ),
    )
    return call(
        top_kernel,
        shape(32, 32, 32),
        (base, *pieces, green_high, green_low, rise, jnp.asarray(np.concatenate([qz_high, qz_low]))),
        (
            pltpu.VMEM((16, 8, 128), F32),
            pltpu.VMEM((32, 32, 32), F32),
            pltpu.SemaphoreType.DMA((4,)),
        ),
        out_spaces={0: ANY},
    )


def solution(mesh):
    return jax.shard_map(
        shards,
        mesh=mesh,
        in_specs=(
            P(("gx", "gy", "gz"), None),
            P(("gx", "gy", "gz")),
            P(("gx", "gy", "gz")),
            P(("gx", "gy", "gz"), None, None, None),
            P(),
            P(),
            P(),
        ),
        out_specs=P("gx", "gy", "gz"),
        check_vma=False,
    )
```

```python
import functools

import jax
import jax.numpy as jnp
import numpy as np
from jax import lax
from jax.experimental import pallas as pl
from jax.experimental.pallas import tpu as pltpu
from jax.sharding import PartitionSpec as P

W = (0.125, 0.5, 0.75, 0.5, 0.125)
F32 = jnp.float32
BF16 = jnp.bfloat16
CELLS = 384
ATOMS = 128
SPAN_2 = 18
SPAN_3 = 11
SPAN_4 = 7
SEC = 32
THI = 64
VMEM = pl.BlockSpec(memory_space=pltpu.VMEM)
SMEM = pl.BlockSpec(memory_space=pltpu.SMEM)
HBM = pl.BlockSpec(memory_space=pltpu.HBM)
ANY = pl.BlockSpec(memory_space=pl.ANY)


def weight(t):
    return W[t] if 0 <= t <= 4 else 0.0


def table(rows, columns, offset, turned):
    out = np.zeros((128, 128), np.float32)
    for r in range(rows):
        for c in range(columns):
            out[r, c] = weight(c - 2 * r + offset if turned else r - 2 * c + offset)
    return out


PROL_2 = table(SPAN_3, SPAN_2, 3, True)
PROL_1 = table(SPAN_2, 32, 4, True)


BANDS = (
    (256, 256, ((0, 32, 2), (160, 2, 0), (192, 2, 34)), 32, 32),
    (256, 128, ((0, 18, 2), (128, 4, 0), (160, 4, 18)), 24, 18),
    (128, 128, ((0, 11, 2), (64, 5, 0), (96, 5, 10)), 16, 11),
)
DIVIDE = {32: (1, 5), 2: (1, 1), 18: (57, 10), 4: (1, 2), 11: (94, 10), 5: (52, 8), 24: (43, 10), 16: (1, 4)}


def composite(first, last):
    p3 = np.array([[weight(i - 2 * j + 3) for j in range(7)] for i in range(11)])
    p2 = np.array([[weight(i - 2 * j + 3) for j in range(11)] for i in range(18)])
    p1 = np.array([[weight(i - 2 * j + 4) for j in range(18)] for i in range(32)])
    m4, m3, m2 = np.ones(7), np.ones(11), np.ones(18)
    if first:
        m4[0] = m3[0] = m2[0] = 0
    if last:
        m4[5:] = 0
        m3[9:] = 0
        m2[17:] = 0
    return (p1 * m2) @ (p2 * m3) @ (p3 * m4)


def composites():
    qx = np.zeros((4, 32, 128), np.float32)
    qy = np.zeros((4, 32, 128), np.float32)
    qz = np.zeros((4, 128, 128), np.float32)
    for v in range(4):
        q = composite(v % 2 == 1, v >= 2)
        for lane in range(64):
            if lane // 8 < 7 and lane % 8 < 7:
                qx[v, :, lane] = q[:, lane // 8]
                qy[v, :, lane] = q[:, lane % 8]
        for row in range(128):
            if row % 8 < 7:
                qz[v, row, :32] = q[:, row % 8]
    return qx, qy, qz


def split(x):
    high = x.astype(BF16)
    return high, (x - high.astype(F32)).astype(BF16)


def dot(a, b):
    return jnp.dot(a, b, preferred_element_type=F32)


def dot_exact(x, right):
    high, low = split(x)
    return dot(high, right) + dot(low, right)


def dot_split(x, right_high, right_low):
    high, low = split(x)
    return dot(high, right_high) + (dot(low, right_high) + dot(high, right_low))


def iota(shape, dim):
    return lax.broadcasted_iota(jnp.int32, shape, dim)


def roll(x, shift, axis=None):
    axis = x.ndim - 1 if axis is None else axis
    shift = shift % x.shape[axis]
    return x if shift == 0 else pltpu.roll(x, shift, axis)


def lanes_of(x, low, count):
    lane = iota(x.shape, x.ndim - 1)
    return jnp.where((lane >= low) & (lane < low + count), x, 0.0)


def as_rows(x):
    return x.reshape(x.shape[0] * x.shape[1], x.shape[2])


def taps(pieces):
    total = None
    for factor, value in pieces:
        term = value if factor == 1.0 else factor * value
        total = term if total is None else total + term
    return total


def restrict_planes(read, span, size, offset):
    planes = []
    for p in range(span):
        planes.append(
            taps([(W[t], read(2 * p + t - offset)) for t in range(5) if 0 <= 2 * p + t - offset < size])
        )
    return planes


def place():
    sizes = [lax.axis_size(a) for a in ("gx", "gy", "gz")]
    index = [lax.axis_index(a) for a in ("gx", "gy", "gz")]
    return index, sizes


def inside_mask(shape, spans, high, place_of):
    index, sizes = place_of
    keep = None
    for dim in range(3):
        at = iota(shape, dim)
        low = jnp.where(index[dim] == 0, 1, 0)
        top = jnp.where(index[dim] == sizes[dim] - 1, high, spans)
        part = (at >= low) & (at < top)
        keep = part if keep is None else keep & part
    return keep


def nearest(index):
    even = lax.rem(index, 2) == 0
    return even, index == 1, index == 2


def deposit_kernel(
    codes, charges_hbm, spline_hbm,
    packed_hbm, raw_out, face,
    packed, charges, spline, wide, patch, fine, buf_2, buf_3, buf_4, sems,
):
    where = place()
    index, sizes = where
    part = CELLS * 12 // 3
    copies = [pltpu.make_async_copy(charges_hbm, charges, sems.at[3])]
    for chunk in range(3):
        rows = slice(part * chunk, part * chunk + part)
        copies.append(
            pltpu.make_async_copy(spline_hbm.at[rows, :], spline.at[rows, :], sems.at[chunk])
        )
    for copy in copies:
        copy.start()
    buf_2[...] = jnp.zeros_like(buf_2)
    buf_3[...] = jnp.zeros_like(buf_3)
    buf_4[...] = jnp.zeros_like(buf_4)
    row, column = iota((512, 64), 0), iota((512, 64), 1)
    spread = (row // 32 * 4 + row % 4 == column).astype(F32).astype(BF16)
    row, column = iota((128, 128), 0), iota((128, 128), 1)

    def restriction(rows, columns, offset):
        t = row - 2 * column + offset
        out = jnp.zeros((128, 128), F32)
        for tap in range(5):
            out = jnp.where(t == tap, W[tap], out)
        return jnp.where((row < rows) & (column < columns), out, 0.0).astype(BF16)

    rest_2 = restriction(32, SPAN_2, 4)
    rest_3 = restriction(SPAN_2, SPAN_3, 3)
    rest_4 = restriction(SPAN_3, SPAN_4, 3)
    slot = lax.shift_right_logical(codes[...].reshape(1, CELLS), 8)
    fits = (iota((512, CELLS), 0) // 4 % 8) == slot % 8
    hot = (iota((64, CELLS), 0) == slot // 8).astype(F32).astype(BF16)
    copies[0].wait()
    alive = iota((ATOMS, CELLS), 0) < (codes[...].reshape(1, CELLS) & 255)
    weighted = jnp.where(alive, charges[...].T, 0.0)
    for chunk in range(CELLS // 128):
        lanes = slice(128 * chunk, 128 * chunk + 128)
        copies[1 + chunk].wait()
        rows = slice(part * chunk, part * chunk + part)
        wide[rows, :] = spline[rows, :].astype(F32)

        def column_of(d, i):
            return wide[pl.ds(chunk * part + 4 * d + i, 128, stride=12), :].T

        charge = weighted[:, lanes]
        depth = [charge * column_of(2, k) for k in range(4)]
        ys = [column_of(1, j) for j in range(4)]
        for i in range(4):
            xs = column_of(0, i)
            for j in range(4):
                cross = xs * ys[j]
                for k in range(4):
                    patch[16 * i + 4 * j + k : 16 * i + 4 * j + k + 1, lanes] = jnp.sum(
                        cross * depth[k], axis=0, keepdims=True
                    )
    high, low = split(patch[...])
    spread_high = jnp.where(fits, dot(spread, high), 0.0).astype(BF16)
    spread_low = jnp.where(fits, dot(spread, low), 0.0).astype(BF16)
    nt = (((1,), (1,)), ((), ()))
    placed = lax.dot_general(hot, spread_high, nt, preferred_element_type=F32) + lax.dot_general(
        hot, spread_low, nt, preferred_element_type=F32
    )
    for i in range(4):
        for j in range(4):
            rows = lanes_of(roll(placed[:, 128 * i : 128 * i + 128], -32 * j), 0, 32)
            for sx in range(8):
                fine[4 * sx + i, pl.ds(j, 8, stride=4), :] = rows[8 * sx : 8 * sx + 8]

    for p, plane in enumerate(restrict_planes(lambda x: fine[x], SPAN_2, 32, 4)):
        buf_2[p, 4:36, :] = plane
    second = taps([(W[t], buf_2[:, pl.ds(t, 24, stride=2), :]) for t in range(5)])
    second = dot_exact(as_rows(second), rest_2).reshape(SPAN_2, 24, 128)
    second = jnp.where(inside_mask(second.shape, SPAN_2, 17, where), second, 0.0)
    for p, plane in enumerate(restrict_planes(lambda x: second[x], SPAN_3, SPAN_2, 3)):
        buf_3[p, 3:27, :] = plane
    third = taps([(W[t], buf_3[:, pl.ds(t, 16, stride=2), :]) for t in range(5)])
    third = dot_exact(as_rows(third), rest_3).reshape(SPAN_3, 16, 128)
    third = jnp.where(inside_mask(third.shape, SPAN_3, 9, where), third, 0.0)
    packed[...] = fine[...]
    packed[0:SPAN_2, 0:24, :] += roll(second, SEC)
    packed[0:SPAN_3, 0:16, :] += roll(third, THI)
    leave = pltpu.make_async_copy(packed, packed_hbm, sems.at[4])
    leave.start()
    for p, plane in enumerate(restrict_planes(lambda x: third[x], SPAN_4, SPAN_3, 3)):
        buf_4[p, 3:19, :] = plane
    last = taps([(W[t], buf_4[:, pl.ds(t, 8, stride=2), :]) for t in range(5)])
    last = dot_exact(as_rows(last), rest_4).reshape(SPAN_4, 8, 128)
    last = jnp.where(inside_mask(last.shape, SPAN_4, 5, where), last, 0.0)
    raw = taps([(1.0, roll(last[x], 8 * x)) for x in range(SPAN_4)])
    raw_out[...] = raw

    even, _, _ = nearest(index[1])
    low = pack_y(packed, FIRST_ROWS)
    high = pack_y(packed, LAST_ROWS)
    for v in range(4):
        face[8 * v : 8 * v + 8, :] = jnp.where(even, high[v], low[v])
        face[FACE + 8 * v : FACE + 8 * v + 8, :] = jnp.where(even, low[v], high[v])
    face[2 * FACE : 2 * FACE + 8, :] = raw
    leave.wait()


def spot_1(p):
    return p // 16, p % 16 // 4 * 2, p % 4 * 32


def spot_2(p):
    return 2 + p // 14, p % 14 // 7 * 4, p % 7 * 18


def spot_3(p):
    return 3, 4, p * 11


def spot_4(p):
    return 3, p // 5, 72 + p % 5 * 11


FACE = 32
LEVELS = (
    (32, 2, 0, 32, spot_1),
    (SPAN_2, 4, SEC, 18, spot_2),
    (SPAN_3, 4, THI, 11, spot_3),
    (SPAN_3, 1, THI, 11, spot_4),
)
FIRST_ROWS = (0, 0, 0, 4)
LAST_ROWS = (30, 14, 6, 10)
ROWS_ABOVE = (34, 18, 10, 14)


def pack_y(source, at):
    tiles = [jnp.zeros((8, 128), F32) for _ in range(4)]
    row, at_lane = iota((8, 128), 0), iota((8, 128), 1)
    for (planes, count, lane, width, spot), start in zip(LEVELS, at):
        for p in range(planes):
            v, r, to = spot(p)
            if start == 30:
                slab = roll(source[p, 24:32, :], r - 6, 0)
            else:
                slab = roll(source[p, start : start + 8, :], r, 0)
            slab = roll(slab, to - lane)
            keep = (row >= r) & (row < r + count) & (at_lane >= to) & (at_lane < to + width)
            tiles[v] = jnp.where(keep, slab, tiles[v])
    return tiles


def place_y(tile, index):
    tall = jnp.concatenate([tile, jnp.zeros((8, 128), F32)], axis=0)
    tall = pltpu.roll(tall, lax.rem(4 * index + 15, 16), 0)
    return tall[0:8] + roll(tall[8:16], 64)


def relay_kernel(raw, got, out):
    index, _ = place()
    out[0:FACE, :] = got[FACE : 2 * FACE, :]
    partner = jnp.bitwise_xor(index[1], 1)
    other = got[2 * FACE : 2 * FACE + 8, :]
    out[FACE : FACE + 8, :] = place_y(raw[...], index[1]) + place_y(other, partner)


def widen_y_kernel(framed, own, got_1, got_2, after, out, raw_out, face_1, face_3):
    index, _ = place()
    even, one, two = nearest(index[1])
    total = own[FACE : FACE + 8, :] + got_2[FACE : FACE + 8, :]
    raw_out[...] = total
    a, b = got_1[0:FACE, :], got_2[0:FACE, :]
    low = jnp.where(even, 0.0, a) + jnp.where(two, b, 0.0)
    high = jnp.where(even, a, 0.0) + jnp.where(one, b, 0.0)
    for face, at in ((low, FIRST_ROWS), (high, ROWS_ABOVE)):
        for (planes, count, lane, width, spot), start in zip(LEVELS, at):
            for p in range(planes):
                v, r, to = spot(p)
                slab = roll(roll(face[8 * v : 8 * v + 8], -r, 0), lane - to)
                slab = lanes_of(slab, lane, width)
                out[p, start : start + count, :] += slab[0:count]
    even, one, _ = nearest(index[0])
    for ref, to_high in ((face_1, even), (face_3, one)):
        f = jnp.where(to_high, 30, 0)
        s = jnp.where(to_high, 14, 0)
        t = jnp.where(to_high, 6, 0)
        ref[0:40, :] = lanes_of(out[f], 0, 32) + lanes_of(roll(out[f + 1], 32), 32, 32)
        ref[0:16, :] += taps(
            [(1.0, lanes_of(roll(out[t + k, 0:16, :], 11 * k), THI + 11 * k, 11)) for k in range(5)]
        )
        ref[40:64, :] = taps(
            [(1.0, lanes_of(roll(out[s + k, 0:24, :], 18 * k - SEC), 18 * k, 18)) for k in range(4)]
        )
        ref[64:72, :] = total


def x_faces(index, got_1, got_3):
    even, one, two = nearest(index)
    a, b = got_1[0:64, :], got_3[0:64, :]
    low = jnp.where(even, 0.0, a) + jnp.where(two, b, 0.0)
    high = jnp.where(even, a, 0.0) + jnp.where(one, b, 0.0)
    planes = []
    for face, at in ((low, (0, 0, 0)), (high, (34, 18, 10))):
        for k in range(2):
            planes.append((0, at[0] + k, lanes_of(roll(face[0:40], -32 * k), 0, 32)))
        for k in range(4):
            planes.append((1, at[1] + k, lanes_of(roll(face[40:64], -18 * k), 0, 18)))
        for k in range(5):
            planes.append((2, at[2] + k, lanes_of(roll(face[0:16], -THI - 11 * k), 0, 11)))
    return planes


def widen_x_kernel(wide_y, after, got_1, got_3, out):
    index, _ = place()
    out[0:2] = jnp.zeros((2, 40, 128), F32)
    out[34:36] = jnp.zeros((2, 40, 128), F32)
    out[2:34] = wide_y[...]
    for level, at, values in x_faces(index[0], got_1, got_3):
        rows = values.shape[0]
        out[at, 0:rows, :] += roll(values, (0, SEC, THI)[level])


Z_LEVELS = ((40, 2, 0, 30), (24, 4, SEC, 14), (16, 5, THI, 6))


def chosen_lanes(values, first, count):
    at = iota(values.shape, 1)
    return jnp.where((at >= first) & (at < first + count), values, 0.0)


def own_z_kernel(wide_y, after, high, low):
    for ref, to_high in ((high, True), (low, False)):
        start = 0
        for (rows, count, lane, top), planes in zip(Z_LEVELS, (32, SPAN_2, SPAN_3)):
            first = lane + top if to_high else lane
            total = jnp.zeros((rows, 128), F32)
            for x in range(planes):
                kept = chosen_lanes(wide_y[x, 0:rows, :], first, count)
                total = total + roll(kept, count * (x + 2) - first)
            ref[start : start + rows, :] = total
            start += rows


def edge_x_kernel(own, got_2, got_1, got_3, high, low, raw_out, to_high, to_low):
    index, _ = place()
    total = None
    lane = iota((16, 128), 1)
    for step, tile in ((0, own[...]), (1, got_1[64:72, :]), (2, got_2[...]), (3, got_3[64:72, :])):
        tall = jnp.concatenate([tile, roll(tile, 64)], axis=0)
        tall = jnp.where(lane < 64, tall, 0.0)
        at = lax.rem(32 * jnp.bitwise_xor(index[0], step) + 120, 128)
        moved = pltpu.roll(tall, at, 1)
        total = moved if total is None else total + moved
    raw_out[...] = total
    planes = x_faces(index[0], got_1, got_3)
    for face, own_face, is_high in ((to_high, high, True), (to_low, low, False)):
        sums = [own_face[0:40, :], own_face[40:64, :], own_face[64:80, :]]
        for level, at, values in planes:
            _, count, _, top = Z_LEVELS[level]
            first = top if is_high else 0
            kept = chosen_lanes(values, first, count)
            sums[level] = sums[level] + roll(kept, count * at - first)
        face[0:40, :] = sums[0]
        face[40:64, :] = sums[1]
        face[0:16, :] += lanes_of(roll(sums[2], 72), 72, 55)
        face[40:56, :] += lanes_of(roll(sums[2], 88 - 55), 88, 20)
        face[64:80, :] = total


def unpack_z(message):
    third = lanes_of(roll(message[0:16], -72), 0, 55) + lanes_of(roll(message[40:56], 55 - 88), 55, 20)
    return message[0:40], message[40:64], third


def window_kernel(own, got_2, from_low, from_high, after_1, after_2, out):
    index, _ = place()
    early = lax.rem(index[2], 4) < 2
    ends = got_2[...]
    first, second, third = from_low[64:80, :], own[...], from_high[64:80, :]
    pieces = (
        jnp.where(early, first, ends),
        jnp.where(early, second, first),
        jnp.where(early, third, second),
        jnp.where(early, ends, third),
    )
    for group in range(3):
        total = None
        for q in range(min(6, 16 - 6 * group)):
            for d, piece in enumerate(pieces):
                to = 20 * q + 4 * d
                moved = lanes_of(roll(piece, to - 48 * group - 8 * q), to, 8)
                total = moved if total is None else total + moved
        out[group] = total


def divided(n, d):
    factor, bits = DIVIDE[d]
    return lax.shift_right_logical(n * factor, bits)


def build_bands(kernel, band):
    rows, columns, runs, group, outs = band
    row = iota((rows, 128), 0)
    shift = jnp.full((rows, 128), 99, jnp.int32)
    point = jnp.full((rows, 128), 99, jnp.int32)
    for start, count, offset in runs:
        at = row - start
        a = divided(at, count)
        inside = (at >= 0) & (at < 5 * count)
        shift = jnp.where(inside, a, shift)
        point = jnp.where(inside, offset + at - a * count, point)
    chosen = (shift == iota((rows, 128), 1)).astype(F32).astype(BF16)
    column = iota((8, columns), 1)
    block = divided(column, group)
    out_at = (column - block * group)[0:1]
    block = jnp.where((column - block * group) < outs, block, 9)
    sub = iota((8, columns), 0)
    entry = jnp.concatenate([point] * (columns // 128), axis=1) - out_at
    total_high = jnp.zeros((rows, columns), F32)
    total_low = jnp.zeros((rows, columns), F32)
    for c in range(5):
        source = jnp.zeros((8, columns), F32)
        for b in range(5):
            column_of = jnp.zeros((8, columns), F32)
            for a in range(5):
                column_of = jnp.where(sub == a, kernel[a, b, c], column_of)
            source = jnp.where(block == b, column_of, source)
        source = jnp.concatenate([source, jnp.zeros((120, columns), F32)], axis=0)
        high, low = split(source)
        fits = entry == c
        total_high = jnp.where(fits, dot(chosen, high), total_high)
        total_low = jnp.where(fits, dot(chosen, low), total_low)
    return total_high.astype(BF16), total_low.astype(BF16)


def bands_kernel(bands, *refs):
    kernels, outs = refs[: len(bands)], refs[len(bands) :]
    for n, (kernel, band) in enumerate(zip(kernels, bands)):
        high, low = build_bands(kernel, band)
        outs[2 * n][...] = high
        outs[2 * n + 1][...] = low


def green_kernel(factors, packed, green_high, green_low, rise, framed, block_high, block_low):
    index, sizes = place()
    row, lane = iota((64, 128), 0), iota((64, 128), 1)
    delta_x = (lane // 8).astype(F32)
    delta_z = (4 * index[2] - 1 + lane % 8 - row).astype(F32)
    plain = delta_z * delta_z + (1.0 + delta_x * delta_x)
    for apart in range(18):
        high, low = split(0.0625 * lax.rsqrt(plain + float(apart * apart)))
        block_high[apart] = high
        block_low[apart] = low
    for ty in range(SPAN_4):
        columns = slice(128 * ty, 128 * ty + 128)
        for sy in range(16):
            apart = jnp.abs(4 * index[1] - 1 + ty - sy)
            first = sy % 8 * 128 + sy // 8 * 64
            green_high[first : first + 64, columns] = block_high[apart]
            green_low[first : first + 64, columns] = block_low[apart]
    variant = [
        jnp.where(index[d] == 0, 1, 0) + jnp.where(index[d] == sizes[d] - 1, 2, 0) for d in range(3)
    ]
    factor_x, factor_y = factors[variant[0]], factors[4 + variant[1]]
    kept = as_rows(factor_x[:, None, :] * factor_y[None, :, :])
    high, low = split(kept)
    rise[:, 0:128] = (high.astype(F32) + roll(low.astype(F32), 64)).astype(BF16)
    rise[:, 128:256] = high
    framed[:, 0:2, :] = jnp.zeros((32, 2, 128), F32)
    framed[:, 34:40, :] = jnp.zeros((32, 6, 128), F32)
    framed[:, 2:34, :] = packed[...]


def prolong_rows(source, target, count, whole):
    size = target.shape[1] // 2
    q0 = source[:, 0:size, :]
    q1 = source[:, 1 : size + 1, :]
    q2 = source[:, 2 : size + 2, :]
    even = 0.75 * q1 + 0.125 * (q0 + q2)
    odd = 0.5 * (q0 + q1) if whole else 0.5 * (q1 + q2)
    target[:, pl.ds(1 if whole else 0, size, stride=2), :] = even
    target[:, pl.ds(0 if whole else 1, size, stride=2), :] = odd


def prolong_plane(read, p, whole):
    half = p // 2
    if (p % 2 == 1) == whole:
        return 0.75 * read(half + 1) + 0.125 * (read(half) + read(half + 2))
    first = half if whole else half + 1
    return 0.5 * (read(first) + read(first + 1))


def near_kernel(
    wide, from_low, from_high, b1h, b1l, b2h, b2l, b3h, b3l, prol_2, prol_1,
    out,
    near_1, near_2, near_3, tall_3, tall_3y, tall_2, tall_2y,
):
    where = place()
    index, sizes = where
    low_faces = unpack_z(jnp.where(index[2] == 0, 0.0, from_low[0:64, :]))
    high_faces = unpack_z(jnp.where(index[2] == sizes[2] - 1, 0.0, from_high[0:64, :]))

    def halo(x, level, count, low_at, high_at):
        low = roll(low_faces[level], low_at - count * x)
        high = roll(high_faces[level], high_at - count * x)
        return lanes_of(low, low_at, 5 * count) + lanes_of(high, high_at, 5 * count)

    planes = [lanes_of(wide[x, 0:16, :], THI, 11) for x in range(15)]
    left = []
    for x in range(SPAN_3):
        main = taps([(1.0, roll(planes[x + a], 11 * a - THI)) for a in range(5)])
        left.append(main + halo(x, 2, 5, 64, 96))
    left = jnp.concatenate(left, axis=0)
    near_3[...] = jnp.zeros_like(near_3)
    near_3[:, 0:16, :] = dot_split(left, b3h[...], b3l[...]).reshape(SPAN_3, 16, 128)
    third = taps([(1.0, roll(near_3[:, b : b + 16, :], -16 * b)) for b in range(5)])
    third = jnp.where(inside_mask(third.shape, SPAN_3, 9, where), third, 0.0)
    tall_3[...] = jnp.zeros_like(tall_3)
    tall_3[:, 0:16, :] = dot_exact(as_rows(third), prol_2[...]).reshape(SPAN_3, 16, 128)
    prolong_rows(tall_3, tall_3y, SPAN_2, True)

    planes = [lanes_of(wide[x, 0:24, :], SEC, 18) for x in range(22)]
    left_a, left_b = [], []
    for x in range(SPAN_2):
        left_a.append(taps([(1.0, roll(planes[x + a], 18 * a - SEC)) for a in range(5)]))
        left_b.append(halo(x, 1, 4, 0, 32))
    left = jnp.concatenate(
        [jnp.concatenate(left_a, axis=0), jnp.concatenate(left_b, axis=0)], axis=1
    )
    near_2[...] = jnp.zeros_like(near_2)
    near_2[:, 0:24, :] = dot_split(left, b2h[...], b2l[...]).reshape(SPAN_2, 24, 128)
    second = taps([(1.0, roll(near_2[:, b : b + 24, :], -24 * b)) for b in range(5)])
    raised = jnp.stack(
        [prolong_plane(lambda x: tall_3y[x], p, True) for p in range(SPAN_2)], axis=0
    )
    second = jnp.where(inside_mask(second.shape, SPAN_2, 17, where), second + raised, 0.0)
    tall_2[...] = jnp.zeros_like(tall_2)
    tall_2[:, 0:24, :] = dot_exact(as_rows(second), prol_1[...]).reshape(SPAN_2, 24, 128)
    prolong_rows(tall_2, tall_2y, 32, False)

    planes = [lanes_of(wide[x], 0, 32) for x in range(36)]
    left_a, left_b = [], []
    for x in range(32):
        left_a.append(taps([(1.0, roll(planes[x + a], 32 * a)) for a in range(4)]))
        left_b.append(planes[x + 4] + halo(x, 0, 2, 32, 64))
    left = jnp.concatenate(
        [jnp.concatenate(left_a, axis=0), jnp.concatenate(left_b, axis=0)], axis=1
    )
    near_1[...] = dot_split(left, b1h[...], b1l[...]).reshape(32, 40, 256)
    for x in range(32):
        first = taps(
            [(1.0, roll(near_1[x, b : b + 32, 0:128], -32 * b)) for b in range(4)]
            + [(1.0, near_1[x, 4:36, 128:256])]
        )
        out[x] = first + prolong_plane(lambda q: tall_2y[q], x, False)


def window_starts(index):
    ring = lax.rem(index, 4)
    first = 4 * (ring == 3).astype(jnp.int32) - 4 * (ring == 0).astype(jnp.int32) + 127
    return [lax.rem(16 * lax.rem(index // 4 + step, 4) + first, 128) for step in (0, 2, 1, 3)]


def placed_row(piece, at, x):
    kept = lanes_of(piece[x // 6], 20 * (x % 6), 20)
    return pltpu.roll(kept, lax.rem(at + 128 - 20 * (x % 6), 128), 1)


def place_kernel(piece_0, piece_1, piece_2, after, out):
    index, _ = place()
    starts = window_starts(index[2])
    for x in range(16):
        out[x] = taps(
            [(1.0, placed_row(p, at, x)) for p, at in zip((piece_0, piece_1, piece_2), starts)]
        )


def top_kernel(
    base, early, piece_3, green_high, green_low, rise, qz,
    out_hbm,
    fourth, out, sems,
):
    index, sizes = place()
    lane = iota((8, 128), 1)
    at = window_starts(index[2])[3]
    for x in range(16):
        total = early[x] + placed_row(piece_3, at, x)
        total = total + roll(total, 64)
        fourth[x] = jnp.where(lane < 64, total[0:8], total[8:16])
    total = jnp.zeros((32, 128 * SPAN_4), F32)
    extra = jnp.zeros((16, 128 * SPAN_4), F32)
    for s in range(0, 8, 2):
        left = jnp.concatenate([fourth[:, s, :], fourth[:, s + 1, :]], axis=1)
        high, low = split(left)
        rows = slice(128 * s, 128 * s + 256)
        total = total + dot(jnp.concatenate([high, low], axis=0), green_high[rows, :])
        extra = extra + dot(high, green_low[rows, :])
    sums = total[0:16] + (total[16:32] + extra)
    row, lane = iota((16, 128), 0), iota((16, 128), 1)
    tops = []
    for tx in range(SPAN_4):
        keep = jnp.abs(4 * index[0] - 1 + tx - row) == lane // 8
        for ty in range(SPAN_4):
            picked = jnp.where(keep, sums[:, 128 * ty : 128 * ty + 128], 0.0)
            tops.append(jnp.sum(picked, axis=0, keepdims=True))
        tops.append(jnp.zeros((1, 128), F32))
    tops = jnp.concatenate(tops + [jnp.zeros((8, 128), F32)], axis=0)
    variant = jnp.where(index[2] == 0, 1, 0) + jnp.where(index[2] == sizes[2] - 1, 2, 0)
    high, low = split(dot_split(tops, qz[variant], qz[4 + variant]))
    right = jnp.concatenate([high, high, low, jnp.zeros_like(low)], axis=0)
    copies = []
    for part in range(4):
        planes = slice(8 * part, 8 * part + 8)
        far = dot(rise[256 * part : 256 * part + 256, :], right)
        out[planes] = (base[planes] + far.reshape(8, 32, 128))[:, :, 0:32]
        copies.append(pltpu.make_async_copy(out.at[planes], out_hbm.at[planes], sems.at[part]))
        copies[-1].start()
    for copy in copies:
        copy.wait()


def call(kernel, outs, ins, scratch=(), megabytes=16, spaces=None, out_spaces=None, aliases=None, flops=1000000):
    spaces, out_spaces = spaces or {}, out_spaces or {}
    single = not isinstance(outs, tuple)
    out_specs = [out_spaces.get(i, VMEM) for i in range(1 if single else len(outs))]
    return pl.pallas_call(
        kernel,
        out_shape=outs,
        in_specs=[spaces.get(i, VMEM) for i in range(len(ins))],
        out_specs=out_specs[0] if single else out_specs,
        scratch_shapes=list(scratch),
        input_output_aliases=aliases or {},
        compiler_params=pltpu.CompilerParams(vmem_limit_bytes=int(megabytes * 2**20)),
        cost_estimate=pl.CostEstimate(flops=flops, bytes_accessed=2**21, transcendentals=0),
    )(*ins)


def shape(*dims, dtype=F32):
    return jax.ShapeDtypeStruct(dims, dtype)


def exchange(values, axis, steps):
    size = lax.axis_size(axis)
    return [
        lax.ppermute(value, axis, [(i, i ^ step) for i in range(size)])
        for value, step in zip(values, steps)
    ]


def turn(value, by):
    size_y, size_z = lax.axis_size("gy"), lax.axis_size("gz")
    half = size_y // 2
    pairs = []
    for core in range(half):
        ring = [(high * half + core) * size_z + z for high in range(2) for z in range(size_z)]
        pairs += [(ring[n], ring[(n + by) % len(ring)]) for n in range(len(ring))]
    return lax.ppermute(value, ("gy", "gz"), pairs)


def banded(bands, *kernels, flops=10**9):
    return call(
        functools.partial(bands_kernel, bands),
        tuple(shape(band[0], band[1], dtype=BF16) for band in bands for _ in range(2)),
        kernels,
        spaces={n: SMEM for n in range(len(kernels))},
        flops=flops,
    )


def shards(charges, counts, slots, spline, kernel_fine, kernel_mid, kernel_coarse):
    cells = charges.shape[0]
    packed, raw, face = call(
        deposit_kernel,
        (shape(32, 32, 128), shape(8, 128), shape(2 * FACE + 8, 128)),
        (256 * slots + counts, charges, spline.reshape(cells * 12, ATOMS)),
        (
            pltpu.VMEM((32, 32, 128), F32),
            pltpu.VMEM((cells, ATOMS), F32),
            pltpu.VMEM((cells * 12, 128), BF16),
            pltpu.VMEM((cells * 12, 128), F32),
            pltpu.VMEM((64, cells), F32),
            pltpu.VMEM((32, 32, 128), F32),
            pltpu.VMEM((SPAN_2, 56, 128), F32),
            pltpu.VMEM((SPAN_3, 40, 128), F32),
            pltpu.VMEM((SPAN_4, 24, 128), F32),
            pltpu.SemaphoreType.DMA((5,)),
        ),
        spaces={1: HBM, 2: HBM},
        out_spaces={0: ANY},
        megabytes=53.75,
    )
    (got_1,) = exchange((face,), "gy", (1,))
    relay = call(relay_kernel, shape(FACE + 8, 128), (raw, got_1))
    (got_2,) = exchange((relay,), "gy", (2,))
    qx, qy, qz = composites()
    qz_high = qz.astype(BF16)
    qz_low = (qz - qz_high.astype(np.float32)).astype(BF16)
    green_high, green_low, rise, framed = call(
        green_kernel,
        (
            shape(1024, 128 * SPAN_4, dtype=BF16),
            shape(1024, 128 * SPAN_4, dtype=BF16),
            shape(1024, 256, dtype=BF16),
            shape(32, 40, 128),
        ),
        (jnp.asarray(np.concatenate([qx, qy])), packed),
        (pltpu.VMEM((18, 64, 128), BF16), pltpu.VMEM((18, 64, 128), BF16)),
    )
    wide_y, raw, face_1, face_3 = call(
        widen_y_kernel,
        (shape(32, 40, 128), shape(8, 128), shape(72, 128), shape(72, 128)),
        (framed, relay, got_1, got_2, rise),
        spaces={4: ANY},
        aliases={0: 0},
    )
    got_3, got_1, got_2 = exchange((face_3, face_1, raw), "gx", (3, 1, 2))
    bands_1 = banded(BANDS[:1], kernel_fine)
    own_high, own_low = call(
        own_z_kernel, (shape(80, 128), shape(80, 128)), (wide_y, bands_1[0]), spaces={1: ANY}
    )
    wide_x = call(
        widen_x_kernel, shape(36, 40, 128), (wide_y, got_2, got_1, got_3), spaces={1: ANY}
    )
    raw, to_high, to_low = call(
        edge_x_kernel,
        (shape(16, 128), shape(80, 128), shape(80, 128)),
        (raw, got_2, got_1, got_3, own_high, own_low),
    )
    from_low, from_high = turn(to_high, 1), turn(to_low, -1)
    (got_2,) = exchange((raw,), "gz", (2,))
    bands_2 = banded(BANDS[1:], kernel_mid, kernel_coarse)
    window = call(
        window_kernel,
        shape(3, 16, 128),
        (raw, got_2, from_low, from_high, bands_2[0], wide_x),
        spaces={4: ANY, 5: ANY},
    )
    pieces = [window] + [turn(window, by) for by in (8, -4, 4)]
    base = call(
        near_kernel,
        shape(32, 32, 128),
        (wide_x, from_low, from_high, *bands_1, *bands_2, jnp.asarray(PROL_2, BF16), jnp.asarray(PROL_1, BF16)),
        (
            pltpu.VMEM((32, 40, 256), F32),
            pltpu.VMEM((SPAN_2, 32, 128), F32),
            pltpu.VMEM((SPAN_3, 24, 128), F32),
            pltpu.VMEM((SPAN_3, 24, 128), F32),
            pltpu.VMEM((SPAN_3, 24, 128), F32),
            pltpu.VMEM((SPAN_2, 32, 128), F32),
            pltpu.VMEM((SPAN_2, 32, 128), F32),
        ),
    )
    early = call(place_kernel, shape(16, 16, 128), (*pieces[:3], base), spaces={3: ANY})
    return call(
        top_kernel,
        shape(32, 32, 32),
        (base, early, pieces[3], green_high, green_low, rise, jnp.asarray(np.concatenate([qz_high, qz_low]))),
        (
            pltpu.VMEM((16, 8, 128), F32),
            pltpu.VMEM((32, 32, 32), F32),
            pltpu.SemaphoreType.DMA((4,)),
        ),
        out_spaces={0: ANY},
    )


def solution(mesh):
    return jax.shard_map(
        shards,
        mesh=mesh,
        in_specs=(
            P(("gx", "gy", "gz"), None),
            P(("gx", "gy", "gz")),
            P(("gx", "gy", "gz")),
            P(("gx", "gy", "gz"), None, None, None),
            P(),
            P(),
            P(),
        ),
        out_specs=P("gx", "gy", "gz"),
        check_vma=False,
    )
```

```python
import functools

import jax
import jax.numpy as jnp
import numpy as np
from jax import lax
from jax.experimental import pallas as pl
from jax.experimental.pallas import tpu as pltpu
from jax.sharding import PartitionSpec as P

W = (0.125, 0.5, 0.75, 0.5, 0.125)
F32 = jnp.float32
BF16 = jnp.bfloat16
CELLS = 384
ATOMS = 128
SPAN_2 = 18
SPAN_3 = 11
SPAN_4 = 7
SEC = 32
THI = 64
VMEM = pl.BlockSpec(memory_space=pltpu.VMEM)
SMEM = pl.BlockSpec(memory_space=pltpu.SMEM)
HBM = pl.BlockSpec(memory_space=pltpu.HBM)
ANY = pl.BlockSpec(memory_space=pl.ANY)


def weight(t):
    return W[t] if 0 <= t <= 4 else 0.0


def table(rows, columns, offset, turned):
    out = np.zeros((128, 128), np.float32)
    for r in range(rows):
        for c in range(columns):
            out[r, c] = weight(c - 2 * r + offset if turned else r - 2 * c + offset)
    return out


PROL_2 = table(SPAN_3, SPAN_2, 3, True)
PROL_1 = table(SPAN_2, 32, 4, True)


BANDS = (
    (256, 256, ((0, 32, 2), (160, 2, 0), (192, 2, 34)), 32, 32),
    (256, 128, ((0, 18, 2), (128, 4, 0), (160, 4, 18)), 24, 18),
    (128, 128, ((0, 11, 2), (64, 5, 0), (96, 5, 10)), 16, 11),
)
DIVIDE = {32: (1, 5), 2: (1, 1), 18: (57, 10), 4: (1, 2), 11: (94, 10), 5: (52, 8), 24: (43, 10), 16: (1, 4)}


def composite(first, last):
    p3 = np.array([[weight(i - 2 * j + 3) for j in range(7)] for i in range(11)])
    p2 = np.array([[weight(i - 2 * j + 3) for j in range(11)] for i in range(18)])
    p1 = np.array([[weight(i - 2 * j + 4) for j in range(18)] for i in range(32)])
    m4, m3, m2 = np.ones(7), np.ones(11), np.ones(18)
    if first:
        m4[0] = m3[0] = m2[0] = 0
    if last:
        m4[5:] = 0
        m3[9:] = 0
        m2[17:] = 0
    return (p1 * m2) @ (p2 * m3) @ (p3 * m4)


def composites():
    qx = np.zeros((4, 32, 128), np.float32)
    qy = np.zeros((4, 32, 128), np.float32)
    qz = np.zeros((4, 128, 128), np.float32)
    for v in range(4):
        q = composite(v % 2 == 1, v >= 2)
        for lane in range(64):
            if lane // 8 < 7 and lane % 8 < 7:
                qx[v, :, lane] = q[:, lane // 8]
                qy[v, :, lane] = q[:, lane % 8]
        for row in range(128):
            if row % 8 < 7:
                qz[v, row, :32] = q[:, row % 8]
    return qx, qy, qz


def split(x):
    high = x.astype(BF16)
    return high, (x - high.astype(F32)).astype(BF16)


def dot(a, b):
    return jnp.dot(a, b, preferred_element_type=F32)


def dot_exact(x, right):
    high, low = split(x)
    return dot(high, right) + dot(low, right)


def dot_split(x, right_high, right_low):
    high, low = split(x)
    return dot(high, right_high) + (dot(low, right_high) + dot(high, right_low))


def iota(shape, dim):
    return lax.broadcasted_iota(jnp.int32, shape, dim)


def roll(x, shift, axis=None):
    axis = x.ndim - 1 if axis is None else axis
    shift = shift % x.shape[axis]
    return x if shift == 0 else pltpu.roll(x, shift, axis)


def lanes_of(x, low, count):
    lane = iota(x.shape, x.ndim - 1)
    return jnp.where((lane >= low) & (lane < low + count), x, 0.0)


def as_rows(x):
    return x.reshape(x.shape[0] * x.shape[1], x.shape[2])


def taps(pieces):
    total = None
    for factor, value in pieces:
        term = value if factor == 1.0 else factor * value
        total = term if total is None else total + term
    return total


def restrict_planes(read, span, size, offset):
    planes = []
    for p in range(span):
        planes.append(
            taps([(W[t], read(2 * p + t - offset)) for t in range(5) if 0 <= 2 * p + t - offset < size])
        )
    return planes


def place():
    sizes = [lax.axis_size(a) for a in ("gx", "gy", "gz")]
    index = [lax.axis_index(a) for a in ("gx", "gy", "gz")]
    return index, sizes


def inside_mask(shape, spans, high, place_of):
    index, sizes = place_of
    keep = None
    for dim in range(3):
        at = iota(shape, dim)
        low = jnp.where(index[dim] == 0, 1, 0)
        top = jnp.where(index[dim] == sizes[dim] - 1, high, spans)
        part = (at >= low) & (at < top)
        keep = part if keep is None else keep & part
    return keep


def nearest(index):
    even = lax.rem(index, 2) == 0
    return even, index == 1, index == 2


def deposit_kernel(
    codes, charges_hbm, spline_hbm,
    packed_hbm, raw_out, face,
    packed, charges, spline, wide, patch, fine, buf_2, buf_3, buf_4, sems,
):
    where = place()
    index, sizes = where
    part = CELLS * 12 // 3
    copies = [pltpu.make_async_copy(charges_hbm, charges, sems.at[3])]
    for chunk in range(3):
        rows = slice(part * chunk, part * chunk + part)
        copies.append(
            pltpu.make_async_copy(spline_hbm.at[rows, :], spline.at[rows, :], sems.at[chunk])
        )
    for copy in copies:
        copy.start()
    buf_2[...] = jnp.zeros_like(buf_2)
    buf_3[...] = jnp.zeros_like(buf_3)
    buf_4[...] = jnp.zeros_like(buf_4)
    row, column = iota((512, 64), 0), iota((512, 64), 1)
    spread = (row // 32 * 4 + row % 4 == column).astype(F32).astype(BF16)
    row, column = iota((128, 128), 0), iota((128, 128), 1)

    def restriction(rows, columns, offset):
        t = row - 2 * column + offset
        out = jnp.zeros((128, 128), F32)
        for tap in range(5):
            out = jnp.where(t == tap, W[tap], out)
        return jnp.where((row < rows) & (column < columns), out, 0.0).astype(BF16)

    rest_2 = restriction(32, SPAN_2, 4)
    rest_3 = restriction(SPAN_2, SPAN_3, 3)
    rest_4 = restriction(SPAN_3, SPAN_4, 3)
    slot = lax.shift_right_logical(codes[...].reshape(1, CELLS), 8)
    fits = (iota((512, CELLS), 0) // 4 % 8) == slot % 8
    hot = (iota((64, CELLS), 0) == slot // 8).astype(F32).astype(BF16)
    copies[0].wait()
    alive = iota((ATOMS, CELLS), 0) < (codes[...].reshape(1, CELLS) & 255)
    weighted = jnp.where(alive, charges[...].T, 0.0)
    for chunk in range(CELLS // 128):
        lanes = slice(128 * chunk, 128 * chunk + 128)
        copies[1 + chunk].wait()
        rows = slice(part * chunk, part * chunk + part)
        wide[rows, :] = spline[rows, :].astype(F32)

        def column_of(d, i):
            return wide[pl.ds(chunk * part + 4 * d + i, 128, stride=12), :].T

        charge = weighted[:, lanes]
        depth = [charge * column_of(2, k) for k in range(4)]
        ys = [column_of(1, j) for j in range(4)]
        for i in range(4):
            xs = column_of(0, i)
            for j in range(4):
                cross = xs * ys[j]
                for k in range(4):
                    patch[16 * i + 4 * j + k : 16 * i + 4 * j + k + 1, lanes] = jnp.sum(
                        cross * depth[k], axis=0, keepdims=True
                    )
    high, low = split(patch[...])
    spread_high = jnp.where(fits, dot(spread, high), 0.0).astype(BF16)
    spread_low = jnp.where(fits, dot(spread, low), 0.0).astype(BF16)
    nt = (((1,), (1,)), ((), ()))
    placed = lax.dot_general(hot, spread_high, nt, preferred_element_type=F32) + lax.dot_general(
        hot, spread_low, nt, preferred_element_type=F32
    )
    for i in range(4):
        for j in range(4):
            rows = lanes_of(roll(placed[:, 128 * i : 128 * i + 128], -32 * j), 0, 32)
            for sx in range(8):
                fine[4 * sx + i, pl.ds(j, 8, stride=4), :] = rows[8 * sx : 8 * sx + 8]

    for p, plane in enumerate(restrict_planes(lambda x: fine[x], SPAN_2, 32, 4)):
        buf_2[p, 4:36, :] = plane
    second = taps([(W[t], buf_2[:, pl.ds(t, 24, stride=2), :]) for t in range(5)])
    second = dot_exact(as_rows(second), rest_2).reshape(SPAN_2, 24, 128)
    second = jnp.where(inside_mask(second.shape, SPAN_2, 17, where), second, 0.0)
    for p, plane in enumerate(restrict_planes(lambda x: second[x], SPAN_3, SPAN_2, 3)):
        buf_3[p, 3:27, :] = plane
    third = taps([(W[t], buf_3[:, pl.ds(t, 16, stride=2), :]) for t in range(5)])
    third = dot_exact(as_rows(third), rest_3).reshape(SPAN_3, 16, 128)
    third = jnp.where(inside_mask(third.shape, SPAN_3, 9, where), third, 0.0)
    packed[...] = fine[...]
    packed[0:SPAN_2, 0:24, :] += roll(second, SEC)
    packed[0:SPAN_3, 0:16, :] += roll(third, THI)
    leave = pltpu.make_async_copy(packed, packed_hbm, sems.at[4])
    leave.start()
    for p, plane in enumerate(restrict_planes(lambda x: third[x], SPAN_4, SPAN_3, 3)):
        buf_4[p, 3:19, :] = plane
    last = taps([(W[t], buf_4[:, pl.ds(t, 8, stride=2), :]) for t in range(5)])
    last = dot_exact(as_rows(last), rest_4).reshape(SPAN_4, 8, 128)
    last = jnp.where(inside_mask(last.shape, SPAN_4, 5, where), last, 0.0)
    raw = taps([(1.0, roll(last[x], 8 * x)) for x in range(SPAN_4)])
    raw_out[...] = raw

    even, _, _ = nearest(index[1])
    low = pack_y(packed, FIRST_ROWS)
    high = pack_y(packed, LAST_ROWS)
    for v in range(4):
        face[8 * v : 8 * v + 8, :] = jnp.where(even, high[v], low[v])
        face[FACE + 8 * v : FACE + 8 * v + 8, :] = jnp.where(even, low[v], high[v])
    face[2 * FACE : 2 * FACE + 8, :] = raw
    leave.wait()


def spot_1(p):
    return p // 16, p % 16 // 4 * 2, p % 4 * 32


def spot_2(p):
    return 2 + p // 14, p % 14 // 7 * 4, p % 7 * 18


def spot_3(p):
    return 3, 4, p * 11


def spot_4(p):
    return 3, p // 5, 72 + p % 5 * 11


FACE = 32
LEVELS = (
    (32, 2, 0, 32, spot_1),
    (SPAN_2, 4, SEC, 18, spot_2),
    (SPAN_3, 4, THI, 11, spot_3),
    (SPAN_3, 1, THI, 11, spot_4),
)
FIRST_ROWS = (0, 0, 0, 4)
LAST_ROWS = (30, 14, 6, 10)
ROWS_ABOVE = (34, 18, 10, 14)


def pack_y(source, at):
    tiles = [jnp.zeros((8, 128), F32) for _ in range(4)]
    row, at_lane = iota((8, 128), 0), iota((8, 128), 1)
    for (planes, count, lane, width, spot), start in zip(LEVELS, at):
        for p in range(planes):
            v, r, to = spot(p)
            if start == 30:
                slab = roll(source[p, 24:32, :], r - 6, 0)
            else:
                slab = roll(source[p, start : start + 8, :], r, 0)
            slab = roll(slab, to - lane)
            keep = (row >= r) & (row < r + count) & (at_lane >= to) & (at_lane < to + width)
            tiles[v] = jnp.where(keep, slab, tiles[v])
    return tiles


def place_y(tile, index):
    tall = jnp.concatenate([tile, jnp.zeros((8, 128), F32)], axis=0)
    tall = pltpu.roll(tall, lax.rem(4 * index + 15, 16), 0)
    return tall[0:8] + roll(tall[8:16], 64)


def relay_kernel(raw, got, out):
    index, _ = place()
    out[0:FACE, :] = got[FACE : 2 * FACE, :]
    partner = jnp.bitwise_xor(index[1], 1)
    other = got[2 * FACE : 2 * FACE + 8, :]
    out[FACE : FACE + 8, :] = place_y(raw[...], index[1]) + place_y(other, partner)


def widen_y_kernel(framed, own, got_1, got_2, after, out, raw_out, face_1, face_3):
    index, _ = place()
    even, one, two = nearest(index[1])
    total = own[FACE : FACE + 8, :] + got_2[FACE : FACE + 8, :]
    raw_out[...] = total
    a, b = got_1[0:FACE, :], got_2[0:FACE, :]
    low = jnp.where(even, 0.0, a) + jnp.where(two, b, 0.0)
    high = jnp.where(even, a, 0.0) + jnp.where(one, b, 0.0)
    for face, at in ((low, FIRST_ROWS), (high, ROWS_ABOVE)):
        for (planes, count, lane, width, spot), start in zip(LEVELS, at):
            for p in range(planes):
                v, r, to = spot(p)
                slab = roll(roll(face[8 * v : 8 * v + 8], -r, 0), lane - to)
                slab = lanes_of(slab, lane, width)
                out[p, start : start + count, :] += slab[0:count]
    even, one, _ = nearest(index[0])
    for ref, to_high in ((face_1, even), (face_3, one)):
        f = jnp.where(to_high, 30, 0)
        s = jnp.where(to_high, 14, 0)
        t = jnp.where(to_high, 6, 0)
        ref[0:40, :] = lanes_of(out[f], 0, 32) + lanes_of(roll(out[f + 1], 32), 32, 32)
        ref[0:16, :] += taps(
            [(1.0, lanes_of(roll(out[t + k, 0:16, :], 11 * k), THI + 11 * k, 11)) for k in range(5)]
        )
        ref[40:64, :] = taps(
            [(1.0, lanes_of(roll(out[s + k, 0:24, :], 18 * k - SEC), 18 * k, 18)) for k in range(4)]
        )
        ref[64:72, :] = total


def x_faces(index, got_1, got_3):
    even, one, two = nearest(index)
    a, b = got_1[0:64, :], got_3[0:64, :]
    low = jnp.where(even, 0.0, a) + jnp.where(two, b, 0.0)
    high = jnp.where(even, a, 0.0) + jnp.where(one, b, 0.0)
    planes = []
    for face, at in ((low, (0, 0, 0)), (high, (34, 18, 10))):
        for k in range(2):
            planes.append((0, at[0] + k, lanes_of(roll(face[0:40], -32 * k), 0, 32)))
        for k in range(4):
            planes.append((1, at[1] + k, lanes_of(roll(face[40:64], -18 * k), 0, 18)))
        for k in range(5):
            planes.append((2, at[2] + k, lanes_of(roll(face[0:16], -THI - 11 * k), 0, 11)))
    return planes


def widen_x_kernel(wide_y, after, got_1, got_3, out):
    index, _ = place()
    out[0:2] = jnp.zeros((2, 40, 128), F32)
    out[34:36] = jnp.zeros((2, 40, 128), F32)
    out[2:34] = wide_y[...]
    for level, at, values in x_faces(index[0], got_1, got_3):
        rows = values.shape[0]
        out[at, 0:rows, :] += roll(values, (0, SEC, THI)[level])


Z_LEVELS = ((40, 2, 0, 30), (24, 4, SEC, 14), (16, 5, THI, 6))


def chosen_lanes(values, first, count):
    at = iota(values.shape, 1)
    return jnp.where((at >= first) & (at < first + count), values, 0.0)


def own_z_kernel(wide_y, after, high, low):
    for ref, to_high in ((high, True), (low, False)):
        start = 0
        for (rows, count, lane, top), planes in zip(Z_LEVELS, (32, SPAN_2, SPAN_3)):
            first = lane + top if to_high else lane
            total = jnp.zeros((rows, 128), F32)
            for x in range(planes):
                kept = chosen_lanes(wide_y[x, 0:rows, :], first, count)
                total = total + roll(kept, count * (x + 2) - first)
            ref[start : start + rows, :] = total
            start += rows


def edge_x_kernel(own, got_2, got_1, got_3, high, low, raw_out, to_high, to_low):
    index, _ = place()
    total = None
    lane = iota((16, 128), 1)
    for step, tile in ((0, own[...]), (1, got_1[64:72, :]), (2, got_2[...]), (3, got_3[64:72, :])):
        tall = jnp.concatenate([tile, roll(tile, 64)], axis=0)
        tall = jnp.where(lane < 64, tall, 0.0)
        at = lax.rem(32 * jnp.bitwise_xor(index[0], step) + 120, 128)
        moved = pltpu.roll(tall, at, 1)
        total = moved if total is None else total + moved
    raw_out[...] = total
    planes = x_faces(index[0], got_1, got_3)
    for face, own_face, is_high in ((to_high, high, True), (to_low, low, False)):
        sums = [own_face[0:40, :], own_face[40:64, :], own_face[64:80, :]]
        for level, at, values in planes:
            _, count, _, top = Z_LEVELS[level]
            first = top if is_high else 0
            kept = chosen_lanes(values, first, count)
            sums[level] = sums[level] + roll(kept, count * at - first)
        face[0:40, :] = sums[0]
        face[40:64, :] = sums[1]
        face[0:16, :] += lanes_of(roll(sums[2], 72), 72, 55)
        face[40:56, :] += lanes_of(roll(sums[2], 88 - 55), 88, 20)
        face[64:80, :] = total


def unpack_z(message):
    third = lanes_of(roll(message[0:16], -72), 0, 55) + lanes_of(roll(message[40:56], 55 - 88), 55, 20)
    return message[0:40], message[40:64], third


def window_kernel(own, got_2, from_low, from_high, after_1, after_2, out):
    index, _ = place()
    early = lax.rem(index[2], 4) < 2
    ends = got_2[...]
    first, second, third = from_low[64:80, :], own[...], from_high[64:80, :]
    pieces = (
        jnp.where(early, first, ends),
        jnp.where(early, second, first),
        jnp.where(early, third, second),
        jnp.where(early, ends, third),
    )
    for group in range(3):
        total = None
        for q in range(min(6, 16 - 6 * group)):
            for d, piece in enumerate(pieces):
                to = 20 * q + 4 * d
                moved = lanes_of(roll(piece, to - 48 * group - 8 * q), to, 8)
                total = moved if total is None else total + moved
        out[group] = total


def divided(n, d):
    factor, bits = DIVIDE[d]
    return lax.shift_right_logical(n * factor, bits)


def build_bands(kernel, band):
    rows, columns, runs, group, outs = band
    row = iota((rows, 128), 0)
    shift = jnp.full((rows, 128), 99, jnp.int32)
    point = jnp.full((rows, 128), 99, jnp.int32)
    for start, count, offset in runs:
        at = row - start
        a = divided(at, count)
        inside = (at >= 0) & (at < 5 * count)
        shift = jnp.where(inside, a, shift)
        point = jnp.where(inside, offset + at - a * count, point)
    chosen = (shift == iota((rows, 128), 1)).astype(F32).astype(BF16)
    column = iota((8, columns), 1)
    block = divided(column, group)
    out_at = (column - block * group)[0:1]
    block = jnp.where((column - block * group) < outs, block, 9)
    sub = iota((8, columns), 0)
    entry = jnp.concatenate([point] * (columns // 128), axis=1) - out_at
    total_high = jnp.zeros((rows, columns), F32)
    total_low = jnp.zeros((rows, columns), F32)
    for c in range(5):
        source = jnp.zeros((8, columns), F32)
        for b in range(5):
            column_of = jnp.zeros((8, columns), F32)
            for a in range(5):
                column_of = jnp.where(sub == a, kernel[a, b, c], column_of)
            source = jnp.where(block == b, column_of, source)
        source = jnp.concatenate([source, jnp.zeros((120, columns), F32)], axis=0)
        high, low = split(source)
        fits = entry == c
        total_high = jnp.where(fits, dot(chosen, high), total_high)
        total_low = jnp.where(fits, dot(chosen, low), total_low)
    return total_high.astype(BF16), total_low.astype(BF16)


def bands_kernel(bands, *refs):
    kernels, outs = refs[: len(bands)], refs[len(bands) :]
    for n, (kernel, band) in enumerate(zip(kernels, bands)):
        high, low = build_bands(kernel, band)
        outs[2 * n][...] = high
        outs[2 * n + 1][...] = low


def green_kernel(factors, packed, green_high, green_low, rise, framed, block_high, block_low):
    index, sizes = place()
    row, lane = iota((64, 128), 0), iota((64, 128), 1)
    delta_x = (lane // 8).astype(F32)
    delta_z = (4 * index[2] - 1 + lane % 8 - row).astype(F32)
    plain = delta_z * delta_z + (1.0 + delta_x * delta_x)
    for apart in range(18):
        high, low = split(0.0625 * lax.rsqrt(plain + float(apart * apart)))
        block_high[apart] = high
        block_low[apart] = low
    for ty in range(SPAN_4):
        columns = slice(128 * ty, 128 * ty + 128)
        for sy in range(16):
            apart = jnp.abs(4 * index[1] - 1 + ty - sy)
            first = sy % 8 * 128 + sy // 8 * 64
            green_high[first : first + 64, columns] = block_high[apart]
            green_low[first : first + 64, columns] = block_low[apart]
    variant = [
        jnp.where(index[d] == 0, 1, 0) + jnp.where(index[d] == sizes[d] - 1, 2, 0) for d in range(3)
    ]
    factor_x, factor_y = factors[variant[0]], factors[4 + variant[1]]
    kept = as_rows(factor_x[:, None, :] * factor_y[None, :, :])
    high, low = split(kept)
    rise[:, 0:128] = (high.astype(F32) + roll(low.astype(F32), 64)).astype(BF16)
    rise[:, 128:256] = high
    framed[:, 0:2, :] = jnp.zeros((32, 2, 128), F32)
    framed[:, 34:40, :] = jnp.zeros((32, 6, 128), F32)
    framed[:, 2:34, :] = packed[...]


def prolong_rows(source, target, count, whole):
    size = target.shape[1] // 2
    q0 = source[:, 0:size, :]
    q1 = source[:, 1 : size + 1, :]
    q2 = source[:, 2 : size + 2, :]
    even = 0.75 * q1 + 0.125 * (q0 + q2)
    odd = 0.5 * (q0 + q1) if whole else 0.5 * (q1 + q2)
    target[:, pl.ds(1 if whole else 0, size, stride=2), :] = even
    target[:, pl.ds(0 if whole else 1, size, stride=2), :] = odd


def prolong_plane(read, p, whole):
    half = p // 2
    if (p % 2 == 1) == whole:
        return 0.75 * read(half + 1) + 0.125 * (read(half) + read(half + 2))
    first = half if whole else half + 1
    return 0.5 * (read(first) + read(first + 1))


def near_kernel(
    wide, from_low, from_high, b1h, b1l, b2h, b2l, b3h, b3l, prol_2, prol_1,
    out,
    near_1, near_2, near_3, tall_3, tall_3y, tall_2, tall_2y,
):
    where = place()
    index, sizes = where
    low_faces = unpack_z(jnp.where(index[2] == 0, 0.0, from_low[0:64, :]))
    high_faces = unpack_z(jnp.where(index[2] == sizes[2] - 1, 0.0, from_high[0:64, :]))

    def halo(x, level, count, low_at, high_at):
        low = roll(low_faces[level], low_at - count * x)
        high = roll(high_faces[level], high_at - count * x)
        return lanes_of(low, low_at, 5 * count) + lanes_of(high, high_at, 5 * count)

    planes = [lanes_of(wide[x, 0:16, :], THI, 11) for x in range(15)]
    left = []
    for x in range(SPAN_3):
        main = taps([(1.0, roll(planes[x + a], 11 * a - THI)) for a in range(5)])
        left.append(main + halo(x, 2, 5, 64, 96))
    left = jnp.concatenate(left, axis=0)
    near_3[...] = jnp.zeros_like(near_3)
    near_3[:, 0:16, :] = dot_split(left, b3h[...], b3l[...]).reshape(SPAN_3, 16, 128)
    third = taps([(1.0, roll(near_3[:, b : b + 16, :], -16 * b)) for b in range(5)])
    third = jnp.where(inside_mask(third.shape, SPAN_3, 9, where), third, 0.0)
    tall_3[...] = jnp.zeros_like(tall_3)
    tall_3[:, 0:16, :] = dot_exact(as_rows(third), prol_2[...]).reshape(SPAN_3, 16, 128)
    prolong_rows(tall_3, tall_3y, SPAN_2, True)

    planes = [lanes_of(wide[x, 0:24, :], SEC, 18) for x in range(22)]
    left_a, left_b = [], []
    for x in range(SPAN_2):
        left_a.append(taps([(1.0, roll(planes[x + a], 18 * a - SEC)) for a in range(5)]))
        left_b.append(halo(x, 1, 4, 0, 32))
    left = jnp.concatenate(
        [jnp.concatenate(left_a, axis=0), jnp.concatenate(left_b, axis=0)], axis=1
    )
    near_2[...] = jnp.zeros_like(near_2)
    near_2[:, 0:24, :] = dot_split(left, b2h[...], b2l[...]).reshape(SPAN_2, 24, 128)
    second = taps([(1.0, roll(near_2[:, b : b + 24, :], -24 * b)) for b in range(5)])
    raised = jnp.stack(
        [prolong_plane(lambda x: tall_3y[x], p, True) for p in range(SPAN_2)], axis=0
    )
    second = jnp.where(inside_mask(second.shape, SPAN_2, 17, where), second + raised, 0.0)
    tall_2[...] = jnp.zeros_like(tall_2)
    tall_2[:, 0:24, :] = dot_exact(as_rows(second), prol_1[...]).reshape(SPAN_2, 24, 128)
    prolong_rows(tall_2, tall_2y, 32, False)

    planes = [lanes_of(wide[x], 0, 32) for x in range(36)]
    left_a, left_b = [], []
    for x in range(32):
        left_a.append(taps([(1.0, roll(planes[x + a], 32 * a)) for a in range(4)]))
        left_b.append(planes[x + 4] + halo(x, 0, 2, 32, 64))
    left = jnp.concatenate(
        [jnp.concatenate(left_a, axis=0), jnp.concatenate(left_b, axis=0)], axis=1
    )
    near_1[...] = dot_split(left, b1h[...], b1l[...]).reshape(32, 40, 256)
    for x in range(32):
        first = taps(
            [(1.0, roll(near_1[x, b : b + 32, 0:128], -32 * b)) for b in range(4)]
            + [(1.0, near_1[x, 4:36, 128:256])]
        )
        out[x] = first + prolong_plane(lambda q: tall_2y[q], x, False)


def top_kernel(
    base, piece_0, piece_1, piece_2, piece_3, green_high, green_low, rise, qz,
    out_hbm,
    fourth, out, sems,
):
    index, sizes = place()
    lane = iota((8, 128), 1)
    ring = lax.rem(index[2], 4)
    first = 4 * (ring == 3).astype(jnp.int32) - 4 * (ring == 0).astype(jnp.int32) + 127
    sources = [lax.rem(16 * lax.rem(index[2] // 4 + step, 4) + first, 128) for step in (0, 1, 2, 3)]
    for x in range(16):
        total = None
        for piece, at in zip((piece_0, piece_1, piece_2, piece_3), sources):
            kept = lanes_of(piece[x // 6], 20 * (x % 6), 20)
            moved = pltpu.roll(kept, lax.rem(at + 128 - 20 * (x % 6), 128), 1)
            total = moved if total is None else total + moved
        total = total + roll(total, 64)
        fourth[x] = jnp.where(lane < 64, total[0:8], total[8:16])
    total = jnp.zeros((32, 128 * SPAN_4), F32)
    extra = jnp.zeros((16, 128 * SPAN_4), F32)
    for s in range(0, 8, 2):
        left = jnp.concatenate([fourth[:, s, :], fourth[:, s + 1, :]], axis=1)
        high, low = split(left)
        rows = slice(128 * s, 128 * s + 256)
        total = total + dot(jnp.concatenate([high, low], axis=0), green_high[rows, :])
        extra = extra + dot(high, green_low[rows, :])
    sums = total[0:16] + (total[16:32] + extra)
    row, lane = iota((16, 128), 0), iota((16, 128), 1)
    tops = []
    for tx in range(SPAN_4):
        keep = jnp.abs(4 * index[0] - 1 + tx - row) == lane // 8
        for ty in range(SPAN_4):
            picked = jnp.where(keep, sums[:, 128 * ty : 128 * ty + 128], 0.0)
            tops.append(jnp.sum(picked, axis=0, keepdims=True))
        tops.append(jnp.zeros((1, 128), F32))
    tops = jnp.concatenate(tops + [jnp.zeros((8, 128), F32)], axis=0)
    variant = jnp.where(index[2] == 0, 1, 0) + jnp.where(index[2] == sizes[2] - 1, 2, 0)
    high, low = split(dot_split(tops, qz[variant], qz[4 + variant]))
    right = jnp.concatenate([high, high, low, jnp.zeros_like(low)], axis=0)
    copies = []
    for part in range(4):
        planes = slice(8 * part, 8 * part + 8)
        far = dot(rise[256 * part : 256 * part + 256, :], right)
        out[planes] = (base[planes] + far.reshape(8, 32, 128))[:, :, 0:32]
        copies.append(pltpu.make_async_copy(out.at[planes], out_hbm.at[planes], sems.at[part]))
        copies[-1].start()
    for copy in copies:
        copy.wait()


def call(kernel, outs, ins, scratch=(), megabytes=16, spaces=None, out_spaces=None, aliases=None, flops=1000000):
    spaces, out_spaces = spaces or {}, out_spaces or {}
    single = not isinstance(outs, tuple)
    out_specs = [out_spaces.get(i, VMEM) for i in range(1 if single else len(outs))]
    return pl.pallas_call(
        kernel,
        out_shape=outs,
        in_specs=[spaces.get(i, VMEM) for i in range(len(ins))],
        out_specs=out_specs[0] if single else out_specs,
        scratch_shapes=list(scratch),
        input_output_aliases=aliases or {},
        compiler_params=pltpu.CompilerParams(vmem_limit_bytes=int(megabytes * 2**20)),
        cost_estimate=pl.CostEstimate(flops=flops, bytes_accessed=2**21, transcendentals=0),
    )(*ins)


def shape(*dims, dtype=F32):
    return jax.ShapeDtypeStruct(dims, dtype)


def exchange(values, axis, steps):
    size = lax.axis_size(axis)
    return [
        lax.ppermute(value, axis, [(i, i ^ step) for i in range(size)])
        for value, step in zip(values, steps)
    ]


def turn(value, by):
    size_y, size_z = lax.axis_size("gy"), lax.axis_size("gz")
    half = size_y // 2
    pairs = []
    for core in range(half):
        ring = [(high * half + core) * size_z + z for high in range(2) for z in range(size_z)]
        pairs += [(ring[n], ring[(n + by) % len(ring)]) for n in range(len(ring))]
    return lax.ppermute(value, ("gy", "gz"), pairs)


def banded(bands, *kernels, flops=10**9):
    return call(
        functools.partial(bands_kernel, bands),
        tuple(shape(band[0], band[1], dtype=BF16) for band in bands for _ in range(2)),
        kernels,
        spaces={n: SMEM for n in range(len(kernels))},
        flops=flops,
    )


def shards(charges, counts, slots, spline, kernel_fine, kernel_mid, kernel_coarse):
    cells = charges.shape[0]
    packed, raw, face = call(
        deposit_kernel,
        (shape(32, 32, 128), shape(8, 128), shape(2 * FACE + 8, 128)),
        (256 * slots + counts, charges, spline.reshape(cells * 12, ATOMS)),
        (
            pltpu.VMEM((32, 32, 128), F32),
            pltpu.VMEM((cells, ATOMS), F32),
            pltpu.VMEM((cells * 12, 128), BF16),
            pltpu.VMEM((cells * 12, 128), F32),
            pltpu.VMEM((64, cells), F32),
            pltpu.VMEM((32, 32, 128), F32),
            pltpu.VMEM((SPAN_2, 56, 128), F32),
            pltpu.VMEM((SPAN_3, 40, 128), F32),
            pltpu.VMEM((SPAN_4, 24, 128), F32),
            pltpu.SemaphoreType.DMA((5,)),
        ),
        spaces={1: HBM, 2: HBM},
        out_spaces={0: ANY},
        megabytes=53.75,
    )
    (got_1,) = exchange((face,), "gy", (1,))
    relay = call(relay_kernel, shape(FACE + 8, 128), (raw, got_1))
    (got_2,) = exchange((relay,), "gy", (2,))
    qx, qy, qz = composites()
    qz_high = qz.astype(BF16)
    qz_low = (qz - qz_high.astype(np.float32)).astype(BF16)
    green_high, green_low, rise, framed = call(
        green_kernel,
        (
            shape(1024, 128 * SPAN_4, dtype=BF16),
            shape(1024, 128 * SPAN_4, dtype=BF16),
            shape(1024, 256, dtype=BF16),
            shape(32, 40, 128),
        ),
        (jnp.asarray(np.concatenate([qx, qy])), packed),
        (pltpu.VMEM((18, 64, 128), BF16), pltpu.VMEM((18, 64, 128), BF16)),
    )
    wide_y, raw, face_1, face_3 = call(
        widen_y_kernel,
        (shape(32, 40, 128), shape(8, 128), shape(72, 128), shape(72, 128)),
        (framed, relay, got_1, got_2, rise),
        spaces={4: ANY},
        aliases={0: 0},
    )
    got_3, got_1, got_2 = exchange((face_3, face_1, raw), "gx", (3, 1, 2))
    bands_1 = banded(BANDS[:1], kernel_fine)
    own_high, own_low = call(
        own_z_kernel, (shape(80, 128), shape(80, 128)), (wide_y, bands_1[0]), spaces={1: ANY}
    )
    wide_x = call(
        widen_x_kernel, shape(36, 40, 128), (wide_y, got_2, got_1, got_3), spaces={1: ANY}
    )
    raw, to_high, to_low = call(
        edge_x_kernel,
        (shape(16, 128), shape(80, 128), shape(80, 128)),
        (raw, got_2, got_1, got_3, own_high, own_low),
    )
    from_low, from_high = turn(to_high, 1), turn(to_low, -1)
    (got_2,) = exchange((raw,), "gz", (2,))
    bands_2 = banded(BANDS[1:], kernel_mid, kernel_coarse)
    window = call(
        window_kernel,
        shape(3, 16, 128),
        (raw, got_2, from_low, from_high, bands_2[0], wide_x),
        spaces={4: ANY, 5: ANY},
    )
    pieces = [window] + [turn(window, by) for by in (-4, 8, 4)]
    base = call(
        near_kernel,
        shape(32, 32, 128),
        (wide_x, from_low, from_high, *bands_1, *bands_2, jnp.asarray(PROL_2, BF16), jnp.asarray(PROL_1, BF16)),
        (
            pltpu.VMEM((32, 40, 256), F32),
            pltpu.VMEM((SPAN_2, 32, 128), F32),
            pltpu.VMEM((SPAN_3, 24, 128), F32),
            pltpu.VMEM((SPAN_3, 24, 128), F32),
            pltpu.VMEM((SPAN_3, 24, 128), F32),
            pltpu.VMEM((SPAN_2, 32, 128), F32),
            pltpu.VMEM((SPAN_2, 32, 128), F32),
        ),
    )
    return call(
        top_kernel,
        shape(32, 32, 32),
        (base, *pieces, green_high, green_low, rise, jnp.asarray(np.concatenate([qz_high, qz_low]))),
        (
            pltpu.VMEM((16, 8, 128), F32),
            pltpu.VMEM((32, 32, 32), F32),
            pltpu.SemaphoreType.DMA((4,)),
        ),
        out_spaces={0: ANY},
    )


def solution(mesh):
    return jax.shard_map(
        shards,
        mesh=mesh,
        in_specs=(
            P(("gx", "gy", "gz"), None),
            P(("gx", "gy", "gz")),
            P(("gx", "gy", "gz")),
            P(("gx", "gy", "gz"), None, None, None),
            P(),
            P(),
            P(),
        ),
        out_specs=P("gx", "gy", "gz"),
        check_vma=False,
    )
```
